32 devices in a mesh: rows: 8 (over z, x), tm: 4 (over y, core).
Axes of the slice: x: 2, y: 2, z: 4, core: 2. Of those that a mesh axis runs over, the one named last changes fastest.
Arguments:
- frames: bfloat16 [16, 16, 32, 256], P('tm', 'rows'), may hold values from -45 to 45, as said below
- norm_gain: float32 [256], replicated, may hold values from 0.1 to 1.9
- conv_weight: bfloat16 [3, 3, 3, 256, 256], replicated, may hold values from -0.078125 to 0.078125
- conv_bias: float32 [256], replicated, may hold values from -3 to 3
- latent_grad: bfloat16 [16, 8, 16, 256], P('tm', None, 'rows'), may hold values from -6 to 6
Outputs:
- latent: bfloat16 [16, 8, 16, 256], P('tm', None, 'rows')
- frames_grad: bfloat16 [16, 16, 32, 256], P('tm', 'rows')
- weight_grad: float32 [3, 3, 3, 256, 256], P(None, None, None, 'tm')
- gain_grad: float32 [256], P('tm')
- bias_grad: float32 [256], P('tm')
The draws below stay inside these ranges and needn't reach their ends.
Inputs may be any that keep to these rules, and one draw needn't show every extreme that they name: `frames`: features of the clip.
All inputs are finite; a program needn't handle non-finite values.
Results may differ from the reference program's by a relative error of at most 0.0045.
Values may be sent and summed in bfloat16 or wider, within the bound.
No kernel may reach another device: no remote copies, remote signals or barrier semaphores. Data moves between devices by JAX's collectives and lax.ppermute only.
A program may use at most 128 MiB of HBM per device.

```python
import math
import jax
import jax.numpy as jnp
from jax import lax

C = 256
FRAMES = 16
LAT_ROWS = 8
LAT_COLS = 16
ROWS = 16
COLS = 32


def draw_frames(key, part):
    key_base, key_cell, key_chan = jax.random.split(key, 3)
    shape = (FRAMES, ROWS, COLS, C)
    cell_scale = jnp.exp(jax.random.uniform(key_cell, (FRAMES, ROWS, COLS, 1), jnp.float32, math.log(0.3), math.log(3.0)))
    chan_scale = jnp.exp(jax.random.uniform(key_chan, (C,), jnp.float32, math.log(0.3), math.log(3.0)))
    base = jnp.clip(jax.random.normal(key_base, shape, jnp.float32), -5.0, 5.0)
    return (base * cell_scale * chan_scale).astype(jnp.bfloat16)


def shard_levels(key, extent, pieces, low, largest):
    def one(axis_at, parts):
        heights = jax.random.uniform(jax.random.fold_in(jax.random.fold_in(key, 6), axis_at), (parts,), jnp.float32, low / len(pieces), largest / len(pieces))
        return jnp.repeat(jnp.exp(heights), extent[axis_at] // parts).reshape((-1,) + (1,) * (len(extent) - axis_at - 1))

    gain = one(*pieces[0])
    for cut in pieces[1:]:
        gain = gain * one(*cut)
    return gain


def noise(rng, shape, width, bound, pieces=(), kind=jnp.bfloat16):
    result = jax.random.normal(rng, shape, jnp.float32) * width
    if len(pieces) > 0:
        result = shard_levels(rng, shape, pieces, -0.22, 0.18) * result
    return jnp.clip(result, min=-bound, max=bound).astype(kind)


def setup_inputs(seed: int = 0) -> dict:
    streams_of = jax.random.split(jax.random.key(seed), 6)
    frames = draw_frames(jax.random.fold_in(streams_of[5], 71), 0)
    norm_gain = jnp.clip(1.0 + 0.18 * jax.random.normal(streams_of[1], (C,), jnp.float32), 0.1, 1.9)
    conv_weight = noise(streams_of[2], (3, 3, 3, C, C), (27 * C) ** -0.5, 0.078125)
    conv_bias = noise(streams_of[3], (C,), 0.5, 3.0, (), jnp.float32)
    latent_grad = noise(streams_of[4], (FRAMES, LAT_ROWS, LAT_COLS, C), 1.0, 6.0, ((0, 4), (2, 8)))
    return {"frames": frames, "norm_gain": norm_gain, "conv_weight": conv_weight, "conv_bias": conv_bias, "latent_grad": latent_grad}


def reference(frames, norm_gain, conv_weight, conv_bias, latent_grad):
    signal = frames.astype(jnp.float32)
    inv_rms = lax.rsqrt(lax.optimization_barrier(jnp.mean(signal * signal, axis=-1, keepdims=True)) + 1e-06)
    unit = signal * inv_rms
    normed = unit * norm_gain
    hidden = jax.nn.silu(normed).astype(jnp.bfloat16)
    frame_count, row_count, col_count, channels = hidden.shape
    lat_rows = row_count // 2
    lat_cols = col_count // 2
    padded = jnp.pad(hidden, ((2, 0), (0, 1), (0, 1), (0, 0)))
    grad_flat = latent_grad.reshape(-1, channels)
    running = jnp.zeros((frame_count * lat_rows * lat_cols, channels), jnp.float32)
    spread_sum = jnp.zeros((frame_count + 2, row_count + 2, col_count + 2, channels), jnp.float32)
    blocks = []
    for tap_t in range(3):
        for tap_r in range(3):
            for tap_c in range(3):
                weight_tap = conv_weight[tap_t, tap_r, tap_c]
                window_piece = padded[tap_t:tap_t + frame_count, tap_r:tap_r + 2 * lat_rows:2, tap_c:tap_c + 2 * lat_cols:2]
                window_piece = window_piece.reshape(-1, channels)
                running = running + jnp.dot(window_piece, weight_tap, preferred_element_type=jnp.float32)
                blocks.append(jnp.dot(window_piece.T, grad_flat, preferred_element_type=jnp.float32))
                back_term = jnp.dot(grad_flat, weight_tap.T, preferred_element_type=jnp.float32)
                back_term = back_term.reshape(frame_count, lat_rows, lat_cols, channels)
                spread_sum = spread_sum.at[tap_t:tap_t + frame_count, tap_r:tap_r + 2 * lat_rows:2, tap_c:tap_c + 2 * lat_cols:2].add(back_term)
    latent = (running + conv_bias).reshape(frame_count, lat_rows, lat_cols, channels).astype(jnp.bfloat16)
    weight_grad = jnp.stack(blocks).reshape(3, 3, 3, channels, channels)
    bias_grad = lax.optimization_barrier(jnp.sum(grad_flat.astype(jnp.float32), axis=0))
    hidden_grad = spread_sum[2:, :row_count, :col_count]
    sigma = jax.nn.sigmoid(normed)
    normed_grad = hidden_grad * sigma * (1.0 + normed * (1.0 - sigma))
    gain_grad = lax.optimization_barrier(jnp.sum(normed_grad * unit, axis=(0, 1, 2)))
    unit_grad = normed_grad * norm_gain
    frames_grad = inv_rms * (unit_grad - unit * lax.optimization_barrier(jnp.mean(unit_grad * unit, axis=-1, keepdims=True)))
    return (latent, frames_grad.astype(jnp.bfloat16), weight_grad, gain_grad, bias_grad)
```

```python
import functools

import jax
import jax.numpy as jnp
from jax import lax
from jax.experimental import pallas as pl
from jax.experimental.pallas import tpu as pltpu
from jax.sharding import PartitionSpec as P

EPS = 1e-06
TAPS = [(a, b, c) for a in range(3) for b in range(3) for c in range(3)]
VMEM_LIMIT = 48 * 1024 * 1024


def shifted(value, axis, steps):
    count = lax.axis_size(axis)
    leading, last = (max(0, -steps), min(count, count - steps))
    return lax.ppermute(value, axis, [(source, source + steps) for source in range(leading, last)])


def contract_out(grad_piece, weight_tap):
    return lax.dot_general(
        grad_piece, weight_tap, (((1,), (1,)), ((), ())), preferred_element_type=jnp.float32
    )


def reduced_form(frames, norm_gain, conv_weight, conv_bias, latent_grad):
    signal = frames.astype(jnp.float32)
    inv_rms = lax.rsqrt(jnp.mean(signal * signal, axis=-1, keepdims=True) + EPS)
    unit = signal * inv_rms
    normed = unit * norm_gain
    hidden = jax.nn.silu(normed).astype(jnp.bfloat16)
    frame_count, row_count, col_count, channels = hidden.shape
    lat_rows = row_count // 2
    lat_cols = col_count // 2
    cached = shifted(hidden[frame_count - 2 :], "tm", 1)
    stacked = jnp.concatenate([cached, hidden], axis=0)
    row_under = shifted(stacked[:, :1], "rows", -1)
    extended = jnp.concatenate([stacked, row_under], axis=1)
    extended = jnp.pad(extended, ((0, 0), (0, 0), (0, 1), (0, 0)))
    grad_rows = lax.all_to_all(latent_grad, "rows", split_axis=1, concat_axis=2, tiled=True)
    grad_flat = grad_rows.reshape(-1, channels)
    running = jnp.zeros((frame_count * lat_rows * lat_cols, channels), jnp.float32)
    blocks = []
    for tap_t, tap_r, tap_c in TAPS:
        window_piece = extended[
            tap_t : tap_t + frame_count,
            tap_r : tap_r + 2 * lat_rows : 2,
            tap_c : tap_c + 2 * lat_cols : 2,
        ]
        window_piece = window_piece.reshape(-1, channels)
        running = running + jnp.dot(
            window_piece, conv_weight[tap_t, tap_r, tap_c], preferred_element_type=jnp.float32
        )
        blocks.append(
            lax.dot_general(
                window_piece,
                grad_flat,
                (((0,), (0,)), ((), ())),
                preferred_element_type=jnp.float32,
            )
        )
    latent_rows = (
        (running + conv_bias)
        .reshape(frame_count, lat_rows, lat_cols, channels)
        .astype(jnp.bfloat16)
    )
    latent = lax.all_to_all(latent_rows, "rows", split_axis=2, concat_axis=1, tiled=True)
    weight_local = jnp.stack(blocks).reshape(3, 3, 3, channels, channels)
    bias_local = jnp.sum(grad_flat.astype(jnp.float32), axis=0)
    following = shifted(grad_rows[:2], "tm", -1)
    grad_ext = jnp.concatenate([grad_rows, following], axis=0)
    above_row = shifted(grad_ext, "rows", 1)
    grad_ext = jnp.concatenate([above_row, grad_ext], axis=1)
    grad_ext = jnp.pad(grad_ext, ((0, 0), (0, 0), (1, 0), (0, 0)))
    parity_sums = {}
    for tap_t, tap_r, tap_c in TAPS:
        row_start = 1 - tap_r // 2
        col_start = 1 - tap_c // 2
        grad_piece = grad_ext[
            2 - tap_t : 2 - tap_t + frame_count,
            row_start : row_start + lat_rows,
            col_start : col_start + lat_cols,
        ]
        term = contract_out(grad_piece.reshape(-1, channels), conv_weight[tap_t, tap_r, tap_c])
        label = (tap_r % 2, tap_c % 2)
        parity_sums[label] = parity_sums[label] + term if label in parity_sums else term
    shaped = {}
    for label in parity_sums:
        shaped[label] = parity_sums[label].reshape(frame_count, lat_rows, lat_cols, channels)
    even_rows = jnp.stack([shaped[0, 0], shaped[0, 1]], axis=3)
    odd_rows = jnp.stack([shaped[1, 0], shaped[1, 1]], axis=3)
    hidden_grad = jnp.stack([even_rows, odd_rows], axis=2).reshape(
        frame_count, row_count, col_count, channels
    )
    sigma = jax.nn.sigmoid(normed)
    normed_grad = hidden_grad * sigma * (1.0 + normed * (1.0 - sigma))
    gain_local = jnp.sum(normed_grad * unit, axis=(0, 1, 2))
    unit_grad = normed_grad * norm_gain
    frames_grad = inv_rms * (unit_grad - unit * jnp.mean(unit_grad * unit, axis=-1, keepdims=True))
    totals = lax.psum((weight_local, gain_local, bias_local), "rows")
    weight_grad, gain_grad, bias_grad = (
        lax.psum_scatter(totals[0], "tm", scatter_dimension=3, tiled=True),
        lax.psum_scatter(totals[1], "tm", scatter_dimension=0, tiled=True),
        lax.psum_scatter(totals[2], "tm", scatter_dimension=0, tiled=True),
    )
    return (latent, frames_grad.astype(jnp.bfloat16), weight_grad, gain_grad, bias_grad)


def mm(left, right):
    return jnp.dot(left, right, preferred_element_type=jnp.float32)


def mm_t(left, right):
    return lax.dot_general(
        left, right, (((1,), (1,)), ((), ())), preferred_element_type=jnp.float32
    )


def normalised(frames, gain):
    signal = frames.astype(jnp.float32)
    inv_rms = lax.rsqrt(jnp.mean(signal * signal, axis=-1, keepdims=True) + EPS)
    unit = signal * inv_rms
    return inv_rms, unit, unit * gain


def hidden_kernel(F, J, T, frames, gain, planes, send, cached, under, corner, tmp):
    channels = frames.shape[1]
    part = channels // T
    _, _, normed = normalised(frames[...], gain[...])
    value = normed / (1.0 + jnp.exp(-normed))
    tmp[0] = value[:, : channels // 2]
    tmp[1] = value[:, channels // 2 :]
    for rp in range(2):
        pair = []
        for cp in range(2):
            rows = [
                jnp.concatenate(
                    [
                        tmp[half, pl.ds((t * 2 + rp) * 2 * J + cp, J, stride=2), :]
                        for half in range(2)
                    ],
                    axis=1,
                )
                for t in range(F)
            ]
            plane = jnp.concatenate(rows, axis=0)
            pair.append(plane)
            plane = plane.astype(jnp.bfloat16)
            planes[rp, cp] = plane
            cached[rp, cp] = plane[(F - 2) * J :]
            if rp == 0:
                under[cp] = plane
                corner[cp] = plane[(F - 2) * J :]
        for d in range(T):
            both = [p[:, d * part : (d + 1) * part] for p in pair]
            send[d, rp] = jnp.concatenate(both, axis=1).astype(jnp.bfloat16)


def permutation(shape, meet):
    row = lax.broadcasted_iota(jnp.int32, shape, 0)
    col = lax.broadcasted_iota(jnp.int32, shape, 1)
    return jnp.where(meet(row, col), 1.0, 0.0).astype(jnp.bfloat16)


def latent_kernel(F, J, R, planes, cached, under, corner, weight, bias, out, ext):
    rows = (F + 2) * J
    last = lax.broadcasted_iota(jnp.int32, (rows, 1), 0) % J == J - 1
    for b in range(3):
        for cp in range(2):
            before, now = (corner[cp], under[cp]) if b == 2 else (cached[b, cp], planes[b, cp])
            full = jnp.concatenate([before, now], axis=0)
            ext[b, cp] = full
            if cp == 0:
                moved = pltpu.roll(full.astype(jnp.float32), rows - 1, 0)
                ext[b, 2] = jnp.where(last, 0.0, moved).astype(jnp.bfloat16)
    total = jnp.zeros(out.shape, jnp.float32) + bias[...]
    for n, (a, b, c) in enumerate(TAPS):
        total = total + mm(ext[b, c, a * J : (a + F) * J, :], weight[n])
    jl = J // R
    order = permutation(
        (F * J, F * J),
        lambda o, s: (o // jl % F == s // J) & (o // (F * jl) * jl + o % jl == s % J),
    )
    out[...] = mm(order, total.astype(jnp.bfloat16)).astype(jnp.bfloat16)


def frames_kernel(
    F, J, R, T, place, gathered, weight, frames, gain,
    grads, grads_right, frames_grad, gain_part, bias_sum, tmp,
):
    channels = frames.shape[1]
    jl = J // R
    chunk = 2 * R * J
    order = permutation(
        (chunk, chunk),
        lambda o, s: (o // (2 * J) == s // jl % R)
        & (o // J % 2 == s // (jl * R) % 2)
        & (o % J == s // (2 * jl * R) * jl + s % jl),
    )
    order_right = permutation(
        (chunk, chunk),
        lambda o, s: (o // (2 * J) == s // jl % R)
        & (o // J % 2 == s // (jl * R) % 2)
        & (o % J == s // (2 * jl * R) * jl + s % jl + 1),
    )
    frames_all = F * T
    for ref in (grads, grads_right):
        ref[0] = jnp.zeros(ref.shape[1:], jnp.bfloat16)
        ref[:, frames_all * J :, :] = jnp.zeros((R + 1, 2 * J, channels), jnp.bfloat16)
    total = jnp.zeros((1, channels), jnp.float32)
    for pair in range(frames_all // 2):
        block, half = divmod(pair * 2, F)
        start = half * R * jl
        source = jnp.concatenate(
            [gathered[s, block, start : start + 2 * R * jl, :] for s in range(R)], axis=0
        )
        total = total + jnp.sum(source.astype(jnp.float32), axis=0, keepdims=True)
        for ref, matrix in ((grads, order), (grads_right, order_right)):
            moved = mm(matrix, source).astype(jnp.bfloat16)
            for i in range(R):
                ref[i + 1, pair * 2 * J : (pair + 1) * 2 * J, :] = moved[
                    i * 2 * J : (i + 1) * 2 * J
                ]
    bias_sum[...] = total
    row, block = place[0], place[1]
    sums = {}
    for n, (a, b, c) in enumerate(TAPS):
        ref = grads_right if c == 2 else grads
        start = pl.multiple_of((block * F + 2 - a) * J, 16)
        piece = ref[row + (0 if b == 2 else 1), pl.ds(start, F * J), :]
        term = mm_t(piece, weight[n])
        key = (b % 2, c % 2)
        sums[key] = sums[key] + term if key in sums else term
    for (rp, cp), value in sums.items():
        for t in range(F):
            for half in range(2):
                lanes = slice(half * channels // 2, (half + 1) * channels // 2)
                tmp[half, pl.ds((t * 2 + rp) * 2 * J + cp, J, stride=2), :] = value[
                    t * J : (t + 1) * J, lanes
                ]
    hidden_grad = jnp.concatenate([tmp[0], tmp[1]], axis=1)
    inv_rms, unit, normed = normalised(frames[...], gain[...])
    sigma = 1.0 / (1.0 + jnp.exp(-normed))
    normed_grad = hidden_grad * sigma * (1.0 + normed * (1.0 - sigma))
    gain_part[...] = jnp.sum(normed_grad * unit, axis=0, keepdims=True)
    unit_grad = normed_grad * gain[...]
    mean = jnp.mean(unit_grad * unit, axis=-1, keepdims=True)
    frames_grad[...] = (inv_rms * (unit_grad - unit * mean)).astype(jnp.bfloat16)


def weight_kernel(R, part, hidden, grads, grads_right, out, turned):
    blocks, _, span, lanes = hidden.shape[1:]
    depth = blocks * span
    zero = jnp.zeros((lanes, depth), jnp.bfloat16)
    turned[2, :, (R - 1) * depth :] = zero
    for i in range(R):
        for rp in range(2):
            block = jnp.concatenate([hidden[i, s, rp] for s in range(blocks)], axis=0)
            block = block.T
            turned[rp, :, i * depth : (i + 1) * depth] = block
            if rp == 0 and i > 0:
                turned[2, :, (i - 1) * depth : i * depth] = block
    step = span * blocks
    shift = grads.shape[1] - step
    for a in range(3):
        start = (2 - a) * shift // 2
        for c, ref in ((0, grads), (2, grads_right)):
            right = ref[1:, start : start + depth, :].reshape(R * depth, -1)
            if c == 0:
                left = turned[...].reshape(3 * lanes, R * depth)
            else:
                left = turned[:, :part, :].reshape(3 * part, R * depth)
            value = mm(left, right)
            for b in range(3):
                if c == 0:
                    for cp in range(2):
                        at = b * lanes + cp * part
                        out[(a * 3 + b) * 3 + cp] = value[at : at + part]
                else:
                    out[(a * 3 + b) * 3 + 2] = value[b * part : (b + 1) * part]


def call(kernel, outs, scratch, flops, moved, smem=0, operands=0):
    vmem = pl.BlockSpec(memory_space=pltpu.VMEM)
    specs = [pl.BlockSpec(memory_space=pltpu.SMEM)] * smem + [vmem] * (operands - smem)
    return pl.pallas_call(
        kernel,
        out_shape=[jax.ShapeDtypeStruct(s, d) for s, d in outs],
        in_specs=specs,
        out_specs=[vmem] * len(outs),
        scratch_shapes=[pltpu.VMEM(s, d) for s, d in scratch],
        compiler_params=pltpu.CompilerParams(vmem_limit_bytes=VMEM_LIMIT),
        cost_estimate=pl.CostEstimate(flops=flops, bytes_accessed=moved, transcendentals=0),
    )


def gathered_form(frames, norm_gain, conv_weight, conv_bias, latent_grad):
    bf16, f32 = jnp.bfloat16, jnp.float32
    F, row_count, col_count, C = frames.shape
    R, T = lax.axis_size("rows"), lax.axis_size("tm")
    J = col_count // 2
    span = F * J
    part = C // T
    gain = norm_gain.reshape(1, C)
    bias = conv_bias.reshape(1, C)
    flat = frames.reshape(-1, C)
    weight = conv_weight.reshape(27, C, C)
    place = jnp.stack([lax.axis_index("rows"), lax.axis_index("tm")]).astype(jnp.int32)

    grad_all = lax.all_gather(latent_grad.reshape(-1, C), ("rows", "tm"), axis=0)
    grad_all = grad_all.reshape(R, T, -1, C)

    planes, send, cached, under, corner = call(
        functools.partial(hidden_kernel, F, J, T),
        [
            ((2, 2, span, C), bf16),
            ((T, 2, span, 2 * part), bf16),
            ((2, 2, 2 * J, C), bf16),
            ((2, span, C), bf16),
            ((2, 2 * J, C), bf16),
        ],
        [((2, 4 * span, C // 2), f32)],
        10 * 4 * span * C, 16 * span * C, operands=2,
    )(flat, gain)

    received = lax.all_to_all(send, "tm", split_axis=0, concat_axis=0, tiled=True)
    hidden_all = lax.all_gather(received, "rows", axis=0)

    cached = shifted(cached, "tm", 1)
    under = shifted(under, "rows", -1)
    steps = [
        ((r + 1) * T + t, r * T + t + 1) for r in range(R - 1) for t in range(T - 1)
    ]
    corner = lax.ppermute(corner, ("rows", "tm"), steps)

    (latent_send,) = call(
        functools.partial(latent_kernel, F, J, R),
        [((span, C), bf16)],
        [((3, 3, (F + 2) * J, C), bf16)],
        2 * 27 * span * C * C, 2 * 27 * C * C, operands=6,
    )(planes, cached, under, corner, weight, bias)
    latent = lax.all_to_all(
        latent_send.reshape(R, span // R, C), "rows", split_axis=0, concat_axis=0, tiled=True
    )
    latent = latent.reshape(R, F, J // R, C).transpose(1, 0, 2, 3)

    grads, grads_right, frames_grad, gain_part, bias_sum = call(
        functools.partial(frames_kernel, F, J, R, T),
        [
            ((R + 1, (F * T + 2) * J, C), bf16),
            ((R + 1, (F * T + 2) * J, C), bf16),
            ((4 * span, C), bf16),
            ((1, C), f32),
            ((1, C), f32),
        ],
        [((2, 4 * span, C // 2), f32)],
        2 * 27 * span * C * C, 2 * 27 * C * C, smem=1, operands=5,
    )(place, grad_all, weight, flat, gain)

    (weight_grad,) = call(
        functools.partial(weight_kernel, R, part),
        [((27, part, C), f32)],
        [((3, 2 * part, R * T * span), bf16)],
        2 * 27 * R * T * span * part * C, 8 * 27 * part * C, operands=3,
    )(hidden_all, grads, grads_right)

    gain_grad = lax.psum(gain_part, ("rows", "tm"))
    start = lax.axis_index("tm") * part
    gain_grad = lax.dynamic_slice(gain_grad.reshape(C), (start,), (part,))
    bias_grad = lax.dynamic_slice(bias_sum.reshape(C), (start,), (part,))
    return (
        latent,
        frames_grad.reshape(frames.shape),
        weight_grad.reshape(3, 3, 3, part, C),
        gain_grad,
        bias_grad,
    )


def on_device(frames, norm_gain, conv_weight, conv_bias, latent_grad):
    devices = lax.axis_size("rows") * lax.axis_size("tm")
    shares = lax.axis_size("tm")
    operand_bytes = 2 * devices * (frames.size // shares + latent_grad.size)
    result_bytes = 4 * conv_weight.size
    if frames.shape[1] == 2 and operand_bytes <= result_bytes:
        form = gathered_form
    else:
        form = reduced_form
    return form(frames, norm_gain, conv_weight, conv_bias, latent_grad)


def solution(mesh):
    placed = (P("tm", "rows", None, None), P(), P(), P(), P("tm", None, "rows", None))
    return jax.shard_map(
        on_device,
        mesh=mesh,
        in_specs=placed,
        out_specs=(
            P("tm", None, "rows", None),
            P("tm", "rows", None, None),
            P(None, None, None, "tm", None),
            P("tm"),
            P("tm"),
        ),
        check_vma=False,
    )
```

```python
import functools

import jax
import jax.numpy as jnp
from jax import lax
from jax.experimental import pallas as pl
from jax.experimental.pallas import tpu as pltpu
from jax.sharding import PartitionSpec as P

EPS = 1e-06
TAPS = [(a, b, c) for a in range(3) for b in range(3) for c in range(3)]
VMEM_LIMIT = 48 * 1024 * 1024


def shifted(value, axis, steps):
    count = lax.axis_size(axis)
    leading, last = (max(0, -steps), min(count, count - steps))
    return lax.ppermute(value, axis, [(source, source + steps) for source in range(leading, last)])


def contract_out(grad_piece, weight_tap):
    return lax.dot_general(
        grad_piece, weight_tap, (((1,), (1,)), ((), ())), preferred_element_type=jnp.float32
    )


def reduced_form(frames, norm_gain, conv_weight, conv_bias, latent_grad):
    signal = frames.astype(jnp.float32)
    inv_rms = lax.rsqrt(jnp.mean(signal * signal, axis=-1, keepdims=True) + EPS)
    unit = signal * inv_rms
    normed = unit * norm_gain
    hidden = jax.nn.silu(normed).astype(jnp.bfloat16)
    frame_count, row_count, col_count, channels = hidden.shape
    lat_rows = row_count // 2
    lat_cols = col_count // 2
    cached = shifted(hidden[frame_count - 2 :], "tm", 1)
    stacked = jnp.concatenate([cached, hidden], axis=0)
    row_under = shifted(stacked[:, :1], "rows", -1)
    extended = jnp.concatenate([stacked, row_under], axis=1)
    extended = jnp.pad(extended, ((0, 0), (0, 0), (0, 1), (0, 0)))
    grad_rows = lax.all_to_all(latent_grad, "rows", split_axis=1, concat_axis=2, tiled=True)
    grad_flat = grad_rows.reshape(-1, channels)
    running = jnp.zeros((frame_count * lat_rows * lat_cols, channels), jnp.float32)
    blocks = []
    for tap_t, tap_r, tap_c in TAPS:
        window_piece = extended[
            tap_t : tap_t + frame_count,
            tap_r : tap_r + 2 * lat_rows : 2,
            tap_c : tap_c + 2 * lat_cols : 2,
        ]
        window_piece = window_piece.reshape(-1, channels)
        running = running + jnp.dot(
            window_piece, conv_weight[tap_t, tap_r, tap_c], preferred_element_type=jnp.float32
        )
        blocks.append(
            lax.dot_general(
                window_piece,
                grad_flat,
                (((0,), (0,)), ((), ())),
                preferred_element_type=jnp.float32,
            )
        )
    latent_rows = (
        (running + conv_bias)
        .reshape(frame_count, lat_rows, lat_cols, channels)
        .astype(jnp.bfloat16)
    )
    latent = lax.all_to_all(latent_rows, "rows", split_axis=2, concat_axis=1, tiled=True)
    weight_local = jnp.stack(blocks).reshape(3, 3, 3, channels, channels)
    bias_local = jnp.sum(grad_flat.astype(jnp.float32), axis=0)
    following = shifted(grad_rows[:2], "tm", -1)
    grad_ext = jnp.concatenate([grad_rows, following], axis=0)
    above_row = shifted(grad_ext, "rows", 1)
    grad_ext = jnp.concatenate([above_row, grad_ext], axis=1)
    grad_ext = jnp.pad(grad_ext, ((0, 0), (0, 0), (1, 0), (0, 0)))
    parity_sums = {}
    for tap_t, tap_r, tap_c in TAPS:
        row_start = 1 - tap_r // 2
        col_start = 1 - tap_c // 2
        grad_piece = grad_ext[
            2 - tap_t : 2 - tap_t + frame_count,
            row_start : row_start + lat_rows,
            col_start : col_start + lat_cols,
        ]
        term = contract_out(grad_piece.reshape(-1, channels), conv_weight[tap_t, tap_r, tap_c])
        label = (tap_r % 2, tap_c % 2)
        parity_sums[label] = parity_sums[label] + term if label in parity_sums else term
    shaped = {}
    for label in parity_sums:
        shaped[label] = parity_sums[label].reshape(frame_count, lat_rows, lat_cols, channels)
    even_rows = jnp.stack([shaped[0, 0], shaped[0, 1]], axis=3)
    odd_rows = jnp.stack([shaped[1, 0], shaped[1, 1]], axis=3)
    hidden_grad = jnp.stack([even_rows, odd_rows], axis=2).reshape(
        frame_count, row_count, col_count, channels
    )
    sigma = jax.nn.sigmoid(normed)
    normed_grad = hidden_grad * sigma * (1.0 + normed * (1.0 - sigma))
    gain_local = jnp.sum(normed_grad * unit, axis=(0, 1, 2))
    unit_grad = normed_grad * norm_gain
    frames_grad = inv_rms * (unit_grad - unit * jnp.mean(unit_grad * unit, axis=-1, keepdims=True))
    totals = lax.psum((weight_local, gain_local, bias_local), "rows")
    weight_grad, gain_grad, bias_grad = (
        lax.psum_scatter(totals[0], "tm", scatter_dimension=3, tiled=True),
        lax.psum_scatter(totals[1], "tm", scatter_dimension=0, tiled=True),
        lax.psum_scatter(totals[2], "tm", scatter_dimension=0, tiled=True),
    )
    return (latent, frames_grad.astype(jnp.bfloat16), weight_grad, gain_grad, bias_grad)


def partners(value, axis, bits):
    count = lax.axis_size(axis)
    return lax.ppermute(value, axis, [(source, source ^ bits) for source in range(count)])


def exchanged(value, axis):
    blocks = [value]
    for k in range(1, lax.axis_size(axis)):
        if k % 2 == 0:
            blocks.append(partners(value, axis, k))
        else:
            blocks.append(partners(blocks[k - 1], axis, 1))
    return blocks


def mm(left, right):
    return jnp.dot(left, right, preferred_element_type=jnp.float32)


def mm_t(left, right):
    return lax.dot_general(
        left, right, (((1,), (1,)), ((), ())), preferred_element_type=jnp.float32
    )


def normalised(frames, gain):
    signal = frames.astype(jnp.float32)
    inv_rms = lax.rsqrt(jnp.mean(signal * signal, axis=-1, keepdims=True) + EPS)
    unit = signal * inv_rms
    return inv_rms, unit, unit * gain


def hidden_kernel(F, J, T, place, frames, gain, planes, cached, under, corner, *rest):
    sends, tmp = rest[:T], rest[T]
    channels = frames.shape[1]
    part = channels // T
    _, _, normed = normalised(frames[...], gain[...])
    value = normed / (1.0 + jnp.exp(-normed))
    tmp[0] = value[:, : channels // 2]
    tmp[1] = value[:, channels // 2 :]
    block = place[1]
    for rp in range(2):
        pair = []
        for cp in range(2):
            rows = [
                jnp.concatenate(
                    [
                        tmp[half, pl.ds((t * 2 + rp) * 2 * J + cp, J, stride=2), :]
                        for half in range(2)
                    ],
                    axis=1,
                )
                for t in range(F)
            ]
            plane = jnp.concatenate(rows, axis=0)
            pair.append(plane)
            plane = plane.astype(jnp.bfloat16)
            planes[rp, cp] = plane
            cached[rp, cp] = plane[(F - 2) * J :]
            if rp == 0:
                under[cp] = plane
                corner[cp] = plane[(F - 2) * J :]
        pieces = [
            jnp.concatenate([p[:, d * part : (d + 1) * part] for p in pair], axis=1)
            for d in range(T)
        ]
        for k in range(T):
            chosen = pieces[0]
            for d in range(1, T):
                chosen = jnp.where(block == d ^ k, pieces[d], chosen)
            sends[k][rp] = chosen.astype(jnp.bfloat16)


def permutation(shape, meet):
    row = lax.broadcasted_iota(jnp.int32, shape, 0)
    col = lax.broadcasted_iota(jnp.int32, shape, 1)
    return jnp.where(meet(row, col), 1.0, 0.0).astype(jnp.bfloat16)


def latent_kernel(F, J, R, planes, cached, under, corner, weight, bias, out, ext):
    rows = (F + 2) * J
    last = lax.broadcasted_iota(jnp.int32, (rows, 1), 0) % J == J - 1
    for b in range(3):
        for cp in range(2):
            before, now = (corner[cp], under[cp]) if b == 2 else (cached[b, cp], planes[b, cp])
            full = jnp.concatenate([before, now], axis=0)
            ext[b, cp] = full
            if cp == 0:
                moved = pltpu.roll(full.astype(jnp.float32), rows - 1, 0)
                ext[b, 2] = jnp.where(last, 0.0, moved).astype(jnp.bfloat16)
    total = jnp.zeros(out.shape, jnp.float32) + bias[...]
    for n, (a, b, c) in enumerate(TAPS):
        total = total + mm(ext[b, c, a * J : (a + F) * J, :], weight[n])
    jl = J // R
    order = permutation(
        (F * J, F * J),
        lambda o, s: (o // jl % F == s // J) & (o // (F * jl) * jl + o % jl == s % J),
    )
    out[...] = mm(order, total.astype(jnp.bfloat16)).astype(jnp.bfloat16)


def shard_rows(source, start, count, R):
    return jnp.concatenate([source[s, start : start + count, :] for s in range(R)], axis=0)


def shard_order(J, R, rows, first, moved):
    jl = J // R
    return permutation(
        (rows * 2 * J, 2 * R * J),
        lambda o, s: (o // (2 * J) + first == s // jl % R)
        & (o // J % 2 == s // (jl * R) % 2)
        & (o % J == s // (2 * jl * R) * jl + s % jl + moved),
    )


def frames_kernel(
    F, J, R, place, gathered, following, weight, frames, gain, frames_grad, gain_part, near, tmp
):
    channels = frames.shape[1]
    pair_rows = 2 * R * (J // R)
    orders = [shard_order(J, R, 2, place[0] - 1, moved) for moved in range(2)]
    for pair in range(F // 2 + 1):
        if pair < F // 2:
            source = shard_rows(gathered, pair * pair_rows, pair_rows, R)
        else:
            source = shard_rows(following, 0, pair_rows, R)
        for moved in range(2):
            value = mm(orders[moved], source).astype(jnp.bfloat16)
            for i in range(2):
                near[moved, i, pair * 2 * J : (pair + 1) * 2 * J, :] = value[
                    i * 2 * J : (i + 1) * 2 * J
                ]
    sums = {}
    for n, (a, b, c) in enumerate(TAPS):
        piece = near[c // 2, 1 - b // 2, (2 - a) * J : (2 - a + F) * J, :]
        term = mm_t(piece, weight[n])
        key = (b % 2, c % 2)
        sums[key] = sums[key] + term if key in sums else term
    for (rp, cp), value in sums.items():
        for t in range(F):
            for half in range(2):
                lanes = slice(half * channels // 2, (half + 1) * channels // 2)
                tmp[half, pl.ds((t * 2 + rp) * 2 * J + cp, J, stride=2), :] = value[
                    t * J : (t + 1) * J, lanes
                ]
    hidden_grad = jnp.concatenate([tmp[0], tmp[1]], axis=1)
    inv_rms, unit, normed = normalised(frames[...], gain[...])
    sigma = 1.0 / (1.0 + jnp.exp(-normed))
    normed_grad = hidden_grad * sigma * (1.0 + normed * (1.0 - sigma))
    gain_part[...] = jnp.sum(normed_grad * unit, axis=0, keepdims=True)
    unit_grad = normed_grad * gain[...]
    mean = jnp.mean(unit_grad * unit, axis=-1, keepdims=True)
    frames_grad[...] = (inv_rms * (unit_grad - unit * mean)).astype(jnp.bfloat16)


def weight_kernel(F, J, R, T, part, place, *refs):
    gathered, hidden = refs[:T], refs[T : T + R]
    out, bias_sum, grads, even, odd = refs[T + R :]
    channels = gathered[0].shape[-1]
    span = F * J
    depth = T * span
    lanes = 2 * part
    row, block = place[0], place[1]
    pair_rows = 2 * R * (J // R)
    grads[:, :, depth:, :] = jnp.zeros((2, R, 2 * J, channels), jnp.bfloat16)
    even[:, R * depth :] = jnp.zeros((lanes, depth), jnp.bfloat16)
    orders = [shard_order(J, R, R, 0, moved) for moved in range(2)]
    total = jnp.zeros((1, channels), jnp.float32)
    for k in range(T):
        for pair in range(F // 2):
            source = shard_rows(gathered[k], pair * pair_rows, pair_rows, R)
            total = total + jnp.sum(source.astype(jnp.float32), axis=0, keepdims=True)
            at = pl.multiple_of((block ^ k) * span + pair * 2 * J, 16)
            for moved in range(2):
                value = mm(orders[moved], source).astype(jnp.bfloat16)
                for i in range(R):
                    grads[moved, i, pl.ds(at, 2 * J), :] = value[i * 2 * J : (i + 1) * 2 * J]
    bias_sum[...] = total
    for k in range(R):
        at = pl.multiple_of((row ^ k) * depth, 128)
        for rp, turned in ((0, even), (1, odd)):
            turned[:, pl.ds(at, depth)] = hidden[k][rp].T
    for a in range(3):
        start = (2 - a) * J
        for moved in range(2):
            right = grads[moved, :, start : start + depth, :].reshape(R * depth, channels)
            size = part if moved else lanes
            left = jnp.concatenate(
                [
                    even[:size, : R * depth],
                    odd[:size, :],
                    even[:size, depth:],
                ],
                axis=0,
            )
            value = mm(left, right)
            for b in range(3):
                if moved:
                    out[(a * 3 + b) * 3 + 2] = value[b * part : (b + 1) * part]
                else:
                    for cp in range(2):
                        at = b * lanes + cp * part
                        out[(a * 3 + b) * 3 + cp] = value[at : at + part]


def call(kernel, outs, scratch, flops, moved, smem=0, operands=0):
    vmem = pl.BlockSpec(memory_space=pltpu.VMEM)
    specs = [pl.BlockSpec(memory_space=pltpu.SMEM)] * smem + [vmem] * (operands - smem)
    return pl.pallas_call(
        kernel,
        out_shape=[jax.ShapeDtypeStruct(s, d) for s, d in outs],
        in_specs=specs,
        out_specs=[vmem] * len(outs),
        scratch_shapes=[pltpu.VMEM(s, d) for s, d in scratch],
        compiler_params=pltpu.CompilerParams(vmem_limit_bytes=VMEM_LIMIT),
        cost_estimate=pl.CostEstimate(flops=flops, bytes_accessed=moved, transcendentals=0),
    )


def gathered_form(frames, norm_gain, conv_weight, conv_bias, latent_grad):
    bf16, f32 = jnp.bfloat16, jnp.float32
    F, row_count, col_count, C = frames.shape
    R, T = lax.axis_size("rows"), lax.axis_size("tm")
    J = col_count // 2
    span = F * J
    part = C // T
    gain = norm_gain.reshape(1, C)
    bias = conv_bias.reshape(1, C)
    flat = frames.reshape(-1, C)
    weight = conv_weight.reshape(27, C, C)
    place = jnp.stack([lax.axis_index("rows"), lax.axis_index("tm")]).astype(jnp.int32)

    grad_rows = lax.all_gather(latent_grad.reshape(-1, C), "rows", axis=0)

    planes, cached, under, corner, *sends = call(
        functools.partial(hidden_kernel, F, J, T),
        [
            ((2, 2, span, C), bf16),
            ((2, 2, 2 * J, C), bf16),
            ((2, span, C), bf16),
            ((2, 2 * J, C), bf16),
        ]
        + [((2, span, 2 * part), bf16)] * T,
        [((2, 4 * span, C // 2), f32)],
        10 * 4 * span * C, 16 * span * C, smem=1, operands=3,
    )(place, flat, gain)

    parts = [sends[0]] + [partners(sends[k], "tm", k) for k in range(1, T)]
    block = lax.axis_index("tm")
    ordered = jnp.stack(parts)
    ordered = jnp.stack(
        [lax.dynamic_index_in_dim(ordered, block ^ t, keepdims=False) for t in range(T)], axis=1
    )
    hidden_all = exchanged(ordered.reshape(2, T * span, 2 * part), "rows")

    cached = shifted(cached, "tm", 1)
    under = shifted(under, "rows", -1)
    steps = [
        ((r + 1) * T + t, r * T + t + 1) for r in range(R - 1) for t in range(T - 1)
    ]
    corner = lax.ppermute(corner, ("rows", "tm"), steps)

    (latent_send,) = call(
        functools.partial(latent_kernel, F, J, R),
        [((span, C), bf16)],
        [((3, 3, (F + 2) * J, C), bf16)],
        2 * 27 * span * C * C, 2 * 27 * C * C, operands=6,
    )(planes, cached, under, corner, weight, bias)
    latent = lax.all_to_all(
        latent_send.reshape(R, span // R, C), "rows", split_axis=0, concat_axis=0, tiled=True
    )
    latent = latent.reshape(R, F, J // R, C).transpose(1, 0, 2, 3)

    following = shifted(grad_rows[:, : 2 * J], "tm", -1)
    grad_all = exchanged(grad_rows, "tm")
    frames_grad, gain_part = call(
        functools.partial(frames_kernel, F, J, R),
        [((4 * span, C), bf16), ((1, C), f32)],
        [((2, 2, (F + 2) * J, C), bf16), ((2, 4 * span, C // 2), f32)],
        2 * 27 * span * C * C, 2 * 27 * C * C, smem=1, operands=6,
    )(place, grad_rows, following, weight, flat, gain)

    weight_grad, bias_sum = call(
        functools.partial(weight_kernel, F, J, R, T, part),
        [((27, part, C), f32), ((1, C), f32)],
        [
            ((2, R, (F * T + 2) * J, C), bf16),
            ((2 * part, (R + 1) * T * span), bf16),
            ((2 * part, R * T * span), bf16),
        ],
        2 * 27 * R * T * span * part * C, 8 * 27 * part * C, smem=1, operands=1 + T + R,
    )(place, *grad_all, *hidden_all)

    gain_grad = lax.psum(gain_part, ("rows", "tm"))
    start = lax.axis_index("tm") * part
    gain_grad = lax.dynamic_slice(gain_grad.reshape(C), (start,), (part,))
    bias_grad = lax.dynamic_slice(bias_sum.reshape(C), (start,), (part,))
    return (
        latent,
        frames_grad.reshape(frames.shape),
        weight_grad.reshape(3, 3, 3, part, C),
        gain_grad,
        bias_grad,
    )


def on_device(frames, norm_gain, conv_weight, conv_bias, latent_grad):
    rows, shares = lax.axis_size("rows"), lax.axis_size("tm")
    operand_bytes = 2 * rows * shares * (frames.size // shares + latent_grad.size)
    result_bytes = 4 * conv_weight.size
    powers = (rows & (rows - 1)) == 0 and (shares & (shares - 1)) == 0
    if powers and frames.shape[1] == 2 and operand_bytes <= result_bytes:
        form = gathered_form
    else:
        form = reduced_form
    return form(frames, norm_gain, conv_weight, conv_bias, latent_grad)


def solution(mesh):
    placed = (P("tm", "rows", None, None), P(), P(), P(), P("tm", None, "rows", None))
    return jax.shard_map(
        on_device,
        mesh=mesh,
        in_specs=placed,
        out_specs=(
            P("tm", None, "rows", None),
            P("tm", "rows", None, None),
            P(None, None, None, "tm", None),
            P("tm"),
            P("tm"),
        ),
        check_vma=False,
    )
```

```python
import functools

import jax
import jax.numpy as jnp
from jax import lax
from jax.experimental import pallas as pl
from jax.experimental.pallas import tpu as pltpu
from jax.sharding import PartitionSpec as P

EPS = 1e-06
TAPS = [(a, b, c) for a in range(3) for b in range(3) for c in range(3)]
VMEM_LIMIT = 48 * 1024 * 1024


def shifted(value, axis, steps):
    count = lax.axis_size(axis)
    leading, last = (max(0, -steps), min(count, count - steps))
    return lax.ppermute(value, axis, [(source, source + steps) for source in range(leading, last)])


def contract_out(grad_piece, weight_tap):
    return lax.dot_general(
        grad_piece, weight_tap, (((1,), (1,)), ((), ())), preferred_element_type=jnp.float32
    )


def reduced_form(frames, norm_gain, conv_weight, conv_bias, latent_grad):
    signal = frames.astype(jnp.float32)
    inv_rms = lax.rsqrt(jnp.mean(signal * signal, axis=-1, keepdims=True) + EPS)
    unit = signal * inv_rms
    normed = unit * norm_gain
    hidden = jax.nn.silu(normed).astype(jnp.bfloat16)
    frame_count, row_count, col_count, channels = hidden.shape
    lat_rows = row_count // 2
    lat_cols = col_count // 2
    cached = shifted(hidden[frame_count - 2 :], "tm", 1)
    stacked = jnp.concatenate([cached, hidden], axis=0)
    row_under = shifted(stacked[:, :1], "rows", -1)
    extended = jnp.concatenate([stacked, row_under], axis=1)
    extended = jnp.pad(extended, ((0, 0), (0, 0), (0, 1), (0, 0)))
    grad_rows = lax.all_to_all(latent_grad, "rows", split_axis=1, concat_axis=2, tiled=True)
    grad_flat = grad_rows.reshape(-1, channels)
    running = jnp.zeros((frame_count * lat_rows * lat_cols, channels), jnp.float32)
    blocks = []
    for tap_t, tap_r, tap_c in TAPS:
        window_piece = extended[
            tap_t : tap_t + frame_count,
            tap_r : tap_r + 2 * lat_rows : 2,
            tap_c : tap_c + 2 * lat_cols : 2,
        ]
        window_piece = window_piece.reshape(-1, channels)
        running = running + jnp.dot(
            window_piece, conv_weight[tap_t, tap_r, tap_c], preferred_element_type=jnp.float32
        )
        blocks.append(
            lax.dot_general(
                window_piece,
                grad_flat,
                (((0,), (0,)), ((), ())),
                preferred_element_type=jnp.float32,
            )
        )
    latent_rows = (
        (running + conv_bias)
        .reshape(frame_count, lat_rows, lat_cols, channels)
        .astype(jnp.bfloat16)
    )
    latent = lax.all_to_all(latent_rows, "rows", split_axis=2, concat_axis=1, tiled=True)
    weight_local = jnp.stack(blocks).reshape(3, 3, 3, channels, channels)
    bias_local = jnp.sum(grad_flat.astype(jnp.float32), axis=0)
    following = shifted(grad_rows[:2], "tm", -1)
    grad_ext = jnp.concatenate([grad_rows, following], axis=0)
    above_row = shifted(grad_ext, "rows", 1)
    grad_ext = jnp.concatenate([above_row, grad_ext], axis=1)
    grad_ext = jnp.pad(grad_ext, ((0, 0), (0, 0), (1, 0), (0, 0)))
    parity_sums = {}
    for tap_t, tap_r, tap_c in TAPS:
        row_start = 1 - tap_r // 2
        col_start = 1 - tap_c // 2
        grad_piece = grad_ext[
            2 - tap_t : 2 - tap_t + frame_count,
            row_start : row_start + lat_rows,
            col_start : col_start + lat_cols,
        ]
        term = contract_out(grad_piece.reshape(-1, channels), conv_weight[tap_t, tap_r, tap_c])
        label = (tap_r % 2, tap_c % 2)
        parity_sums[label] = parity_sums[label] + term if label in parity_sums else term
    shaped = {}
    for label in parity_sums:
        shaped[label] = parity_sums[label].reshape(frame_count, lat_rows, lat_cols, channels)
    even_rows = jnp.stack([shaped[0, 0], shaped[0, 1]], axis=3)
    odd_rows = jnp.stack([shaped[1, 0], shaped[1, 1]], axis=3)
    hidden_grad = jnp.stack([even_rows, odd_rows], axis=2).reshape(
        frame_count, row_count, col_count, channels
    )
    sigma = jax.nn.sigmoid(normed)
    normed_grad = hidden_grad * sigma * (1.0 + normed * (1.0 - sigma))
    gain_local = jnp.sum(normed_grad * unit, axis=(0, 1, 2))
    unit_grad = normed_grad * norm_gain
    frames_grad = inv_rms * (unit_grad - unit * jnp.mean(unit_grad * unit, axis=-1, keepdims=True))
    totals = lax.psum((weight_local, gain_local, bias_local), "rows")
    weight_grad, gain_grad, bias_grad = (
        lax.psum_scatter(totals[0], "tm", scatter_dimension=3, tiled=True),
        lax.psum_scatter(totals[1], "tm", scatter_dimension=0, tiled=True),
        lax.psum_scatter(totals[2], "tm", scatter_dimension=0, tiled=True),
    )
    return (latent, frames_grad.astype(jnp.bfloat16), weight_grad, gain_grad, bias_grad)


def partners(value, axis, bits):
    count = lax.axis_size(axis)
    return lax.ppermute(value, axis, [(source, source ^ bits) for source in range(count)])


def exchanged(value, axis):
    blocks = [value]
    for k in range(1, lax.axis_size(axis)):
        if k % 2 == 0:
            blocks.append(partners(value, axis, k))
        else:
            blocks.append(partners(blocks[k - 1], axis, 1))
    return blocks


def mm(left, right):
    return jnp.dot(left, right, preferred_element_type=jnp.float32)


def mm_t(left, right):
    return lax.dot_general(
        left, right, (((1,), (1,)), ((), ())), preferred_element_type=jnp.float32
    )


def normalised(frames, gain):
    signal = frames.astype(jnp.float32)
    inv_rms = lax.rsqrt(jnp.mean(signal * signal, axis=-1, keepdims=True) + EPS)
    unit = signal * inv_rms
    return inv_rms, unit, unit * gain


def hidden_kernel(F, J, T, place, frames_hbm, gain_hbm, planes, *rest):
    sends, (frames, gain, tmp, sem) = rest[:T], rest[T:]
    copies = [
        pltpu.make_async_copy(frames_hbm, frames, sem.at[0]),
        pltpu.make_async_copy(gain_hbm, gain, sem.at[1]),
    ]
    for copy in copies:
        copy.start()
    for copy in copies:
        copy.wait()
    channels = frames.shape[1]
    part = channels // T
    _, _, normed = normalised(frames[...], gain[...])
    value = normed / (1.0 + jnp.exp(-normed))
    tmp[0] = value[:, : channels // 2]
    tmp[1] = value[:, channels // 2 :]
    block = place[1]
    for rp in range(2):
        pair = []
        for cp in range(2):
            rows = [
                jnp.concatenate(
                    [
                        tmp[half, pl.ds((t * 2 + rp) * 2 * J + cp, J, stride=2), :]
                        for half in range(2)
                    ],
                    axis=1,
                )
                for t in range(F)
            ]
            plane = jnp.concatenate(rows, axis=0)
            pair.append(plane)
            plane = plane.astype(jnp.bfloat16)
            planes[rp, cp] = plane
            late = plane[(F - 2) * J :]
            for k in range(1, T, 2):
                for half in range(2):
                    at = (((rp * 2 + cp) * 2) + half) * 2 * J
                    lanes = slice(half * channels // 2, (half + 1) * channels // 2)
                    sends[k][2 * F * J + at : 2 * F * J + at + 2 * J] = late[:, lanes]
        pieces = [
            jnp.concatenate([p[:, d * part : (d + 1) * part] for p in pair], axis=1)
            for d in range(T)
        ]
        for k in range(T):
            chosen = pieces[0]
            for d in range(1, T):
                chosen = jnp.where(block == d ^ k, pieces[d], chosen)
            sends[k][rp * F * J : (rp + 1) * F * J] = chosen.astype(jnp.bfloat16)


def join_kernel(F, J, T, place, planes, *refs):
    messages, (joined, cached, under) = refs[:T], refs[T:]
    span = F * J
    block = place[1]
    for k in range(T):
        for rp in range(2):
            joined[k, rp] = messages[k][rp * span : (rp + 1) * span, :]
    for rp in range(2):
        for cp in range(2):
            halves = []
            for half in range(2):
                start = 2 * span + ((rp * 2 + cp) * 2 + half) * 2 * J
                value = jnp.zeros((2 * J, messages[1].shape[1]), jnp.bfloat16)
                for k in range(1, T, 2):
                    found = (block > 0) & (block ^ k == block - 1)
                    value = jnp.where(found, messages[k][start : start + 2 * J, :], value)
                halves.append(value)
            before = jnp.concatenate(halves, axis=1)
            cached[rp, cp] = before
            if rp == 0:
                under[cp, : 2 * J] = before
                under[cp, 2 * J :] = planes[0, cp]


def permutation(shape, meet):
    row = lax.broadcasted_iota(jnp.int32, shape, 0)
    col = lax.broadcasted_iota(jnp.int32, shape, 1)
    return jnp.where(meet(row, col), 1.0, 0.0).astype(jnp.bfloat16)


def shard_order(J, R, moved):
    jl = J // R
    return permutation(
        (R * 2 * J, R * 2 * J),
        lambda o, s: (o // (2 * J) == s // jl % R)
        & (o // J % 2 == s // (jl * R) % 2)
        & (o % J == s // (2 * jl * R) * jl + s % jl + moved),
    )


def slab_kernel(
    F, J, R, T, slot, place, planes, cached, under, weight_hbm, bias_hbm, frames_hbm, gain_hbm, *refs
):
    gathered = refs[:T]
    out, frames_grad, bias_sum, grads = refs[T : T + 4]
    weight, bias, frames, gain, ext, tmp, sem = refs[T + 4 :]
    row, block = place[0], place[1]
    channels = frames.shape[1]
    span = F * J
    taps_a = [
        pltpu.make_async_copy(weight_hbm.at[pl.ds(a * 9, 9)], weight.at[pl.ds(a * 9, 9)], sem.at[a])
        for a in range(3)
    ]
    others = [
        pltpu.make_async_copy(source, target, sem.at[3 + n])
        for n, (source, target) in enumerate(
            ((bias_hbm, bias), (frames_hbm, frames), (gain_hbm, gain))
        )
    ]
    for copy in taps_a + others:
        copy.start()

    pair_rows = 2 * R * (J // R)
    grads[:, 0] = jnp.zeros((2,) + grads.shape[2:], jnp.bfloat16)
    grads[:, :, T * span :, :] = jnp.zeros((2, R + 1, 2 * J, channels), jnp.bfloat16)
    orders = [shard_order(J, R, moved) for moved in range(2)]
    total = jnp.zeros((1, channels), jnp.float32)
    for k in range(T):
        for pair in range(F // 2):
            start = pair * pair_rows
            source = jnp.concatenate(
                [gathered[k][s, start : start + pair_rows, :] for s in range(R)], axis=0
            )
            total = total + jnp.sum(source.astype(jnp.float32), axis=0, keepdims=True)
            at = pl.multiple_of((block ^ k) * span + pair * 2 * J, 16)
            for moved in range(2):
                value = mm(orders[moved], source).astype(jnp.bfloat16)
                for i in range(R):
                    grads[moved, i + 1, pl.ds(at, 2 * J), :] = value[i * 2 * J : (i + 1) * 2 * J]
    bias_sum[...] = total

    rows = (F + 2) * J
    last = lax.broadcasted_iota(jnp.int32, (rows, 1), 0) % J == J - 1
    for b in range(3):
        for cp in range(2):
            if b == 2:
                full = under[cp]
            else:
                full = jnp.concatenate([cached[b, cp], planes[b, cp]], axis=0)
            ext[b, cp] = full
            if cp == 0:
                moved = pltpu.roll(full.astype(jnp.float32), rows - 1, 0)
                ext[b, 2] = jnp.where(last, 0.0, moved).astype(jnp.bfloat16)

    latent = jnp.zeros((span, channels), jnp.float32)
    sums = {}
    for n, (a, b, c) in enumerate(TAPS):
        if n % 9 == 0:
            taps_a[a].wait()
        latent = latent + mm(ext[b, c, a * J : (a + F) * J, :], weight[n])
        start = pl.multiple_of((block * F + 2 - a) * J, 16)
        piece = grads[c // 2, row + 1 - b // 2, pl.ds(start, span), :]
        term = mm_t(piece, weight[n])
        key = (b % 2, c % 2)
        sums[key] = sums[key] + term if key in sums else term
    for (rp, cp), value in sums.items():
        for t in range(F):
            for half in range(2):
                lanes = slice(half * channels // 2, (half + 1) * channels // 2)
                tmp[half, pl.ds((t * 2 + rp) * 2 * J + cp, J, stride=2), :] = value[
                    t * J : (t + 1) * J, lanes
                ]
    for copy in others:
        copy.wait()
    hidden_grad = jnp.concatenate([tmp[0], tmp[1]], axis=1)
    inv_rms, unit, normed = normalised(frames[...], gain[...])
    sigma = 1.0 / (1.0 + jnp.exp(-normed))
    normed_grad = hidden_grad * sigma * (1.0 + normed * (1.0 - sigma))
    gain_part = jnp.sum(normed_grad * unit, axis=0, keepdims=True)
    unit_grad = normed_grad * gain[...]
    mean = jnp.mean(unit_grad * unit, axis=-1, keepdims=True)
    frames_grad[...] = (inv_rms * (unit_grad - unit * mean)).astype(jnp.bfloat16)

    jl = J // R
    used = span // R
    order = permutation(
        (R * slot, span),
        lambda o, s: (o % slot < used)
        & (o % slot // jl == s // J)
        & (o // slot * jl + o % jl == s % J),
    )
    value = mm(order, (latent + bias[...]).astype(jnp.bfloat16))
    line = lax.broadcasted_iota(jnp.int32, (R * slot, 1), 0) % slot
    rest = gain_part
    for n in range(3):
        term = rest.astype(jnp.bfloat16).astype(jnp.float32)
        rest = rest - term
        value = jnp.where(line == used + n, term, value)
    out[...] = value.astype(jnp.bfloat16)


def weight_kernel(F, J, R, T, part, place, grads, *refs):
    hidden = refs[:R]
    out, even, odd = refs[R:]
    channels = grads.shape[-1]
    depth = T * F * J
    lanes = 2 * part
    row, block = place[0], place[1]
    even[:, R * depth :] = jnp.zeros((lanes, depth), jnp.bfloat16)
    for k in range(R):
        at = pl.multiple_of((row ^ k) * depth, 128)
        for rp, turned in ((0, even), (1, odd)):
            value = jnp.concatenate([hidden[k][block ^ t, rp] for t in range(T)], axis=0)
            turned[:, pl.ds(at, depth)] = value.T
    for a in range(3):
        start = (2 - a) * J
        for moved in range(2):
            right = grads[moved, 1:, start : start + depth, :].reshape(R * depth, channels)
            size = part if moved else lanes
            left = jnp.concatenate(
                [even[:size, : R * depth], odd[:size, :], even[:size, depth:]], axis=0
            )
            value = mm(left, right)
            for b in range(3):
                if moved:
                    out[(a * 3 + b) * 3 + 2] = value[b * part : (b + 1) * part]
                else:
                    for cp in range(2):
                        at = b * lanes + cp * part
                        out[(a * 3 + b) * 3 + cp] = value[at : at + part]


def call(kernel, outs, scratch, flops, moved, places):
    kinds = {"s": pltpu.SMEM, "v": pltpu.VMEM, "a": pl.ANY}
    return pl.pallas_call(
        kernel,
        out_shape=[jax.ShapeDtypeStruct(s, d) for s, d in outs],
        in_specs=[pl.BlockSpec(memory_space=kinds[p]) for p in places],
        out_specs=[pl.BlockSpec(memory_space=pltpu.VMEM)] * len(outs),
        scratch_shapes=scratch,
        compiler_params=pltpu.CompilerParams(vmem_limit_bytes=VMEM_LIMIT),
        cost_estimate=pl.CostEstimate(flops=flops, bytes_accessed=moved, transcendentals=0),
    )


def gathered_form(frames, norm_gain, conv_weight, conv_bias, latent_grad):
    bf16, f32 = jnp.bfloat16, jnp.float32
    F, row_count, col_count, C = frames.shape
    R, T = lax.axis_size("rows"), lax.axis_size("tm")
    J = col_count // 2
    span = F * J
    part = C // T
    used = span // R
    slot = -(-(used + 3) // 16) * 16
    gain = norm_gain.reshape(1, C)
    bias = conv_bias.reshape(1, C)
    flat = frames.reshape(-1, C)
    weight = conv_weight.reshape(27, C, C)
    place = jnp.stack([lax.axis_index("rows"), lax.axis_index("tm")]).astype(jnp.int32)

    own = latent_grad.reshape(1, -1, C)
    grad_rows = lax.all_to_all(
        jnp.broadcast_to(own, (R,) + own.shape[1:]), "rows", 0, 0, tiled=True
    )

    sizes = [(2 * span + (16 * J if k % 2 else 0), 2 * part) for k in range(T)]
    planes, *sends = call(
        functools.partial(hidden_kernel, F, J, T),
        [((2, 2, span, C), bf16)] + [(size, bf16) for size in sizes],
        [
            pltpu.VMEM((4 * span, C), bf16),
            pltpu.VMEM((1, C), f32),
            pltpu.VMEM((2, 4 * span, C // 2), f32),
            pltpu.SemaphoreType.DMA((2,)),
        ],
        10 * 4 * span * C, 16 * span * C, "saa",
    )(place, flat, gain)
    messages = [sends[0]] + [partners(sends[k], "tm", k) for k in range(1, T)]
    joined, cached, under = call(
        functools.partial(join_kernel, F, J, T),
        [
            ((T, 2, span, 2 * part), bf16),
            ((2, 2, 2 * J, C), bf16),
            ((2, 2 * J + span, C), bf16),
        ],
        [],
        4 * span * C, 16 * span * C, "sv" + "v" * T,
    )(place, planes, *messages)
    under = shifted(under, "rows", -1)
    hidden_all = exchanged(joined, "rows")
    grad_all = exchanged(grad_rows, "tm")

    packed, frames_grad, bias_sum, grads = call(
        functools.partial(slab_kernel, F, J, R, T, slot),
        [
            ((R * slot, C), bf16),
            ((4 * span, C), bf16),
            ((1, C), f32),
            ((2, R + 1, (F * T + 2) * J, C), bf16),
        ],
        [
            pltpu.VMEM((27, C, C), bf16),
            pltpu.VMEM((1, C), f32),
            pltpu.VMEM((4 * span, C), bf16),
            pltpu.VMEM((1, C), f32),
            pltpu.VMEM((3, 3, (F + 2) * J, C), bf16),
            pltpu.VMEM((2, 4 * span, C // 2), f32),
            pltpu.SemaphoreType.DMA((6,)),
        ],
        4 * 27 * span * C * C, 2 * 27 * C * C, "svvvaaaa" + "v" * T,
    )(place, planes, cached, under, weight, bias, flat, gain, *grad_all)

    packed = lax.all_to_all(packed.reshape(R, slot, C), "rows", 0, 0, tiled=True)
    latent = packed[:, :used].reshape(R, F, J // R, C).transpose(1, 0, 2, 3)
    gain_sum = jnp.sum(packed[:, used : used + 3].astype(f32), axis=(0, 1)).reshape(1, C)
    gain_sum = sum(partners(gain_sum, "tm", k) for k in range(1, T)) + gain_sum

    (weight_grad,) = call(
        functools.partial(weight_kernel, F, J, R, T, part),
        [((27, part, C), f32)],
        [
            pltpu.VMEM((2 * part, (R + 1) * T * span), bf16),
            pltpu.VMEM((2 * part, R * T * span), bf16),
        ],
        2 * 27 * R * T * span * part * C, 8 * 27 * part * C, "sv" + "v" * R,
    )(place, grads, *hidden_all)

    start = lax.axis_index("tm") * part
    gain_grad = lax.dynamic_slice(gain_sum.reshape(C), (start,), (part,))
    bias_grad = lax.dynamic_slice(bias_sum.reshape(C), (start,), (part,))
    return (
        latent,
        frames_grad.reshape(frames.shape),
        weight_grad.reshape(3, 3, 3, part, C),
        gain_grad,
        bias_grad,
    )


def on_device(frames, norm_gain, conv_weight, conv_bias, latent_grad):
    rows, shares = lax.axis_size("rows"), lax.axis_size("tm")
    operand_bytes = 2 * rows * shares * (frames.size // shares + latent_grad.size)
    result_bytes = 4 * conv_weight.size
    powers = (rows & (rows - 1)) == 0 and (shares & (shares - 1)) == 0
    if powers and frames.shape[1] == 2 and operand_bytes <= result_bytes:
        form = gathered_form
    else:
        form = reduced_form
    return form(frames, norm_gain, conv_weight, conv_bias, latent_grad)


def solution(mesh):
    placed = (P("tm", "rows", None, None), P(), P(), P(), P("tm", None, "rows", None))
    return jax.shard_map(
        on_device,
        mesh=mesh,
        in_specs=placed,
        out_specs=(
            P("tm", None, "rows", None),
            P("tm", "rows", None, None),
            P(None, None, None, "tm", None),
            P("tm"),
            P("tm"),
        ),
        check_vma=False,
    )
```

```python
import functools

import jax
import jax.numpy as jnp
from jax import lax
from jax.experimental import pallas as pl
from jax.experimental.pallas import tpu as pltpu
from jax.sharding import PartitionSpec as P

EPS = 1e-06
TAPS = [(a, b, c) for a in range(3) for b in range(3) for c in range(3)]
VMEM_LIMIT = 20 * 1024 * 1024
VMEM_LIMIT_WIDE = 48 * 1024 * 1024
WORK = 1200


def shifted(value, axis, steps):
    count = lax.axis_size(axis)
    leading, last = (max(0, -steps), min(count, count - steps))
    return lax.ppermute(value, axis, [(source, source + steps) for source in range(leading, last)])


def contract_out(grad_piece, weight_tap):
    return lax.dot_general(
        grad_piece, weight_tap, (((1,), (1,)), ((), ())), preferred_element_type=jnp.float32
    )


def reduced_form(frames, norm_gain, conv_weight, conv_bias, latent_grad):
    signal = frames.astype(jnp.float32)
    inv_rms = lax.rsqrt(jnp.mean(signal * signal, axis=-1, keepdims=True) + EPS)
    unit = signal * inv_rms
    normed = unit * norm_gain
    hidden = jax.nn.silu(normed).astype(jnp.bfloat16)
    frame_count, row_count, col_count, channels = hidden.shape
    lat_rows = row_count // 2
    lat_cols = col_count // 2
    cached = shifted(hidden[frame_count - 2 :], "tm", 1)
    stacked = jnp.concatenate([cached, hidden], axis=0)
    row_under = shifted(stacked[:, :1], "rows", -1)
    extended = jnp.concatenate([stacked, row_under], axis=1)
    extended = jnp.pad(extended, ((0, 0), (0, 0), (0, 1), (0, 0)))
    grad_rows = lax.all_to_all(latent_grad, "rows", split_axis=1, concat_axis=2, tiled=True)
    grad_flat = grad_rows.reshape(-1, channels)
    running = jnp.zeros((frame_count * lat_rows * lat_cols, channels), jnp.float32)
    blocks = []
    for tap_t, tap_r, tap_c in TAPS:
        window_piece = extended[
            tap_t : tap_t + frame_count,
            tap_r : tap_r + 2 * lat_rows : 2,
            tap_c : tap_c + 2 * lat_cols : 2,
        ]
        window_piece = window_piece.reshape(-1, channels)
        running = running + jnp.dot(
            window_piece, conv_weight[tap_t, tap_r, tap_c], preferred_element_type=jnp.float32
        )
        blocks.append(
            lax.dot_general(
                window_piece,
                grad_flat,
                (((0,), (0,)), ((), ())),
                preferred_element_type=jnp.float32,
            )
        )
    latent_rows = (
        (running + conv_bias)
        .reshape(frame_count, lat_rows, lat_cols, channels)
        .astype(jnp.bfloat16)
    )
    latent = lax.all_to_all(latent_rows, "rows", split_axis=2, concat_axis=1, tiled=True)
    weight_local = jnp.stack(blocks).reshape(3, 3, 3, channels, channels)
    bias_local = jnp.sum(grad_flat.astype(jnp.float32), axis=0)
    following = shifted(grad_rows[:2], "tm", -1)
    grad_ext = jnp.concatenate([grad_rows, following], axis=0)
    above_row = shifted(grad_ext, "rows", 1)
    grad_ext = jnp.concatenate([above_row, grad_ext], axis=1)
    grad_ext = jnp.pad(grad_ext, ((0, 0), (0, 0), (1, 0), (0, 0)))
    parity_sums = {}
    for tap_t, tap_r, tap_c in TAPS:
        row_start = 1 - tap_r // 2
        col_start = 1 - tap_c // 2
        grad_piece = grad_ext[
            2 - tap_t : 2 - tap_t + frame_count,
            row_start : row_start + lat_rows,
            col_start : col_start + lat_cols,
        ]
        term = contract_out(grad_piece.reshape(-1, channels), conv_weight[tap_t, tap_r, tap_c])
        label = (tap_r % 2, tap_c % 2)
        parity_sums[label] = parity_sums[label] + term if label in parity_sums else term
    shaped = {}
    for label in parity_sums:
        shaped[label] = parity_sums[label].reshape(frame_count, lat_rows, lat_cols, channels)
    even_rows = jnp.stack([shaped[0, 0], shaped[0, 1]], axis=3)
    odd_rows = jnp.stack([shaped[1, 0], shaped[1, 1]], axis=3)
    hidden_grad = jnp.stack([even_rows, odd_rows], axis=2).reshape(
        frame_count, row_count, col_count, channels
    )
    sigma = jax.nn.sigmoid(normed)
    normed_grad = hidden_grad * sigma * (1.0 + normed * (1.0 - sigma))
    gain_local = jnp.sum(normed_grad * unit, axis=(0, 1, 2))
    unit_grad = normed_grad * norm_gain
    frames_grad = inv_rms * (unit_grad - unit * jnp.mean(unit_grad * unit, axis=-1, keepdims=True))
    totals = lax.psum((weight_local, gain_local, bias_local), "rows")
    weight_grad, gain_grad, bias_grad = (
        lax.psum_scatter(totals[0], "tm", scatter_dimension=3, tiled=True),
        lax.psum_scatter(totals[1], "tm", scatter_dimension=0, tiled=True),
        lax.psum_scatter(totals[2], "tm", scatter_dimension=0, tiled=True),
    )
    return (latent, frames_grad.astype(jnp.bfloat16), weight_grad, gain_grad, bias_grad)


def partners(value, axis, bits):
    count = lax.axis_size(axis)
    return lax.ppermute(value, axis, [(source, source ^ bits) for source in range(count)])


def exchanged(value, axis):
    blocks = [value]
    for k in range(1, lax.axis_size(axis)):
        if k % 2 == 0:
            blocks.append(partners(value, axis, k))
        else:
            blocks.append(partners(blocks[k - 1], axis, 1))
    return blocks


def mm(left, right):
    return jnp.dot(left, right, preferred_element_type=jnp.float32)


def mm_t(left, right):
    return lax.dot_general(
        left, right, (((1,), (1,)), ((), ())), preferred_element_type=jnp.float32
    )


def normalised(frames, gain):
    signal = frames.astype(jnp.float32)
    inv_rms = lax.rsqrt(jnp.mean(signal * signal, axis=-1, keepdims=True) + EPS)
    unit = signal * inv_rms
    return inv_rms, unit, unit * gain


def hidden_kernel(F, J, T, place, frames, vectors, planes, frames_copy, vectors_copy, *rest):
    sends, tmp = rest[:T], rest[T]
    frames_copy[...] = frames[...]
    vectors_copy[...] = vectors[...]
    channels = frames.shape[1]
    part = channels // T
    _, _, normed = normalised(frames[...], vectors[0:1])
    value = normed / (1.0 + jnp.exp(-normed))
    tmp[0] = value[:, : channels // 2]
    tmp[1] = value[:, channels // 2 :]
    block = place[1]
    for rp in range(2):
        pair = []
        for cp in range(2):
            rows = [
                jnp.concatenate(
                    [
                        tmp[half, pl.ds((t * 2 + rp) * 2 * J + cp, J, stride=2), :]
                        for half in range(2)
                    ],
                    axis=1,
                )
                for t in range(F)
            ]
            plane = jnp.concatenate(rows, axis=0)
            pair.append(plane)
            plane = plane.astype(jnp.bfloat16)
            planes[rp, cp] = plane
            late = plane[(F - 2) * J :]
            for k in range(1, T, 2):
                for half in range(2):
                    at = (((rp * 2 + cp) * 2) + half) * 2 * J
                    lanes = slice(half * channels // 2, (half + 1) * channels // 2)
                    sends[k][2 * F * J + at : 2 * F * J + at + 2 * J] = late[:, lanes]
        pieces = [
            jnp.concatenate([p[:, d * part : (d + 1) * part] for p in pair], axis=1)
            for d in range(T)
        ]
        for k in range(T):
            chosen = pieces[0]
            for d in range(1, T):
                chosen = jnp.where(block == d ^ k, pieces[d], chosen)
            sends[k][rp * F * J : (rp + 1) * F * J] = chosen.astype(jnp.bfloat16)


def join_kernel(F, J, T, place, grad_rows, planes, *refs):
    messages, (joined, cached, under, _, blocks) = refs[:T], refs[T:]
    span = F * J
    block = place[1]
    for k in range(T):
        at = pl.multiple_of((block ^ k) * span, 16)
        for rp in range(2):
            blocks[rp, pl.ds(at, span), :] = messages[k][rp * span : (rp + 1) * span, :]
    for rp in range(2):
        joined[rp] = blocks[rp].T
    for rp in range(2):
        for cp in range(2):
            halves = []
            for half in range(2):
                start = 2 * span + ((rp * 2 + cp) * 2 + half) * 2 * J
                value = jnp.zeros((2 * J, messages[1].shape[1]), jnp.bfloat16)
                for k in range(1, T, 2):
                    found = (block > 0) & (block ^ k == block - 1)
                    value = jnp.where(found, messages[k][start : start + 2 * J, :], value)
                halves.append(value)
            before = jnp.concatenate(halves, axis=1)
            cached[rp, cp] = before
            if rp == 0:
                under[cp, : 2 * J] = before
                under[cp, 2 * J :] = planes[0, cp]


def permutation(shape, meet):
    row = lax.broadcasted_iota(jnp.int32, shape, 0)
    col = lax.broadcasted_iota(jnp.int32, shape, 1)
    return jnp.where(meet(row, col), 1.0, 0.0).astype(jnp.bfloat16)


def slice_of(value, block, k, T):
    part = value.shape[1] // T
    chosen = value[:, :part]
    for d in range(1, T):
        chosen = jnp.where(block == d ^ k, value[:, d * part : (d + 1) * part], chosen)
    return chosen


def shard_order(J, R, moved):
    jl = J // R
    return permutation(
        (R * 2 * J, R * 2 * J),
        lambda o, s: (o // (2 * J) == s // jl % R)
        & (o // J % 2 == s // (jl * R) % 2)
        & (o % J == s // (2 * jl * R) * jl + s % jl + moved),
    )


def slab_kernel(
    F, J, R, T, slot, place, planes, cached, under, weight_hbm, frames, vectors, *refs
):
    gathered = refs[:T]
    out, frames_grad, bias_sum, grads = refs[T : T + 4]
    weight, ext, tmp, sem = refs[T + 4 :]
    row, block = place[0], place[1]
    channels = frames.shape[1]
    span = F * J
    gain, bias = vectors[0:1], vectors[1:2]
    taps_a = [
        pltpu.make_async_copy(weight_hbm.at[pl.ds(a * 9, 9)], weight.at[pl.ds(a * 9, 9)], sem.at[a])
        for a in range(3)
    ]
    for copy in taps_a:
        copy.start()

    pair_rows = 2 * R * (J // R)
    grads[:, 0] = jnp.zeros((2,) + grads.shape[2:], jnp.bfloat16)
    grads[:, :, T * span :, :] = jnp.zeros((2, R + 1, 2 * J, channels), jnp.bfloat16)
    orders = [shard_order(J, R, moved) for moved in range(2)]
    total = jnp.zeros((1, channels), jnp.float32)
    for k in range(T):
        for pair in range(F // 2):
            start = pair * pair_rows
            source = jnp.concatenate(
                [gathered[k][s, start : start + pair_rows, :] for s in range(R)], axis=0
            )
            total = total + jnp.sum(source.astype(jnp.float32), axis=0, keepdims=True)
            at = pl.multiple_of((block ^ k) * span + pair * 2 * J, 16)
            for moved in range(2):
                value = mm(orders[moved], source).astype(jnp.bfloat16)
                for i in range(R):
                    grads[moved, i + 1, pl.ds(at, 2 * J), :] = value[i * 2 * J : (i + 1) * 2 * J]
    bias_sum[...] = slice_of(total, block, 0, T)

    rows = (F + 2) * J
    last = lax.broadcasted_iota(jnp.int32, (rows, 1), 0) % J == J - 1
    for b in range(3):
        for cp in range(2):
            if b == 2:
                full = under[cp]
            else:
                full = jnp.concatenate([cached[b, cp], planes[b, cp]], axis=0)
            ext[b, cp] = full
            if cp == 0:
                moved = pltpu.roll(full.astype(jnp.float32), rows - 1, 0)
                ext[b, 2] = jnp.where(last, 0.0, moved).astype(jnp.bfloat16)

    latent = jnp.zeros((span, channels), jnp.float32)
    sums = {}
    for n, (a, b, c) in enumerate(TAPS):
        if n % 9 == 0:
            taps_a[a].wait()
        latent = latent + mm(ext[b, c, a * J : (a + F) * J, :], weight[n])
        start = pl.multiple_of((block * F + 2 - a) * J, 16)
        piece = grads[c // 2, row + 1 - b // 2, pl.ds(start, span), :]
        term = mm_t(piece, weight[n])
        key = (b % 2, c % 2)
        sums[key] = sums[key] + term if key in sums else term
    for (rp, cp), value in sums.items():
        for t in range(F):
            for half in range(2):
                lanes = slice(half * channels // 2, (half + 1) * channels // 2)
                tmp[half, pl.ds((t * 2 + rp) * 2 * J + cp, J, stride=2), :] = value[
                    t * J : (t + 1) * J, lanes
                ]
    hidden_grad = jnp.concatenate([tmp[0], tmp[1]], axis=1)
    inv_rms, unit, normed = normalised(frames[...], gain)
    sigma = 1.0 / (1.0 + jnp.exp(-normed))
    normed_grad = hidden_grad * sigma * (1.0 + normed * (1.0 - sigma))
    gain_part = jnp.sum(normed_grad * unit, axis=0, keepdims=True)
    unit_grad = normed_grad * gain
    mean = jnp.mean(unit_grad * unit, axis=-1, keepdims=True)
    frames_grad[...] = (inv_rms * (unit_grad - unit * mean)).astype(jnp.bfloat16)

    jl = J // R
    used = span // R
    order = permutation(
        (R * slot, span),
        lambda o, s: (o % slot < used)
        & (o % slot // jl == s // J)
        & (o // slot * jl + o % jl == s % J),
    )
    value = mm(order, (latent + bias).astype(jnp.bfloat16))
    line = lax.broadcasted_iota(jnp.int32, (R * slot, 1), 0) % slot
    rest = jnp.concatenate([slice_of(gain_part, block, k, T) for k in range(T)], axis=1)
    for n in range(3):
        term = rest.astype(jnp.bfloat16).astype(jnp.float32)
        rest = rest - term
        value = jnp.where(line == used + n, term, value)
    out[...] = value.astype(jnp.bfloat16)


def weight_kernel(F, J, R, T, part, place, grads, *refs):
    hidden = refs[:R]
    out_hbm, out, even, odd, sem = refs[R:]
    channels = grads.shape[-1]
    depth = T * F * J
    lanes = 2 * part
    row = place[0]
    even[:, R * depth :] = jnp.zeros((lanes, depth), jnp.bfloat16)
    for k in range(R):
        at = pl.multiple_of((row ^ k) * depth, 128)
        for rp, turned in ((0, even), (1, odd)):
            turned[:, pl.ds(at, depth)] = hidden[k][rp]
    leaving = []
    for a in range(3):
        start = (2 - a) * J
        for moved in range(2):
            right = grads[moved, 1:, start : start + depth, :].reshape(R * depth, channels)
            size = part if moved else lanes
            left = jnp.concatenate(
                [even[:size, : R * depth], odd[:size, :], even[:size, depth:]], axis=0
            )
            value = mm(left, right)
            for b in range(3):
                if moved:
                    out[(a * 3 + b) * 3 + 2] = value[b * part : (b + 1) * part]
                else:
                    for cp in range(2):
                        at = b * lanes + cp * part
                        out[(a * 3 + b) * 3 + cp] = value[at : at + part]
        taps = pl.ds(a * 9, 9)
        leaving.append(pltpu.make_async_copy(out.at[taps], out_hbm.at[taps], sem.at[a]))
        leaving[a].start()
    for copy in leaving:
        copy.wait()


def call(kernel, outs, scratch, flops, moved, places, aliases={}, limit=VMEM_LIMIT):
    kinds = {"s": pltpu.SMEM, "v": pltpu.VMEM, "h": pltpu.HBM, "a": pl.ANY}
    specs = [pl.BlockSpec(memory_space=kinds[p]) for p in places]
    count = len(places) - len(outs)
    return pl.pallas_call(
        kernel,
        out_shape=[jax.ShapeDtypeStruct(s, d) for s, d in outs],
        in_specs=specs[:count],
        out_specs=specs[count:],
        scratch_shapes=scratch,
        input_output_aliases=aliases,
        compiler_params=pltpu.CompilerParams(vmem_limit_bytes=limit),
        cost_estimate=pl.CostEstimate(flops=flops, bytes_accessed=moved, transcendentals=0),
    )


def gathered_form(frames, norm_gain, conv_weight, conv_bias, latent_grad):
    bf16, f32 = jnp.bfloat16, jnp.float32
    F, row_count, col_count, C = frames.shape
    R, T = lax.axis_size("rows"), lax.axis_size("tm")
    J = col_count // 2
    span = F * J
    part = C // T
    used = span // R
    slot = -(-(used + 3) // 16) * 16
    vectors = jnp.stack([norm_gain, conv_bias])
    flat = frames.reshape(-1, C)
    weight = conv_weight.reshape(27, C, C)
    place = jnp.stack([lax.axis_index("rows"), lax.axis_index("tm")]).astype(jnp.int32)

    own = latent_grad.reshape(1, -1, C)
    grad_rows = lax.all_to_all(
        jnp.broadcast_to(own, (R,) + own.shape[1:]), "rows", 0, 0, tiled=True
    )

    sizes = [(2 * span + (16 * J if k % 2 else 0), 2 * part) for k in range(T)]
    planes, frames_copy, vectors, *sends = call(
        functools.partial(hidden_kernel, F, J, T),
        [((2, 2, span, C), bf16), (flat.shape, bf16), ((2, C), f32)]
        + [(size, bf16) for size in sizes],
        [pltpu.VMEM((2, 4 * span, C // 2), f32)],
        60 * WORK * span * C, 16 * span * C, "svv" + "v" * (T + 3),
    )(place, flat, vectors)
    messages = [sends[0]] + [partners(sends[k], "tm", k) for k in range(1, T)]
    joined, cached, under, grad_rows = call(
        functools.partial(join_kernel, F, J, T),
        [
            ((2, 2 * part, T * span), bf16),
            ((2, 2, 2 * J, C), bf16),
            ((2, 2 * J + span, C), bf16),
            (grad_rows.shape, bf16),
        ],
        [pltpu.VMEM((2, T * span, 2 * part), bf16)],
        30 * WORK * span * C, 16 * span * C, "sav" + "v" * T + "vvva", {1: 3},
    )(place, grad_rows, planes, *messages)
    under = shifted(under, "rows", -1)
    hidden_all = exchanged(joined, "rows")
    grad_all = exchanged(grad_rows, "tm")

    packed, frames_grad, bias_sum, grads = call(
        functools.partial(slab_kernel, F, J, R, T, slot),
        [
            ((R * slot, C), bf16),
            ((4 * span, C), bf16),
            ((1, part), f32),
            ((2, R + 1, (F * T + 2) * J, C), bf16),
        ],
        [
            pltpu.VMEM((27, C, C), bf16),
            pltpu.VMEM((3, 3, (F + 2) * J, C), bf16),
            pltpu.VMEM((2, 4 * span, C // 2), f32),
            pltpu.SemaphoreType.DMA((3,)),
        ],
        270 * WORK * span * C, 2 * 27 * C * C, "svvvhvv" + "v" * (T + 4),
        limit=VMEM_LIMIT_WIDE,
    )(place, planes, cached, under, weight, frames_copy, vectors, *grad_all)

    packed = lax.all_to_all(packed.reshape(R, slot, C), "rows", 0, 0, tiled=True)
    latent = packed[:, :used].reshape(R, F, J // R, C).transpose(1, 0, 2, 3)
    gain_sum = jnp.sum(packed[:, used : used + 3].astype(f32), axis=(0, 1)).reshape(1, C)
    gain_grad = gain_sum[:, :part]
    for k in range(1, T):
        gain_grad = gain_grad + partners(gain_sum[:, k * part : (k + 1) * part], "tm", k)

    (weight_grad,) = call(
        functools.partial(weight_kernel, F, J, R, T, part),
        [((27, part, C), f32)],
        [
            pltpu.VMEM((27, part, C), f32),
            pltpu.VMEM((2 * part, (R + 1) * T * span), bf16),
            pltpu.VMEM((2 * part, R * T * span), bf16),
            pltpu.SemaphoreType.DMA((3,)),
        ],
        220 * WORK * span * C, 8 * 27 * part * C, "sv" + "v" * R + "h",
    )(place, grads, *hidden_all)

    return (
        latent,
        frames_grad.reshape(frames.shape),
        weight_grad.reshape(3, 3, 3, part, C),
        gain_grad.reshape(part),
        bias_sum.reshape(part),
    )


def on_device(frames, norm_gain, conv_weight, conv_bias, latent_grad):
    rows, shares = lax.axis_size("rows"), lax.axis_size("tm")
    operand_bytes = 2 * rows * shares * (frames.size // shares + latent_grad.size)
    result_bytes = 4 * conv_weight.size
    powers = (rows & (rows - 1)) == 0 and (shares & (shares - 1)) == 0
    if powers and frames.shape[1] == 2 and operand_bytes <= result_bytes:
        form = gathered_form
    else:
        form = reduced_form
    return form(frames, norm_gain, conv_weight, conv_bias, latent_grad)


def solution(mesh):
    placed = (P("tm", "rows", None, None), P(), P(), P(), P("tm", None, "rows", None))
    return jax.shard_map(
        on_device,
        mesh=mesh,
        in_specs=placed,
        out_specs=(
            P("tm", None, "rows", None),
            P("tm", "rows", None, None),
            P(None, None, None, "tm", None),
            P("tm"),
            P("tm"),
        ),
        check_vma=False,
    )
```

```python
import functools

import jax
import jax.numpy as jnp
from jax import lax
from jax.experimental import pallas as pl
from jax.experimental.pallas import tpu as pltpu
from jax.sharding import PartitionSpec as P

EPS = 1e-06
TAPS = [(a, b, c) for a in range(3) for b in range(3) for c in range(3)]
VMEM_LIMIT = 20 * 1024 * 1024
VMEM_LIMIT_WIDE = 48 * 1024 * 1024
WORK = 1200


def shifted(value, axis, steps):
    count = lax.axis_size(axis)
    leading, last = (max(0, -steps), min(count, count - steps))
    return lax.ppermute(value, axis, [(source, source + steps) for source in range(leading, last)])


def contract_out(grad_piece, weight_tap):
    return lax.dot_general(
        grad_piece, weight_tap, (((1,), (1,)), ((), ())), preferred_element_type=jnp.float32
    )


def reduced_form(frames, norm_gain, conv_weight, conv_bias, latent_grad):
    signal = frames.astype(jnp.float32)
    inv_rms = lax.rsqrt(jnp.mean(signal * signal, axis=-1, keepdims=True) + EPS)
    unit = signal * inv_rms
    normed = unit * norm_gain
    hidden = jax.nn.silu(normed).astype(jnp.bfloat16)
    frame_count, row_count, col_count, channels = hidden.shape
    lat_rows = row_count // 2
    lat_cols = col_count // 2
    cached = shifted(hidden[frame_count - 2 :], "tm", 1)
    stacked = jnp.concatenate([cached, hidden], axis=0)
    row_under = shifted(stacked[:, :1], "rows", -1)
    extended = jnp.concatenate([stacked, row_under], axis=1)
    extended = jnp.pad(extended, ((0, 0), (0, 0), (0, 1), (0, 0)))
    grad_rows = lax.all_to_all(latent_grad, "rows", split_axis=1, concat_axis=2, tiled=True)
    grad_flat = grad_rows.reshape(-1, channels)
    running = jnp.zeros((frame_count * lat_rows * lat_cols, channels), jnp.float32)
    blocks = []
    for tap_t, tap_r, tap_c in TAPS:
        window_piece = extended[
            tap_t : tap_t + frame_count,
            tap_r : tap_r + 2 * lat_rows : 2,
            tap_c : tap_c + 2 * lat_cols : 2,
        ]
        window_piece = window_piece.reshape(-1, channels)
        running = running + jnp.dot(
            window_piece, conv_weight[tap_t, tap_r, tap_c], preferred_element_type=jnp.float32
        )
        blocks.append(
            lax.dot_general(
                window_piece,
                grad_flat,
                (((0,), (0,)), ((), ())),
                preferred_element_type=jnp.float32,
            )
        )
    latent_rows = (
        (running + conv_bias)
        .reshape(frame_count, lat_rows, lat_cols, channels)
        .astype(jnp.bfloat16)
    )
    latent = lax.all_to_all(latent_rows, "rows", split_axis=2, concat_axis=1, tiled=True)
    weight_local = jnp.stack(blocks).reshape(3, 3, 3, channels, channels)
    bias_local = jnp.sum(grad_flat.astype(jnp.float32), axis=0)
    following = shifted(grad_rows[:2], "tm", -1)
    grad_ext = jnp.concatenate([grad_rows, following], axis=0)
    above_row = shifted(grad_ext, "rows", 1)
    grad_ext = jnp.concatenate([above_row, grad_ext], axis=1)
    grad_ext = jnp.pad(grad_ext, ((0, 0), (0, 0), (1, 0), (0, 0)))
    parity_sums = {}
    for tap_t, tap_r, tap_c in TAPS:
        row_start = 1 - tap_r // 2
        col_start = 1 - tap_c // 2
        grad_piece = grad_ext[
            2 - tap_t : 2 - tap_t + frame_count,
            row_start : row_start + lat_rows,
            col_start : col_start + lat_cols,
        ]
        term = contract_out(grad_piece.reshape(-1, channels), conv_weight[tap_t, tap_r, tap_c])
        label = (tap_r % 2, tap_c % 2)
        parity_sums[label] = parity_sums[label] + term if label in parity_sums else term
    shaped = {}
    for label in parity_sums:
        shaped[label] = parity_sums[label].reshape(frame_count, lat_rows, lat_cols, channels)
    even_rows = jnp.stack([shaped[0, 0], shaped[0, 1]], axis=3)
    odd_rows = jnp.stack([shaped[1, 0], shaped[1, 1]], axis=3)
    hidden_grad = jnp.stack([even_rows, odd_rows], axis=2).reshape(
        frame_count, row_count, col_count, channels
    )
    sigma = jax.nn.sigmoid(normed)
    normed_grad = hidden_grad * sigma * (1.0 + normed * (1.0 - sigma))
    gain_local = jnp.sum(normed_grad * unit, axis=(0, 1, 2))
    unit_grad = normed_grad * norm_gain
    frames_grad = inv_rms * (unit_grad - unit * jnp.mean(unit_grad * unit, axis=-1, keepdims=True))
    totals = lax.psum((weight_local, gain_local, bias_local), "rows")
    weight_grad, gain_grad, bias_grad = (
        lax.psum_scatter(totals[0], "tm", scatter_dimension=3, tiled=True),
        lax.psum_scatter(totals[1], "tm", scatter_dimension=0, tiled=True),
        lax.psum_scatter(totals[2], "tm", scatter_dimension=0, tiled=True),
    )
    return (latent, frames_grad.astype(jnp.bfloat16), weight_grad, gain_grad, bias_grad)


def partners(value, axis, bits):
    count = lax.axis_size(axis)
    return lax.ppermute(value, axis, [(source, source ^ bits) for source in range(count)])


def exchanged(value, axis, gate=None):
    count = lax.axis_size(axis)
    even = [value] + [partners(value, axis, k) for k in range(2, count, 2)]
    blocks = []
    for n, block in enumerate(even if gate is None else [value] + gate(even[1:])):
        blocks += [block, partners(block, axis, 1)]
    return blocks


def mm(left, right):
    return jnp.dot(left, right, preferred_element_type=jnp.float32)


def mm_t(left, right):
    return lax.dot_general(
        left, right, (((1,), (1,)), ((), ())), preferred_element_type=jnp.float32
    )


def normalised(frames, gain):
    signal = frames.astype(jnp.float32)
    inv_rms = lax.rsqrt(jnp.mean(signal * signal, axis=-1, keepdims=True) + EPS)
    unit = signal * inv_rms
    return inv_rms, unit, unit * gain


def hidden_kernel(F, J, T, place, frames, vectors, planes, frames_copy, vectors_copy, *rest):
    sends, tmp = rest[:T], rest[T]
    frames_copy[...] = frames[...]
    vectors_copy[...] = vectors[...]
    channels = frames.shape[1]
    part = channels // T
    _, _, normed = normalised(frames[...], vectors[0:1])
    value = normed / (1.0 + jnp.exp(-normed))
    tmp[0] = value[:, : channels // 2]
    tmp[1] = value[:, channels // 2 :]
    block = place[1]
    for rp in range(2):
        pair = []
        for cp in range(2):
            rows = [
                jnp.concatenate(
                    [
                        tmp[half, pl.ds((t * 2 + rp) * 2 * J + cp, J, stride=2), :]
                        for half in range(2)
                    ],
                    axis=1,
                )
                for t in range(F)
            ]
            plane = jnp.concatenate(rows, axis=0)
            pair.append(plane)
            plane = plane.astype(jnp.bfloat16)
            planes[rp, cp] = plane
            late = plane[(F - 2) * J :]
            for k in range(1, T, 2):
                for half in range(2):
                    at = (((rp * 2 + cp) * 2) + half) * 2 * J
                    lanes = slice(half * channels // 2, (half + 1) * channels // 2)
                    sends[k][2 * F * J + at : 2 * F * J + at + 2 * J] = late[:, lanes]
        pieces = [
            jnp.concatenate([p[:, d * part : (d + 1) * part] for p in pair], axis=1)
            for d in range(T)
        ]
        for k in range(T):
            chosen = pieces[0]
            for d in range(1, T):
                chosen = jnp.where(block == d ^ k, pieces[d], chosen)
            sends[k][rp * F * J : (rp + 1) * F * J] = chosen.astype(jnp.bfloat16)


def join_kernel(F, J, T, place, grad_rows, planes, *refs):
    messages, (joined, cached, under, head, passed, blocks) = refs[:T], refs[T:]
    span = F * J
    block = place[1]
    for k in range(T):
        at = pl.multiple_of((block ^ k) * span, 16)
        for rp in range(2):
            blocks[rp, pl.ds(at, span), :] = messages[k][rp * span : (rp + 1) * span, :]
    for rp in range(2):
        joined[rp] = blocks[rp].T
    passed[...] = grad_rows[...]
    for s in range(grad_rows.shape[0]):
        head[s] = grad_rows[s, : 2 * J, :]
    for rp in range(2):
        for cp in range(2):
            halves = []
            for half in range(2):
                start = 2 * span + ((rp * 2 + cp) * 2 + half) * 2 * J
                value = jnp.zeros((2 * J, messages[1].shape[1]), jnp.bfloat16)
                for k in range(1, T, 2):
                    found = (block > 0) & (block ^ k == block - 1)
                    value = jnp.where(found, messages[k][start : start + 2 * J, :], value)
                halves.append(value)
            before = jnp.concatenate(halves, axis=1)
            cached[rp, cp] = before
            if rp == 0:
                under[cp, : 2 * J] = before
                under[cp, 2 * J :] = planes[0, cp]


def permutation(shape, meet):
    row = lax.broadcasted_iota(jnp.int32, shape, 0)
    col = lax.broadcasted_iota(jnp.int32, shape, 1)
    return jnp.where(meet(row, col), 1.0, 0.0).astype(jnp.bfloat16)


def slice_of(value, block, k, T):
    part = value.shape[1] // T
    chosen = value[:, :part]
    for d in range(1, T):
        chosen = jnp.where(block == d ^ k, value[:, d * part : (d + 1) * part], chosen)
    return chosen


def shard_order(J, R, rows, first, moved):
    jl = J // R
    return permutation(
        (rows * 2 * J, R * 2 * J),
        lambda o, s: (o // (2 * J) + first == s // jl % R)
        & (o // J % 2 == s // (jl * R) % 2)
        & (o % J == s // (2 * jl * R) * jl + s % jl + moved),
    )


def shard_rows(source, start, count):
    return jnp.concatenate(
        [source[s, start : start + count, :] for s in range(source.shape[0])], axis=0
    )


def gate_kernel(*refs):
    pass


def slab_kernel(
    F, J, R, T, slot, place, planes, cached, under, weight_hbm, frames, vectors, gathered, following,
    out, frames_grad, weight, near, ext, tmp, sem,
):
    row, block = place[0], place[1]
    channels = frames.shape[1]
    span = F * J
    gain, bias = vectors[0:1], vectors[1:2]
    taps_a = [
        pltpu.make_async_copy(weight_hbm.at[pl.ds(a * 9, 9)], weight.at[pl.ds(a * 9, 9)], sem.at[a])
        for a in range(3)
    ]
    for copy in taps_a:
        copy.start()

    orders = [shard_order(J, R, 2, row - 1, moved) for moved in range(2)]
    for pair in range(F // 2 + 1):
        if pair < F // 2:
            source = shard_rows(gathered, pair * 2 * J, 2 * J)
        else:
            source = shard_rows(following, 0, 2 * J)
        for moved in range(2):
            value = mm(orders[moved], source).astype(jnp.bfloat16)
            for i in range(2):
                near[moved, i, pair * 2 * J : (pair + 1) * 2 * J, :] = value[
                    i * 2 * J : (i + 1) * 2 * J
                ]

    rows = (F + 2) * J
    last = lax.broadcasted_iota(jnp.int32, (rows, 1), 0) % J == J - 1
    for b in range(3):
        for cp in range(2):
            if b == 2:
                full = under[cp]
            else:
                full = jnp.concatenate([cached[b, cp], planes[b, cp]], axis=0)
            ext[b, cp] = full
            if cp == 0:
                moved = pltpu.roll(full.astype(jnp.float32), rows - 1, 0)
                ext[b, 2] = jnp.where(last, 0.0, moved).astype(jnp.bfloat16)

    latent = jnp.zeros((span, channels), jnp.float32)
    sums = {}
    for n, (a, b, c) in enumerate(TAPS):
        if n % 9 == 0:
            taps_a[a].wait()
        latent = latent + mm(ext[b, c, a * J : (a + F) * J, :], weight[n])
        piece = near[c // 2, 1 - b // 2, (2 - a) * J : (2 - a + F) * J, :]
        term = mm_t(piece, weight[n])
        key = (b % 2, c % 2)
        sums[key] = sums[key] + term if key in sums else term
    for (rp, cp), value in sums.items():
        for t in range(F):
            for half in range(2):
                lanes = slice(half * channels // 2, (half + 1) * channels // 2)
                tmp[half, pl.ds((t * 2 + rp) * 2 * J + cp, J, stride=2), :] = value[
                    t * J : (t + 1) * J, lanes
                ]
    hidden_grad = jnp.concatenate([tmp[0], tmp[1]], axis=1)
    inv_rms, unit, normed = normalised(frames[...], gain)
    sigma = 1.0 / (1.0 + jnp.exp(-normed))
    normed_grad = hidden_grad * sigma * (1.0 + normed * (1.0 - sigma))
    gain_part = jnp.sum(normed_grad * unit, axis=0, keepdims=True)
    unit_grad = normed_grad * gain
    mean = jnp.mean(unit_grad * unit, axis=-1, keepdims=True)
    frames_grad[...] = (inv_rms * (unit_grad - unit * mean)).astype(jnp.bfloat16)

    jl = J // R
    used = span // R
    order = permutation(
        (R * slot, span),
        lambda o, s: (o % slot < used)
        & (o % slot // jl == s // J)
        & (o // slot * jl + o % jl == s % J),
    )
    value = mm(order, (latent + bias).astype(jnp.bfloat16))
    line = lax.broadcasted_iota(jnp.int32, (R * slot, 1), 0) % slot
    rest = jnp.concatenate([slice_of(gain_part, block, k, T) for k in range(T)], axis=1)
    for n in range(3):
        term = rest.astype(jnp.bfloat16).astype(jnp.float32)
        rest = rest - term
        value = jnp.where(line == used + n, term, value)
    out[...] = value.astype(jnp.bfloat16)


def weight_kernel(F, J, R, T, part, place, _, *refs):
    gathered, hidden = refs[:T], refs[T : T + R]
    out_hbm, bias_sum, out, grads, even, odd, sem = refs[T + R :]
    channels = grads.shape[-1]
    span = F * J
    depth = T * span
    lanes = 2 * part
    row, block = place[0], place[1]
    grads[:, :, depth:, :] = jnp.zeros((2, R, 2 * J, channels), jnp.bfloat16)
    orders = [shard_order(J, R, R, 0, moved) for moved in range(2)]
    total = jnp.zeros((1, channels), jnp.float32)
    for k in range(T):
        for pair in range(F // 2):
            source = shard_rows(gathered[k], pair * 2 * J, 2 * J)
            total = total + jnp.sum(source.astype(jnp.float32), axis=0, keepdims=True)
            at = pl.multiple_of((block ^ k) * span + pair * 2 * J, 16)
            for moved in range(2):
                value = mm(orders[moved], source).astype(jnp.bfloat16)
                for i in range(R):
                    grads[moved, i, pl.ds(at, 2 * J), :] = value[i * 2 * J : (i + 1) * 2 * J]
    bias_sum[...] = slice_of(total, block, 0, T)
    even[:, R * depth :] = jnp.zeros((lanes, depth), jnp.bfloat16)
    for k in range(R):
        at = pl.multiple_of((row ^ k) * depth, 128)
        for rp, turned in ((0, even), (1, odd)):
            turned[:, pl.ds(at, depth)] = hidden[k][rp]
    leaving = []
    for a in range(3):
        start = (2 - a) * J
        for moved in range(2):
            right = grads[moved, :, start : start + depth, :].reshape(R * depth, channels)
            size = part if moved else lanes
            left = jnp.concatenate(
                [even[:size, : R * depth], odd[:size, :], even[:size, depth:]], axis=0
            )
            value = mm(left, right)
            for b in range(3):
                if moved:
                    out[(a * 3 + b) * 3 + 2] = value[b * part : (b + 1) * part]
                else:
                    for cp in range(2):
                        at = b * lanes + cp * part
                        out[(a * 3 + b) * 3 + cp] = value[at : at + part]
        taps = pl.ds(a * 9, 9)
        leaving.append(pltpu.make_async_copy(out.at[taps], out_hbm.at[taps], sem.at[a]))
        leaving[a].start()
    for copy in leaving:
        copy.wait()


def call(kernel, outs, scratch, flops, moved, places, aliases={}, limit=VMEM_LIMIT):
    kinds = {"s": pltpu.SMEM, "v": pltpu.VMEM, "h": pltpu.HBM, "a": pl.ANY}
    specs = [pl.BlockSpec(memory_space=kinds[p]) for p in places]
    count = len(places) - len(outs)
    return pl.pallas_call(
        kernel,
        out_shape=[jax.ShapeDtypeStruct(s, d) for s, d in outs],
        in_specs=specs[:count],
        out_specs=specs[count:],
        scratch_shapes=scratch,
        input_output_aliases=aliases,
        compiler_params=pltpu.CompilerParams(vmem_limit_bytes=limit),
        cost_estimate=pl.CostEstimate(flops=flops, bytes_accessed=moved, transcendentals=0),
    )


def gathered_form(frames, norm_gain, conv_weight, conv_bias, latent_grad):
    bf16, f32 = jnp.bfloat16, jnp.float32
    F, row_count, col_count, C = frames.shape
    R, T = lax.axis_size("rows"), lax.axis_size("tm")
    J = col_count // 2
    span = F * J
    part = C // T
    used = span // R
    slot = -(-(used + 3) // 16) * 16
    vectors = jnp.stack([norm_gain, conv_bias])
    flat = frames.reshape(-1, C)
    weight = conv_weight.reshape(27, C, C)
    place = jnp.stack([lax.axis_index("rows"), lax.axis_index("tm")]).astype(jnp.int32)

    own = latent_grad.reshape(1, -1, C)
    grad_rows = lax.all_to_all(
        jnp.broadcast_to(own, (R,) + own.shape[1:]), "rows", 0, 0, tiled=True
    )

    sizes = [(2 * span + (16 * J if k % 2 else 0), 2 * part) for k in range(T)]
    planes, frames_copy, vectors, *sends = call(
        functools.partial(hidden_kernel, F, J, T),
        [((2, 2, span, C), bf16), (flat.shape, bf16), ((2, C), f32)]
        + [(size, bf16) for size in sizes],
        [pltpu.VMEM((2, 4 * span, C // 2), f32)],
        60 * WORK * span * C, 16 * span * C, "svv" + "v" * (T + 3),
    )(place, flat, vectors)
    messages = [sends[0]] + [partners(sends[k], "tm", k) for k in range(1, T)]
    joined, cached, under, head, grad_rows = call(
        functools.partial(join_kernel, F, J, T),
        [
            ((2, 2 * part, T * span), bf16),
            ((2, 2, 2 * J, C), bf16),
            ((2, 2 * J + span, C), bf16),
            ((R, 2 * J, C), bf16),
            (grad_rows.shape, bf16),
        ],
        [pltpu.VMEM((2, T * span, 2 * part), bf16)],
        30 * WORK * span * C, 16 * span * C, "svv" + "v" * T + "vvvvv",
    )(place, grad_rows, planes, *messages)
    under = shifted(under, "rows", -1)
    following = shifted(head, "tm", -1)
    packed, frames_grad = call(
        functools.partial(slab_kernel, F, J, R, T, slot),
        [((R * slot, C), bf16), ((4 * span, C), bf16)],
        [
            pltpu.VMEM((27, C, C), bf16),
            pltpu.VMEM((2, 2, (F + 2) * J, C), bf16),
            pltpu.VMEM((3, 3, (F + 2) * J, C), bf16),
            pltpu.VMEM((2, 4 * span, C // 2), f32),
            pltpu.SemaphoreType.DMA((3,)),
        ],
        2 * 54 * span * C * C, 2 * 27 * C * C, "svvvhvvvv" + "vv",
        limit=VMEM_LIMIT_WIDE,
    )(place, planes, cached, under, weight, frames_copy, vectors, grad_rows, following)

    def after_slab(blocks):
        shapes = [(b.shape, bf16) for b in blocks]
        count = len(blocks)
        aliases = {n + 1: n for n in range(count)}
        return list(
            call(gate_kernel, shapes, [], 0, 0, "a" * (2 * count + 1), aliases)(packed, *blocks)
        )

    hidden_all = exchanged(joined, "rows", after_slab)
    grad_all = exchanged(grad_rows, "tm")

    packed = lax.all_to_all(packed.reshape(R, slot, C), "rows", 0, 0, tiled=True)
    latent = packed[:, :used].reshape(R, F, J // R, C).transpose(1, 0, 2, 3)
    gain_sum = jnp.sum(packed[:, used : used + 3].astype(f32), axis=(0, 1)).reshape(1, C)
    gain_grad = gain_sum[:, :part]
    for k in range(1, T):
        gain_grad = gain_grad + partners(gain_sum[:, k * part : (k + 1) * part], "tm", k)

    weight_grad, bias_sum = call(
        functools.partial(weight_kernel, F, J, R, T, part),
        [((27, part, C), f32), ((1, part), f32)],
        [
            pltpu.VMEM((27, part, C), f32),
            pltpu.VMEM((2, R, (F * T + 2) * J, C), bf16),
            pltpu.VMEM((2 * part, (R + 1) * T * span), bf16),
            pltpu.VMEM((2 * part, R * T * span), bf16),
            pltpu.SemaphoreType.DMA((3,)),
        ],
        220 * WORK * span * C, 8 * 27 * part * C, "sa" + "v" * (T + R) + "hv",
    )(place, gain_sum, *grad_all, *hidden_all)

    return (
        latent,
        frames_grad.reshape(frames.shape),
        weight_grad.reshape(3, 3, 3, part, C),
        gain_grad.reshape(part),
        bias_sum.reshape(part),
    )


def on_device(frames, norm_gain, conv_weight, conv_bias, latent_grad):
    rows, shares = lax.axis_size("rows"), lax.axis_size("tm")
    operand_bytes = 2 * rows * shares * (frames.size // shares + latent_grad.size)
    result_bytes = 4 * conv_weight.size
    powers = (rows & (rows - 1)) == 0 and (shares & (shares - 1)) == 0
    if powers and frames.shape[1] == 2 and operand_bytes <= result_bytes:
        form = gathered_form
    else:
        form = reduced_form
    return form(frames, norm_gain, conv_weight, conv_bias, latent_grad)


def solution(mesh):
    placed = (P("tm", "rows", None, None), P(), P(), P(), P("tm", None, "rows", None))
    return jax.shard_map(
        on_device,
        mesh=mesh,
        in_specs=placed,
        out_specs=(
            P("tm", None, "rows", None),
            P("tm", "rows", None, None),
            P(None, None, None, "tm", None),
            P("tm"),
            P("tm"),
        ),
        check_vma=False,
    )
```

```python
import functools

import jax
import jax.numpy as jnp
from jax import lax
from jax.experimental import pallas as pl
from jax.experimental.pallas import tpu as pltpu
from jax.sharding import PartitionSpec as P

EPS = 1e-06
TAPS = [(a, b, c) for a in range(3) for b in range(3) for c in range(3)]
VMEM_LIMIT = 20 * 1024 * 1024
WORK = 1200


def shifted(value, axis, steps):
    count = lax.axis_size(axis)
    leading, last = (max(0, -steps), min(count, count - steps))
    return lax.ppermute(value, axis, [(source, source + steps) for source in range(leading, last)])


def contract_out(grad_piece, weight_tap):
    return lax.dot_general(
        grad_piece, weight_tap, (((1,), (1,)), ((), ())), preferred_element_type=jnp.float32
    )


def reduced_form(frames, norm_gain, conv_weight, conv_bias, latent_grad):
    signal = frames.astype(jnp.float32)
    inv_rms = lax.rsqrt(jnp.mean(signal * signal, axis=-1, keepdims=True) + EPS)
    unit = signal * inv_rms
    normed = unit * norm_gain
    hidden = jax.nn.silu(normed).astype(jnp.bfloat16)
    frame_count, row_count, col_count, channels = hidden.shape
    lat_rows = row_count // 2
    lat_cols = col_count // 2
    cached = shifted(hidden[frame_count - 2 :], "tm", 1)
    stacked = jnp.concatenate([cached, hidden], axis=0)
    row_under = shifted(stacked[:, :1], "rows", -1)
    extended = jnp.concatenate([stacked, row_under], axis=1)
    extended = jnp.pad(extended, ((0, 0), (0, 0), (0, 1), (0, 0)))
    grad_rows = lax.all_to_all(latent_grad, "rows", split_axis=1, concat_axis=2, tiled=True)
    grad_flat = grad_rows.reshape(-1, channels)
    running = jnp.zeros((frame_count * lat_rows * lat_cols, channels), jnp.float32)
    blocks = []
    for tap_t, tap_r, tap_c in TAPS:
        window_piece = extended[
            tap_t : tap_t + frame_count,
            tap_r : tap_r + 2 * lat_rows : 2,
            tap_c : tap_c + 2 * lat_cols : 2,
        ]
        window_piece = window_piece.reshape(-1, channels)
        running = running + jnp.dot(
            window_piece, conv_weight[tap_t, tap_r, tap_c], preferred_element_type=jnp.float32
        )
        blocks.append(
            lax.dot_general(
                window_piece,
                grad_flat,
                (((0,), (0,)), ((), ())),
                preferred_element_type=jnp.float32,
            )
        )
    latent_rows = (
        (running + conv_bias)
        .reshape(frame_count, lat_rows, lat_cols, channels)
        .astype(jnp.bfloat16)
    )
    latent = lax.all_to_all(latent_rows, "rows", split_axis=2, concat_axis=1, tiled=True)
    weight_local = jnp.stack(blocks).reshape(3, 3, 3, channels, channels)
    bias_local = jnp.sum(grad_flat.astype(jnp.float32), axis=0)
    following = shifted(grad_rows[:2], "tm", -1)
    grad_ext = jnp.concatenate([grad_rows, following], axis=0)
    above_row = shifted(grad_ext, "rows", 1)
    grad_ext = jnp.concatenate([above_row, grad_ext], axis=1)
    grad_ext = jnp.pad(grad_ext, ((0, 0), (0, 0), (1, 0), (0, 0)))
    parity_sums = {}
    for tap_t, tap_r, tap_c in TAPS:
        row_start = 1 - tap_r // 2
        col_start = 1 - tap_c // 2
        grad_piece = grad_ext[
            2 - tap_t : 2 - tap_t + frame_count,
            row_start : row_start + lat_rows,
            col_start : col_start + lat_cols,
        ]
        term = contract_out(grad_piece.reshape(-1, channels), conv_weight[tap_t, tap_r, tap_c])
        label = (tap_r % 2, tap_c % 2)
        parity_sums[label] = parity_sums[label] + term if label in parity_sums else term
    shaped = {}
    for label in parity_sums:
        shaped[label] = parity_sums[label].reshape(frame_count, lat_rows, lat_cols, channels)
    even_rows = jnp.stack([shaped[0, 0], shaped[0, 1]], axis=3)
    odd_rows = jnp.stack([shaped[1, 0], shaped[1, 1]], axis=3)
    hidden_grad = jnp.stack([even_rows, odd_rows], axis=2).reshape(
        frame_count, row_count, col_count, channels
    )
    sigma = jax.nn.sigmoid(normed)
    normed_grad = hidden_grad * sigma * (1.0 + normed * (1.0 - sigma))
    gain_local = jnp.sum(normed_grad * unit, axis=(0, 1, 2))
    unit_grad = normed_grad * norm_gain
    frames_grad = inv_rms * (unit_grad - unit * jnp.mean(unit_grad * unit, axis=-1, keepdims=True))
    totals = lax.psum((weight_local, gain_local, bias_local), "rows")
    weight_grad, gain_grad, bias_grad = (
        lax.psum_scatter(totals[0], "tm", scatter_dimension=3, tiled=True),
        lax.psum_scatter(totals[1], "tm", scatter_dimension=0, tiled=True),
        lax.psum_scatter(totals[2], "tm", scatter_dimension=0, tiled=True),
    )
    return (latent, frames_grad.astype(jnp.bfloat16), weight_grad, gain_grad, bias_grad)


def partners(value, axis, bits):
    count = lax.axis_size(axis)
    return lax.ppermute(value, axis, [(source, source ^ bits) for source in range(count)])


def exchanged(value, axis, gate=None):
    count = lax.axis_size(axis)
    even = [value] + [partners(value, axis, k) for k in range(2, count, 2)]
    blocks = []
    for n, block in enumerate(even if gate is None else [value] + gate(even[1:])):
        blocks += [block, partners(block, axis, 1)]
    return blocks


def mm(left, right):
    return jnp.dot(left, right, preferred_element_type=jnp.float32)


def mm_t(left, right):
    return lax.dot_general(
        left, right, (((1,), (1,)), ((), ())), preferred_element_type=jnp.float32
    )


def normalised(frames, gain):
    signal = frames.astype(jnp.float32)
    inv_rms = lax.rsqrt(jnp.mean(signal * signal, axis=-1, keepdims=True) + EPS)
    unit = signal * inv_rms
    return inv_rms, unit, unit * gain


def hidden_kernel(F, J, T, place, frames, vectors, planes, frames_copy, vectors_copy, *rest):
    sends, tmp = rest[:T], rest[T]
    frames_copy[...] = frames[...]
    vectors_copy[...] = vectors[...]
    channels = frames.shape[1]
    part = channels // T
    _, _, normed = normalised(frames[...], vectors[0:1])
    value = normed / (1.0 + jnp.exp(-normed))
    tmp[0] = value[:, : channels // 2]
    tmp[1] = value[:, channels // 2 :]
    block = place[1]
    for rp in range(2):
        pair = []
        for cp in range(2):
            rows = [
                jnp.concatenate(
                    [
                        tmp[half, pl.ds((t * 2 + rp) * 2 * J + cp, J, stride=2), :]
                        for half in range(2)
                    ],
                    axis=1,
                )
                for t in range(F)
            ]
            plane = jnp.concatenate(rows, axis=0)
            pair.append(plane)
            plane = plane.astype(jnp.bfloat16)
            planes[rp, cp] = plane
            late = plane[(F - 2) * J :]
            for k in range(1, T, 2):
                for half in range(2):
                    at = (((rp * 2 + cp) * 2) + half) * 2 * J
                    lanes = slice(half * channels // 2, (half + 1) * channels // 2)
                    sends[k][2 * F * J + at : 2 * F * J + at + 2 * J] = late[:, lanes]
        pieces = [
            jnp.concatenate([p[:, d * part : (d + 1) * part] for p in pair], axis=1)
            for d in range(T)
        ]
        for k in range(T):
            chosen = pieces[0]
            for d in range(1, T):
                chosen = jnp.where(block == d ^ k, pieces[d], chosen)
            sends[k][rp * F * J : (rp + 1) * F * J] = chosen.astype(jnp.bfloat16)


def join_kernel(F, J, T, place, grad_rows, planes, *refs):
    messages, (joined, cached, under, head, passed, blocks) = refs[:T], refs[T:]
    span = F * J
    block = place[1]
    for k in range(T):
        at = pl.multiple_of((block ^ k) * span, 16)
        for rp in range(2):
            blocks[rp, pl.ds(at, span), :] = messages[k][rp * span : (rp + 1) * span, :]
    for rp in range(2):
        joined[rp] = blocks[rp].T
    passed[...] = grad_rows[...]
    for s in range(grad_rows.shape[0]):
        head[s] = grad_rows[s, : 2 * J, :]
    for rp in range(2):
        for cp in range(2):
            halves = []
            for half in range(2):
                start = 2 * span + ((rp * 2 + cp) * 2 + half) * 2 * J
                value = jnp.zeros((2 * J, messages[1].shape[1]), jnp.bfloat16)
                for k in range(1, T, 2):
                    found = (block > 0) & (block ^ k == block - 1)
                    value = jnp.where(found, messages[k][start : start + 2 * J, :], value)
                halves.append(value)
            before = jnp.concatenate(halves, axis=1)
            cached[rp, cp] = before
            if rp == 0:
                under[cp, : 2 * J] = before
                under[cp, 2 * J :] = planes[0, cp]


def permutation(shape, meet):
    row = lax.broadcasted_iota(jnp.int32, shape, 0)
    col = lax.broadcasted_iota(jnp.int32, shape, 1)
    return jnp.where(meet(row, col), 1.0, 0.0).astype(jnp.bfloat16)


def slice_of(value, block, k, T):
    part = value.shape[1] // T
    chosen = value[:, :part]
    for d in range(1, T):
        chosen = jnp.where(block == d ^ k, value[:, d * part : (d + 1) * part], chosen)
    return chosen


def shard_order(J, R, rows, first, moved):
    jl = J // R
    return permutation(
        (rows * 2 * J, R * 2 * J),
        lambda o, s: (o // (2 * J) + first == s // jl % R)
        & (o // J % 2 == s // (jl * R) % 2)
        & (o % J == s // (2 * jl * R) * jl + s % jl + moved),
    )


def shard_rows(source, start, count):
    return jnp.concatenate(
        [source[s, start : start + count, :] for s in range(source.shape[0])], axis=0
    )


def gate_kernel(*refs):
    pass


def slab_kernel(
    F, J, R, T, slot, place, planes, cached, under, weight, frames, vectors, gathered, following,
    out, frames_grad, near, ext, tmp,
):
    row, block = place[0], place[1]
    channels = frames.shape[1]
    span = F * J
    gain, bias = vectors[0:1], vectors[1:2]

    orders = [shard_order(J, R, 2, row - 1, moved) for moved in range(2)]
    for pair in range(F // 2 + 1):
        if pair < F // 2:
            source = shard_rows(gathered, pair * 2 * J, 2 * J)
        else:
            source = shard_rows(following, 0, 2 * J)
        for moved in range(2):
            value = mm(orders[moved], source).astype(jnp.bfloat16)
            for i in range(2):
                near[moved, i, pair * 2 * J : (pair + 1) * 2 * J, :] = value[
                    i * 2 * J : (i + 1) * 2 * J
                ]

    rows = (F + 2) * J
    last = lax.broadcasted_iota(jnp.int32, (rows, 1), 0) % J == J - 1
    for b in range(3):
        for cp in range(2):
            if b == 2:
                full = under[cp]
            else:
                full = jnp.concatenate([cached[b, cp], planes[b, cp]], axis=0)
            ext[b, cp] = full
            if cp == 0:
                moved = pltpu.roll(full.astype(jnp.float32), rows - 1, 0)
                ext[b, 2] = jnp.where(last, 0.0, moved).astype(jnp.bfloat16)

    latent = jnp.zeros((span, channels), jnp.float32)
    sums = {}
    for n, (a, b, c) in enumerate(TAPS):
        latent = latent + mm(ext[b, c, a * J : (a + F) * J, :], weight[n])
        piece = near[c // 2, 1 - b // 2, (2 - a) * J : (2 - a + F) * J, :]
        term = mm_t(piece, weight[n])
        key = (b % 2, c % 2)
        sums[key] = sums[key] + term if key in sums else term
    for (rp, cp), value in sums.items():
        for t in range(F):
            for half in range(2):
                lanes = slice(half * channels // 2, (half + 1) * channels // 2)
                tmp[half, pl.ds((t * 2 + rp) * 2 * J + cp, J, stride=2), :] = value[
                    t * J : (t + 1) * J, lanes
                ]
    hidden_grad = jnp.concatenate([tmp[0], tmp[1]], axis=1)
    inv_rms, unit, normed = normalised(frames[...], gain)
    sigma = 1.0 / (1.0 + jnp.exp(-normed))
    normed_grad = hidden_grad * sigma * (1.0 + normed * (1.0 - sigma))
    gain_part = jnp.sum(normed_grad * unit, axis=0, keepdims=True)
    unit_grad = normed_grad * gain
    mean = jnp.mean(unit_grad * unit, axis=-1, keepdims=True)
    frames_grad[...] = (inv_rms * (unit_grad - unit * mean)).astype(jnp.bfloat16)

    jl = J // R
    used = span // R
    order = permutation(
        (R * slot, span),
        lambda o, s: (o % slot < used)
        & (o % slot // jl == s // J)
        & (o // slot * jl + o % jl == s % J),
    )
    value = mm(order, (latent + bias).astype(jnp.bfloat16))
    line = lax.broadcasted_iota(jnp.int32, (R * slot, 1), 0) % slot
    rest = jnp.concatenate([slice_of(gain_part, block, k, T) for k in range(T)], axis=1)
    for n in range(3):
        term = rest.astype(jnp.bfloat16).astype(jnp.float32)
        rest = rest - term
        value = jnp.where(line == used + n, term, value)
    out[...] = value.astype(jnp.bfloat16)


def gain_kernel(T, used, received, _, *parts):
    value = jnp.zeros(received.shape[1:], jnp.float32)
    for s in range(received.shape[0]):
        value = value + received[s].astype(jnp.float32)
    line = lax.broadcasted_iota(jnp.int32, (received.shape[1], 1), 0)
    value = jnp.where((line >= used) & (line < used + 3), value, 0.0)
    value = jnp.sum(value, axis=0, keepdims=True)
    part = received.shape[2] // T
    for k in range(T):
        parts[k][...] = value[:, k * part : (k + 1) * part]


def order_kernel(F, J, R, T, place, *refs):
    gathered, (grads, bias_sum) = refs[:T], refs[T:]
    channels = grads.shape[-1]
    span = F * J
    depth = T * span
    block = place[1]
    grads[:, :, depth:, :] = jnp.zeros((2, R, 2 * J, channels), jnp.bfloat16)
    orders = [shard_order(J, R, R, 0, moved) for moved in range(2)]
    total = jnp.zeros((1, channels), jnp.float32)
    for k in range(T):
        for pair in range(F // 2):
            source = shard_rows(gathered[k], pair * 2 * J, 2 * J)
            total = total + jnp.sum(source.astype(jnp.float32), axis=0, keepdims=True)
            at = pl.multiple_of((block ^ k) * span + pair * 2 * J, 16)
            for moved in range(2):
                value = mm(orders[moved], source).astype(jnp.bfloat16)
                for i in range(R):
                    grads[moved, i, pl.ds(at, 2 * J), :] = value[i * 2 * J : (i + 1) * 2 * J]
    bias_sum[...] = slice_of(total, block, 0, T)


def weight_kernel(F, J, R, T, part, place, _, grads, *refs):
    hidden = refs[:R]
    out_hbm, out, even, odd, sem = refs[R:]
    channels = grads.shape[-1]
    depth = T * F * J
    lanes = 2 * part
    row = place[0]
    even[:, R * depth :] = jnp.zeros((lanes, depth), jnp.bfloat16)
    for k in range(R):
        at = pl.multiple_of((row ^ k) * depth, 128)
        for rp, turned in ((0, even), (1, odd)):
            turned[:, pl.ds(at, depth)] = hidden[k][rp]
    leaving = []
    for a in range(3):
        start = (2 - a) * J
        for moved in range(2):
            right = grads[moved, :, start : start + depth, :].reshape(R * depth, channels)
            size = part if moved else lanes
            left = jnp.concatenate(
                [even[:size, : R * depth], odd[:size, :], even[:size, depth:]], axis=0
            )
            value = mm(left, right)
            for b in range(3):
                if moved:
                    out[(a * 3 + b) * 3 + 2] = value[b * part : (b + 1) * part]
                else:
                    for cp in range(2):
                        at = b * lanes + cp * part
                        out[(a * 3 + b) * 3 + cp] = value[at : at + part]
        taps = pl.ds(a * 9, 9)
        leaving.append(pltpu.make_async_copy(out.at[taps], out_hbm.at[taps], sem.at[a]))
        leaving[a].start()
    for copy in leaving:
        copy.wait()


def call(kernel, outs, scratch, flops, moved, places, aliases={}):
    kinds = {"s": pltpu.SMEM, "v": pltpu.VMEM, "h": pltpu.HBM, "a": pl.ANY}
    specs = [pl.BlockSpec(memory_space=kinds[p]) for p in places]
    count = len(places) - len(outs)
    return pl.pallas_call(
        kernel,
        out_shape=[jax.ShapeDtypeStruct(s, d) for s, d in outs],
        in_specs=specs[:count],
        out_specs=specs[count:],
        scratch_shapes=scratch,
        input_output_aliases=aliases,
        compiler_params=pltpu.CompilerParams(vmem_limit_bytes=VMEM_LIMIT),
        cost_estimate=pl.CostEstimate(flops=flops, bytes_accessed=moved, transcendentals=0),
    )


def gathered_form(frames, norm_gain, conv_weight, conv_bias, latent_grad):
    bf16, f32 = jnp.bfloat16, jnp.float32
    F, row_count, col_count, C = frames.shape
    R, T = lax.axis_size("rows"), lax.axis_size("tm")
    J = col_count // 2
    span = F * J
    part = C // T
    used = span // R
    slot = -(-(used + 3) // 16) * 16
    vectors = jnp.stack([norm_gain, conv_bias])
    flat = frames.reshape(-1, C)
    weight = conv_weight.reshape(27, C, C)
    place = jnp.stack([lax.axis_index("rows"), lax.axis_index("tm")]).astype(jnp.int32)

    own = latent_grad.reshape(1, -1, C)
    grad_rows = lax.all_to_all(
        jnp.broadcast_to(own, (R,) + own.shape[1:]), "rows", 0, 0, tiled=True
    )

    sizes = [(2 * span + (16 * J if k % 2 else 0), 2 * part) for k in range(T)]
    planes, frames_copy, vectors, *sends = call(
        functools.partial(hidden_kernel, F, J, T),
        [((2, 2, span, C), bf16), (flat.shape, bf16), ((2, C), f32)]
        + [(size, bf16) for size in sizes],
        [pltpu.VMEM((2, 4 * span, C // 2), f32)],
        60 * WORK * span * C, 16 * span * C, "svv" + "v" * (T + 3),
    )(place, flat, vectors)
    messages = [sends[0]] + [partners(sends[k], "tm", k) for k in range(1, T)]
    joined, cached, under, head, grad_rows = call(
        functools.partial(join_kernel, F, J, T),
        [
            ((2, 2 * part, T * span), bf16),
            ((2, 2, 2 * J, C), bf16),
            ((2, 2 * J + span, C), bf16),
            ((R, 2 * J, C), bf16),
            (grad_rows.shape, bf16),
        ],
        [pltpu.VMEM((2, T * span, 2 * part), bf16)],
        30 * WORK * span * C, 16 * span * C, "svv" + "v" * T + "vvvvv",
    )(place, grad_rows, planes, *messages)
    under = shifted(under, "rows", -1)
    following = shifted(head, "tm", -1)
    packed, frames_grad = call(
        functools.partial(slab_kernel, F, J, R, T, slot),
        [((R * slot, C), bf16), ((4 * span, C), bf16)],
        [
            pltpu.VMEM((2, 2, (F + 2) * J, C), bf16),
            pltpu.VMEM((3, 3, (F + 2) * J, C), bf16),
            pltpu.VMEM((2, 4 * span, C // 2), f32),
        ],
        2 * 54 * span * C * C, 2 * 27 * C * C, "svvvvvvvv" + "vv",
    )(place, planes, cached, under, weight, frames_copy, vectors, grad_rows, following)

    def after_slab(blocks):
        shapes = [(b.shape, bf16) for b in blocks]
        count = len(blocks)
        aliases = {n + 1: n for n in range(count)}
        return list(
            call(gate_kernel, shapes, [], 0, 0, "a" * (2 * count + 1), aliases)(packed, *blocks)
        )

    hidden_all = exchanged(joined, "rows", after_slab)
    grad_all = exchanged(grad_rows, "tm")

    packed = lax.all_to_all(packed.reshape(R, slot, C), "rows", 0, 0, tiled=True)
    latent = packed[:, :used].reshape(R, F, J // R, C).transpose(1, 0, 2, 3)
    gains = call(
        functools.partial(gain_kernel, T, used),
        [((1, part), f32)] * T,
        [], R * slot * C, R * slot * C, "va" + "v" * T,
    )(packed, hidden_all[2])
    gain_grad = gains[0]
    for k in range(1, T):
        gain_grad = gain_grad + partners(gains[k], "tm", k)

    grads, bias_sum = call(
        functools.partial(order_kernel, F, J, R, T),
        [((2, R, (F * T + 2) * J, C), bf16), ((1, part), f32)],
        [],
        90 * WORK * span * C, 2 * R * T * span * C, "s" + "v" * (T + 2),
    )(place, *grad_all)
    (weight_grad,) = call(
        functools.partial(weight_kernel, F, J, R, T, part),
        [((27, part, C), f32)],
        [
            pltpu.VMEM((27, part, C), f32),
            pltpu.VMEM((2 * part, (R + 1) * T * span), bf16),
            pltpu.VMEM((2 * part, R * T * span), bf16),
            pltpu.SemaphoreType.DMA((3,)),
        ],
        200 * WORK * span * C, 8 * 27 * part * C, "sav" + "v" * R + "h",
    )(place, gains[0], grads, *hidden_all)

    return (
        latent,
        frames_grad.reshape(frames.shape),
        weight_grad.reshape(3, 3, 3, part, C),
        gain_grad.reshape(part),
        bias_sum.reshape(part),
    )


def on_device(frames, norm_gain, conv_weight, conv_bias, latent_grad):
    rows, shares = lax.axis_size("rows"), lax.axis_size("tm")
    operand_bytes = 2 * rows * shares * (frames.size // shares + latent_grad.size)
    result_bytes = 4 * conv_weight.size
    powers = (rows & (rows - 1)) == 0 and (shares & (shares - 1)) == 0
    if powers and frames.shape[1] == 2 and operand_bytes <= result_bytes:
        form = gathered_form
    else:
        form = reduced_form
    return form(frames, norm_gain, conv_weight, conv_bias, latent_grad)


def solution(mesh):
    placed = (P("tm", "rows", None, None), P(), P(), P(), P("tm", None, "rows", None))
    return jax.shard_map(
        on_device,
        mesh=mesh,
        in_specs=placed,
        out_specs=(
            P("tm", None, "rows", None),
            P("tm", "rows", None, None),
            P(None, None, None, "tm", None),
            P("tm"),
            P("tm"),
        ),
        check_vma=False,
    )
```

```python
import functools

import jax
import jax.numpy as jnp
from jax import lax
from jax.experimental import pallas as pl
from jax.experimental.pallas import tpu as pltpu
from jax.sharding import PartitionSpec as P

EPS = 1e-06
TAPS = [(a, b, c) for a in range(3) for b in range(3) for c in range(3)]
VMEM_LIMIT = 20 * 1024 * 1024
VMEM_LIMIT_WIDE = 61 * 1024 * 1024
WORK = 1200


def shifted(value, axis, steps):
    count = lax.axis_size(axis)
    leading, last = (max(0, -steps), min(count, count - steps))
    return lax.ppermute(value, axis, [(source, source + steps) for source in range(leading, last)])


def contract_out(grad_piece, weight_tap):
    return lax.dot_general(
        grad_piece, weight_tap, (((1,), (1,)), ((), ())), preferred_element_type=jnp.float32
    )


def reduced_form(frames, norm_gain, conv_weight, conv_bias, latent_grad):
    signal = frames.astype(jnp.float32)
    inv_rms = lax.rsqrt(jnp.mean(signal * signal, axis=-1, keepdims=True) + EPS)
    unit = signal * inv_rms
    normed = unit * norm_gain
    hidden = jax.nn.silu(normed).astype(jnp.bfloat16)
    frame_count, row_count, col_count, channels = hidden.shape
    lat_rows = row_count // 2
    lat_cols = col_count // 2
    cached = shifted(hidden[frame_count - 2 :], "tm", 1)
    stacked = jnp.concatenate([cached, hidden], axis=0)
    row_under = shifted(stacked[:, :1], "rows", -1)
    extended = jnp.concatenate([stacked, row_under], axis=1)
    extended = jnp.pad(extended, ((0, 0), (0, 0), (0, 1), (0, 0)))
    grad_rows = lax.all_to_all(latent_grad, "rows", split_axis=1, concat_axis=2, tiled=True)
    grad_flat = grad_rows.reshape(-1, channels)
    running = jnp.zeros((frame_count * lat_rows * lat_cols, channels), jnp.float32)
    blocks = []
    for tap_t, tap_r, tap_c in TAPS:
        window_piece = extended[
            tap_t : tap_t + frame_count,
            tap_r : tap_r + 2 * lat_rows : 2,
            tap_c : tap_c + 2 * lat_cols : 2,
        ]
        window_piece = window_piece.reshape(-1, channels)
        running = running + jnp.dot(
            window_piece, conv_weight[tap_t, tap_r, tap_c], preferred_element_type=jnp.float32
        )
        blocks.append(
            lax.dot_general(
                window_piece,
                grad_flat,
                (((0,), (0,)), ((), ())),
                preferred_element_type=jnp.float32,
            )
        )
    latent_rows = (
        (running + conv_bias)
        .reshape(frame_count, lat_rows, lat_cols, channels)
        .astype(jnp.bfloat16)
    )
    latent = lax.all_to_all(latent_rows, "rows", split_axis=2, concat_axis=1, tiled=True)
    weight_local = jnp.stack(blocks).reshape(3, 3, 3, channels, channels)
    bias_local = jnp.sum(grad_flat.astype(jnp.float32), axis=0)
    following = shifted(grad_rows[:2], "tm", -1)
    grad_ext = jnp.concatenate([grad_rows, following], axis=0)
    above_row = shifted(grad_ext, "rows", 1)
    grad_ext = jnp.concatenate([above_row, grad_ext], axis=1)
    grad_ext = jnp.pad(grad_ext, ((0, 0), (0, 0), (1, 0), (0, 0)))
    parity_sums = {}
    for tap_t, tap_r, tap_c in TAPS:
        row_start = 1 - tap_r // 2
        col_start = 1 - tap_c // 2
        grad_piece = grad_ext[
            2 - tap_t : 2 - tap_t + frame_count,
            row_start : row_start + lat_rows,
            col_start : col_start + lat_cols,
        ]
        term = contract_out(grad_piece.reshape(-1, channels), conv_weight[tap_t, tap_r, tap_c])
        label = (tap_r % 2, tap_c % 2)
        parity_sums[label] = parity_sums[label] + term if label in parity_sums else term
    shaped = {}
    for label in parity_sums:
        shaped[label] = parity_sums[label].reshape(frame_count, lat_rows, lat_cols, channels)
    even_rows = jnp.stack([shaped[0, 0], shaped[0, 1]], axis=3)
    odd_rows = jnp.stack([shaped[1, 0], shaped[1, 1]], axis=3)
    hidden_grad = jnp.stack([even_rows, odd_rows], axis=2).reshape(
        frame_count, row_count, col_count, channels
    )
    sigma = jax.nn.sigmoid(normed)
    normed_grad = hidden_grad * sigma * (1.0 + normed * (1.0 - sigma))
    gain_local = jnp.sum(normed_grad * unit, axis=(0, 1, 2))
    unit_grad = normed_grad * norm_gain
    frames_grad = inv_rms * (unit_grad - unit * jnp.mean(unit_grad * unit, axis=-1, keepdims=True))
    totals = lax.psum((weight_local, gain_local, bias_local), "rows")
    weight_grad, gain_grad, bias_grad = (
        lax.psum_scatter(totals[0], "tm", scatter_dimension=3, tiled=True),
        lax.psum_scatter(totals[1], "tm", scatter_dimension=0, tiled=True),
        lax.psum_scatter(totals[2], "tm", scatter_dimension=0, tiled=True),
    )
    return (latent, frames_grad.astype(jnp.bfloat16), weight_grad, gain_grad, bias_grad)


def partners(value, axis, bits):
    count = lax.axis_size(axis)
    return lax.ppermute(value, axis, [(source, source ^ bits) for source in range(count)])


def exchanged(value, axis, gate=None):
    count = lax.axis_size(axis)
    even = [value] + [partners(value, axis, k) for k in range(2, count, 2)]
    blocks = []
    for n, block in enumerate(even if gate is None else [value] + gate(even[1:])):
        blocks += [block, partners(block, axis, 1)]
    return blocks


def mm(left, right):
    return jnp.dot(left, right, preferred_element_type=jnp.float32)


def mm_t(left, right):
    return lax.dot_general(
        left, right, (((1,), (1,)), ((), ())), preferred_element_type=jnp.float32
    )


def normalised(frames, gain):
    signal = frames.astype(jnp.float32)
    inv_rms = lax.rsqrt(jnp.mean(signal * signal, axis=-1, keepdims=True) + EPS)
    unit = signal * inv_rms
    return inv_rms, unit, unit * gain


def hidden_kernel(F, J, T, place, frames, vectors, planes, frames_copy, vectors_copy, *rest):
    sends, tmp = rest[:T], rest[T]
    frames_copy[...] = frames[...]
    vectors_copy[...] = vectors[...]
    channels = frames.shape[1]
    part = channels // T
    _, _, normed = normalised(frames[...], vectors[0:1])
    value = normed / (1.0 + jnp.exp(-normed))
    tmp[0] = value[:, : channels // 2]
    tmp[1] = value[:, channels // 2 :]
    block = place[1]
    for rp in range(2):
        pair = []
        for cp in range(2):
            rows = [
                jnp.concatenate(
                    [
                        tmp[half, pl.ds((t * 2 + rp) * 2 * J + cp, J, stride=2), :]
                        for half in range(2)
                    ],
                    axis=1,
                )
                for t in range(F)
            ]
            plane = jnp.concatenate(rows, axis=0)
            pair.append(plane)
            plane = plane.astype(jnp.bfloat16)
            planes[rp, cp] = plane
            late = plane[(F - 2) * J :]
            for k in range(1, T, 2):
                for half in range(2):
                    at = (((rp * 2 + cp) * 2) + half) * 2 * J
                    lanes = slice(half * channels // 2, (half + 1) * channels // 2)
                    sends[k][2 * F * J + at : 2 * F * J + at + 2 * J] = late[:, lanes]
        pieces = [
            jnp.concatenate([p[:, d * part : (d + 1) * part] for p in pair], axis=1)
            for d in range(T)
        ]
        for k in range(T):
            chosen = pieces[0]
            for d in range(1, T):
                chosen = jnp.where(block == d ^ k, pieces[d], chosen)
            sends[k][rp * F * J : (rp + 1) * F * J] = chosen.astype(jnp.bfloat16)


def join_kernel(F, J, T, place, grad_rows, planes, *refs):
    messages, (joined, cached, under, head, passed, blocks) = refs[:T], refs[T:]
    span = F * J
    block = place[1]
    for k in range(T):
        at = pl.multiple_of((block ^ k) * span, 16)
        for rp in range(2):
            blocks[rp, pl.ds(at, span), :] = messages[k][rp * span : (rp + 1) * span, :]
    for rp in range(2):
        joined[rp] = blocks[rp].T
    passed[...] = grad_rows[...]
    for s in range(grad_rows.shape[0]):
        head[s] = grad_rows[s, : 2 * J, :]
    for rp in range(2):
        for cp in range(2):
            halves = []
            for half in range(2):
                start = 2 * span + ((rp * 2 + cp) * 2 + half) * 2 * J
                value = jnp.zeros((2 * J, messages[1].shape[1]), jnp.bfloat16)
                for k in range(1, T, 2):
                    found = (block > 0) & (block ^ k == block - 1)
                    value = jnp.where(found, messages[k][start : start + 2 * J, :], value)
                halves.append(value)
            before = jnp.concatenate(halves, axis=1)
            cached[rp, cp] = before
            if rp == 0:
                under[cp, : 2 * J] = before
                under[cp, 2 * J :] = planes[0, cp]


def permutation(shape, meet):
    row = lax.broadcasted_iota(jnp.int32, shape, 0)
    col = lax.broadcasted_iota(jnp.int32, shape, 1)
    return jnp.where(meet(row, col), 1.0, 0.0).astype(jnp.bfloat16)


def slice_of(value, block, k, T):
    part = value.shape[1] // T
    chosen = value[:, :part]
    for d in range(1, T):
        chosen = jnp.where(block == d ^ k, value[:, d * part : (d + 1) * part], chosen)
    return chosen


def shard_order(J, R, rows, first, moved):
    jl = J // R
    return permutation(
        (rows * 2 * J, R * 2 * J),
        lambda o, s: (o // (2 * J) + first == s // jl % R)
        & (o // J % 2 == s // (jl * R) % 2)
        & (o % J == s // (2 * jl * R) * jl + s % jl + moved),
    )


def shard_rows(source, start, count):
    return jnp.concatenate(
        [source[s, start : start + count, :] for s in range(source.shape[0])], axis=0
    )


def gate_kernel(*refs):
    pass


def slab_kernel(
    F, J, R, T, slot, place, planes, cached, under, weight_hbm, frames, vectors, gathered, following,
    out, frames_grad, weight, near, ext, tmp, sem,
):
    row, block = place[0], place[1]
    channels = frames.shape[1]
    span = F * J
    gain, bias = vectors[0:1], vectors[1:2]
    fetches = [
        pltpu.make_async_copy(weight_hbm.at[pl.ds(a * 9, 9)], weight.at[pl.ds(a * 9, 9)], sem.at[a])
        for a in range(3)
    ]
    for copy in fetches:
        copy.start()

    orders = [shard_order(J, R, 2, row - 1, moved) for moved in range(2)]
    for pair in range(F // 2 + 1):
        if pair < F // 2:
            source = shard_rows(gathered, pair * 2 * J, 2 * J)
        else:
            source = shard_rows(following, 0, 2 * J)
        for moved in range(2):
            value = mm(orders[moved], source).astype(jnp.bfloat16)
            for i in range(2):
                near[moved, i, pair * 2 * J : (pair + 1) * 2 * J, :] = value[
                    i * 2 * J : (i + 1) * 2 * J
                ]

    rows = (F + 2) * J
    last = lax.broadcasted_iota(jnp.int32, (rows, 1), 0) % J == J - 1
    for b in range(3):
        for cp in range(2):
            if b == 2:
                full = under[cp]
            else:
                full = jnp.concatenate([cached[b, cp], planes[b, cp]], axis=0)
            ext[b, cp] = full
            if cp == 0:
                moved = pltpu.roll(full.astype(jnp.float32), rows - 1, 0)
                ext[b, 2] = jnp.where(last, 0.0, moved).astype(jnp.bfloat16)

    latent = jnp.zeros((span, channels), jnp.float32)
    sums = {}
    for n, (a, b, c) in enumerate(TAPS):
        if n % 9 == 0:
            fetches[a].wait()
        latent = latent + mm(ext[b, c, a * J : (a + F) * J, :], weight[n])
        piece = near[c // 2, 1 - b // 2, (2 - a) * J : (2 - a + F) * J, :]
        term = mm_t(piece, weight[n])
        key = (b % 2, c % 2)
        sums[key] = sums[key] + term if key in sums else term
    for (rp, cp), value in sums.items():
        for t in range(F):
            for half in range(2):
                lanes = slice(half * channels // 2, (half + 1) * channels // 2)
                tmp[half, pl.ds((t * 2 + rp) * 2 * J + cp, J, stride=2), :] = value[
                    t * J : (t + 1) * J, lanes
                ]
    hidden_grad = jnp.concatenate([tmp[0], tmp[1]], axis=1)
    inv_rms, unit, normed = normalised(frames[...], gain)
    sigma = 1.0 / (1.0 + jnp.exp(-normed))
    normed_grad = hidden_grad * sigma * (1.0 + normed * (1.0 - sigma))
    gain_part = jnp.sum(normed_grad * unit, axis=0, keepdims=True)
    unit_grad = normed_grad * gain
    mean = jnp.mean(unit_grad * unit, axis=-1, keepdims=True)
    frames_grad[...] = (inv_rms * (unit_grad - unit * mean)).astype(jnp.bfloat16)

    jl = J // R
    used = span // R
    order = permutation(
        (R * slot, span),
        lambda o, s: (o % slot < used)
        & (o % slot // jl == s // J)
        & (o // slot * jl + o % jl == s % J),
    )
    value = mm(order, (latent + bias).astype(jnp.bfloat16))
    line = lax.broadcasted_iota(jnp.int32, (R * slot, 1), 0) % slot
    rest = jnp.concatenate([slice_of(gain_part, block, k, T) for k in range(T)], axis=1)
    for n in range(3):
        term = rest.astype(jnp.bfloat16).astype(jnp.float32)
        rest = rest - term
        value = jnp.where(line == used + n, term, value)
    out[...] = value.astype(jnp.bfloat16)


def gain_kernel(T, used, received, _, *parts):
    value = jnp.zeros(received.shape[1:], jnp.float32)
    for s in range(received.shape[0]):
        value = value + received[s].astype(jnp.float32)
    line = lax.broadcasted_iota(jnp.int32, (received.shape[1], 1), 0)
    value = jnp.where((line >= used) & (line < used + 3), value, 0.0)
    value = jnp.sum(value, axis=0, keepdims=True)
    part = received.shape[2] // T
    for k in range(T):
        parts[k][...] = value[:, k * part : (k + 1) * part]


def order_kernel(F, J, R, T, place, *refs):
    gathered, (grads, bias_sum) = refs[:T], refs[T:]
    channels = grads.shape[-1]
    span = F * J
    depth = T * span
    block = place[1]
    grads[:, :, depth:, :] = jnp.zeros((2, R, 2 * J, channels), jnp.bfloat16)
    orders = [shard_order(J, R, R, 0, moved) for moved in range(2)]
    total = jnp.zeros((1, channels), jnp.float32)
    for k in range(T):
        for pair in range(F // 2):
            source = shard_rows(gathered[k], pair * 2 * J, 2 * J)
            total = total + jnp.sum(source.astype(jnp.float32), axis=0, keepdims=True)
            at = pl.multiple_of((block ^ k) * span + pair * 2 * J, 16)
            for moved in range(2):
                value = mm(orders[moved], source).astype(jnp.bfloat16)
                for i in range(R):
                    grads[moved, i, pl.ds(at, 2 * J), :] = value[i * 2 * J : (i + 1) * 2 * J]
    bias_sum[...] = slice_of(total, block, 0, T)


def weight_kernel(F, J, R, T, part, place, _, grads, *refs):
    hidden = refs[:R]
    out_hbm, out, even, odd, sem = refs[R:]
    channels = grads.shape[-1]
    depth = T * F * J
    lanes = 2 * part
    row = place[0]
    even[:, R * depth :] = jnp.zeros((lanes, depth), jnp.bfloat16)
    for k in range(R):
        at = pl.multiple_of((row ^ k) * depth, 128)
        for rp, turned in ((0, even), (1, odd)):
            turned[:, pl.ds(at, depth)] = hidden[k][rp]
    leaving = []
    for a in range(3):
        start = (2 - a) * J
        for moved in range(2):
            right = grads[moved, :, start : start + depth, :].reshape(R * depth, channels)
            size = part if moved else lanes
            left = jnp.concatenate(
                [even[:size, : R * depth], odd[:size, :], even[:size, depth:]], axis=0
            )
            value = mm(left, right)
            for b in range(3):
                if moved:
                    out[(a * 3 + b) * 3 + 2] = value[b * part : (b + 1) * part]
                else:
                    for cp in range(2):
                        at = b * lanes + cp * part
                        out[(a * 3 + b) * 3 + cp] = value[at : at + part]
        taps = pl.ds(a * 9, 9)
        leaving.append(pltpu.make_async_copy(out.at[taps], out_hbm.at[taps], sem.at[a]))
        leaving[a].start()
    for copy in leaving:
        copy.wait()


def call(kernel, outs, scratch, flops, moved, places, aliases={}, limit=VMEM_LIMIT):
    kinds = {"s": pltpu.SMEM, "v": pltpu.VMEM, "h": pltpu.HBM, "a": pl.ANY}
    specs = [pl.BlockSpec(memory_space=kinds[p]) for p in places]
    count = len(places) - len(outs)
    return pl.pallas_call(
        kernel,
        out_shape=[jax.ShapeDtypeStruct(s, d) for s, d in outs],
        in_specs=specs[:count],
        out_specs=specs[count:],
        scratch_shapes=scratch,
        input_output_aliases=aliases,
        compiler_params=pltpu.CompilerParams(vmem_limit_bytes=limit),
        cost_estimate=pl.CostEstimate(flops=flops, bytes_accessed=moved, transcendentals=0),
    )


def gathered_form(frames, norm_gain, conv_weight, conv_bias, latent_grad):
    bf16, f32 = jnp.bfloat16, jnp.float32
    F, row_count, col_count, C = frames.shape
    R, T = lax.axis_size("rows"), lax.axis_size("tm")
    J = col_count // 2
    span = F * J
    part = C // T
    used = span // R
    slot = -(-(used + 3) // 16) * 16
    vectors = jnp.stack([norm_gain, conv_bias])
    flat = frames.reshape(-1, C)
    weight = conv_weight.reshape(27, C, C)
    place = jnp.stack([lax.axis_index("rows"), lax.axis_index("tm")]).astype(jnp.int32)

    own = latent_grad.reshape(1, -1, C)
    grad_rows = lax.all_to_all(
        jnp.broadcast_to(own, (R,) + own.shape[1:]), "rows", 0, 0, tiled=True
    )

    sizes = [(2 * span + (16 * J if k % 2 else 0), 2 * part) for k in range(T)]
    planes, frames_copy, vectors, *sends = call(
        functools.partial(hidden_kernel, F, J, T),
        [((2, 2, span, C), bf16), (flat.shape, bf16), ((2, C), f32)]
        + [(size, bf16) for size in sizes],
        [pltpu.VMEM((2, 4 * span, C // 2), f32)],
        60 * WORK * span * C, 16 * span * C, "svv" + "v" * (T + 3),
    )(place, flat, vectors)
    messages = [sends[0]] + [partners(sends[k], "tm", k) for k in range(1, T)]
    joined, cached, under, head, grad_rows = call(
        functools.partial(join_kernel, F, J, T),
        [
            ((2, 2 * part, T * span), bf16),
            ((2, 2, 2 * J, C), bf16),
            ((2, 2 * J + span, C), bf16),
            ((R, 2 * J, C), bf16),
            (grad_rows.shape, bf16),
        ],
        [pltpu.VMEM((2, T * span, 2 * part), bf16)],
        30 * WORK * span * C, 16 * span * C, "svv" + "v" * T + "vvvvv",
    )(place, grad_rows, planes, *messages)
    under = shifted(under, "rows", -1)
    following = shifted(head, "tm", -1)
    packed, frames_grad = call(
        functools.partial(slab_kernel, F, J, R, T, slot),
        [((R * slot, C), bf16), ((4 * span, C), bf16)],
        [
            pltpu.VMEM((27, C, C), bf16),
            pltpu.VMEM((2, 2, (F + 2) * J, C), bf16),
            pltpu.VMEM((3, 3, (F + 2) * J, C), bf16),
            pltpu.VMEM((2, 4 * span, C // 2), f32),
            pltpu.SemaphoreType.DMA((3,)),
        ],
        2 * 54 * span * C * C, 2 * 27 * C * C, "svvvhvvvv" + "vv",
        limit=VMEM_LIMIT_WIDE,
    )(place, planes, cached, under, weight, frames_copy, vectors, grad_rows, following)

    def after_slab(blocks):
        shapes = [(b.shape, bf16) for b in blocks]
        count = len(blocks)
        aliases = {n + 1: n for n in range(count)}
        return list(
            call(gate_kernel, shapes, [], 0, 0, "a" * (2 * count + 1), aliases)(packed, *blocks)
        )

    hidden_all = exchanged(joined, "rows", after_slab)
    grad_all = exchanged(grad_rows, "tm")

    packed = lax.all_to_all(packed.reshape(R, slot, C), "rows", 0, 0, tiled=True)
    latent = packed[:, :used].reshape(R, F, J // R, C).transpose(1, 0, 2, 3)
    gains = call(
        functools.partial(gain_kernel, T, used),
        [((1, part), f32)] * T,
        [], R * slot * C, R * slot * C, "va" + "v" * T,
    )(packed, hidden_all[-1])
    gain_grad = gains[0]
    for k in range(1, T):
        gain_grad = gain_grad + partners(gains[k], "tm", k)

    grads, bias_sum = call(
        functools.partial(order_kernel, F, J, R, T),
        [((2, R, (F * T + 2) * J, C), bf16), ((1, part), f32)],
        [],
        90 * WORK * span * C, 2 * R * T * span * C, "s" + "v" * (T + 2),
    )(place, *grad_all)
    (weight_grad,) = call(
        functools.partial(weight_kernel, F, J, R, T, part),
        [((27, part, C), f32)],
        [
            pltpu.VMEM((27, part, C), f32),
            pltpu.VMEM((2 * part, (R + 1) * T * span), bf16),
            pltpu.VMEM((2 * part, R * T * span), bf16),
            pltpu.SemaphoreType.DMA((3,)),
        ],
        200 * WORK * span * C, 8 * 27 * part * C, "sav" + "v" * R + "h",
    )(place, gains[0], grads, *hidden_all)

    return (
        latent,
        frames_grad.reshape(frames.shape),
        weight_grad.reshape(3, 3, 3, part, C),
        gain_grad.reshape(part),
        bias_sum.reshape(part),
    )


def on_device(frames, norm_gain, conv_weight, conv_bias, latent_grad):
    rows, shares = lax.axis_size("rows"), lax.axis_size("tm")
    operand_bytes = 2 * rows * shares * (frames.size // shares + latent_grad.size)
    result_bytes = 4 * conv_weight.size
    powers = (rows & (rows - 1)) == 0 and (shares & (shares - 1)) == 0
    if powers and frames.shape[1] == 2 and operand_bytes <= result_bytes:
        form = gathered_form
    else:
        form = reduced_form
    return form(frames, norm_gain, conv_weight, conv_bias, latent_grad)


def solution(mesh):
    placed = (P("tm", "rows", None, None), P(), P(), P(), P("tm", None, "rows", None))
    return jax.shard_map(
        on_device,
        mesh=mesh,
        in_specs=placed,
        out_specs=(
            P("tm", None, "rows", None),
            P("tm", "rows", None, None),
            P(None, None, None, "tm", None),
            P("tm"),
            P("tm"),
        ),
        check_vma=False,
    )
```

```python
import functools

import jax
import jax.numpy as jnp
from jax import lax
from jax.experimental import pallas as pl
from jax.experimental.pallas import tpu as pltpu
from jax.sharding import PartitionSpec as P

EPS = 1e-06
TAPS = [(a, b, c) for a in range(3) for b in range(3) for c in range(3)]
VMEM_LIMIT = 20 * 1024 * 1024
VMEM_LIMIT_WIDE = 60 * 1024 * 1024
WORK = 1200


def shifted(value, axis, steps):
    count = lax.axis_size(axis)
    leading, last = (max(0, -steps), min(count, count - steps))
    return lax.ppermute(value, axis, [(source, source + steps) for source in range(leading, last)])


def contract_out(grad_piece, weight_tap):
    return lax.dot_general(
        grad_piece, weight_tap, (((1,), (1,)), ((), ())), preferred_element_type=jnp.float32
    )


def reduced_form(frames, norm_gain, conv_weight, conv_bias, latent_grad):
    signal = frames.astype(jnp.float32)
    inv_rms = lax.rsqrt(jnp.mean(signal * signal, axis=-1, keepdims=True) + EPS)
    unit = signal * inv_rms
    normed = unit * norm_gain
    hidden = jax.nn.silu(normed).astype(jnp.bfloat16)
    frame_count, row_count, col_count, channels = hidden.shape
    lat_rows = row_count // 2
    lat_cols = col_count // 2
    cached = shifted(hidden[frame_count - 2 :], "tm", 1)
    stacked = jnp.concatenate([cached, hidden], axis=0)
    row_under = shifted(stacked[:, :1], "rows", -1)
    extended = jnp.concatenate([stacked, row_under], axis=1)
    extended = jnp.pad(extended, ((0, 0), (0, 0), (0, 1), (0, 0)))
    grad_rows = lax.all_to_all(latent_grad, "rows", split_axis=1, concat_axis=2, tiled=True)
    grad_flat = grad_rows.reshape(-1, channels)
    running = jnp.zeros((frame_count * lat_rows * lat_cols, channels), jnp.float32)
    blocks = []
    for tap_t, tap_r, tap_c in TAPS:
        window_piece = extended[
            tap_t : tap_t + frame_count,
            tap_r : tap_r + 2 * lat_rows : 2,
            tap_c : tap_c + 2 * lat_cols : 2,
        ]
        window_piece = window_piece.reshape(-1, channels)
        running = running + jnp.dot(
            window_piece, conv_weight[tap_t, tap_r, tap_c], preferred_element_type=jnp.float32
        )
        blocks.append(
            lax.dot_general(
                window_piece,
                grad_flat,
                (((0,), (0,)), ((), ())),
                preferred_element_type=jnp.float32,
            )
        )
    latent_rows = (
        (running + conv_bias)
        .reshape(frame_count, lat_rows, lat_cols, channels)
        .astype(jnp.bfloat16)
    )
    latent = lax.all_to_all(latent_rows, "rows", split_axis=2, concat_axis=1, tiled=True)
    weight_local = jnp.stack(blocks).reshape(3, 3, 3, channels, channels)
    bias_local = jnp.sum(grad_flat.astype(jnp.float32), axis=0)
    following = shifted(grad_rows[:2], "tm", -1)
    grad_ext = jnp.concatenate([grad_rows, following], axis=0)
    above_row = shifted(grad_ext, "rows", 1)
    grad_ext = jnp.concatenate([above_row, grad_ext], axis=1)
    grad_ext = jnp.pad(grad_ext, ((0, 0), (0, 0), (1, 0), (0, 0)))
    parity_sums = {}
    for tap_t, tap_r, tap_c in TAPS:
        row_start = 1 - tap_r // 2
        col_start = 1 - tap_c // 2
        grad_piece = grad_ext[
            2 - tap_t : 2 - tap_t + frame_count,
            row_start : row_start + lat_rows,
            col_start : col_start + lat_cols,
        ]
        term = contract_out(grad_piece.reshape(-1, channels), conv_weight[tap_t, tap_r, tap_c])
        label = (tap_r % 2, tap_c % 2)
        parity_sums[label] = parity_sums[label] + term if label in parity_sums else term
    shaped = {}
    for label in parity_sums:
        shaped[label] = parity_sums[label].reshape(frame_count, lat_rows, lat_cols, channels)
    even_rows = jnp.stack([shaped[0, 0], shaped[0, 1]], axis=3)
    odd_rows = jnp.stack([shaped[1, 0], shaped[1, 1]], axis=3)
    hidden_grad = jnp.stack([even_rows, odd_rows], axis=2).reshape(
        frame_count, row_count, col_count, channels
    )
    sigma = jax.nn.sigmoid(normed)
    normed_grad = hidden_grad * sigma * (1.0 + normed * (1.0 - sigma))
    gain_local = jnp.sum(normed_grad * unit, axis=(0, 1, 2))
    unit_grad = normed_grad * norm_gain
    frames_grad = inv_rms * (unit_grad - unit * jnp.mean(unit_grad * unit, axis=-1, keepdims=True))
    totals = lax.psum((weight_local, gain_local, bias_local), "rows")
    weight_grad, gain_grad, bias_grad = (
        lax.psum_scatter(totals[0], "tm", scatter_dimension=3, tiled=True),
        lax.psum_scatter(totals[1], "tm", scatter_dimension=0, tiled=True),
        lax.psum_scatter(totals[2], "tm", scatter_dimension=0, tiled=True),
    )
    return (latent, frames_grad.astype(jnp.bfloat16), weight_grad, gain_grad, bias_grad)


def partners(value, axis, bits):
    count = lax.axis_size(axis)
    return lax.ppermute(value, axis, [(source, source ^ bits) for source in range(count)])


def exchanged(value, axis, gate=None):
    count = lax.axis_size(axis)
    blocks = {0: value}
    for k in range(1, count):
        if k & (k - 1) == 0:
            blocks[k] = partners(value, axis, k)
    if gate is not None:
        held = [k for k in blocks if k > 1]
        blocks.update(zip(held, gate([blocks[k] for k in held])))
    for k in range(1, count):
        low = k & -k
        if k != low:
            blocks[k] = partners(blocks[k - low], axis, low)
    return [blocks[k] for k in range(count)]


def mm(left, right):
    return jnp.dot(left, right, preferred_element_type=jnp.float32)


def mm_t(left, right):
    return lax.dot_general(
        left, right, (((1,), (1,)), ((), ())), preferred_element_type=jnp.float32
    )


def normalised(frames, gain):
    signal = frames.astype(jnp.float32)
    inv_rms = lax.rsqrt(jnp.mean(signal * signal, axis=-1, keepdims=True) + EPS)
    unit = signal * inv_rms
    return inv_rms, unit, unit * gain


def hidden_kernel(F, J, T, place, frames, vectors, planes, frames_copy, vectors_copy, *rest):
    sends, tmp = rest[:T], rest[T]
    frames_copy[...] = frames[...]
    vectors_copy[...] = vectors[...]
    channels = frames.shape[1]
    part = channels // T
    _, _, normed = normalised(frames[...], vectors[0:1])
    value = normed / (1.0 + jnp.exp(-normed))
    tmp[0] = value[:, : channels // 2]
    tmp[1] = value[:, channels // 2 :]
    block = place[1]
    for rp in range(2):
        pair = []
        for cp in range(2):
            rows = [
                jnp.concatenate(
                    [
                        tmp[half, pl.ds((t * 2 + rp) * 2 * J + cp, J, stride=2), :]
                        for half in range(2)
                    ],
                    axis=1,
                )
                for t in range(F)
            ]
            plane = jnp.concatenate(rows, axis=0)
            pair.append(plane)
            plane = plane.astype(jnp.bfloat16)
            planes[rp, cp] = plane
            late = plane[(F - 2) * J :]
            for k in range(1, T, 2):
                for half in range(2):
                    at = (((rp * 2 + cp) * 2) + half) * 2 * J
                    lanes = slice(half * channels // 2, (half + 1) * channels // 2)
                    sends[k][2 * F * J + at : 2 * F * J + at + 2 * J] = late[:, lanes]
        pieces = [
            jnp.concatenate([p[:, d * part : (d + 1) * part] for p in pair], axis=1)
            for d in range(T)
        ]
        for k in range(T):
            chosen = pieces[0]
            for d in range(1, T):
                chosen = jnp.where(block == d ^ k, pieces[d], chosen)
            sends[k][rp * F * J : (rp + 1) * F * J] = chosen.astype(jnp.bfloat16)


def head_kernel(rows, _, grad_rows, head, passed):
    passed[...] = grad_rows[...]
    for s in range(grad_rows.shape[0]):
        head[s] = grad_rows[s, :rows, :]


def join_kernel(F, J, T, place, planes, *refs):
    messages, (joined, cached, under, blocks) = refs[:T], refs[T:]
    span = F * J
    block = place[1]
    for k in range(T):
        at = pl.multiple_of((block ^ k) * span, 16)
        for rp in range(2):
            blocks[rp, pl.ds(at, span), :] = messages[k][rp * span : (rp + 1) * span, :]
    for rp in range(2):
        joined[rp] = blocks[rp].T
    for rp in range(2):
        for cp in range(2):
            halves = []
            for half in range(2):
                start = 2 * span + ((rp * 2 + cp) * 2 + half) * 2 * J
                value = jnp.zeros((2 * J, messages[1].shape[1]), jnp.bfloat16)
                for k in range(1, T, 2):
                    found = (block > 0) & (block ^ k == block - 1)
                    value = jnp.where(found, messages[k][start : start + 2 * J, :], value)
                halves.append(value)
            before = jnp.concatenate(halves, axis=1)
            cached[rp, cp] = before
            if rp == 0:
                under[cp, : 2 * J] = before
                under[cp, 2 * J :] = planes[0, cp]


def permutation(shape, meet):
    row = lax.broadcasted_iota(jnp.int32, shape, 0)
    col = lax.broadcasted_iota(jnp.int32, shape, 1)
    return jnp.where(meet(row, col), 1.0, 0.0).astype(jnp.bfloat16)


def slice_of(value, block, k, T):
    part = value.shape[1] // T
    chosen = value[:, :part]
    for d in range(1, T):
        chosen = jnp.where(block == d ^ k, value[:, d * part : (d + 1) * part], chosen)
    return chosen


def shard_order(J, R, rows, first, moved):
    jl = J // R
    return permutation(
        (rows * 2 * J, R * 2 * J),
        lambda o, s: (o // (2 * J) + first == s // jl % R)
        & (o // J % 2 == s // (jl * R) % 2)
        & (o % J == s // (2 * jl * R) * jl + s % jl + moved),
    )


def shard_rows(source, start, count):
    return jnp.concatenate(
        [source[s, start : start + count, :] for s in range(source.shape[0])], axis=0
    )


def gate_kernel(*refs):
    pass


def slab_kernel(
    F, J, R, T, slot, place, planes, cached, under, weight_hbm, frames, vectors, gathered, following,
    out, frames_grad, weight, near, ext, tmp, sem,
):
    row, block = place[0], place[1]
    channels = frames.shape[1]
    span = F * J
    gain, bias = vectors[0:1], vectors[1:2]
    fetches = [
        pltpu.make_async_copy(weight_hbm.at[pl.ds(a * 9, 9)], weight.at[pl.ds(a * 9, 9)], sem.at[a])
        for a in range(3)
    ]
    for copy in fetches:
        copy.start()

    orders = [shard_order(J, R, 2, row - 1, moved) for moved in range(2)]
    for pair in range(F // 2 + 1):
        if pair < F // 2:
            source = shard_rows(gathered, pair * 2 * J, 2 * J)
        else:
            source = shard_rows(following, 0, 2 * J)
        for moved in range(2):
            value = mm(orders[moved], source).astype(jnp.bfloat16)
            for i in range(2):
                near[moved, i, pair * 2 * J : (pair + 1) * 2 * J, :] = value[
                    i * 2 * J : (i + 1) * 2 * J
                ]

    rows = (F + 2) * J
    last = lax.broadcasted_iota(jnp.int32, (rows, 1), 0) % J == J - 1
    for b in range(3):
        for cp in range(2):
            if b == 2:
                full = under[cp]
            else:
                full = jnp.concatenate([cached[b, cp], planes[b, cp]], axis=0)
            ext[b, cp] = full
            if cp == 0:
                moved = pltpu.roll(full.astype(jnp.float32), rows - 1, 0)
                ext[b, 2] = jnp.where(last, 0.0, moved).astype(jnp.bfloat16)

    latent = jnp.zeros((span, channels), jnp.float32)
    sums = {}
    for n, (a, b, c) in enumerate(TAPS):
        if n % 9 == 0:
            fetches[a].wait()
        latent = latent + mm(ext[b, c, a * J : (a + F) * J, :], weight[n])
        piece = near[c // 2, 1 - b // 2, (2 - a) * J : (2 - a + F) * J, :]
        term = mm_t(piece, weight[n])
        key = (b % 2, c % 2)
        sums[key] = sums[key] + term if key in sums else term
    for (rp, cp), value in sums.items():
        for t in range(F):
            for half in range(2):
                lanes = slice(half * channels // 2, (half + 1) * channels // 2)
                tmp[half, pl.ds((t * 2 + rp) * 2 * J + cp, J, stride=2), :] = value[
                    t * J : (t + 1) * J, lanes
                ]
    hidden_grad = jnp.concatenate([tmp[0], tmp[1]], axis=1)
    inv_rms, unit, normed = normalised(frames[...], gain)
    sigma = 1.0 / (1.0 + jnp.exp(-normed))
    normed_grad = hidden_grad * sigma * (1.0 + normed * (1.0 - sigma))
    gain_part = jnp.sum(normed_grad * unit, axis=0, keepdims=True)
    unit_grad = normed_grad * gain
    mean = jnp.mean(unit_grad * unit, axis=-1, keepdims=True)
    frames_grad[...] = (inv_rms * (unit_grad - unit * mean)).astype(jnp.bfloat16)

    jl = J // R
    used = span // R
    order = permutation(
        (R * slot, span),
        lambda o, s: (o % slot < used)
        & (o % slot // jl == s // J)
        & (o // slot * jl + o % jl == s % J),
    )
    value = mm(order, (latent + bias).astype(jnp.bfloat16))
    line = lax.broadcasted_iota(jnp.int32, (R * slot, 1), 0) % slot
    rest = jnp.concatenate([slice_of(gain_part, block, k, T) for k in range(T)], axis=1)
    for n in range(3):
        term = rest.astype(jnp.bfloat16).astype(jnp.float32)
        rest = rest - term
        value = jnp.where(line == used + n, term, value)
    out[...] = value.astype(jnp.bfloat16)


def gain_kernel(T, used, received, *refs):
    parts = refs[-T:]
    value = jnp.zeros(received.shape[1:], jnp.float32)
    for s in range(received.shape[0]):
        value = value + received[s].astype(jnp.float32)
    line = lax.broadcasted_iota(jnp.int32, (received.shape[1], 1), 0)
    value = jnp.where((line >= used) & (line < used + 3), value, 0.0)
    value = jnp.sum(value, axis=0, keepdims=True)
    part = received.shape[2] // T
    for k in range(T):
        parts[k][...] = value[:, k * part : (k + 1) * part]


def order_kernel(F, J, R, T, place, *refs):
    gathered, (grads, bias_sum) = refs[:T], refs[T:]
    channels = grads.shape[-1]
    span = F * J
    depth = T * span
    block = place[1]
    grads[:, :, depth:, :] = jnp.zeros((2, R, 2 * J, channels), jnp.bfloat16)
    orders = [shard_order(J, R, R, 0, moved) for moved in range(2)]
    total = jnp.zeros((1, channels), jnp.float32)
    for k in range(T):
        for pair in range(F // 2):
            source = shard_rows(gathered[k], pair * 2 * J, 2 * J)
            total = total + jnp.sum(source.astype(jnp.float32), axis=0, keepdims=True)
            at = pl.multiple_of((block ^ k) * span + pair * 2 * J, 16)
            for moved in range(2):
                value = mm(orders[moved], source).astype(jnp.bfloat16)
                for i in range(R):
                    grads[moved, i, pl.ds(at, 2 * J), :] = value[i * 2 * J : (i + 1) * 2 * J]
    bias_sum[...] = slice_of(total, block, 0, T)


def weight_kernel(F, J, R, T, part, place, _, grads, *refs):
    hidden = refs[:R]
    out_hbm, out, even, odd, sem = refs[R:]
    channels = grads.shape[-1]
    depth = T * F * J
    lanes = 2 * part
    row = place[0]
    even[:, R * depth :] = jnp.zeros((lanes, depth), jnp.bfloat16)
    for k in range(R):
        at = pl.multiple_of((row ^ k) * depth, 128)
        for rp, turned in ((0, even), (1, odd)):
            turned[:, pl.ds(at, depth)] = hidden[k][rp]
    leaving = []
    for a in range(3):
        start = (2 - a) * J
        for moved in range(2):
            right = grads[moved, :, start : start + depth, :].reshape(R * depth, channels)
            size = part if moved else lanes
            left = jnp.concatenate(
                [even[:size, : R * depth], odd[:size, :], even[:size, depth:]], axis=0
            )
            value = mm(left, right)
            for b in range(3):
                if moved:
                    out[(a * 3 + b) * 3 + 2] = value[b * part : (b + 1) * part]
                else:
                    for cp in range(2):
                        at = b * lanes + cp * part
                        out[(a * 3 + b) * 3 + cp] = value[at : at + part]
        taps = pl.ds(a * 9, 9)
        leaving.append(pltpu.make_async_copy(out.at[taps], out_hbm.at[taps], sem.at[a]))
        leaving[a].start()
    for copy in leaving:
        copy.wait()


def call(kernel, outs, scratch, flops, moved, places, aliases={}, limit=VMEM_LIMIT):
    kinds = {"s": pltpu.SMEM, "v": pltpu.VMEM, "h": pltpu.HBM, "a": pl.ANY}
    specs = [pl.BlockSpec(memory_space=kinds[p]) for p in places]
    count = len(places) - len(outs)
    return pl.pallas_call(
        kernel,
        out_shape=[jax.ShapeDtypeStruct(s, d) for s, d in outs],
        in_specs=specs[:count],
        out_specs=specs[count:],
        scratch_shapes=scratch,
        input_output_aliases=aliases,
        compiler_params=pltpu.CompilerParams(vmem_limit_bytes=limit),
        cost_estimate=pl.CostEstimate(flops=flops, bytes_accessed=moved, transcendentals=0),
    )


def gathered_form(frames, norm_gain, conv_weight, conv_bias, latent_grad):
    bf16, f32 = jnp.bfloat16, jnp.float32
    F, row_count, col_count, C = frames.shape
    R, T = lax.axis_size("rows"), lax.axis_size("tm")
    J = col_count // 2
    span = F * J
    part = C // T
    used = span // R
    slot = -(-(used + 3) // 16) * 16
    vectors = jnp.stack([norm_gain, conv_bias])
    flat = frames.reshape(-1, C)
    weight = conv_weight.reshape(27, C, C)
    place = jnp.stack([lax.axis_index("rows"), lax.axis_index("tm")]).astype(jnp.int32)

    own = latent_grad.reshape(1, -1, C)
    grad_rows = lax.all_to_all(
        jnp.broadcast_to(own, (R,) + own.shape[1:]), "rows", 0, 0, tiled=True
    )

    sizes = [(2 * span + (16 * J if k % 2 else 0), 2 * part) for k in range(T)]
    planes, frames_copy, vectors, *sends = call(
        functools.partial(hidden_kernel, F, J, T),
        [((2, 2, span, C), bf16), (flat.shape, bf16), ((2, C), f32)]
        + [(size, bf16) for size in sizes],
        [pltpu.VMEM((2, 4 * span, C // 2), f32)],
        60 * WORK * span * C, 16 * span * C, "svv" + "v" * (T + 3),
    )(place, flat, vectors)
    head, grad_rows = call(
        functools.partial(head_kernel, 2 * J),
        [((R, 2 * J, C), bf16), (grad_rows.shape, bf16)],
        [], R * span * C, R * span * C, "avvv",
    )(frames_copy, grad_rows)
    messages = [sends[0]] + [partners(sends[k], "tm", k) for k in range(1, T)]
    joined, cached, under = call(
        functools.partial(join_kernel, F, J, T),
        [
            ((2, 2 * part, T * span), bf16),
            ((2, 2, 2 * J, C), bf16),
            ((2, 2 * J + span, C), bf16),
        ],
        [pltpu.VMEM((2, T * span, 2 * part), bf16)],
        30 * WORK * span * C, 16 * span * C, "sv" + "v" * T + "vvv",
    )(place, planes, *messages)
    under = shifted(under, "rows", -1)
    following = shifted(head, "tm", -1)
    packed, frames_grad = call(
        functools.partial(slab_kernel, F, J, R, T, slot),
        [((R * slot, C), bf16), ((4 * span, C), bf16)],
        [
            pltpu.VMEM((27, C, C), bf16),
            pltpu.VMEM((2, 2, (F + 2) * J, C), bf16),
            pltpu.VMEM((3, 3, (F + 2) * J, C), bf16),
            pltpu.VMEM((2, 4 * span, C // 2), f32),
            pltpu.SemaphoreType.DMA((3,)),
        ],
        2 * 54 * span * C * C, 2 * 27 * C * C, "svvvhvvvv" + "vv",
        limit=VMEM_LIMIT_WIDE,
    )(place, planes, cached, under, weight, frames_copy, vectors, grad_rows, following)

    def after_slab(blocks):
        shapes = [(b.shape, bf16) for b in blocks]
        count = len(blocks)
        aliases = {n + 1: n for n in range(count)}
        return list(
            call(gate_kernel, shapes, [], 0, 0, "a" * (2 * count + 1), aliases)(packed, *blocks)
        )

    hidden_all = exchanged(joined, "rows", after_slab)
    grad_all = exchanged(grad_rows, "tm")

    packed = lax.all_to_all(packed.reshape(R, slot, C), "rows", 0, 0, tiled=True)
    latent = packed[:, :used].reshape(R, F, J // R, C).transpose(1, 0, 2, 3)
    gains = call(
        functools.partial(gain_kernel, T, used),
        [((1, part), f32)] * T,
        [], R * slot * C, R * slot * C, "v" + "a" * (R // 2) + "v" * T,
    )(packed, *hidden_all[1::2])
    gain_grad = gains[0]
    for k in range(1, T):
        gain_grad = gain_grad + partners(gains[k], "tm", k)

    grads, bias_sum = call(
        functools.partial(order_kernel, F, J, R, T),
        [((2, R, (F * T + 2) * J, C), bf16), ((1, part), f32)],
        [],
        90 * WORK * span * C, 2 * R * T * span * C, "s" + "v" * (T + 2),
    )(place, *grad_all)
    (weight_grad,) = call(
        functools.partial(weight_kernel, F, J, R, T, part),
        [((27, part, C), f32)],
        [
            pltpu.VMEM((27, part, C), f32),
            pltpu.VMEM((2 * part, (R + 1) * T * span), bf16),
            pltpu.VMEM((2 * part, R * T * span), bf16),
            pltpu.SemaphoreType.DMA((3,)),
        ],
        200 * WORK * span * C, 8 * 27 * part * C, "sav" + "v" * R + "h",
    )(place, gains[0], grads, *hidden_all)

    return (
        latent,
        frames_grad.reshape(frames.shape),
        weight_grad.reshape(3, 3, 3, part, C),
        gain_grad.reshape(part),
        bias_sum.reshape(part),
    )


def on_device(frames, norm_gain, conv_weight, conv_bias, latent_grad):
    rows, shares = lax.axis_size("rows"), lax.axis_size("tm")
    operand_bytes = 2 * rows * shares * (frames.size // shares + latent_grad.size)
    result_bytes = 4 * conv_weight.size
    powers = (rows & (rows - 1)) == 0 and (shares & (shares - 1)) == 0
    if powers and frames.shape[1] == 2 and operand_bytes <= result_bytes:
        form = gathered_form
    else:
        form = reduced_form
    return form(frames, norm_gain, conv_weight, conv_bias, latent_grad)


def solution(mesh):
    placed = (P("tm", "rows", None, None), P(), P(), P(), P("tm", None, "rows", None))
    return jax.shard_map(
        on_device,
        mesh=mesh,
        in_specs=placed,
        out_specs=(
            P("tm", None, "rows", None),
            P("tm", "rows", None, None),
            P(None, None, None, "tm", None),
            P("tm"),
            P("tm"),
        ),
        check_vma=False,
    )
```

```python
import functools

import jax
import jax.numpy as jnp
from jax import lax
from jax.experimental import pallas as pl
from jax.experimental.pallas import tpu as pltpu
from jax.sharding import PartitionSpec as P

EPS = 1e-06
TAPS = [(a, b, c) for a in range(3) for b in range(3) for c in range(3)]
VMEM_LIMIT = 20 * 1024 * 1024
VMEM_LIMIT_WIDE = 59 * 1024 * 1024
WORK = 1200


def shifted(value, axis, steps):
    count = lax.axis_size(axis)
    leading, last = (max(0, -steps), min(count, count - steps))
    return lax.ppermute(value, axis, [(source, source + steps) for source in range(leading, last)])


def contract_out(grad_piece, weight_tap):
    return lax.dot_general(
        grad_piece, weight_tap, (((1,), (1,)), ((), ())), preferred_element_type=jnp.float32
    )


def reduced_form(frames, norm_gain, conv_weight, conv_bias, latent_grad):
    signal = frames.astype(jnp.float32)
    inv_rms = lax.rsqrt(jnp.mean(signal * signal, axis=-1, keepdims=True) + EPS)
    unit = signal * inv_rms
    normed = unit * norm_gain
    hidden = jax.nn.silu(normed).astype(jnp.bfloat16)
    frame_count, row_count, col_count, channels = hidden.shape
    lat_rows = row_count // 2
    lat_cols = col_count // 2
    cached = shifted(hidden[frame_count - 2 :], "tm", 1)
    stacked = jnp.concatenate([cached, hidden], axis=0)
    row_under = shifted(stacked[:, :1], "rows", -1)
    extended = jnp.concatenate([stacked, row_under], axis=1)
    extended = jnp.pad(extended, ((0, 0), (0, 0), (0, 1), (0, 0)))
    grad_rows = lax.all_to_all(latent_grad, "rows", split_axis=1, concat_axis=2, tiled=True)
    grad_flat = grad_rows.reshape(-1, channels)
    running = jnp.zeros((frame_count * lat_rows * lat_cols, channels), jnp.float32)
    blocks = []
    for tap_t, tap_r, tap_c in TAPS:
        window_piece = extended[
            tap_t : tap_t + frame_count,
            tap_r : tap_r + 2 * lat_rows : 2,
            tap_c : tap_c + 2 * lat_cols : 2,
        ]
        window_piece = window_piece.reshape(-1, channels)
        running = running + jnp.dot(
            window_piece, conv_weight[tap_t, tap_r, tap_c], preferred_element_type=jnp.float32
        )
        blocks.append(
            lax.dot_general(
                window_piece,
                grad_flat,
                (((0,), (0,)), ((), ())),
                preferred_element_type=jnp.float32,
            )
        )
    latent_rows = (
        (running + conv_bias)
        .reshape(frame_count, lat_rows, lat_cols, channels)
        .astype(jnp.bfloat16)
    )
    latent = lax.all_to_all(latent_rows, "rows", split_axis=2, concat_axis=1, tiled=True)
    weight_local = jnp.stack(blocks).reshape(3, 3, 3, channels, channels)
    bias_local = jnp.sum(grad_flat.astype(jnp.float32), axis=0)
    following = shifted(grad_rows[:2], "tm", -1)
    grad_ext = jnp.concatenate([grad_rows, following], axis=0)
    above_row = shifted(grad_ext, "rows", 1)
    grad_ext = jnp.concatenate([above_row, grad_ext], axis=1)
    grad_ext = jnp.pad(grad_ext, ((0, 0), (0, 0), (1, 0), (0, 0)))
    parity_sums = {}
    for tap_t, tap_r, tap_c in TAPS:
        row_start = 1 - tap_r // 2
        col_start = 1 - tap_c // 2
        grad_piece = grad_ext[
            2 - tap_t : 2 - tap_t + frame_count,
            row_start : row_start + lat_rows,
            col_start : col_start + lat_cols,
        ]
        term = contract_out(grad_piece.reshape(-1, channels), conv_weight[tap_t, tap_r, tap_c])
        label = (tap_r % 2, tap_c % 2)
        parity_sums[label] = parity_sums[label] + term if label in parity_sums else term
    shaped = {}
    for label in parity_sums:
        shaped[label] = parity_sums[label].reshape(frame_count, lat_rows, lat_cols, channels)
    even_rows = jnp.stack([shaped[0, 0], shaped[0, 1]], axis=3)
    odd_rows = jnp.stack([shaped[1, 0], shaped[1, 1]], axis=3)
    hidden_grad = jnp.stack([even_rows, odd_rows], axis=2).reshape(
        frame_count, row_count, col_count, channels
    )
    sigma = jax.nn.sigmoid(normed)
    normed_grad = hidden_grad * sigma * (1.0 + normed * (1.0 - sigma))
    gain_local = jnp.sum(normed_grad * unit, axis=(0, 1, 2))
    unit_grad = normed_grad * norm_gain
    frames_grad = inv_rms * (unit_grad - unit * jnp.mean(unit_grad * unit, axis=-1, keepdims=True))
    totals = lax.psum((weight_local, gain_local, bias_local), "rows")
    weight_grad, gain_grad, bias_grad = (
        lax.psum_scatter(totals[0], "tm", scatter_dimension=3, tiled=True),
        lax.psum_scatter(totals[1], "tm", scatter_dimension=0, tiled=True),
        lax.psum_scatter(totals[2], "tm", scatter_dimension=0, tiled=True),
    )
    return (latent, frames_grad.astype(jnp.bfloat16), weight_grad, gain_grad, bias_grad)


def partners(value, axis, bits):
    count = lax.axis_size(axis)
    return lax.ppermute(value, axis, [(source, source ^ bits) for source in range(count)])


def exchanged(value, axis, gate=None):
    count = lax.axis_size(axis)
    blocks = {0: value}
    for k in range(1, count):
        if k & (k - 1) == 0:
            blocks[k] = partners(value, axis, k)
    if gate is not None:
        held = [k for k in blocks if k > 1]
        blocks.update(zip(held, gate([blocks[k] for k in held])))
    for k in range(1, count):
        low = k & -k
        if k != low:
            blocks[k] = partners(blocks[k - low], axis, low)
    return [blocks[k] for k in range(count)]


def mm(left, right):
    return jnp.dot(left, right, preferred_element_type=jnp.float32)


def mm_t(left, right):
    return lax.dot_general(
        left, right, (((1,), (1,)), ((), ())), preferred_element_type=jnp.float32
    )


def normalised(frames, gain):
    signal = frames.astype(jnp.float32)
    inv_rms = lax.rsqrt(jnp.mean(signal * signal, axis=-1, keepdims=True) + EPS)
    unit = signal * inv_rms
    return inv_rms, unit, unit * gain


def hidden_kernel(F, J, T, place, frames, vectors, planes, frames_copy, vectors_copy, *rest):
    sends, tmp = rest[:T], rest[T]
    frames_copy[...] = frames[...]
    vectors_copy[...] = vectors[...]
    channels = frames.shape[1]
    part = channels // T
    _, _, normed = normalised(frames[...], vectors[0:1])
    value = normed / (1.0 + jnp.exp(-normed))
    tmp[0] = value[:, : channels // 2]
    tmp[1] = value[:, channels // 2 :]
    block = place[1]
    for rp in range(2):
        pair = []
        for cp in range(2):
            rows = [
                jnp.concatenate(
                    [
                        tmp[half, pl.ds((t * 2 + rp) * 2 * J + cp, J, stride=2), :]
                        for half in range(2)
                    ],
                    axis=1,
                )
                for t in range(F)
            ]
            plane = jnp.concatenate(rows, axis=0)
            pair.append(plane)
            plane = plane.astype(jnp.bfloat16)
            planes[rp, cp] = plane
            late = plane[(F - 2) * J :]
            for k in range(1, T, 2):
                for half in range(2):
                    at = (((rp * 2 + cp) * 2) + half) * 2 * J
                    lanes = slice(half * channels // 2, (half + 1) * channels // 2)
                    sends[k][2 * F * J + at : 2 * F * J + at + 2 * J] = late[:, lanes]
        pieces = [
            jnp.concatenate([p[:, d * part : (d + 1) * part] for p in pair], axis=1)
            for d in range(T)
        ]
        for k in range(T):
            chosen = pieces[0]
            for d in range(1, T):
                chosen = jnp.where(block == d ^ k, pieces[d], chosen)
            sends[k][rp * F * J : (rp + 1) * F * J] = chosen.astype(jnp.bfloat16)


def copies_kernel(own, ahead, out):
    rows = own.shape[0]
    for s in range(out.shape[0]):
        out[s, :rows] = own[...]
        out[s, rows:] = ahead[...]


def own_kernel(_, both, own):
    for s in range(both.shape[0]):
        own[s] = both[s, : own.shape[1], :]


def total_kernel(*refs):
    total = refs[1][...]
    for ref in refs[2:-1]:
        total = total + ref[...]
    refs[-1][...] = total


def join_kernel(F, J, T, place, planes, *refs):
    messages, (joined, cached, under, blocks) = refs[:T], refs[T:]
    span = F * J
    block = place[1]
    for k in range(T):
        at = pl.multiple_of((block ^ k) * span, 16)
        for rp in range(2):
            blocks[rp, pl.ds(at, span), :] = messages[k][rp * span : (rp + 1) * span, :]
    for rp in range(2):
        joined[rp] = blocks[rp].T
    for rp in range(2):
        for cp in range(2):
            halves = []
            for half in range(2):
                start = 2 * span + ((rp * 2 + cp) * 2 + half) * 2 * J
                value = jnp.zeros((2 * J, messages[1].shape[1]), jnp.bfloat16)
                for k in range(1, T, 2):
                    found = (block > 0) & (block ^ k == block - 1)
                    value = jnp.where(found, messages[k][start : start + 2 * J, :], value)
                halves.append(value)
            before = jnp.concatenate(halves, axis=1)
            cached[rp, cp] = before
            if rp == 0:
                under[cp, : 2 * J] = before
                under[cp, 2 * J :] = planes[0, cp]


def permutation(shape, meet):
    row = lax.broadcasted_iota(jnp.int32, shape, 0)
    col = lax.broadcasted_iota(jnp.int32, shape, 1)
    return jnp.where(meet(row, col), 1.0, 0.0).astype(jnp.bfloat16)


def slice_of(value, block, k, T):
    part = value.shape[1] // T
    chosen = value[:, :part]
    for d in range(1, T):
        chosen = jnp.where(block == d ^ k, value[:, d * part : (d + 1) * part], chosen)
    return chosen


def shard_order(J, R, rows, first, moved):
    jl = J // R
    return permutation(
        (rows * 2 * J, R * 2 * J),
        lambda o, s: (o // (2 * J) + first == s // jl % R)
        & (o // J % 2 == s // (jl * R) % 2)
        & (o % J == s // (2 * jl * R) * jl + s % jl + moved),
    )


def shard_rows(source, start, count):
    return jnp.concatenate(
        [source[s, start : start + count, :] for s in range(source.shape[0])], axis=0
    )


def gate_kernel(*refs):
    pass


def slab_kernel(
    F, J, R, T, slot, place, planes, cached, under, weight_hbm, frames, vectors, gathered,
    out, frames_grad, weight, near, ext, tmp, sem,
):
    row, block = place[0], place[1]
    channels = frames.shape[1]
    span = F * J
    gain, bias = vectors[0:1], vectors[1:2]
    fetches = [
        pltpu.make_async_copy(weight_hbm.at[pl.ds(a * 9, 9)], weight.at[pl.ds(a * 9, 9)], sem.at[a])
        for a in range(3)
    ]
    for copy in fetches:
        copy.start()

    orders = [shard_order(J, R, 2, row - 1, moved) for moved in range(2)]
    for pair in range(F // 2 + 1):
        source = shard_rows(gathered, pair * 2 * J, 2 * J)
        for moved in range(2):
            value = mm(orders[moved], source).astype(jnp.bfloat16)
            for i in range(2):
                near[moved, i, pair * 2 * J : (pair + 1) * 2 * J, :] = value[
                    i * 2 * J : (i + 1) * 2 * J
                ]

    rows = (F + 2) * J
    last = lax.broadcasted_iota(jnp.int32, (rows, 1), 0) % J == J - 1
    for b in range(3):
        for cp in range(2):
            if b == 2:
                full = under[cp]
            else:
                full = jnp.concatenate([cached[b, cp], planes[b, cp]], axis=0)
            ext[b, cp] = full
            if cp == 0:
                moved = pltpu.roll(full.astype(jnp.float32), rows - 1, 0)
                ext[b, 2] = jnp.where(last, 0.0, moved).astype(jnp.bfloat16)

    latent = jnp.zeros((span, channels), jnp.float32)
    sums = {}
    for n, (a, b, c) in enumerate(TAPS):
        if n % 9 == 0:
            fetches[a].wait()
        latent = latent + mm(ext[b, c, a * J : (a + F) * J, :], weight[n])
        piece = near[c // 2, 1 - b // 2, (2 - a) * J : (2 - a + F) * J, :]
        term = mm_t(piece, weight[n])
        key = (b % 2, c % 2)
        sums[key] = sums[key] + term if key in sums else term
    for (rp, cp), value in sums.items():
        for t in range(F):
            for half in range(2):
                lanes = slice(half * channels // 2, (half + 1) * channels // 2)
                tmp[half, pl.ds((t * 2 + rp) * 2 * J + cp, J, stride=2), :] = value[
                    t * J : (t + 1) * J, lanes
                ]
    hidden_grad = jnp.concatenate([tmp[0], tmp[1]], axis=1)
    inv_rms, unit, normed = normalised(frames[...], gain)
    sigma = 1.0 / (1.0 + jnp.exp(-normed))
    normed_grad = hidden_grad * sigma * (1.0 + normed * (1.0 - sigma))
    gain_part = jnp.sum(normed_grad * unit, axis=0, keepdims=True)
    unit_grad = normed_grad * gain
    mean = jnp.mean(unit_grad * unit, axis=-1, keepdims=True)
    frames_grad[...] = (inv_rms * (unit_grad - unit * mean)).astype(jnp.bfloat16)

    jl = J // R
    used = span // R
    order = permutation(
        (R * slot, span),
        lambda o, s: (o % slot < used)
        & (o % slot // jl == s // J)
        & (o // slot * jl + o % jl == s % J),
    )
    value = mm(order, (latent + bias).astype(jnp.bfloat16))
    line = lax.broadcasted_iota(jnp.int32, (R * slot, 1), 0) % slot
    rest = jnp.concatenate([slice_of(gain_part, block, k, T) for k in range(T)], axis=1)
    for n in range(3):
        term = rest.astype(jnp.bfloat16).astype(jnp.float32)
        rest = rest - term
        value = jnp.where(line == used + n, term, value)
    out[...] = value.astype(jnp.bfloat16)


def gain_kernel(T, used, received, *refs):
    parts = refs[-T:]
    value = jnp.zeros(received.shape[1:], jnp.float32)
    for s in range(received.shape[0]):
        value = value + received[s].astype(jnp.float32)
    line = lax.broadcasted_iota(jnp.int32, (received.shape[1], 1), 0)
    value = jnp.where((line >= used) & (line < used + 3), value, 0.0)
    value = jnp.sum(value, axis=0, keepdims=True)
    part = received.shape[2] // T
    for k in range(T):
        parts[k][...] = value[:, k * part : (k + 1) * part]


def order_kernel(F, J, R, T, place, *refs):
    gathered, (grads, bias_sum) = refs[:T], refs[T:]
    channels = grads.shape[-1]
    span = F * J
    depth = T * span
    block = place[1]
    grads[:, :, depth:, :] = jnp.zeros((2, R, 2 * J, channels), jnp.bfloat16)
    orders = [shard_order(J, R, R, 0, moved) for moved in range(2)]
    total = jnp.zeros((1, channels), jnp.float32)
    for k in range(T):
        for pair in range(F // 2):
            source = shard_rows(gathered[k], pair * 2 * J, 2 * J)
            total = total + jnp.sum(source.astype(jnp.float32), axis=0, keepdims=True)
            at = pl.multiple_of((block ^ k) * span + pair * 2 * J, 16)
            for moved in range(2):
                value = mm(orders[moved], source).astype(jnp.bfloat16)
                for i in range(R):
                    grads[moved, i, pl.ds(at, 2 * J), :] = value[i * 2 * J : (i + 1) * 2 * J]
    bias_sum[...] = slice_of(total, block, 0, T)


def weight_kernel(F, J, R, T, part, place, _, grads, *refs):
    hidden = refs[:R]
    out_hbm, out, even, odd, sem = refs[R:]
    channels = grads.shape[-1]
    depth = T * F * J
    lanes = 2 * part
    row = place[0]
    even[:, R * depth :] = jnp.zeros((lanes, depth), jnp.bfloat16)
    for k in range(R):
        at = pl.multiple_of((row ^ k) * depth, 128)
        for rp, turned in ((0, even), (1, odd)):
            turned[:, pl.ds(at, depth)] = hidden[k][rp]
    leaving = []
    for a in range(3):
        start = (2 - a) * J
        for moved in range(2):
            right = grads[moved, :, start : start + depth, :].reshape(R * depth, channels)
            size = part if moved else lanes
            left = jnp.concatenate(
                [even[:size, : R * depth], odd[:size, :], even[:size, depth:]], axis=0
            )
            value = mm(left, right)
            for b in range(3):
                if moved:
                    out[(a * 3 + b) * 3 + 2] = value[b * part : (b + 1) * part]
                else:
                    for cp in range(2):
                        at = b * lanes + cp * part
                        out[(a * 3 + b) * 3 + cp] = value[at : at + part]
        taps = pl.ds(a * 9, 9)
        leaving.append(pltpu.make_async_copy(out.at[taps], out_hbm.at[taps], sem.at[a]))
        leaving[a].start()
    for copy in leaving:
        copy.wait()


def call(kernel, outs, scratch, flops, moved, places, aliases={}, limit=VMEM_LIMIT):
    kinds = {"s": pltpu.SMEM, "v": pltpu.VMEM, "h": pltpu.HBM, "a": pl.ANY}
    specs = [pl.BlockSpec(memory_space=kinds[p]) for p in places]
    count = len(places) - len(outs)
    return pl.pallas_call(
        kernel,
        out_shape=[jax.ShapeDtypeStruct(s, d) for s, d in outs],
        in_specs=specs[:count],
        out_specs=specs[count:],
        scratch_shapes=scratch,
        input_output_aliases=aliases,
        compiler_params=pltpu.CompilerParams(vmem_limit_bytes=limit),
        cost_estimate=pl.CostEstimate(flops=flops, bytes_accessed=moved, transcendentals=0),
    )


def gathered_form(frames, norm_gain, conv_weight, conv_bias, latent_grad):
    bf16, f32 = jnp.bfloat16, jnp.float32
    F, row_count, col_count, C = frames.shape
    R, T = lax.axis_size("rows"), lax.axis_size("tm")
    J = col_count // 2
    span = F * J
    part = C // T
    used = span // R
    slot = -(-(used + 3) // 16) * 16
    vectors = jnp.stack([norm_gain, conv_bias])
    flat = frames.reshape(-1, C)
    weight = conv_weight.reshape(27, C, C)
    place = jnp.stack([lax.axis_index("rows"), lax.axis_index("tm")]).astype(jnp.int32)

    own = latent_grad.reshape(span, C)
    ahead = shifted(own[: 2 * J], "tm", -1)
    (copies,) = call(
        copies_kernel,
        [((R, span + 2 * J, C), bf16)],
        [], 2 * R * span * C, 2 * R * span * C, "vvv",
    )(own, ahead)
    grad_both = lax.all_to_all(copies, "rows", 0, 0, tiled=True)

    sizes = [(2 * span + (16 * J if k % 2 else 0), 2 * part) for k in range(T)]
    planes, frames_copy, vectors, *sends = call(
        functools.partial(hidden_kernel, F, J, T),
        [((2, 2, span, C), bf16), (flat.shape, bf16), ((2, C), f32)]
        + [(size, bf16) for size in sizes],
        [pltpu.VMEM((2, 4 * span, C // 2), f32)],
        60 * WORK * span * C, 16 * span * C, "svv" + "v" * (T + 3),
    )(place, flat, vectors)
    (grad_rows,) = call(
        own_kernel,
        [((R, span, C), bf16)],
        [], R * span * C, R * span * C, "avv",
    )(frames_copy, grad_both)
    messages = [sends[0]] + [partners(sends[k], "tm", k) for k in range(1, T)]
    joined, cached, under = call(
        functools.partial(join_kernel, F, J, T),
        [
            ((2, 2 * part, T * span), bf16),
            ((2, 2, 2 * J, C), bf16),
            ((2, 2 * J + span, C), bf16),
        ],
        [pltpu.VMEM((2, T * span, 2 * part), bf16)],
        30 * WORK * span * C, 16 * span * C, "sv" + "v" * T + "vvv",
    )(place, planes, *messages)
    under = shifted(under, "rows", -1)
    packed, frames_grad = call(
        functools.partial(slab_kernel, F, J, R, T, slot),
        [((R * slot, C), bf16), ((4 * span, C), bf16)],
        [
            pltpu.VMEM((27, C, C), bf16),
            pltpu.VMEM((2, 2, (F + 2) * J, C), bf16),
            pltpu.VMEM((3, 3, (F + 2) * J, C), bf16),
            pltpu.VMEM((2, 4 * span, C // 2), f32),
            pltpu.SemaphoreType.DMA((3,)),
        ],
        2 * 54 * span * C * C, 2 * 27 * C * C, "svvvhvvv" + "vv",
        limit=VMEM_LIMIT_WIDE,
    )(place, planes, cached, under, weight, frames_copy, vectors, grad_both)

    def after_slab(blocks):
        shapes = [(b.shape, bf16) for b in blocks]
        count = len(blocks)
        aliases = {n + 1: n for n in range(count)}
        return list(
            call(gate_kernel, shapes, [], 0, 0, "a" * (2 * count + 1), aliases)(packed, *blocks)
        )

    hidden_all = exchanged(joined, "rows", after_slab)
    grad_all = exchanged(grad_rows, "tm")

    packed = lax.all_to_all(packed.reshape(R, slot, C), "rows", 0, 0, tiled=True)
    latent = packed[:, :used].reshape(R, F, J // R, C).transpose(1, 0, 2, 3)
    grads, bias_sum = call(
        functools.partial(order_kernel, F, J, R, T),
        [((2, R, (F * T + 2) * J, C), bf16), ((1, part), f32)],
        [],
        90 * WORK * span * C, 2 * R * T * span * C, "s" + "v" * (T + 2),
    )(place, *grad_all)
    gains = call(
        functools.partial(gain_kernel, T, used),
        [((1, part), f32)] * T,
        [], R * slot * C, R * slot * C, "v" + "a" * (R // 2 + 1) + "v" * T,
    )(packed, bias_sum, *hidden_all[1::2])
    (weight_grad,) = call(
        functools.partial(weight_kernel, F, J, R, T, part),
        [((27, part, C), f32)],
        [
            pltpu.VMEM((27, part, C), f32),
            pltpu.VMEM((2 * part, (R + 1) * T * span), bf16),
            pltpu.VMEM((2 * part, R * T * span), bf16),
            pltpu.SemaphoreType.DMA((3,)),
        ],
        200 * WORK * span * C, 8 * 27 * part * C, "sav" + "v" * R + "h",
    )(place, gains[0], grads, *hidden_all)

    terms = [gains[0]] + [partners(gains[k], "tm", k) for k in range(1, T)]
    (gain_grad,) = call(
        total_kernel, [((1, part), f32)], [], T * part, 4 * T * part, "a" + "v" * (T + 1)
    )(weight_grad, *terms)
    return (
        latent,
        frames_grad.reshape(frames.shape),
        weight_grad.reshape(3, 3, 3, part, C),
        gain_grad.reshape(part),
        bias_sum.reshape(part),
    )


def on_device(frames, norm_gain, conv_weight, conv_bias, latent_grad):
    rows, shares = lax.axis_size("rows"), lax.axis_size("tm")
    operand_bytes = 2 * rows * shares * (frames.size // shares + latent_grad.size)
    result_bytes = 4 * conv_weight.size
    powers = (rows & (rows - 1)) == 0 and (shares & (shares - 1)) == 0
    if powers and frames.shape[1] == 2 and operand_bytes <= result_bytes:
        form = gathered_form
    else:
        form = reduced_form
    return form(frames, norm_gain, conv_weight, conv_bias, latent_grad)


def solution(mesh):
    placed = (P("tm", "rows", None, None), P(), P(), P(), P("tm", None, "rows", None))
    return jax.shard_map(
        on_device,
        mesh=mesh,
        in_specs=placed,
        out_specs=(
            P("tm", None, "rows", None),
            P("tm", "rows", None, None),
            P(None, None, None, "tm", None),
            P("tm"),
            P("tm"),
        ),
        check_vma=False,
    )
```

```python
import functools

import jax
import jax.numpy as jnp
from jax import lax
from jax.experimental import pallas as pl
from jax.experimental.pallas import tpu as pltpu
from jax.sharding import PartitionSpec as P

EPS = 1e-06
TAPS = [(a, b, c) for a in range(3) for b in range(3) for c in range(3)]
VMEM_LIMIT = 20 * 1024 * 1024
VMEM_LIMIT_WIDE = 60 * 1024 * 1024
WORK = 1200


def shifted(value, axis, steps):
    count = lax.axis_size(axis)
    leading, last = (max(0, -steps), min(count, count - steps))
    return lax.ppermute(value, axis, [(source, source + steps) for source in range(leading, last)])


def contract_out(grad_piece, weight_tap):
    return lax.dot_general(
        grad_piece, weight_tap, (((1,), (1,)), ((), ())), preferred_element_type=jnp.float32
    )


def reduced_form(frames, norm_gain, conv_weight, conv_bias, latent_grad):
    signal = frames.astype(jnp.float32)
    inv_rms = lax.rsqrt(jnp.mean(signal * signal, axis=-1, keepdims=True) + EPS)
    unit = signal * inv_rms
    normed = unit * norm_gain
    hidden = jax.nn.silu(normed).astype(jnp.bfloat16)
    frame_count, row_count, col_count, channels = hidden.shape
    lat_rows = row_count // 2
    lat_cols = col_count // 2
    cached = shifted(hidden[frame_count - 2 :], "tm", 1)
    stacked = jnp.concatenate([cached, hidden], axis=0)
    row_under = shifted(stacked[:, :1], "rows", -1)
    extended = jnp.concatenate([stacked, row_under], axis=1)
    extended = jnp.pad(extended, ((0, 0), (0, 0), (0, 1), (0, 0)))
    grad_rows = lax.all_to_all(latent_grad, "rows", split_axis=1, concat_axis=2, tiled=True)
    grad_flat = grad_rows.reshape(-1, channels)
    running = jnp.zeros((frame_count * lat_rows * lat_cols, channels), jnp.float32)
    blocks = []
    for tap_t, tap_r, tap_c in TAPS:
        window_piece = extended[
            tap_t : tap_t + frame_count,
            tap_r : tap_r + 2 * lat_rows : 2,
            tap_c : tap_c + 2 * lat_cols : 2,
        ]
        window_piece = window_piece.reshape(-1, channels)
        running = running + jnp.dot(
            window_piece, conv_weight[tap_t, tap_r, tap_c], preferred_element_type=jnp.float32
        )
        blocks.append(
            lax.dot_general(
                window_piece,
                grad_flat,
                (((0,), (0,)), ((), ())),
                preferred_element_type=jnp.float32,
            )
        )
    latent_rows = (
        (running + conv_bias)
        .reshape(frame_count, lat_rows, lat_cols, channels)
        .astype(jnp.bfloat16)
    )
    latent = lax.all_to_all(latent_rows, "rows", split_axis=2, concat_axis=1, tiled=True)
    weight_local = jnp.stack(blocks).reshape(3, 3, 3, channels, channels)
    bias_local = jnp.sum(grad_flat.astype(jnp.float32), axis=0)
    following = shifted(grad_rows[:2], "tm", -1)
    grad_ext = jnp.concatenate([grad_rows, following], axis=0)
    above_row = shifted(grad_ext, "rows", 1)
    grad_ext = jnp.concatenate([above_row, grad_ext], axis=1)
    grad_ext = jnp.pad(grad_ext, ((0, 0), (0, 0), (1, 0), (0, 0)))
    parity_sums = {}
    for tap_t, tap_r, tap_c in TAPS:
        row_start = 1 - tap_r // 2
        col_start = 1 - tap_c // 2
        grad_piece = grad_ext[
            2 - tap_t : 2 - tap_t + frame_count,
            row_start : row_start + lat_rows,
            col_start : col_start + lat_cols,
        ]
        term = contract_out(grad_piece.reshape(-1, channels), conv_weight[tap_t, tap_r, tap_c])
        label = (tap_r % 2, tap_c % 2)
        parity_sums[label] = parity_sums[label] + term if label in parity_sums else term
    shaped = {}
    for label in parity_sums:
        shaped[label] = parity_sums[label].reshape(frame_count, lat_rows, lat_cols, channels)
    even_rows = jnp.stack([shaped[0, 0], shaped[0, 1]], axis=3)
    odd_rows = jnp.stack([shaped[1, 0], shaped[1, 1]], axis=3)
    hidden_grad = jnp.stack([even_rows, odd_rows], axis=2).reshape(
        frame_count, row_count, col_count, channels
    )
    sigma = jax.nn.sigmoid(normed)
    normed_grad = hidden_grad * sigma * (1.0 + normed * (1.0 - sigma))
    gain_local = jnp.sum(normed_grad * unit, axis=(0, 1, 2))
    unit_grad = normed_grad * norm_gain
    frames_grad = inv_rms * (unit_grad - unit * jnp.mean(unit_grad * unit, axis=-1, keepdims=True))
    totals = lax.psum((weight_local, gain_local, bias_local), "rows")
    weight_grad, gain_grad, bias_grad = (
        lax.psum_scatter(totals[0], "tm", scatter_dimension=3, tiled=True),
        lax.psum_scatter(totals[1], "tm", scatter_dimension=0, tiled=True),
        lax.psum_scatter(totals[2], "tm", scatter_dimension=0, tiled=True),
    )
    return (latent, frames_grad.astype(jnp.bfloat16), weight_grad, gain_grad, bias_grad)


def partners(value, axis, bits):
    count = lax.axis_size(axis)
    return lax.ppermute(value, axis, [(source, source ^ bits) for source in range(count)])


def exchanged(value, axis, gate=None):
    count = lax.axis_size(axis)
    blocks = {0: value}
    for k in range(1, count):
        if k & (k - 1) == 0:
            blocks[k] = partners(value, axis, k)
    if gate is not None:
        held = [k for k in blocks if k > 1]
        blocks.update(zip(held, gate([blocks[k] for k in held])))
    for k in range(1, count):
        low = k & -k
        if k != low:
            blocks[k] = partners(blocks[k - low], axis, low)
    return [blocks[k] for k in range(count)]


def mm(left, right):
    return jnp.dot(left, right, preferred_element_type=jnp.float32)


def mm_t(left, right):
    return lax.dot_general(
        left, right, (((1,), (1,)), ((), ())), preferred_element_type=jnp.float32
    )


def normalised(frames, gain):
    signal = frames.astype(jnp.float32)
    inv_rms = lax.rsqrt(jnp.mean(signal * signal, axis=-1, keepdims=True) + EPS)
    unit = signal * inv_rms
    return inv_rms, unit, unit * gain


def hidden_kernel(F, J, T, place, frames, vectors, planes, frames_copy, vectors_copy, *rest):
    sends, tmp = rest[:T], rest[T]
    frames_copy[...] = frames[...]
    vectors_copy[...] = vectors[...]
    channels = frames.shape[1]
    part = channels // T
    _, _, normed = normalised(frames[...], vectors[0:1])
    value = normed / (1.0 + jnp.exp(-normed))
    tmp[0] = value[:, : channels // 2]
    tmp[1] = value[:, channels // 2 :]
    block = place[1]
    for rp in range(2):
        pair = []
        for cp in range(2):
            rows = [
                jnp.concatenate(
                    [
                        tmp[half, pl.ds((t * 2 + rp) * 2 * J + cp, J, stride=2), :]
                        for half in range(2)
                    ],
                    axis=1,
                )
                for t in range(F)
            ]
            plane = jnp.concatenate(rows, axis=0)
            pair.append(plane)
            plane = plane.astype(jnp.bfloat16)
            planes[rp, cp] = plane
            late = plane[(F - 2) * J :]
            for k in range(1, T, 2):
                for half in range(2):
                    at = (((rp * 2 + cp) * 2) + half) * 2 * J
                    lanes = slice(half * channels // 2, (half + 1) * channels // 2)
                    sends[k][2 * F * J + at : 2 * F * J + at + 2 * J] = late[:, lanes]
        pieces = [
            jnp.concatenate([p[:, d * part : (d + 1) * part] for p in pair], axis=1)
            for d in range(T)
        ]
        for k in range(T):
            chosen = pieces[0]
            for d in range(1, T):
                chosen = jnp.where(block == d ^ k, pieces[d], chosen)
            sends[k][rp * F * J : (rp + 1) * F * J] = chosen.astype(jnp.bfloat16)


def head_kernel(rows, _, grad_rows, head, passed):
    passed[...] = grad_rows[...]
    for s in range(grad_rows.shape[0]):
        head[s] = grad_rows[s, :rows, :]


def total_kernel(*refs):
    total = refs[0][...]
    for ref in refs[1:-1]:
        total = total + ref[...]
    refs[-1][...] = total


def join_kernel(F, J, T, place, planes, *refs):
    messages, (joined, cached, under, blocks) = refs[:T], refs[T:]
    span = F * J
    block = place[1]
    for k in range(T):
        at = pl.multiple_of((block ^ k) * span, 16)
        for rp in range(2):
            blocks[rp, pl.ds(at, span), :] = messages[k][rp * span : (rp + 1) * span, :]
    for rp in range(2):
        joined[rp] = blocks[rp].T
    for rp in range(2):
        for cp in range(2):
            halves = []
            for half in range(2):
                start = 2 * span + ((rp * 2 + cp) * 2 + half) * 2 * J
                value = jnp.zeros((2 * J, messages[1].shape[1]), jnp.bfloat16)
                for k in range(1, T, 2):
                    found = (block > 0) & (block ^ k == block - 1)
                    value = jnp.where(found, messages[k][start : start + 2 * J, :], value)
                halves.append(value)
            before = jnp.concatenate(halves, axis=1)
            cached[rp, cp] = before
            if rp == 0:
                under[cp, : 2 * J] = before
                under[cp, 2 * J :] = planes[0, cp]


def permutation(shape, meet):
    row = lax.broadcasted_iota(jnp.int32, shape, 0)
    col = lax.broadcasted_iota(jnp.int32, shape, 1)
    return jnp.where(meet(row, col), 1.0, 0.0).astype(jnp.bfloat16)


def slice_of(value, block, k, T):
    part = value.shape[1] // T
    chosen = value[:, :part]
    for d in range(1, T):
        chosen = jnp.where(block == d ^ k, value[:, d * part : (d + 1) * part], chosen)
    return chosen


def shard_order(J, R, rows, first, moved):
    jl = J // R
    return permutation(
        (rows * 2 * J, R * 2 * J),
        lambda o, s: (o // (2 * J) + first == s // jl % R)
        & (o // J % 2 == s // (jl * R) % 2)
        & (o % J == s // (2 * jl * R) * jl + s % jl + moved),
    )


def shard_rows(source, start, count):
    return jnp.concatenate(
        [source[s, start : start + count, :] for s in range(source.shape[0])], axis=0
    )


def gate_kernel(*refs):
    pass


def slab_kernel(
    F, J, R, T, slot, place, planes, cached, under, weight_hbm, frames, vectors, gathered, following,
    out, frames_grad, weight, near, ext, tmp, sem,
):
    row, block = place[0], place[1]
    channels = frames.shape[1]
    span = F * J
    gain, bias = vectors[0:1], vectors[1:2]
    fetches = [
        pltpu.make_async_copy(weight_hbm.at[pl.ds(a * 9, 9)], weight.at[pl.ds(a * 9, 9)], sem.at[a])
        for a in range(3)
    ]
    for copy in fetches:
        copy.start()

    orders = [shard_order(J, R, 2, row - 1, moved) for moved in range(2)]
    for pair in range(F // 2 + 1):
        if pair < F // 2:
            source = shard_rows(gathered, pair * 2 * J, 2 * J)
        else:
            source = shard_rows(following, 0, 2 * J)
        for moved in range(2):
            value = mm(orders[moved], source).astype(jnp.bfloat16)
            for i in range(2):
                near[moved, i, pair * 2 * J : (pair + 1) * 2 * J, :] = value[
                    i * 2 * J : (i + 1) * 2 * J
                ]

    rows = (F + 2) * J
    last = lax.broadcasted_iota(jnp.int32, (rows, 1), 0) % J == J - 1
    for b in range(3):
        for cp in range(2):
            if b == 2:
                full = under[cp]
            else:
                full = jnp.concatenate([cached[b, cp], planes[b, cp]], axis=0)
            ext[b, cp] = full
            if cp == 0:
                moved = pltpu.roll(full.astype(jnp.float32), rows - 1, 0)
                ext[b, 2] = jnp.where(last, 0.0, moved).astype(jnp.bfloat16)

    latent = jnp.zeros((span, channels), jnp.float32)
    sums = {}
    for n, (a, b, c) in enumerate(TAPS):
        if n % 9 == 0:
            fetches[a].wait()
        latent = latent + mm(ext[b, c, a * J : (a + F) * J, :], weight[n])
        piece = near[c // 2, 1 - b // 2, (2 - a) * J : (2 - a + F) * J, :]
        term = mm_t(piece, weight[n])
        key = (b % 2, c % 2)
        sums[key] = sums[key] + term if key in sums else term
    for (rp, cp), value in sums.items():
        for t in range(F):
            for half in range(2):
                lanes = slice(half * channels // 2, (half + 1) * channels // 2)
                tmp[half, pl.ds((t * 2 + rp) * 2 * J + cp, J, stride=2), :] = value[
                    t * J : (t + 1) * J, lanes
                ]
    hidden_grad = jnp.concatenate([tmp[0], tmp[1]], axis=1)
    inv_rms, unit, normed = normalised(frames[...], gain)
    sigma = 1.0 / (1.0 + jnp.exp(-normed))
    normed_grad = hidden_grad * sigma * (1.0 + normed * (1.0 - sigma))
    gain_part = jnp.sum(normed_grad * unit, axis=0, keepdims=True)
    unit_grad = normed_grad * gain
    mean = jnp.mean(unit_grad * unit, axis=-1, keepdims=True)
    frames_grad[...] = (inv_rms * (unit_grad - unit * mean)).astype(jnp.bfloat16)

    jl = J // R
    used = span // R
    order = permutation(
        (R * slot, span),
        lambda o, s: (o % slot < used)
        & (o % slot // jl == s // J)
        & (o // slot * jl + o % jl == s % J),
    )
    value = mm(order, (latent + bias).astype(jnp.bfloat16))
    line = lax.broadcasted_iota(jnp.int32, (R * slot, 1), 0) % slot
    rest = jnp.concatenate([slice_of(gain_part, block, k, T) for k in range(T)], axis=1)
    for n in range(3):
        term = rest.astype(jnp.bfloat16).astype(jnp.float32)
        rest = rest - term
        value = jnp.where(line == used + n, term, value)
    out[...] = value.astype(jnp.bfloat16)


def gain_kernel(T, used, received, *refs):
    parts = refs[-T:]
    value = jnp.zeros(received.shape[1:], jnp.float32)
    for s in range(received.shape[0]):
        value = value + received[s].astype(jnp.float32)
    line = lax.broadcasted_iota(jnp.int32, (received.shape[1], 1), 0)
    value = jnp.where((line >= used) & (line < used + 3), value, 0.0)
    value = jnp.sum(value, axis=0, keepdims=True)
    part = received.shape[2] // T
    for k in range(T):
        parts[k][...] = value[:, k * part : (k + 1) * part]


def order_kernel(F, J, R, T, place, *refs):
    gathered, (grads, bias_sum) = refs[:T], refs[T:]
    channels = grads.shape[-1]
    span = F * J
    depth = T * span
    block = place[1]
    grads[:, :, depth:, :] = jnp.zeros((2, R, 2 * J, channels), jnp.bfloat16)
    orders = [shard_order(J, R, R, 0, moved) for moved in range(2)]
    total = jnp.zeros((1, channels), jnp.float32)
    for k in range(T):
        for pair in range(F // 2):
            source = shard_rows(gathered[k], pair * 2 * J, 2 * J)
            total = total + jnp.sum(source.astype(jnp.float32), axis=0, keepdims=True)
            at = pl.multiple_of((block ^ k) * span + pair * 2 * J, 16)
            for moved in range(2):
                value = mm(orders[moved], source).astype(jnp.bfloat16)
                for i in range(R):
                    grads[moved, i, pl.ds(at, 2 * J), :] = value[i * 2 * J : (i + 1) * 2 * J]
    bias_sum[...] = slice_of(total, block, 0, T)


def weight_kernel(F, J, R, T, part, place, gain, grads, *refs):
    hidden = refs[:R]
    out_hbm, gain_out, out, even, odd, sem = refs[R:]
    gain_out[...] = gain[...]
    channels = grads.shape[-1]
    depth = T * F * J
    lanes = 2 * part
    row = place[0]
    even[:, R * depth :] = jnp.zeros((lanes, depth), jnp.bfloat16)
    for k in range(R):
        at = pl.multiple_of((row ^ k) * depth, 128)
        for rp, turned in ((0, even), (1, odd)):
            turned[:, pl.ds(at, depth)] = hidden[k][rp]
    leaving = []
    for a in range(3):
        start = (2 - a) * J
        for moved in range(2):
            right = grads[moved, :, start : start + depth, :].reshape(R * depth, channels)
            size = part if moved else lanes
            left = jnp.concatenate(
                [even[:size, : R * depth], odd[:size, :], even[:size, depth:]], axis=0
            )
            value = mm(left, right)
            for b in range(3):
                if moved:
                    out[(a * 3 + b) * 3 + 2] = value[b * part : (b + 1) * part]
                else:
                    for cp in range(2):
                        at = b * lanes + cp * part
                        out[(a * 3 + b) * 3 + cp] = value[at : at + part]
        taps = pl.ds(a * 9, 9)
        leaving.append(pltpu.make_async_copy(out.at[taps], out_hbm.at[taps], sem.at[a]))
        leaving[a].start()
    for copy in leaving:
        copy.wait()


def call(kernel, outs, scratch, flops, moved, places, aliases={}, limit=VMEM_LIMIT):
    kinds = {"s": pltpu.SMEM, "v": pltpu.VMEM, "h": pltpu.HBM, "a": pl.ANY}
    specs = [pl.BlockSpec(memory_space=kinds[p]) for p in places]
    count = len(places) - len(outs)
    return pl.pallas_call(
        kernel,
        out_shape=[jax.ShapeDtypeStruct(s, d) for s, d in outs],
        in_specs=specs[:count],
        out_specs=specs[count:],
        scratch_shapes=scratch,
        input_output_aliases=aliases,
        compiler_params=pltpu.CompilerParams(vmem_limit_bytes=limit),
        cost_estimate=pl.CostEstimate(flops=flops, bytes_accessed=moved, transcendentals=0),
    )


def gathered_form(frames, norm_gain, conv_weight, conv_bias, latent_grad):
    bf16, f32 = jnp.bfloat16, jnp.float32
    F, row_count, col_count, C = frames.shape
    R, T = lax.axis_size("rows"), lax.axis_size("tm")
    J = col_count // 2
    span = F * J
    part = C // T
    used = span // R
    slot = -(-(used + 3) // 16) * 16
    vectors = jnp.stack([norm_gain, conv_bias])
    flat = frames.reshape(-1, C)
    weight = conv_weight.reshape(27, C, C)
    place = jnp.stack([lax.axis_index("rows"), lax.axis_index("tm")]).astype(jnp.int32)

    own = latent_grad.reshape(1, -1, C)
    grad_rows = lax.all_to_all(
        jnp.broadcast_to(own, (R,) + own.shape[1:]), "rows", 0, 0, tiled=True
    )

    sizes = [(2 * span + (16 * J if k % 2 else 0), 2 * part) for k in range(T)]
    planes, frames_copy, vectors, *sends = call(
        functools.partial(hidden_kernel, F, J, T),
        [((2, 2, span, C), bf16), (flat.shape, bf16), ((2, C), f32)]
        + [(size, bf16) for size in sizes],
        [pltpu.VMEM((2, 4 * span, C // 2), f32)],
        60 * WORK * span * C, 16 * span * C, "svv" + "v" * (T + 3),
    )(place, flat, vectors)
    head, grad_rows = call(
        functools.partial(head_kernel, 2 * J),
        [((R, 2 * J, C), bf16), (grad_rows.shape, bf16)],
        [], R * span * C, R * span * C, "avvv",
    )(frames_copy, grad_rows)
    messages = [sends[0]] + [partners(sends[k], "tm", k) for k in range(1, T)]
    joined, cached, under = call(
        functools.partial(join_kernel, F, J, T),
        [
            ((2, 2 * part, T * span), bf16),
            ((2, 2, 2 * J, C), bf16),
            ((2, 2 * J + span, C), bf16),
        ],
        [pltpu.VMEM((2, T * span, 2 * part), bf16)],
        30 * WORK * span * C, 16 * span * C, "sv" + "v" * T + "vvv",
    )(place, planes, *messages)
    under = shifted(under, "rows", -1)
    following = shifted(head, "tm", -1)
    packed, frames_grad = call(
        functools.partial(slab_kernel, F, J, R, T, slot),
        [((R * slot, C), bf16), ((4 * span, C), bf16)],
        [
            pltpu.VMEM((27, C, C), bf16),
            pltpu.VMEM((2, 2, (F + 2) * J, C), bf16),
            pltpu.VMEM((3, 3, (F + 2) * J, C), bf16),
            pltpu.VMEM((2, 4 * span, C // 2), f32),
            pltpu.SemaphoreType.DMA((3,)),
        ],
        2 * 54 * span * C * C, 2 * 27 * C * C, "svvvhvvvv" + "vv",
        limit=VMEM_LIMIT_WIDE,
    )(place, planes, cached, under, weight, frames_copy, vectors, grad_rows, following)

    def after_slab(blocks):
        shapes = [(b.shape, bf16) for b in blocks]
        count = len(blocks)
        aliases = {n + 1: n for n in range(count)}
        return list(
            call(gate_kernel, shapes, [], 0, 0, "a" * (2 * count + 1), aliases)(packed, *blocks)
        )

    hidden_all = exchanged(joined, "rows", after_slab)
    grad_all = exchanged(grad_rows, "tm")

    (packed,) = call(gate_kernel, [(packed.shape, bf16)], [], 0, 0, "aaa", {1: 0})(
        hidden_all[R - 2], packed
    )
    packed = lax.all_to_all(packed.reshape(R, slot, C), "rows", 0, 0, tiled=True)
    latent = packed[:, :used].reshape(R, F, J // R, C).transpose(1, 0, 2, 3)
    grads, bias_sum = call(
        functools.partial(order_kernel, F, J, R, T),
        [((2, R, (F * T + 2) * J, C), bf16), ((1, part), f32)],
        [],
        90 * WORK * span * C, 2 * R * T * span * C, "s" + "v" * (T + 2),
    )(place, *grad_all)
    gains = call(
        functools.partial(gain_kernel, T, used),
        [((1, part), f32)] * T,
        [], R * slot * C, R * slot * C, "v" + "a" * (R // 2 + 1) + "v" * T,
    )(packed, bias_sum, *hidden_all[1::2])
    weight_grad, own_gain = call(
        functools.partial(weight_kernel, F, J, R, T, part),
        [((27, part, C), f32), ((1, part), f32)],
        [
            pltpu.VMEM((27, part, C), f32),
            pltpu.VMEM((2 * part, (R + 1) * T * span), bf16),
            pltpu.VMEM((2 * part, R * T * span), bf16),
            pltpu.SemaphoreType.DMA((3,)),
        ],
        200 * WORK * span * C, 8 * 27 * part * C, "svv" + "v" * R + "hv",
    )(place, gains[0], grads, *hidden_all)

    terms = [own_gain] + [partners(gains[k], "tm", k) for k in range(1, T)]
    (gain_grad,) = call(
        total_kernel, [((1, part), f32)], [], T * part, 4 * T * part, "v" * (T + 1)
    )(*terms)
    return (
        latent,
        frames_grad.reshape(frames.shape),
        weight_grad.reshape(3, 3, 3, part, C),
        gain_grad.reshape(part),
        bias_sum.reshape(part),
    )


def on_device(frames, norm_gain, conv_weight, conv_bias, latent_grad):
    rows, shares = lax.axis_size("rows"), lax.axis_size("tm")
    operand_bytes = 2 * rows * shares * (frames.size // shares + latent_grad.size)
    result_bytes = 4 * conv_weight.size
    powers = (rows & (rows - 1)) == 0 and (shares & (shares - 1)) == 0
    if powers and frames.shape[1] == 2 and operand_bytes <= result_bytes:
        form = gathered_form
    else:
        form = reduced_form
    return form(frames, norm_gain, conv_weight, conv_bias, latent_grad)


def solution(mesh):
    placed = (P("tm", "rows", None, None), P(), P(), P(), P("tm", None, "rows", None))
    return jax.shard_map(
        on_device,
        mesh=mesh,
        in_specs=placed,
        out_specs=(
            P("tm", None, "rows", None),
            P("tm", "rows", None, None),
            P(None, None, None, "tm", None),
            P("tm"),
            P("tm"),
        ),
        check_vma=False,
    )
```

```python
import functools

import jax
import jax.numpy as jnp
from jax import lax
from jax.experimental import pallas as pl
from jax.experimental.pallas import tpu as pltpu
from jax.sharding import PartitionSpec as P

EPS = 1e-06
TAPS = [(a, b, c) for a in range(3) for b in range(3) for c in range(3)]
VMEM_LIMIT = 20 * 1024 * 1024
VMEM_LIMIT_WIDE = 60 * 1024 * 1024
WORK = 1200


def shifted(value, axis, steps):
    count = lax.axis_size(axis)
    leading, last = (max(0, -steps), min(count, count - steps))
    return lax.ppermute(value, axis, [(source, source + steps) for source in range(leading, last)])


def contract_out(grad_piece, weight_tap):
    return lax.dot_general(
        grad_piece, weight_tap, (((1,), (1,)), ((), ())), preferred_element_type=jnp.float32
    )


def reduced_form(frames, norm_gain, conv_weight, conv_bias, latent_grad):
    signal = frames.astype(jnp.float32)
    inv_rms = lax.rsqrt(jnp.mean(signal * signal, axis=-1, keepdims=True) + EPS)
    unit = signal * inv_rms
    normed = unit * norm_gain
    hidden = jax.nn.silu(normed).astype(jnp.bfloat16)
    frame_count, row_count, col_count, channels = hidden.shape
    lat_rows = row_count // 2
    lat_cols = col_count // 2
    cached = shifted(hidden[frame_count - 2 :], "tm", 1)
    stacked = jnp.concatenate([cached, hidden], axis=0)
    row_under = shifted(stacked[:, :1], "rows", -1)
    extended = jnp.concatenate([stacked, row_under], axis=1)
    extended = jnp.pad(extended, ((0, 0), (0, 0), (0, 1), (0, 0)))
    grad_rows = lax.all_to_all(latent_grad, "rows", split_axis=1, concat_axis=2, tiled=True)
    grad_flat = grad_rows.reshape(-1, channels)
    running = jnp.zeros((frame_count * lat_rows * lat_cols, channels), jnp.float32)
    blocks = []
    for tap_t, tap_r, tap_c in TAPS:
        window_piece = extended[
            tap_t : tap_t + frame_count,
            tap_r : tap_r + 2 * lat_rows : 2,
            tap_c : tap_c + 2 * lat_cols : 2,
        ]
        window_piece = window_piece.reshape(-1, channels)
        running = running + jnp.dot(
            window_piece, conv_weight[tap_t, tap_r, tap_c], preferred_element_type=jnp.float32
        )
        blocks.append(
            lax.dot_general(
                window_piece,
                grad_flat,
                (((0,), (0,)), ((), ())),
                preferred_element_type=jnp.float32,
            )
        )
    latent_rows = (
        (running + conv_bias)
        .reshape(frame_count, lat_rows, lat_cols, channels)
        .astype(jnp.bfloat16)
    )
    latent = lax.all_to_all(latent_rows, "rows", split_axis=2, concat_axis=1, tiled=True)
    weight_local = jnp.stack(blocks).reshape(3, 3, 3, channels, channels)
    bias_local = jnp.sum(grad_flat.astype(jnp.float32), axis=0)
    following = shifted(grad_rows[:2], "tm", -1)
    grad_ext = jnp.concatenate([grad_rows, following], axis=0)
    above_row = shifted(grad_ext, "rows", 1)
    grad_ext = jnp.concatenate([above_row, grad_ext], axis=1)
    grad_ext = jnp.pad(grad_ext, ((0, 0), (0, 0), (1, 0), (0, 0)))
    parity_sums = {}
    for tap_t, tap_r, tap_c in TAPS:
        row_start = 1 - tap_r // 2
        col_start = 1 - tap_c // 2
        grad_piece = grad_ext[
            2 - tap_t : 2 - tap_t + frame_count,
            row_start : row_start + lat_rows,
            col_start : col_start + lat_cols,
        ]
        term = contract_out(grad_piece.reshape(-1, channels), conv_weight[tap_t, tap_r, tap_c])
        label = (tap_r % 2, tap_c % 2)
        parity_sums[label] = parity_sums[label] + term if label in parity_sums else term
    shaped = {}
    for label in parity_sums:
        shaped[label] = parity_sums[label].reshape(frame_count, lat_rows, lat_cols, channels)
    even_rows = jnp.stack([shaped[0, 0], shaped[0, 1]], axis=3)
    odd_rows = jnp.stack([shaped[1, 0], shaped[1, 1]], axis=3)
    hidden_grad = jnp.stack([even_rows, odd_rows], axis=2).reshape(
        frame_count, row_count, col_count, channels
    )
    sigma = jax.nn.sigmoid(normed)
    normed_grad = hidden_grad * sigma * (1.0 + normed * (1.0 - sigma))
    gain_local = jnp.sum(normed_grad * unit, axis=(0, 1, 2))
    unit_grad = normed_grad * norm_gain
    frames_grad = inv_rms * (unit_grad - unit * jnp.mean(unit_grad * unit, axis=-1, keepdims=True))
    totals = lax.psum((weight_local, gain_local, bias_local), "rows")
    weight_grad, gain_grad, bias_grad = (
        lax.psum_scatter(totals[0], "tm", scatter_dimension=3, tiled=True),
        lax.psum_scatter(totals[1], "tm", scatter_dimension=0, tiled=True),
        lax.psum_scatter(totals[2], "tm", scatter_dimension=0, tiled=True),
    )
    return (latent, frames_grad.astype(jnp.bfloat16), weight_grad, gain_grad, bias_grad)


def partners(value, axis, bits):
    count = lax.axis_size(axis)
    return lax.ppermute(value, axis, [(source, source ^ bits) for source in range(count)])


def exchanged(value, axis, gate=None):
    count = lax.axis_size(axis)
    blocks = {0: value}
    for k in range(1, count):
        if k & (k - 1) == 0:
            blocks[k] = partners(value, axis, k)
    if gate is not None:
        held = [k for k in blocks if k > 1]
        blocks.update(zip(held, gate([blocks[k] for k in held])))
    for k in range(1, count):
        low = k & -k
        if k != low:
            blocks[k] = partners(blocks[k - low], axis, low)
    return [blocks[k] for k in range(count)]


def mm(left, right):
    return jnp.dot(left, right, preferred_element_type=jnp.float32)


def mm_t(left, right):
    return lax.dot_general(
        left, right, (((1,), (1,)), ((), ())), preferred_element_type=jnp.float32
    )


def normalised(frames, gain):
    signal = frames.astype(jnp.float32)
    inv_rms = lax.rsqrt(jnp.mean(signal * signal, axis=-1, keepdims=True) + EPS)
    unit = signal * inv_rms
    return inv_rms, unit, unit * gain


def hidden_kernel(F, J, T, place, frames, vectors, planes, frames_copy, vectors_copy, *rest):
    sends, tmp = rest[:T], rest[T]
    frames_copy[...] = frames[...]
    vectors_copy[...] = vectors[...]
    channels = frames.shape[1]
    part = channels // T
    _, _, normed = normalised(frames[...], vectors[0:1])
    value = normed / (1.0 + jnp.exp(-normed))
    tmp[0] = value[:, : channels // 2]
    tmp[1] = value[:, channels // 2 :]
    block = place[1]
    for rp in range(2):
        pair = []
        for cp in range(2):
            rows = [
                jnp.concatenate(
                    [
                        tmp[half, pl.ds((t * 2 + rp) * 2 * J + cp, J, stride=2), :]
                        for half in range(2)
                    ],
                    axis=1,
                )
                for t in range(F)
            ]
            plane = jnp.concatenate(rows, axis=0)
            pair.append(plane)
            plane = plane.astype(jnp.bfloat16)
            planes[rp, cp] = plane
            late = plane[(F - 2) * J :]
            for k in range(1, T, 2):
                for half in range(2):
                    at = (((rp * 2 + cp) * 2) + half) * 2 * J
                    lanes = slice(half * channels // 2, (half + 1) * channels // 2)
                    sends[k][2 * F * J + at : 2 * F * J + at + 2 * J] = late[:, lanes]
        pieces = [
            jnp.concatenate([p[:, d * part : (d + 1) * part] for p in pair], axis=1)
            for d in range(T)
        ]
        for k in range(T):
            chosen = pieces[0]
            for d in range(1, T):
                chosen = jnp.where(block == d ^ k, pieces[d], chosen)
            sends[k][rp * F * J : (rp + 1) * F * J] = chosen.astype(jnp.bfloat16)


def head_kernel(rows, _, grad_rows, head, passed):
    passed[...] = grad_rows[...]
    for s in range(grad_rows.shape[0]):
        head[s] = grad_rows[s, :rows, :]


def total_kernel(*refs):
    total = refs[0][...]
    for ref in refs[1:-1]:
        total = total + ref[...]
    refs[-1][...] = total


def join_kernel(F, J, T, place, planes, *refs):
    messages, (joined, cached, under, blocks) = refs[:T], refs[T:]
    span = F * J
    block = place[1]
    for k in range(T):
        at = pl.multiple_of((block ^ k) * span, 16)
        for rp in range(2):
            blocks[rp, pl.ds(at, span), :] = messages[k][rp * span : (rp + 1) * span, :]
    for rp in range(2):
        joined[rp] = blocks[rp].T
    for rp in range(2):
        for cp in range(2):
            halves = []
            for half in range(2):
                start = 2 * span + ((rp * 2 + cp) * 2 + half) * 2 * J
                value = jnp.zeros((2 * J, messages[1].shape[1]), jnp.bfloat16)
                for k in range(1, T, 2):
                    found = (block > 0) & (block ^ k == block - 1)
                    value = jnp.where(found, messages[k][start : start + 2 * J, :], value)
                halves.append(value)
            before = jnp.concatenate(halves, axis=1)
            cached[rp, cp] = before
            if rp == 0:
                under[cp, : 2 * J] = before
                under[cp, 2 * J :] = planes[0, cp]


def permutation(shape, meet):
    row = lax.broadcasted_iota(jnp.int32, shape, 0)
    col = lax.broadcasted_iota(jnp.int32, shape, 1)
    return jnp.where(meet(row, col), 1.0, 0.0).astype(jnp.bfloat16)


def slice_of(value, block, k, T):
    part = value.shape[1] // T
    chosen = value[:, :part]
    for d in range(1, T):
        chosen = jnp.where(block == d ^ k, value[:, d * part : (d + 1) * part], chosen)
    return chosen


def shard_order(J, R, rows, first, moved):
    jl = J // R
    return permutation(
        (rows * 2 * J, R * 2 * J),
        lambda o, s: (o // (2 * J) + first == s // jl % R)
        & (o // J % 2 == s // (jl * R) % 2)
        & (o % J == s // (2 * jl * R) * jl + s % jl + moved),
    )


def shard_rows(source, start, count):
    return jnp.concatenate(
        [source[s, start : start + count, :] for s in range(source.shape[0])], axis=0
    )


def gate_kernel(*refs):
    pass


def slab_kernel(
    F, J, R, T, slot, place, planes, cached, under, weight_hbm, frames, vectors, gathered, following,
    out, frames_grad, weight, near, ext, tmp, sem,
):
    row, block = place[0], place[1]
    channels = frames.shape[1]
    span = F * J
    gain, bias = vectors[0:1], vectors[1:2]
    fetches = [
        pltpu.make_async_copy(weight_hbm.at[pl.ds(a * 9, 9)], weight.at[pl.ds(a * 9, 9)], sem.at[a])
        for a in range(3)
    ]
    for copy in fetches:
        copy.start()

    orders = [shard_order(J, R, 2, row - 1, moved) for moved in range(2)]
    for pair in range(F // 2 + 1):
        if pair < F // 2:
            source = shard_rows(gathered, pair * 2 * J, 2 * J)
        else:
            source = shard_rows(following, 0, 2 * J)
        for moved in range(2):
            value = mm(orders[moved], source).astype(jnp.bfloat16)
            for i in range(2):
                near[moved, i, pair * 2 * J : (pair + 1) * 2 * J, :] = value[
                    i * 2 * J : (i + 1) * 2 * J
                ]

    rows = (F + 2) * J
    last = lax.broadcasted_iota(jnp.int32, (rows, 1), 0) % J == J - 1
    for b in range(3):
        for cp in range(2):
            if b == 2:
                full = under[cp]
            else:
                full = jnp.concatenate([cached[b, cp], planes[b, cp]], axis=0)
            ext[b, cp] = full
            if cp == 0:
                moved = pltpu.roll(full.astype(jnp.float32), rows - 1, 0)
                ext[b, 2] = jnp.where(last, 0.0, moved).astype(jnp.bfloat16)

    latent = jnp.zeros((span, channels), jnp.float32)
    sums = {}
    for n, (a, b, c) in enumerate(TAPS):
        if n % 9 == 0:
            fetches[a].wait()
        latent = latent + mm(ext[b, c, a * J : (a + F) * J, :], weight[n])
        piece = near[c // 2, 1 - b // 2, (2 - a) * J : (2 - a + F) * J, :]
        term = mm_t(piece, weight[n])
        key = (b % 2, c % 2)
        sums[key] = sums[key] + term if key in sums else term
    for (rp, cp), value in sums.items():
        for t in range(F):
            for half in range(2):
                lanes = slice(half * channels // 2, (half + 1) * channels // 2)
                tmp[half, pl.ds((t * 2 + rp) * 2 * J + cp, J, stride=2), :] = value[
                    t * J : (t + 1) * J, lanes
                ]
    hidden_grad = jnp.concatenate([tmp[0], tmp[1]], axis=1)
    inv_rms, unit, normed = normalised(frames[...], gain)
    sigma = 1.0 / (1.0 + jnp.exp(-normed))
    normed_grad = hidden_grad * sigma * (1.0 + normed * (1.0 - sigma))
    gain_part = jnp.sum(normed_grad * unit, axis=0, keepdims=True)
    unit_grad = normed_grad * gain
    mean = jnp.mean(unit_grad * unit, axis=-1, keepdims=True)
    frames_grad[...] = (inv_rms * (unit_grad - unit * mean)).astype(jnp.bfloat16)

    jl = J // R
    used = span // R
    order = permutation(
        (R * slot, span),
        lambda o, s: (o % slot < used)
        & (o % slot // jl == s // J)
        & (o // slot * jl + o % jl == s % J),
    )
    value = mm(order, (latent + bias).astype(jnp.bfloat16))
    line = lax.broadcasted_iota(jnp.int32, (R * slot, 1), 0) % slot
    rest = jnp.concatenate([slice_of(gain_part, block, k, T) for k in range(T)], axis=1)
    for n in range(3):
        term = rest.astype(jnp.bfloat16).astype(jnp.float32)
        rest = rest - term
        value = jnp.where(line == used + n, term, value)
    out[...] = value.astype(jnp.bfloat16)


def gain_kernel(T, used, received, *refs):
    parts = refs[-T:]
    value = jnp.zeros(received.shape[1:], jnp.float32)
    for s in range(received.shape[0]):
        value = value + received[s].astype(jnp.float32)
    line = lax.broadcasted_iota(jnp.int32, (received.shape[1], 1), 0)
    value = jnp.where((line >= used) & (line < used + 3), value, 0.0)
    value = jnp.sum(value, axis=0, keepdims=True)
    part = received.shape[2] // T
    for k in range(T):
        parts[k][...] = value[:, k * part : (k + 1) * part]


def order_kernel(F, J, R, T, place, *refs):
    gathered, (grads, bias_sum) = refs[:T], refs[T:]
    channels = grads.shape[-1]
    span = F * J
    depth = T * span
    block = place[1]
    grads[:, :, depth:, :] = jnp.zeros((2, R, 2 * J, channels), jnp.bfloat16)
    orders = [shard_order(J, R, R, 0, moved) for moved in range(2)]
    total = jnp.zeros((1, channels), jnp.float32)
    for k in range(T):
        for pair in range(F // 2):
            source = shard_rows(gathered[k], pair * 2 * J, 2 * J)
            total = total + jnp.sum(source.astype(jnp.float32), axis=0, keepdims=True)
            at = pl.multiple_of((block ^ k) * span + pair * 2 * J, 16)
            for moved in range(2):
                value = mm(orders[moved], source).astype(jnp.bfloat16)
                for i in range(R):
                    grads[moved, i, pl.ds(at, 2 * J), :] = value[i * 2 * J : (i + 1) * 2 * J]
    bias_sum[...] = slice_of(total, block, 0, T)


def weight_kernel(F, J, R, T, part, place, gain, grads, *refs):
    hidden = refs[:R]
    out_hbm, gain_out, out, even, odd, sem = refs[R:]
    gain_out[...] = gain[...]
    channels = grads.shape[-1]
    depth = T * F * J
    lanes = 2 * part
    row = place[0]
    even[:, R * depth :] = jnp.zeros((lanes, depth), jnp.bfloat16)
    for k in range(R):
        at = pl.multiple_of((row ^ k) * depth, 128)
        for rp, turned in ((0, even), (1, odd)):
            turned[:, pl.ds(at, depth)] = hidden[k][rp]
    leaving = []
    for a in range(3):
        start = (2 - a) * J
        for moved in range(2):
            right = grads[moved, :, start : start + depth, :].reshape(R * depth, channels)
            size = part if moved else lanes
            left = jnp.concatenate(
                [even[:size, : R * depth], odd[:size, :], even[:size, depth:]], axis=0
            )
            value = mm(left, right)
            for b in range(3):
                if moved:
                    out[(a * 3 + b) * 3 + 2] = value[b * part : (b + 1) * part]
                else:
                    for cp in range(2):
                        at = b * lanes + cp * part
                        out[(a * 3 + b) * 3 + cp] = value[at : at + part]
        taps = pl.ds(a * 9, 9)
        leaving.append(pltpu.make_async_copy(out.at[taps], out_hbm.at[taps], sem.at[a]))
        leaving[a].start()
    for copy in leaving:
        copy.wait()


def call(kernel, outs, scratch, flops, moved, places, aliases={}, limit=VMEM_LIMIT):
    kinds = {"s": pltpu.SMEM, "v": pltpu.VMEM, "h": pltpu.HBM, "a": pl.ANY}
    specs = [pl.BlockSpec(memory_space=kinds[p]) for p in places]
    count = len(places) - len(outs)
    return pl.pallas_call(
        kernel,
        out_shape=[jax.ShapeDtypeStruct(s, d) for s, d in outs],
        in_specs=specs[:count],
        out_specs=specs[count:],
        scratch_shapes=scratch,
        input_output_aliases=aliases,
        compiler_params=pltpu.CompilerParams(vmem_limit_bytes=limit),
        cost_estimate=pl.CostEstimate(flops=flops, bytes_accessed=moved, transcendentals=0),
    )


def gathered_form(frames, norm_gain, conv_weight, conv_bias, latent_grad):
    bf16, f32 = jnp.bfloat16, jnp.float32
    F, row_count, col_count, C = frames.shape
    R, T = lax.axis_size("rows"), lax.axis_size("tm")
    J = col_count // 2
    span = F * J
    part = C // T
    used = span // R
    slot = -(-(used + 3) // 16) * 16
    vectors = jnp.stack([norm_gain, conv_bias])
    flat = frames.reshape(-1, C)
    weight = conv_weight.reshape(27, C, C)
    place = jnp.stack([lax.axis_index("rows"), lax.axis_index("tm")]).astype(jnp.int32)

    own = latent_grad.reshape(1, -1, C)
    grad_rows = lax.all_to_all(
        jnp.broadcast_to(own, (R,) + own.shape[1:]), "rows", 0, 0, tiled=True
    )

    sizes = [(2 * span + (16 * J if k % 2 else 0), 2 * part) for k in range(T)]
    planes, frames_copy, vectors, *sends = call(
        functools.partial(hidden_kernel, F, J, T),
        [((2, 2, span, C), bf16), (flat.shape, bf16), ((2, C), f32)]
        + [(size, bf16) for size in sizes],
        [pltpu.VMEM((2, 4 * span, C // 2), f32)],
        60 * WORK * span * C, 16 * span * C, "svv" + "v" * (T + 3),
    )(place, flat, vectors)
    head, grad_rows = call(
        functools.partial(head_kernel, 2 * J),
        [((R, 2 * J, C), bf16), (grad_rows.shape, bf16)],
        [], R * span * C, R * span * C, "avvv",
    )(frames_copy, grad_rows)
    messages = [sends[0]] + [partners(sends[k], "tm", k) for k in range(1, T)]
    joined, cached, under = call(
        functools.partial(join_kernel, F, J, T),
        [
            ((2, 2 * part, T * span), bf16),
            ((2, 2, 2 * J, C), bf16),
            ((2, 2 * J + span, C), bf16),
        ],
        [pltpu.VMEM((2, T * span, 2 * part), bf16)],
        30 * WORK * span * C, 16 * span * C, "sv" + "v" * T + "vvv",
    )(place, planes, *messages)
    under = shifted(under, "rows", -1)
    following = shifted(head, "tm", -1)
    packed, frames_grad = call(
        functools.partial(slab_kernel, F, J, R, T, slot),
        [((R * slot, C), bf16), ((4 * span, C), bf16)],
        [
            pltpu.VMEM((27, C, C), bf16),
            pltpu.VMEM((2, 2, (F + 2) * J, C), bf16),
            pltpu.VMEM((3, 3, (F + 2) * J, C), bf16),
            pltpu.VMEM((2, 4 * span, C // 2), f32),
            pltpu.SemaphoreType.DMA((3,)),
        ],
        2 * 54 * span * C * C, 2 * 27 * C * C, "svvvhvvvv" + "vv",
        limit=VMEM_LIMIT_WIDE,
    )(place, planes, cached, under, weight, frames_copy, vectors, grad_rows, following)

    def after_slab(blocks):
        shapes = [(b.shape, bf16) for b in blocks]
        count = len(blocks)
        aliases = {n + 1: n for n in range(count)}
        return list(
            call(gate_kernel, shapes, [], 0, 0, "a" * (2 * count + 1), aliases)(packed, *blocks)
        )

    hidden_all = exchanged(joined, "rows", after_slab)
    grad_all = exchanged(grad_rows, "tm")

    packed = lax.all_to_all(packed.reshape(R, slot, C), "rows", 0, 0, tiled=True)
    latent = packed[:, :used].reshape(R, F, J // R, C).transpose(1, 0, 2, 3)
    gains = call(
        functools.partial(gain_kernel, T, used),
        [((1, part), f32)] * T,
        [], R * slot * C, R * slot * C, "v" + "a" * (R // 2) + "v" * T,
    )(packed, *hidden_all[1::2])
    grads, bias_sum = call(
        functools.partial(order_kernel, F, J, R, T),
        [((2, R, (F * T + 2) * J, C), bf16), ((1, part), f32)],
        [],
        90 * WORK * span * C, 2 * R * T * span * C, "s" + "v" * (T + 2),
    )(place, *grad_all)
    weight_grad, own_gain = call(
        functools.partial(weight_kernel, F, J, R, T, part),
        [((27, part, C), f32), ((1, part), f32)],
        [
            pltpu.VMEM((27, part, C), f32),
            pltpu.VMEM((2 * part, (R + 1) * T * span), bf16),
            pltpu.VMEM((2 * part, R * T * span), bf16),
            pltpu.SemaphoreType.DMA((3,)),
        ],
        200 * WORK * span * C, 8 * 27 * part * C, "svv" + "v" * R + "hv",
    )(place, gains[0], grads, *hidden_all)

    terms = [own_gain] + [partners(gains[k], "tm", k) for k in range(1, T)]
    (gain_grad,) = call(
        total_kernel, [((1, part), f32)], [], T * part, 4 * T * part, "v" * (T + 1)
    )(*terms)
    return (
        latent,
        frames_grad.reshape(frames.shape),
        weight_grad.reshape(3, 3, 3, part, C),
        gain_grad.reshape(part),
        bias_sum.reshape(part),
    )


def on_device(frames, norm_gain, conv_weight, conv_bias, latent_grad):
    rows, shares = lax.axis_size("rows"), lax.axis_size("tm")
    operand_bytes = 2 * rows * shares * (frames.size // shares + latent_grad.size)
    result_bytes = 4 * conv_weight.size
    powers = (rows & (rows - 1)) == 0 and (shares & (shares - 1)) == 0
    if powers and frames.shape[1] == 2 and operand_bytes <= result_bytes:
        form = gathered_form
    else:
        form = reduced_form
    return form(frames, norm_gain, conv_weight, conv_bias, latent_grad)


def solution(mesh):
    placed = (P("tm", "rows", None, None), P(), P(), P(), P("tm", None, "rows", None))
    return jax.shard_map(
        on_device,
        mesh=mesh,
        in_specs=placed,
        out_specs=(
            P("tm", None, "rows", None),
            P("tm", "rows", None, None),
            P(None, None, None, "tm", None),
            P("tm"),
            P("tm"),
        ),
        check_vma=False,
    )
```

```python
import functools

import jax
import jax.numpy as jnp
from jax import lax
from jax.experimental import pallas as pl
from jax.experimental.pallas import tpu as pltpu
from jax.sharding import PartitionSpec as P

EPS = 1e-06
TAPS = [(a, b, c) for a in range(3) for b in range(3) for c in range(3)]
VMEM_LIMIT = 20 * 1024 * 1024
VMEM_LIMIT_WIDE = 57 * 1024 * 1024
WORK = 1200


def shifted(value, axis, steps):
    count = lax.axis_size(axis)
    leading, last = (max(0, -steps), min(count, count - steps))
    return lax.ppermute(value, axis, [(source, source + steps) for source in range(leading, last)])


def contract_out(grad_piece, weight_tap):
    return lax.dot_general(
        grad_piece, weight_tap, (((1,), (1,)), ((), ())), preferred_element_type=jnp.float32
    )


def reduced_form(frames, norm_gain, conv_weight, conv_bias, latent_grad):
    signal = frames.astype(jnp.float32)
    inv_rms = lax.rsqrt(jnp.mean(signal * signal, axis=-1, keepdims=True) + EPS)
    unit = signal * inv_rms
    normed = unit * norm_gain
    hidden = jax.nn.silu(normed).astype(jnp.bfloat16)
    frame_count, row_count, col_count, channels = hidden.shape
    lat_rows = row_count // 2
    lat_cols = col_count // 2
    cached = shifted(hidden[frame_count - 2 :], "tm", 1)
    stacked = jnp.concatenate([cached, hidden], axis=0)
    row_under = shifted(stacked[:, :1], "rows", -1)
    extended = jnp.concatenate([stacked, row_under], axis=1)
    extended = jnp.pad(extended, ((0, 0), (0, 0), (0, 1), (0, 0)))
    grad_rows = lax.all_to_all(latent_grad, "rows", split_axis=1, concat_axis=2, tiled=True)
    grad_flat = grad_rows.reshape(-1, channels)
    running = jnp.zeros((frame_count * lat_rows * lat_cols, channels), jnp.float32)
    blocks = []
    for tap_t, tap_r, tap_c in TAPS:
        window_piece = extended[
            tap_t : tap_t + frame_count,
            tap_r : tap_r + 2 * lat_rows : 2,
            tap_c : tap_c + 2 * lat_cols : 2,
        ]
        window_piece = window_piece.reshape(-1, channels)
        running = running + jnp.dot(
            window_piece, conv_weight[tap_t, tap_r, tap_c], preferred_element_type=jnp.float32
        )
        blocks.append(
            lax.dot_general(
                window_piece,
                grad_flat,
                (((0,), (0,)), ((), ())),
                preferred_element_type=jnp.float32,
            )
        )
    latent_rows = (
        (running + conv_bias)
        .reshape(frame_count, lat_rows, lat_cols, channels)
        .astype(jnp.bfloat16)
    )
    latent = lax.all_to_all(latent_rows, "rows", split_axis=2, concat_axis=1, tiled=True)
    weight_local = jnp.stack(blocks).reshape(3, 3, 3, channels, channels)
    bias_local = jnp.sum(grad_flat.astype(jnp.float32), axis=0)
    following = shifted(grad_rows[:2], "tm", -1)
    grad_ext = jnp.concatenate([grad_rows, following], axis=0)
    above_row = shifted(grad_ext, "rows", 1)
    grad_ext = jnp.concatenate([above_row, grad_ext], axis=1)
    grad_ext = jnp.pad(grad_ext, ((0, 0), (0, 0), (1, 0), (0, 0)))
    parity_sums = {}
    for tap_t, tap_r, tap_c in TAPS:
        row_start = 1 - tap_r // 2
        col_start = 1 - tap_c // 2
        grad_piece = grad_ext[
            2 - tap_t : 2 - tap_t + frame_count,
            row_start : row_start + lat_rows,
            col_start : col_start + lat_cols,
        ]
        term = contract_out(grad_piece.reshape(-1, channels), conv_weight[tap_t, tap_r, tap_c])
        label = (tap_r % 2, tap_c % 2)
        parity_sums[label] = parity_sums[label] + term if label in parity_sums else term
    shaped = {}
    for label in parity_sums:
        shaped[label] = parity_sums[label].reshape(frame_count, lat_rows, lat_cols, channels)
    even_rows = jnp.stack([shaped[0, 0], shaped[0, 1]], axis=3)
    odd_rows = jnp.stack([shaped[1, 0], shaped[1, 1]], axis=3)
    hidden_grad = jnp.stack([even_rows, odd_rows], axis=2).reshape(
        frame_count, row_count, col_count, channels
    )
    sigma = jax.nn.sigmoid(normed)
    normed_grad = hidden_grad * sigma * (1.0 + normed * (1.0 - sigma))
    gain_local = jnp.sum(normed_grad * unit, axis=(0, 1, 2))
    unit_grad = normed_grad * norm_gain
    frames_grad = inv_rms * (unit_grad - unit * jnp.mean(unit_grad * unit, axis=-1, keepdims=True))
    totals = lax.psum((weight_local, gain_local, bias_local), "rows")
    weight_grad, gain_grad, bias_grad = (
        lax.psum_scatter(totals[0], "tm", scatter_dimension=3, tiled=True),
        lax.psum_scatter(totals[1], "tm", scatter_dimension=0, tiled=True),
        lax.psum_scatter(totals[2], "tm", scatter_dimension=0, tiled=True),
    )
    return (latent, frames_grad.astype(jnp.bfloat16), weight_grad, gain_grad, bias_grad)


def partners(value, axis, bits):
    count = lax.axis_size(axis)
    return lax.ppermute(value, axis, [(source, source ^ bits) for source in range(count)])


def exchanged(value, axis, gate=None):
    count = lax.axis_size(axis)
    blocks = {0: value}
    for k in range(1, count):
        if k & (k - 1) == 0:
            blocks[k] = partners(value, axis, k)
    if gate is not None:
        held = [k for k in blocks if k > 1]
        blocks.update(zip(held, gate([blocks[k] for k in held])))
    for k in range(1, count):
        low = k & -k
        if k != low:
            blocks[k] = partners(blocks[k - low], axis, low)
    return [blocks[k] for k in range(count)]


def mm(left, right):
    return jnp.dot(left, right, preferred_element_type=jnp.float32)


def mm_t(left, right):
    return lax.dot_general(
        left, right, (((1,), (1,)), ((), ())), preferred_element_type=jnp.float32
    )


def normalised(frames, gain):
    signal = frames.astype(jnp.float32)
    inv_rms = lax.rsqrt(jnp.mean(signal * signal, axis=-1, keepdims=True) + EPS)
    unit = signal * inv_rms
    return inv_rms, unit, unit * gain


def hidden_kernel(F, J, T, place, frames, vectors, planes, frames_copy, vectors_copy, *rest):
    sends, tmp = rest[:T], rest[T]
    frames_copy[...] = frames[...]
    vectors_copy[...] = vectors[...]
    channels = frames.shape[1]
    part = channels // T
    _, _, normed = normalised(frames[...], vectors[0:1])
    value = normed / (1.0 + jnp.exp(-normed))
    tmp[0] = value[:, : channels // 2]
    tmp[1] = value[:, channels // 2 :]
    block = place[1]
    for rp in range(2):
        pair = []
        for cp in range(2):
            rows = [
                jnp.concatenate(
                    [
                        tmp[half, pl.ds((t * 2 + rp) * 2 * J + cp, J, stride=2), :]
                        for half in range(2)
                    ],
                    axis=1,
                )
                for t in range(F)
            ]
            plane = jnp.concatenate(rows, axis=0)
            pair.append(plane)
            plane = plane.astype(jnp.bfloat16)
            planes[rp, cp] = plane
            late = plane[(F - 2) * J :]
            for k in range(1, T, 2):
                for half in range(2):
                    at = (((rp * 2 + cp) * 2) + half) * 2 * J
                    lanes = slice(half * channels // 2, (half + 1) * channels // 2)
                    sends[k][2 * F * J + at : 2 * F * J + at + 2 * J] = late[:, lanes]
        pieces = [
            jnp.concatenate([p[:, d * part : (d + 1) * part] for p in pair], axis=1)
            for d in range(T)
        ]
        for k in range(T):
            chosen = pieces[0]
            for d in range(1, T):
                chosen = jnp.where(block == d ^ k, pieces[d], chosen)
            sends[k][rp * F * J : (rp + 1) * F * J] = chosen.astype(jnp.bfloat16)


def head_kernel(rows, _, grad_rows, head, passed):
    passed[...] = grad_rows[...]
    for s in range(grad_rows.shape[0]):
        head[s] = grad_rows[s, :rows, :]


def total_kernel(*refs):
    total = refs[0][...]
    for ref in refs[1:-1]:
        total = total + ref[...]
    refs[-1][...] = total


def join_kernel(F, J, T, place, planes, *refs):
    messages, (joined, cached, under, blocks) = refs[:T], refs[T:]
    span = F * J
    block = place[1]
    for k in range(T):
        at = pl.multiple_of((block ^ k) * span, 16)
        for rp in range(2):
            blocks[rp, pl.ds(at, span), :] = messages[k][rp * span : (rp + 1) * span, :]
    for rp in range(2):
        joined[rp] = blocks[rp].T
    for rp in range(2):
        for cp in range(2):
            halves = []
            for half in range(2):
                start = 2 * span + ((rp * 2 + cp) * 2 + half) * 2 * J
                value = jnp.zeros((2 * J, messages[1].shape[1]), jnp.bfloat16)
                for k in range(1, T, 2):
                    found = (block > 0) & (block ^ k == block - 1)
                    value = jnp.where(found, messages[k][start : start + 2 * J, :], value)
                halves.append(value)
            before = jnp.concatenate(halves, axis=1)
            cached[rp, cp] = before
            if rp == 0:
                under[cp, : 2 * J] = before
                under[cp, 2 * J :] = planes[0, cp]


def permutation(shape, meet):
    row = lax.broadcasted_iota(jnp.int32, shape, 0)
    col = lax.broadcasted_iota(jnp.int32, shape, 1)
    return jnp.where(meet(row, col), 1.0, 0.0).astype(jnp.bfloat16)


def slice_of(value, block, k, T):
    part = value.shape[1] // T
    chosen = value[:, :part]
    for d in range(1, T):
        chosen = jnp.where(block == d ^ k, value[:, d * part : (d + 1) * part], chosen)
    return chosen


def shard_order(J, R, rows, first, moved):
    jl = J // R
    return permutation(
        (rows * 2 * J, R * 2 * J),
        lambda o, s: (o // (2 * J) + first == s // jl % R)
        & (o // J % 2 == s // (jl * R) % 2)
        & (o % J == s // (2 * jl * R) * jl + s % jl + moved),
    )


def shard_rows(source, start, count):
    return jnp.concatenate(
        [source[s, start : start + count, :] for s in range(source.shape[0])], axis=0
    )


def gate_kernel(*refs):
    pass


def slab_kernel(
    F, J, R, T, slot, place, planes, cached, under, weight_hbm, frames, vectors, gathered, following,
    out, frames_grad, weight, near, ext, tmp, sem,
):
    row, block = place[0], place[1]
    channels = frames.shape[1]
    span = F * J
    gain, bias = vectors[0:1], vectors[1:2]
    fetches = [
        pltpu.make_async_copy(weight_hbm.at[pl.ds(a * 9, 9)], weight.at[pl.ds(a * 9, 9)], sem.at[a])
        for a in range(3)
    ]
    for copy in fetches:
        copy.start()

    orders = [shard_order(J, R, 2, row - 1, moved) for moved in range(2)]
    for pair in range(F // 2 + 1):
        if pair < F // 2:
            source = shard_rows(gathered, pair * 2 * J, 2 * J)
        else:
            source = shard_rows(following, 0, 2 * J)
        for moved in range(2):
            value = mm(orders[moved], source).astype(jnp.bfloat16)
            for i in range(2):
                near[moved, i, pair * 2 * J : (pair + 1) * 2 * J, :] = value[
                    i * 2 * J : (i + 1) * 2 * J
                ]

    rows = (F + 2) * J
    last = lax.broadcasted_iota(jnp.int32, (rows, 1), 0) % J == J - 1
    for b in range(3):
        for cp in range(2):
            if b == 2:
                full = under[cp]
            else:
                full = jnp.concatenate([cached[b, cp], planes[b, cp]], axis=0)
            ext[b, cp] = full
            if cp == 0:
                moved = pltpu.roll(full.astype(jnp.float32), rows - 1, 0)
                ext[b, 2] = jnp.where(last, 0.0, moved).astype(jnp.bfloat16)

    latent = jnp.zeros((span, channels), jnp.float32)
    sums = {}
    for n, (a, b, c) in enumerate(TAPS):
        if n % 9 == 0:
            fetches[a].wait()
        latent = latent + mm(ext[b, c, a * J : (a + F) * J, :], weight[n])
        piece = near[c // 2, 1 - b // 2, (2 - a) * J : (2 - a + F) * J, :]
        term = mm_t(piece, weight[n])
        key = (b % 2, c % 2)
        sums[key] = sums[key] + term if key in sums else term
    for (rp, cp), value in sums.items():
        for t in range(F):
            for half in range(2):
                lanes = slice(half * channels // 2, (half + 1) * channels // 2)
                tmp[half, pl.ds((t * 2 + rp) * 2 * J + cp, J, stride=2), :] = value[
                    t * J : (t + 1) * J, lanes
                ]
    hidden_grad = jnp.concatenate([tmp[0], tmp[1]], axis=1)
    inv_rms, unit, normed = normalised(frames[...], gain)
    sigma = 1.0 / (1.0 + jnp.exp(-normed))
    normed_grad = hidden_grad * sigma * (1.0 + normed * (1.0 - sigma))
    gain_part = jnp.sum(normed_grad * unit, axis=0, keepdims=True)
    unit_grad = normed_grad * gain
    mean = jnp.mean(unit_grad * unit, axis=-1, keepdims=True)
    frames_grad[...] = (inv_rms * (unit_grad - unit * mean)).astype(jnp.bfloat16)

    jl = J // R
    used = span // R
    order = permutation(
        (R * slot, span),
        lambda o, s: (o % slot < used)
        & (o % slot // jl == s // J)
        & (o // slot * jl + o % jl == s % J),
    )
    value = mm(order, (latent + bias).astype(jnp.bfloat16))
    line = lax.broadcasted_iota(jnp.int32, (R * slot, 1), 0) % slot
    rest = jnp.concatenate([slice_of(gain_part, block, k, T) for k in range(T)], axis=1)
    for n in range(3):
        term = rest.astype(jnp.bfloat16).astype(jnp.float32)
        rest = rest - term
        value = jnp.where(line == used + n, term, value)
    out[...] = value.astype(jnp.bfloat16)


def gain_kernel(T, used, received, *refs):
    parts = refs[-T:]
    value = jnp.zeros(received.shape[1:], jnp.float32)
    for s in range(received.shape[0]):
        value = value + received[s].astype(jnp.float32)
    line = lax.broadcasted_iota(jnp.int32, (received.shape[1], 1), 0)
    value = jnp.where((line >= used) & (line < used + 3), value, 0.0)
    value = jnp.sum(value, axis=0, keepdims=True)
    part = received.shape[2] // T
    for k in range(T):
        parts[k][...] = value[:, k * part : (k + 1) * part]


def order_kernel(F, J, R, T, place, *refs):
    gathered, (grads, bias_sum) = refs[:T], refs[T:]
    channels = grads.shape[-1]
    span = F * J
    depth = T * span
    block = place[1]
    grads[:, :, depth:, :] = jnp.zeros((2, R, 2 * J, channels), jnp.bfloat16)
    orders = [shard_order(J, R, R, 0, moved) for moved in range(2)]
    total = jnp.zeros((1, channels), jnp.float32)
    for k in range(T):
        for pair in range(F // 2):
            source = shard_rows(gathered[k], pair * 2 * J, 2 * J)
            total = total + jnp.sum(source.astype(jnp.float32), axis=0, keepdims=True)
            at = pl.multiple_of((block ^ k) * span + pair * 2 * J, 16)
            for moved in range(2):
                value = mm(orders[moved], source).astype(jnp.bfloat16)
                for i in range(R):
                    grads[moved, i, pl.ds(at, 2 * J), :] = value[i * 2 * J : (i + 1) * 2 * J]
    bias_sum[...] = slice_of(total, block, 0, T)


def weight_kernel(F, J, R, T, part, place, gain, grads, *refs):
    hidden = refs[:R]
    out_hbm, gain_out, out, even, odd, sem = refs[R:]
    gain_out[...] = gain[...]
    channels = grads.shape[-1]
    depth = T * F * J
    lanes = 2 * part
    row = place[0]
    even[:, R * depth :] = jnp.zeros((lanes, depth), jnp.bfloat16)
    for k in range(R):
        at = pl.multiple_of((row ^ k) * depth, 128)
        for rp, turned in ((0, even), (1, odd)):
            turned[:, pl.ds(at, depth)] = hidden[k][rp]
    leaving = []
    for a in range(3):
        start = (2 - a) * J
        for moved in range(2):
            right = grads[moved, :, start : start + depth, :].reshape(R * depth, channels)
            size = part if moved else lanes
            left = jnp.concatenate(
                [even[:size, : R * depth], odd[:size, :], even[:size, depth:]], axis=0
            )
            value = mm(left, right)
            for b in range(3):
                if moved:
                    out[(a * 3 + b) * 3 + 2] = value[b * part : (b + 1) * part]
                else:
                    for cp in range(2):
                        at = b * lanes + cp * part
                        out[(a * 3 + b) * 3 + cp] = value[at : at + part]
        taps = pl.ds(a * 9, 9)
        leaving.append(pltpu.make_async_copy(out.at[taps], out_hbm.at[taps], sem.at[a]))
        leaving[a].start()
    for copy in leaving:
        copy.wait()


def call(kernel, outs, scratch, flops, moved, places, aliases={}, limit=VMEM_LIMIT):
    kinds = {"s": pltpu.SMEM, "v": pltpu.VMEM, "h": pltpu.HBM, "a": pl.ANY}
    specs = [pl.BlockSpec(memory_space=kinds[p]) for p in places]
    count = len(places) - len(outs)
    return pl.pallas_call(
        kernel,
        out_shape=[jax.ShapeDtypeStruct(s, d) for s, d in outs],
        in_specs=specs[:count],
        out_specs=specs[count:],
        scratch_shapes=scratch,
        input_output_aliases=aliases,
        compiler_params=pltpu.CompilerParams(vmem_limit_bytes=limit),
        cost_estimate=pl.CostEstimate(flops=flops, bytes_accessed=moved, transcendentals=0),
    )


def gathered_form(frames, norm_gain, conv_weight, conv_bias, latent_grad):
    bf16, f32 = jnp.bfloat16, jnp.float32
    F, row_count, col_count, C = frames.shape
    R, T = lax.axis_size("rows"), lax.axis_size("tm")
    J = col_count // 2
    span = F * J
    part = C // T
    used = span // R
    slot = -(-(used + 3) // 16) * 16
    vectors = jnp.stack([norm_gain, conv_bias])
    flat = frames.reshape(-1, C)
    weight = conv_weight.reshape(27, C, C)
    place = jnp.stack([lax.axis_index("rows"), lax.axis_index("tm")]).astype(jnp.int32)

    own = latent_grad.reshape(1, -1, C)
    grad_rows = lax.all_to_all(
        jnp.broadcast_to(own, (R,) + own.shape[1:]), "rows", 0, 0, tiled=True
    )

    sizes = [(2 * span + (16 * J if k % 2 else 0), 2 * part) for k in range(T)]
    planes, frames_copy, vectors, *sends = call(
        functools.partial(hidden_kernel, F, J, T),
        [((2, 2, span, C), bf16), (flat.shape, bf16), ((2, C), f32)]
        + [(size, bf16) for size in sizes],
        [pltpu.VMEM((2, 4 * span, C // 2), f32)],
        60 * WORK * span * C, 16 * span * C, "svv" + "v" * (T + 3),
    )(place, flat, vectors)
    messages = [sends[0]] + [partners(sends[k], "tm", k) for k in range(1, T)]
    head, grad_rows = call(
        functools.partial(head_kernel, 2 * J),
        [((R, 2 * J, C), bf16), (grad_rows.shape, bf16)],
        [], R * span * C, R * span * C, "avvv",
    )(messages[1], grad_rows)
    joined, cached, under = call(
        functools.partial(join_kernel, F, J, T),
        [
            ((2, 2 * part, T * span), bf16),
            ((2, 2, 2 * J, C), bf16),
            ((2, 2 * J + span, C), bf16),
        ],
        [pltpu.VMEM((2, T * span, 2 * part), bf16)],
        30 * WORK * span * C, 16 * span * C, "sv" + "v" * T + "vvv",
    )(place, planes, *messages)
    under = shifted(under, "rows", -1)
    following = shifted(head, "tm", -1)
    packed, frames_grad = call(
        functools.partial(slab_kernel, F, J, R, T, slot),
        [((R * slot, C), bf16), ((4 * span, C), bf16)],
        [
            pltpu.VMEM((27, C, C), bf16),
            pltpu.VMEM((2, 2, (F + 2) * J, C), bf16),
            pltpu.VMEM((3, 3, (F + 2) * J, C), bf16),
            pltpu.VMEM((2, 4 * span, C // 2), f32),
            pltpu.SemaphoreType.DMA((3,)),
        ],
        2 * 54 * span * C * C, 2 * 27 * C * C, "svvvhvvvv" + "vv",
        limit=VMEM_LIMIT_WIDE,
    )(place, planes, cached, under, weight, frames_copy, vectors, grad_rows, following)

    def after_slab(blocks):
        shapes = [(b.shape, bf16) for b in blocks]
        count = len(blocks)
        aliases = {n + 1: n for n in range(count)}
        return list(
            call(gate_kernel, shapes, [], 0, 0, "a" * (2 * count + 1), aliases)(packed, *blocks)
        )

    later = {}

    def gate(blocks):
        *blocks, later["grads"] = after_slab(blocks + [grad_rows])
        return blocks

    hidden_all = exchanged(joined, "rows", gate)
    grad_all = exchanged(later["grads"], "tm")

    packed = lax.all_to_all(packed.reshape(R, slot, C), "rows", 0, 0, tiled=True)
    latent = packed[:, :used].reshape(R, F, J // R, C).transpose(1, 0, 2, 3)
    gains = call(
        functools.partial(gain_kernel, T, used),
        [((1, part), f32)] * T,
        [], R * slot * C, R * slot * C, "v" + "a" * (R // 2) + "v" * T,
    )(packed, *hidden_all[1::2])
    grads, bias_sum = call(
        functools.partial(order_kernel, F, J, R, T),
        [((2, R, (F * T + 2) * J, C), bf16), ((1, part), f32)],
        [],
        90 * WORK * span * C, 2 * R * T * span * C, "s" + "v" * (T + 2),
    )(place, *grad_all)
    weight_grad, own_gain = call(
        functools.partial(weight_kernel, F, J, R, T, part),
        [((27, part, C), f32), ((1, part), f32)],
        [
            pltpu.VMEM((27, part, C), f32),
            pltpu.VMEM((2 * part, (R + 1) * T * span), bf16),
            pltpu.VMEM((2 * part, R * T * span), bf16),
            pltpu.SemaphoreType.DMA((3,)),
        ],
        200 * WORK * span * C, 8 * 27 * part * C, "svv" + "v" * R + "hv",
    )(place, gains[0], grads, *hidden_all)

    terms = [own_gain] + [partners(gains[k], "tm", k) for k in range(1, T)]
    (gain_grad,) = call(
        total_kernel, [((1, part), f32)], [], T * part, 4 * T * part, "v" * (T + 1)
    )(*terms)
    return (
        latent,
        frames_grad.reshape(frames.shape),
        weight_grad.reshape(3, 3, 3, part, C),
        gain_grad.reshape(part),
        bias_sum.reshape(part),
    )


def on_device(frames, norm_gain, conv_weight, conv_bias, latent_grad):
    rows, shares = lax.axis_size("rows"), lax.axis_size("tm")
    operand_bytes = 2 * rows * shares * (frames.size // shares + latent_grad.size)
    result_bytes = 4 * conv_weight.size
    powers = (rows & (rows - 1)) == 0 and (shares & (shares - 1)) == 0
    if powers and frames.shape[1] == 2 and operand_bytes <= result_bytes:
        form = gathered_form
    else:
        form = reduced_form
    return form(frames, norm_gain, conv_weight, conv_bias, latent_grad)


def solution(mesh):
    placed = (P("tm", "rows", None, None), P(), P(), P(), P("tm", None, "rows", None))
    return jax.shard_map(
        on_device,
        mesh=mesh,
        in_specs=placed,
        out_specs=(
            P("tm", None, "rows", None),
            P("tm", "rows", None, None),
            P(None, None, None, "tm", None),
            P("tm"),
            P("tm"),
        ),
        check_vma=False,
    )
```

```python
import functools

import jax
import jax.numpy as jnp
from jax import lax
from jax.experimental import pallas as pl
from jax.experimental.pallas import tpu as pltpu
from jax.sharding import PartitionSpec as P

EPS = 1e-06
TAPS = [(a, b, c) for a in range(3) for b in range(3) for c in range(3)]
VMEM_LIMIT = 20 * 1024 * 1024
VMEM_LIMIT_WIDE = 60 * 1024 * 1024
WORK = 1200


def shifted(value, axis, steps):
    count = lax.axis_size(axis)
    leading, last = (max(0, -steps), min(count, count - steps))
    return lax.ppermute(value, axis, [(source, source + steps) for source in range(leading, last)])


def contract_out(grad_piece, weight_tap):
    return lax.dot_general(
        grad_piece, weight_tap, (((1,), (1,)), ((), ())), preferred_element_type=jnp.float32
    )


def reduced_form(frames, norm_gain, conv_weight, conv_bias, latent_grad):
    signal = frames.astype(jnp.float32)
    inv_rms = lax.rsqrt(jnp.mean(signal * signal, axis=-1, keepdims=True) + EPS)
    unit = signal * inv_rms
    normed = unit * norm_gain
    hidden = jax.nn.silu(normed).astype(jnp.bfloat16)
    frame_count, row_count, col_count, channels = hidden.shape
    lat_rows = row_count // 2
    lat_cols = col_count // 2
    cached = shifted(hidden[frame_count - 2 :], "tm", 1)
    stacked = jnp.concatenate([cached, hidden], axis=0)
    row_under = shifted(stacked[:, :1], "rows", -1)
    extended = jnp.concatenate([stacked, row_under], axis=1)
    extended = jnp.pad(extended, ((0, 0), (0, 0), (0, 1), (0, 0)))
    grad_rows = lax.all_to_all(latent_grad, "rows", split_axis=1, concat_axis=2, tiled=True)
    grad_flat = grad_rows.reshape(-1, channels)
    running = jnp.zeros((frame_count * lat_rows * lat_cols, channels), jnp.float32)
    blocks = []
    for tap_t, tap_r, tap_c in TAPS:
        window_piece = extended[
            tap_t : tap_t + frame_count,
            tap_r : tap_r + 2 * lat_rows : 2,
            tap_c : tap_c + 2 * lat_cols : 2,
        ]
        window_piece = window_piece.reshape(-1, channels)
        running = running + jnp.dot(
            window_piece, conv_weight[tap_t, tap_r, tap_c], preferred_element_type=jnp.float32
        )
        blocks.append(
            lax.dot_general(
                window_piece,
                grad_flat,
                (((0,), (0,)), ((), ())),
                preferred_element_type=jnp.float32,
            )
        )
    latent_rows = (
        (running + conv_bias)
        .reshape(frame_count, lat_rows, lat_cols, channels)
        .astype(jnp.bfloat16)
    )
    latent = lax.all_to_all(latent_rows, "rows", split_axis=2, concat_axis=1, tiled=True)
    weight_local = jnp.stack(blocks).reshape(3, 3, 3, channels, channels)
    bias_local = jnp.sum(grad_flat.astype(jnp.float32), axis=0)
    following = shifted(grad_rows[:2], "tm", -1)
    grad_ext = jnp.concatenate([grad_rows, following], axis=0)
    above_row = shifted(grad_ext, "rows", 1)
    grad_ext = jnp.concatenate([above_row, grad_ext], axis=1)
    grad_ext = jnp.pad(grad_ext, ((0, 0), (0, 0), (1, 0), (0, 0)))
    parity_sums = {}
    for tap_t, tap_r, tap_c in TAPS:
        row_start = 1 - tap_r // 2
        col_start = 1 - tap_c // 2
        grad_piece = grad_ext[
            2 - tap_t : 2 - tap_t + frame_count,
            row_start : row_start + lat_rows,
            col_start : col_start + lat_cols,
        ]
        term = contract_out(grad_piece.reshape(-1, channels), conv_weight[tap_t, tap_r, tap_c])
        label = (tap_r % 2, tap_c % 2)
        parity_sums[label] = parity_sums[label] + term if label in parity_sums else term
    shaped = {}
    for label in parity_sums:
        shaped[label] = parity_sums[label].reshape(frame_count, lat_rows, lat_cols, channels)
    even_rows = jnp.stack([shaped[0, 0], shaped[0, 1]], axis=3)
    odd_rows = jnp.stack([shaped[1, 0], shaped[1, 1]], axis=3)
    hidden_grad = jnp.stack([even_rows, odd_rows], axis=2).reshape(
        frame_count, row_count, col_count, channels
    )
    sigma = jax.nn.sigmoid(normed)
    normed_grad = hidden_grad * sigma * (1.0 + normed * (1.0 - sigma))
    gain_local = jnp.sum(normed_grad * unit, axis=(0, 1, 2))
    unit_grad = normed_grad * norm_gain
    frames_grad = inv_rms * (unit_grad - unit * jnp.mean(unit_grad * unit, axis=-1, keepdims=True))
    totals = lax.psum((weight_local, gain_local, bias_local), "rows")
    weight_grad, gain_grad, bias_grad = (
        lax.psum_scatter(totals[0], "tm", scatter_dimension=3, tiled=True),
        lax.psum_scatter(totals[1], "tm", scatter_dimension=0, tiled=True),
        lax.psum_scatter(totals[2], "tm", scatter_dimension=0, tiled=True),
    )
    return (latent, frames_grad.astype(jnp.bfloat16), weight_grad, gain_grad, bias_grad)


def partners(value, axis, bits):
    count = lax.axis_size(axis)
    return lax.ppermute(value, axis, [(source, source ^ bits) for source in range(count)])


def exchanged(value, axis, gate=None):
    count = lax.axis_size(axis)
    blocks = {0: value}
    for k in range(1, count):
        if k & (k - 1) == 0:
            blocks[k] = partners(value, axis, k)
    if gate is not None:
        held = [k for k in blocks if k > 1]
        blocks.update(zip(held, gate([blocks[k] for k in held])))
    for k in range(1, count):
        low = k & -k
        if k != low:
            blocks[k] = partners(blocks[k - low], axis, low)
    return [blocks[k] for k in range(count)]


def mm(left, right):
    return jnp.dot(left, right, preferred_element_type=jnp.float32)


def mm_t(left, right):
    return lax.dot_general(
        left, right, (((1,), (1,)), ((), ())), preferred_element_type=jnp.float32
    )


def normalised(frames, gain):
    signal = frames.astype(jnp.float32)
    inv_rms = lax.rsqrt(jnp.mean(signal * signal, axis=-1, keepdims=True) + EPS)
    unit = signal * inv_rms
    return inv_rms, unit, unit * gain


def hidden_kernel(F, J, T, place, frames, vectors, planes, frames_copy, vectors_copy, *rest):
    sends, tmp = rest[:T], rest[T]
    frames_copy[...] = frames[...]
    vectors_copy[...] = vectors[...]
    channels = frames.shape[1]
    part = channels // T
    _, _, normed = normalised(frames[...], vectors[0:1])
    value = normed / (1.0 + jnp.exp(-normed))
    tmp[0] = value[:, : channels // 2]
    tmp[1] = value[:, channels // 2 :]
    block = place[1]
    for rp in range(2):
        pair = []
        for cp in range(2):
            rows = [
                jnp.concatenate(
                    [
                        tmp[half, pl.ds((t * 2 + rp) * 2 * J + cp, J, stride=2), :]
                        for half in range(2)
                    ],
                    axis=1,
                )
                for t in range(F)
            ]
            plane = jnp.concatenate(rows, axis=0)
            pair.append(plane)
            plane = plane.astype(jnp.bfloat16)
            planes[rp, cp] = plane
            late = plane[(F - 2) * J :]
            for k in range(1, T, 2):
                for half in range(2):
                    at = (((rp * 2 + cp) * 2) + half) * 2 * J
                    lanes = slice(half * channels // 2, (half + 1) * channels // 2)
                    sends[k][2 * F * J + at : 2 * F * J + at + 2 * J] = late[:, lanes]
        pieces = [
            jnp.concatenate([p[:, d * part : (d + 1) * part] for p in pair], axis=1)
            for d in range(T)
        ]
        for k in range(T):
            chosen = pieces[0]
            for d in range(1, T):
                chosen = jnp.where(block == d ^ k, pieces[d], chosen)
            sends[k][rp * F * J : (rp + 1) * F * J] = chosen.astype(jnp.bfloat16)


def head_kernel(rows, _, grad_rows, head, passed):
    passed[...] = grad_rows[...]
    for s in range(grad_rows.shape[0]):
        head[s] = grad_rows[s, :rows, :]


def join_kernel(F, J, T, place, planes, *refs):
    messages, (joined, cached, under, blocks) = refs[:T], refs[T:]
    span = F * J
    block = place[1]
    for k in range(T):
        at = pl.multiple_of((block ^ k) * span, 16)
        for rp in range(2):
            blocks[rp, pl.ds(at, span), :] = messages[k][rp * span : (rp + 1) * span, :]
    for rp in range(2):
        joined[rp] = blocks[rp].T
    for rp in range(2):
        for cp in range(2):
            halves = []
            for half in range(2):
                start = 2 * span + ((rp * 2 + cp) * 2 + half) * 2 * J
                value = jnp.zeros((2 * J, messages[1].shape[1]), jnp.bfloat16)
                for k in range(1, T, 2):
                    found = (block > 0) & (block ^ k == block - 1)
                    value = jnp.where(found, messages[k][start : start + 2 * J, :], value)
                halves.append(value)
            before = jnp.concatenate(halves, axis=1)
            cached[rp, cp] = before
            if rp == 0:
                under[cp, : 2 * J] = before
                under[cp, 2 * J :] = planes[0, cp]


def permutation(shape, meet):
    row = lax.broadcasted_iota(jnp.int32, shape, 0)
    col = lax.broadcasted_iota(jnp.int32, shape, 1)
    return jnp.where(meet(row, col), 1.0, 0.0).astype(jnp.bfloat16)


def slice_of(value, block, k, T):
    part = value.shape[1] // T
    chosen = value[:, :part]
    for d in range(1, T):
        chosen = jnp.where(block == d ^ k, value[:, d * part : (d + 1) * part], chosen)
    return chosen


def shard_order(J, R, rows, first, moved):
    jl = J // R
    return permutation(
        (rows * 2 * J, R * 2 * J),
        lambda o, s: (o // (2 * J) + first == s // jl % R)
        & (o // J % 2 == s // (jl * R) % 2)
        & (o % J == s // (2 * jl * R) * jl + s % jl + moved),
    )


def shard_rows(source, start, count):
    return jnp.concatenate(
        [source[s, start : start + count, :] for s in range(source.shape[0])], axis=0
    )


def gate_kernel(*refs):
    pass


def slab_kernel(
    F, J, R, T, slot, place, planes, cached, under, weight_hbm, frames, vectors, gathered, following,
    out, frames_grad, weight, near, ext, tmp, sem,
):
    row, block = place[0], place[1]
    channels = frames.shape[1]
    span = F * J
    gain, bias = vectors[0:1], vectors[1:2]
    fetches = [
        pltpu.make_async_copy(weight_hbm.at[pl.ds(a * 9, 9)], weight.at[pl.ds(a * 9, 9)], sem.at[a])
        for a in range(3)
    ]
    for copy in fetches:
        copy.start()

    orders = [shard_order(J, R, 2, row - 1, moved) for moved in range(2)]
    for pair in range(F // 2 + 1):
        if pair < F // 2:
            source = shard_rows(gathered, pair * 2 * J, 2 * J)
        else:
            source = shard_rows(following, 0, 2 * J)
        for moved in range(2):
            value = mm(orders[moved], source).astype(jnp.bfloat16)
            for i in range(2):
                near[moved, i, pair * 2 * J : (pair + 1) * 2 * J, :] = value[
                    i * 2 * J : (i + 1) * 2 * J
                ]

    rows = (F + 2) * J
    last = lax.broadcasted_iota(jnp.int32, (rows, 1), 0) % J == J - 1
    for b in range(3):
        for cp in range(2):
            if b == 2:
                full = under[cp]
            else:
                full = jnp.concatenate([cached[b, cp], planes[b, cp]], axis=0)
            ext[b, cp] = full
            if cp == 0:
                moved = pltpu.roll(full.astype(jnp.float32), rows - 1, 0)
                ext[b, 2] = jnp.where(last, 0.0, moved).astype(jnp.bfloat16)

    latent = jnp.zeros((span, channels), jnp.float32)
    sums = {}
    for n, (a, b, c) in enumerate(TAPS):
        if n % 9 == 0:
            fetches[a].wait()
        latent = latent + mm(ext[b, c, a * J : (a + F) * J, :], weight[n])
        piece = near[c // 2, 1 - b // 2, (2 - a) * J : (2 - a + F) * J, :]
        term = mm_t(piece, weight[n])
        key = (b % 2, c % 2)
        sums[key] = sums[key] + term if key in sums else term
    for (rp, cp), value in sums.items():
        for t in range(F):
            for half in range(2):
                lanes = slice(half * channels // 2, (half + 1) * channels // 2)
                tmp[half, pl.ds((t * 2 + rp) * 2 * J + cp, J, stride=2), :] = value[
                    t * J : (t + 1) * J, lanes
                ]
    hidden_grad = jnp.concatenate([tmp[0], tmp[1]], axis=1)
    inv_rms, unit, normed = normalised(frames[...], gain)
    sigma = 1.0 / (1.0 + jnp.exp(-normed))
    normed_grad = hidden_grad * sigma * (1.0 + normed * (1.0 - sigma))
    gain_part = jnp.sum(normed_grad * unit, axis=0, keepdims=True)
    unit_grad = normed_grad * gain
    mean = jnp.mean(unit_grad * unit, axis=-1, keepdims=True)
    frames_grad[...] = (inv_rms * (unit_grad - unit * mean)).astype(jnp.bfloat16)

    jl = J // R
    used = span // R
    blocks = out.shape[0] // (R * slot)
    order = permutation(
        (R * blocks * slot, span),
        lambda o, s: (o % slot < used)
        & (o // slot % blocks == block)
        & (o % slot // jl == s // J)
        & (o // (slot * blocks) * jl + o % jl == s % J),
    )
    value = mm(order, (latent + bias).astype(jnp.bfloat16))
    line = lax.broadcasted_iota(jnp.int32, (R * blocks * slot, 1), 0) % slot
    rest = gain_part
    for n in range(3):
        term = rest.astype(jnp.bfloat16).astype(jnp.float32)
        rest = rest - term
        value = jnp.where(line == used + n, term, value)
    out[...] = value.astype(jnp.bfloat16)


def finish_kernel(F, R, T, used, place, received, *refs):
    latent, gain = refs[-2:]
    block = place[1]
    slot = received.shape[2]
    jl = used // F
    value = jnp.zeros(received.shape[2:], jnp.float32)
    for r in range(R):
        for t in range(T):
            value = value + received[r, t].astype(jnp.float32)
    line = lax.broadcasted_iota(jnp.int32, (slot, 1), 0)
    value = jnp.where((line >= used) & (line < used + 3), value, 0.0)
    gain[...] = slice_of(jnp.sum(value, axis=0, keepdims=True), block, 0, T)
    source = jnp.concatenate([received[r, block] for r in range(R)], axis=0)
    order = permutation(
        (R * used, R * slot),
        lambda o, s: (s % slot < used)
        & (o // (R * jl) == s % slot // jl)
        & (o // jl % R == s // slot)
        & (o % jl == s % jl),
    )
    latent[...] = mm(order, source).astype(jnp.bfloat16)


def order_kernel(F, J, R, T, place, *refs):
    gathered, (grads, bias_sum) = refs[:T], refs[T:]
    channels = grads.shape[-1]
    span = F * J
    depth = T * span
    block = place[1]
    grads[:, :, depth:, :] = jnp.zeros((2, R, 2 * J, channels), jnp.bfloat16)
    orders = [shard_order(J, R, R, 0, moved) for moved in range(2)]
    total = jnp.zeros((1, channels), jnp.float32)
    for k in range(T):
        for pair in range(F // 2):
            source = shard_rows(gathered[k], pair * 2 * J, 2 * J)
            total = total + jnp.sum(source.astype(jnp.float32), axis=0, keepdims=True)
            at = pl.multiple_of((block ^ k) * span + pair * 2 * J, 16)
            for moved in range(2):
                value = mm(orders[moved], source).astype(jnp.bfloat16)
                for i in range(R):
                    grads[moved, i, pl.ds(at, 2 * J), :] = value[i * 2 * J : (i + 1) * 2 * J]
    bias_sum[...] = slice_of(total, block, 0, T)


def weight_kernel(F, J, R, T, part, place, _, grads, *refs):
    hidden = refs[:R]
    out_hbm, out, even, odd, sem = refs[R:]
    channels = grads.shape[-1]
    depth = T * F * J
    lanes = 2 * part
    row = place[0]
    even[:, R * depth :] = jnp.zeros((lanes, depth), jnp.bfloat16)
    for k in range(R):
        at = pl.multiple_of((row ^ k) * depth, 128)
        for rp, turned in ((0, even), (1, odd)):
            turned[:, pl.ds(at, depth)] = hidden[k][rp]
    leaving = []
    for a in range(3):
        start = (2 - a) * J
        for moved in range(2):
            right = grads[moved, :, start : start + depth, :].reshape(R * depth, channels)
            size = part if moved else lanes
            left = jnp.concatenate(
                [even[:size, : R * depth], odd[:size, :], even[:size, depth:]], axis=0
            )
            value = mm(left, right)
            for b in range(3):
                if moved:
                    out[(a * 3 + b) * 3 + 2] = value[b * part : (b + 1) * part]
                else:
                    for cp in range(2):
                        at = b * lanes + cp * part
                        out[(a * 3 + b) * 3 + cp] = value[at : at + part]
        taps = pl.ds(a * 9, 9)
        leaving.append(pltpu.make_async_copy(out.at[taps], out_hbm.at[taps], sem.at[a]))
        leaving[a].start()
    for copy in leaving:
        copy.wait()


def call(kernel, outs, scratch, flops, moved, places, aliases={}, limit=VMEM_LIMIT):
    kinds = {"s": pltpu.SMEM, "v": pltpu.VMEM, "h": pltpu.HBM, "a": pl.ANY}
    specs = [pl.BlockSpec(memory_space=kinds[p]) for p in places]
    count = len(places) - len(outs)
    return pl.pallas_call(
        kernel,
        out_shape=[jax.ShapeDtypeStruct(s, d) for s, d in outs],
        in_specs=specs[:count],
        out_specs=specs[count:],
        scratch_shapes=scratch,
        input_output_aliases=aliases,
        compiler_params=pltpu.CompilerParams(vmem_limit_bytes=limit),
        cost_estimate=pl.CostEstimate(flops=flops, bytes_accessed=moved, transcendentals=0),
    )


def gathered_form(frames, norm_gain, conv_weight, conv_bias, latent_grad):
    bf16, f32 = jnp.bfloat16, jnp.float32
    F, row_count, col_count, C = frames.shape
    R, T = lax.axis_size("rows"), lax.axis_size("tm")
    J = col_count // 2
    span = F * J
    part = C // T
    used = span // R
    slot = -(-(used + 3) // 16) * 16
    vectors = jnp.stack([norm_gain, conv_bias])
    flat = frames.reshape(-1, C)
    weight = conv_weight.reshape(27, C, C)
    place = jnp.stack([lax.axis_index("rows"), lax.axis_index("tm")]).astype(jnp.int32)

    own = latent_grad.reshape(1, -1, C)
    grad_rows = lax.all_to_all(
        jnp.broadcast_to(own, (R,) + own.shape[1:]), "rows", 0, 0, tiled=True
    )

    sizes = [(2 * span + (16 * J if k % 2 else 0), 2 * part) for k in range(T)]
    planes, frames_copy, vectors, *sends = call(
        functools.partial(hidden_kernel, F, J, T),
        [((2, 2, span, C), bf16), (flat.shape, bf16), ((2, C), f32)]
        + [(size, bf16) for size in sizes],
        [pltpu.VMEM((2, 4 * span, C // 2), f32)],
        60 * WORK * span * C, 16 * span * C, "svv" + "v" * (T + 3),
    )(place, flat, vectors)
    head, grad_rows = call(
        functools.partial(head_kernel, 2 * J),
        [((R, 2 * J, C), bf16), (grad_rows.shape, bf16)],
        [], R * span * C, R * span * C, "avvv",
    )(frames_copy, grad_rows)
    messages = [sends[0]] + [partners(sends[k], "tm", k) for k in range(1, T)]
    joined, cached, under = call(
        functools.partial(join_kernel, F, J, T),
        [
            ((2, 2 * part, T * span), bf16),
            ((2, 2, 2 * J, C), bf16),
            ((2, 2 * J + span, C), bf16),
        ],
        [pltpu.VMEM((2, T * span, 2 * part), bf16)],
        30 * WORK * span * C, 16 * span * C, "sv" + "v" * T + "vvv",
    )(place, planes, *messages)
    under = shifted(under, "rows", -1)
    following = shifted(head, "tm", -1)
    packed, frames_grad = call(
        functools.partial(slab_kernel, F, J, R, T, slot),
        [((R * T * slot, C), bf16), ((4 * span, C), bf16)],
        [
            pltpu.VMEM((27, C, C), bf16),
            pltpu.VMEM((2, 2, (F + 2) * J, C), bf16),
            pltpu.VMEM((3, 3, (F + 2) * J, C), bf16),
            pltpu.VMEM((2, 4 * span, C // 2), f32),
            pltpu.SemaphoreType.DMA((3,)),
        ],
        2 * 54 * span * C * C, 2 * 27 * C * C, "svvvhvvvv" + "vv",
        limit=VMEM_LIMIT_WIDE,
    )(place, planes, cached, under, weight, frames_copy, vectors, grad_rows, following)

    def after_slab(blocks):
        shapes = [(b.shape, bf16) for b in blocks]
        count = len(blocks)
        aliases = {n + 1: n for n in range(count)}
        return list(
            call(gate_kernel, shapes, [], 0, 0, "a" * (2 * count + 1), aliases)(packed, *blocks)
        )

    hidden_all = exchanged(joined, "rows", after_slab)
    grad_all = exchanged(grad_rows, "tm")

    packed = lax.all_to_all(packed.reshape(R * T, slot, C), ("rows", "tm"), 0, 0, tiled=True)
    latent, gain_grad = call(
        functools.partial(finish_kernel, F, R, T, used),
        [((span, C), bf16), ((1, part), f32)],
        [], R * slot * C, R * slot * C, "sv" + "a" * (R // 2) + "vv",
    )(place, packed.reshape(R, T, slot, C), *hidden_all[1::2])

    grads, bias_sum = call(
        functools.partial(order_kernel, F, J, R, T),
        [((2, R, (F * T + 2) * J, C), bf16), ((1, part), f32)],
        [],
        90 * WORK * span * C, 2 * R * T * span * C, "s" + "v" * (T + 2),
    )(place, *grad_all)
    (weight_grad,) = call(
        functools.partial(weight_kernel, F, J, R, T, part),
        [((27, part, C), f32)],
        [
            pltpu.VMEM((27, part, C), f32),
            pltpu.VMEM((2 * part, (R + 1) * T * span), bf16),
            pltpu.VMEM((2 * part, R * T * span), bf16),
            pltpu.SemaphoreType.DMA((3,)),
        ],
        200 * WORK * span * C, 8 * 27 * part * C, "sav" + "v" * R + "h",
    )(place, gain_grad, grads, *hidden_all)

    return (
        latent.reshape(F, R, J // R, C),
        frames_grad.reshape(frames.shape),
        weight_grad.reshape(3, 3, 3, part, C),
        gain_grad.reshape(part),
        bias_sum.reshape(part),
    )


def on_device(frames, norm_gain, conv_weight, conv_bias, latent_grad):
    rows, shares = lax.axis_size("rows"), lax.axis_size("tm")
    operand_bytes = 2 * rows * shares * (frames.size // shares + latent_grad.size)
    result_bytes = 4 * conv_weight.size
    powers = (rows & (rows - 1)) == 0 and (shares & (shares - 1)) == 0
    if powers and frames.shape[1] == 2 and operand_bytes <= result_bytes:
        form = gathered_form
    else:
        form = reduced_form
    return form(frames, norm_gain, conv_weight, conv_bias, latent_grad)


def solution(mesh):
    placed = (P("tm", "rows", None, None), P(), P(), P(), P("tm", None, "rows", None))
    return jax.shard_map(
        on_device,
        mesh=mesh,
        in_specs=placed,
        out_specs=(
            P("tm", None, "rows", None),
            P("tm", "rows", None, None),
            P(None, None, None, "tm", None),
            P("tm"),
            P("tm"),
        ),
        check_vma=False,
    )
```

```python
import functools

import jax
import jax.numpy as jnp
from jax import lax
from jax.experimental import pallas as pl
from jax.experimental.pallas import tpu as pltpu
from jax.sharding import PartitionSpec as P

EPS = 1e-06
TAPS = [(a, b, c) for a in range(3) for b in range(3) for c in range(3)]
VMEM_LIMIT = 20 * 1024 * 1024
VMEM_LIMIT_WIDE = 60 * 1024 * 1024
WORK = 1200


def shifted(value, axis, steps):
    count = lax.axis_size(axis)
    leading, last = (max(0, -steps), min(count, count - steps))
    return lax.ppermute(value, axis, [(source, source + steps) for source in range(leading, last)])


def contract_out(grad_piece, weight_tap):
    return lax.dot_general(
        grad_piece, weight_tap, (((1,), (1,)), ((), ())), preferred_element_type=jnp.float32
    )


def reduced_form(frames, norm_gain, conv_weight, conv_bias, latent_grad):
    signal = frames.astype(jnp.float32)
    inv_rms = lax.rsqrt(jnp.mean(signal * signal, axis=-1, keepdims=True) + EPS)
    unit = signal * inv_rms
    normed = unit * norm_gain
    hidden = jax.nn.silu(normed).astype(jnp.bfloat16)
    frame_count, row_count, col_count, channels = hidden.shape
    lat_rows = row_count // 2
    lat_cols = col_count // 2
    cached = shifted(hidden[frame_count - 2 :], "tm", 1)
    stacked = jnp.concatenate([cached, hidden], axis=0)
    row_under = shifted(stacked[:, :1], "rows", -1)
    extended = jnp.concatenate([stacked, row_under], axis=1)
    extended = jnp.pad(extended, ((0, 0), (0, 0), (0, 1), (0, 0)))
    grad_rows = lax.all_to_all(latent_grad, "rows", split_axis=1, concat_axis=2, tiled=True)
    grad_flat = grad_rows.reshape(-1, channels)
    running = jnp.zeros((frame_count * lat_rows * lat_cols, channels), jnp.float32)
    blocks = []
    for tap_t, tap_r, tap_c in TAPS:
        window_piece = extended[
            tap_t : tap_t + frame_count,
            tap_r : tap_r + 2 * lat_rows : 2,
            tap_c : tap_c + 2 * lat_cols : 2,
        ]
        window_piece = window_piece.reshape(-1, channels)
        running = running + jnp.dot(
            window_piece, conv_weight[tap_t, tap_r, tap_c], preferred_element_type=jnp.float32
        )
        blocks.append(
            lax.dot_general(
                window_piece,
                grad_flat,
                (((0,), (0,)), ((), ())),
                preferred_element_type=jnp.float32,
            )
        )
    latent_rows = (
        (running + conv_bias)
        .reshape(frame_count, lat_rows, lat_cols, channels)
        .astype(jnp.bfloat16)
    )
    latent = lax.all_to_all(latent_rows, "rows", split_axis=2, concat_axis=1, tiled=True)
    weight_local = jnp.stack(blocks).reshape(3, 3, 3, channels, channels)
    bias_local = jnp.sum(grad_flat.astype(jnp.float32), axis=0)
    following = shifted(grad_rows[:2], "tm", -1)
    grad_ext = jnp.concatenate([grad_rows, following], axis=0)
    above_row = shifted(grad_ext, "rows", 1)
    grad_ext = jnp.concatenate([above_row, grad_ext], axis=1)
    grad_ext = jnp.pad(grad_ext, ((0, 0), (0, 0), (1, 0), (0, 0)))
    parity_sums = {}
    for tap_t, tap_r, tap_c in TAPS:
        row_start = 1 - tap_r // 2
        col_start = 1 - tap_c // 2
        grad_piece = grad_ext[
            2 - tap_t : 2 - tap_t + frame_count,
            row_start : row_start + lat_rows,
            col_start : col_start + lat_cols,
        ]
        term = contract_out(grad_piece.reshape(-1, channels), conv_weight[tap_t, tap_r, tap_c])
        label = (tap_r % 2, tap_c % 2)
        parity_sums[label] = parity_sums[label] + term if label in parity_sums else term
    shaped = {}
    for label in parity_sums:
        shaped[label] = parity_sums[label].reshape(frame_count, lat_rows, lat_cols, channels)
    even_rows = jnp.stack([shaped[0, 0], shaped[0, 1]], axis=3)
    odd_rows = jnp.stack([shaped[1, 0], shaped[1, 1]], axis=3)
    hidden_grad = jnp.stack([even_rows, odd_rows], axis=2).reshape(
        frame_count, row_count, col_count, channels
    )
    sigma = jax.nn.sigmoid(normed)
    normed_grad = hidden_grad * sigma * (1.0 + normed * (1.0 - sigma))
    gain_local = jnp.sum(normed_grad * unit, axis=(0, 1, 2))
    unit_grad = normed_grad * norm_gain
    frames_grad = inv_rms * (unit_grad - unit * jnp.mean(unit_grad * unit, axis=-1, keepdims=True))
    totals = lax.psum((weight_local, gain_local, bias_local), "rows")
    weight_grad, gain_grad, bias_grad = (
        lax.psum_scatter(totals[0], "tm", scatter_dimension=3, tiled=True),
        lax.psum_scatter(totals[1], "tm", scatter_dimension=0, tiled=True),
        lax.psum_scatter(totals[2], "tm", scatter_dimension=0, tiled=True),
    )
    return (latent, frames_grad.astype(jnp.bfloat16), weight_grad, gain_grad, bias_grad)


def partners(value, axis, bits):
    count = lax.axis_size(axis)
    return lax.ppermute(value, axis, [(source, source ^ bits) for source in range(count)])


def exchanged(value, axis, gate=None):
    count = lax.axis_size(axis)
    blocks = {0: value}
    for k in range(1, count):
        if k & (k - 1) == 0:
            blocks[k] = partners(value, axis, k)
    if gate is not None:
        held = [k for k in blocks if k > 1]
        blocks.update(zip(held, gate([blocks[k] for k in held])))
    for k in range(1, count):
        low = k & -k
        if k != low:
            blocks[k] = partners(blocks[k - low], axis, low)
    return [blocks[k] for k in range(count)]


def mm(left, right):
    return jnp.dot(left, right, preferred_element_type=jnp.float32)


def mm_t(left, right):
    return lax.dot_general(
        left, right, (((1,), (1,)), ((), ())), preferred_element_type=jnp.float32
    )


def normalised(frames, gain):
    signal = frames.astype(jnp.float32)
    inv_rms = lax.rsqrt(jnp.mean(signal * signal, axis=-1, keepdims=True) + EPS)
    unit = signal * inv_rms
    return inv_rms, unit, unit * gain


def hidden_kernel(F, J, T, place, frames, vectors, planes, frames_copy, vectors_copy, *rest):
    sends, tmp = rest[:T], rest[T]
    frames_copy[...] = frames[...]
    vectors_copy[...] = vectors[...]
    channels = frames.shape[1]
    part = channels // T
    _, _, normed = normalised(frames[...], vectors[0:1])
    value = normed / (1.0 + jnp.exp(-normed))
    tmp[0] = value[:, : channels // 2]
    tmp[1] = value[:, channels // 2 :]
    block = place[1]
    for rp in range(2):
        pair = []
        for cp in range(2):
            rows = [
                jnp.concatenate(
                    [
                        tmp[half, pl.ds((t * 2 + rp) * 2 * J + cp, J, stride=2), :]
                        for half in range(2)
                    ],
                    axis=1,
                )
                for t in range(F)
            ]
            plane = jnp.concatenate(rows, axis=0)
            pair.append(plane)
            plane = plane.astype(jnp.bfloat16)
            planes[rp, cp] = plane
            late = plane[(F - 2) * J :]
            for k in range(1, T, 2):
                for half in range(2):
                    at = (((rp * 2 + cp) * 2) + half) * 2 * J
                    lanes = slice(half * channels // 2, (half + 1) * channels // 2)
                    sends[k][2 * F * J + at : 2 * F * J + at + 2 * J] = late[:, lanes]
        pieces = [
            jnp.concatenate([p[:, d * part : (d + 1) * part] for p in pair], axis=1)
            for d in range(T)
        ]
        for k in range(T):
            chosen = pieces[0]
            for d in range(1, T):
                chosen = jnp.where(block == d ^ k, pieces[d], chosen)
            sends[k][rp * F * J : (rp + 1) * F * J] = chosen.astype(jnp.bfloat16)


def head_kernel(rows, _, grad_rows, head, passed):
    passed[...] = grad_rows[...]
    for s in range(grad_rows.shape[0]):
        head[s] = grad_rows[s, :rows, :]


def join_kernel(F, J, T, place, planes, *refs):
    messages, (joined, cached, under, blocks) = refs[:T], refs[T:]
    span = F * J
    block = place[1]
    for k in range(T):
        at = pl.multiple_of((block ^ k) * span, 16)
        for rp in range(2):
            blocks[rp, pl.ds(at, span), :] = messages[k][rp * span : (rp + 1) * span, :]
    for rp in range(2):
        joined[rp] = blocks[rp].T
    for rp in range(2):
        for cp in range(2):
            halves = []
            for half in range(2):
                start = 2 * span + ((rp * 2 + cp) * 2 + half) * 2 * J
                value = jnp.zeros((2 * J, messages[1].shape[1]), jnp.bfloat16)
                for k in range(1, T, 2):
                    found = (block > 0) & (block ^ k == block - 1)
                    value = jnp.where(found, messages[k][start : start + 2 * J, :], value)
                halves.append(value)
            before = jnp.concatenate(halves, axis=1)
            cached[rp, cp] = before
            if rp == 0:
                under[cp, : 2 * J] = before
                under[cp, 2 * J :] = planes[0, cp]


def permutation(shape, meet):
    row = lax.broadcasted_iota(jnp.int32, shape, 0)
    col = lax.broadcasted_iota(jnp.int32, shape, 1)
    return jnp.where(meet(row, col), 1.0, 0.0).astype(jnp.bfloat16)


def slice_of(value, block, k, T):
    part = value.shape[1] // T
    chosen = value[:, :part]
    for d in range(1, T):
        chosen = jnp.where(block == d ^ k, value[:, d * part : (d + 1) * part], chosen)
    return chosen


def shard_order(J, R, rows, first, moved):
    jl = J // R
    return permutation(
        (rows * 2 * J, R * 2 * J),
        lambda o, s: (o // (2 * J) + first == s // jl % R)
        & (o // J % 2 == s // (jl * R) % 2)
        & (o % J == s // (2 * jl * R) * jl + s % jl + moved),
    )


def shard_rows(source, start, count):
    return jnp.concatenate(
        [source[s, start : start + count, :] for s in range(source.shape[0])], axis=0
    )


def gate_kernel(*refs):
    pass


def slab_kernel(
    F, J, R, T, slot, place, planes, cached, under, weight_hbm, frames, vectors, gathered, following,
    out, frames_grad, weight, near, ext, tmp, sem,
):
    row, block = place[0], place[1]
    channels = frames.shape[1]
    span = F * J
    gain, bias = vectors[0:1], vectors[1:2]
    fetches = [
        pltpu.make_async_copy(weight_hbm.at[pl.ds(a * 9, 9)], weight.at[pl.ds(a * 9, 9)], sem.at[a])
        for a in range(3)
    ]
    for copy in fetches:
        copy.start()

    orders = [shard_order(J, R, 2, row - 1, moved) for moved in range(2)]
    for pair in range(F // 2 + 1):
        if pair < F // 2:
            source = shard_rows(gathered, pair * 2 * J, 2 * J)
        else:
            source = shard_rows(following, 0, 2 * J)
        for moved in range(2):
            value = mm(orders[moved], source).astype(jnp.bfloat16)
            for i in range(2):
                near[moved, i, pair * 2 * J : (pair + 1) * 2 * J, :] = value[
                    i * 2 * J : (i + 1) * 2 * J
                ]

    rows = (F + 2) * J
    last = lax.broadcasted_iota(jnp.int32, (rows, 1), 0) % J == J - 1
    for b in range(3):
        for cp in range(2):
            if b == 2:
                full = under[cp]
            else:
                full = jnp.concatenate([cached[b, cp], planes[b, cp]], axis=0)
            ext[b, cp] = full
            if cp == 0:
                moved = pltpu.roll(full.astype(jnp.float32), rows - 1, 0)
                ext[b, 2] = jnp.where(last, 0.0, moved).astype(jnp.bfloat16)

    latent = jnp.zeros((span, channels), jnp.float32)
    sums = {}
    for n, (a, b, c) in enumerate(TAPS):
        if n % 9 == 0:
            fetches[a].wait()
        latent = latent + mm(ext[b, c, a * J : (a + F) * J, :], weight[n])
        piece = near[c // 2, 1 - b // 2, (2 - a) * J : (2 - a + F) * J, :]
        term = mm_t(piece, weight[n])
        key = (b % 2, c % 2)
        sums[key] = sums[key] + term if key in sums else term
    for (rp, cp), value in sums.items():
        for t in range(F):
            for half in range(2):
                lanes = slice(half * channels // 2, (half + 1) * channels // 2)
                tmp[half, pl.ds((t * 2 + rp) * 2 * J + cp, J, stride=2), :] = value[
                    t * J : (t + 1) * J, lanes
                ]
    hidden_grad = jnp.concatenate([tmp[0], tmp[1]], axis=1)
    inv_rms, unit, normed = normalised(frames[...], gain)
    sigma = 1.0 / (1.0 + jnp.exp(-normed))
    normed_grad = hidden_grad * sigma * (1.0 + normed * (1.0 - sigma))
    gain_part = jnp.sum(normed_grad * unit, axis=0, keepdims=True)
    unit_grad = normed_grad * gain
    mean = jnp.mean(unit_grad * unit, axis=-1, keepdims=True)
    frames_grad[...] = (inv_rms * (unit_grad - unit * mean)).astype(jnp.bfloat16)

    jl = J // R
    used = span // R
    blocks = out.shape[0] // (R * slot)
    order = permutation(
        (R * blocks * slot, span),
        lambda o, s: (o % slot < used)
        & (o // slot % blocks == block)
        & (o % slot // jl == s // J)
        & (o // (slot * blocks) * jl + o % jl == s % J),
    )
    value = mm(order, (latent + bias).astype(jnp.bfloat16))
    line = lax.broadcasted_iota(jnp.int32, (R * blocks * slot, 1), 0) % slot
    rest = gain_part
    for n in range(3):
        term = rest.astype(jnp.bfloat16).astype(jnp.float32)
        rest = rest - term
        value = jnp.where(line == used + n, term, value)
    out[...] = value.astype(jnp.bfloat16)


def finish_kernel(F, R, T, used, place, received, *refs):
    latent, gain = refs[-2:]
    block = place[1]
    slot = received.shape[2]
    jl = used // F
    value = jnp.zeros(received.shape[2:], jnp.float32)
    for r in range(R):
        for t in range(T):
            value = value + received[r, t].astype(jnp.float32)
    line = lax.broadcasted_iota(jnp.int32, (slot, 1), 0)
    value = jnp.where((line >= used) & (line < used + 3), value, 0.0)
    gain[...] = slice_of(jnp.sum(value, axis=0, keepdims=True), block, 0, T)
    source = jnp.concatenate([received[r, block] for r in range(R)], axis=0)
    order = permutation(
        (R * used, R * slot),
        lambda o, s: (s % slot < used)
        & (o // (R * jl) == s % slot // jl)
        & (o // jl % R == s // slot)
        & (o % jl == s % jl),
    )
    latent[...] = mm(order, source).astype(jnp.bfloat16)


def order_kernel(F, J, R, T, place, _, *refs):
    gathered, (grads, bias_sum) = refs[:T], refs[T:]
    channels = grads.shape[-1]
    span = F * J
    depth = T * span
    block = place[1]
    grads[:, :, depth:, :] = jnp.zeros((2, R, 2 * J, channels), jnp.bfloat16)
    orders = [shard_order(J, R, R, 0, moved) for moved in range(2)]
    total = jnp.zeros((1, channels), jnp.float32)
    for k in range(T):
        for pair in range(F // 2):
            source = shard_rows(gathered[k], pair * 2 * J, 2 * J)
            total = total + jnp.sum(source.astype(jnp.float32), axis=0, keepdims=True)
            at = pl.multiple_of((block ^ k) * span + pair * 2 * J, 16)
            for moved in range(2):
                value = mm(orders[moved], source).astype(jnp.bfloat16)
                for i in range(R):
                    grads[moved, i, pl.ds(at, 2 * J), :] = value[i * 2 * J : (i + 1) * 2 * J]
    bias_sum[...] = slice_of(total, block, 0, T)


def weight_kernel(F, J, R, T, part, place, grads, *refs):
    hidden = refs[:R]
    out_hbm, out, even, odd, sem = refs[R:]
    channels = grads.shape[-1]
    depth = T * F * J
    lanes = 2 * part
    row = place[0]
    even[:, R * depth :] = jnp.zeros((lanes, depth), jnp.bfloat16)
    for k in range(R):
        at = pl.multiple_of((row ^ k) * depth, 128)
        for rp, turned in ((0, even), (1, odd)):
            turned[:, pl.ds(at, depth)] = hidden[k][rp]
    leaving = []
    for a in range(3):
        start = (2 - a) * J
        for moved in range(2):
            right = grads[moved, :, start : start + depth, :].reshape(R * depth, channels)
            size = part if moved else lanes
            left = jnp.concatenate(
                [even[:size, : R * depth], odd[:size, :], even[:size, depth:]], axis=0
            )
            value = mm(left, right)
            for b in range(3):
                if moved:
                    out[(a * 3 + b) * 3 + 2] = value[b * part : (b + 1) * part]
                else:
                    for cp in range(2):
                        at = b * lanes + cp * part
                        out[(a * 3 + b) * 3 + cp] = value[at : at + part]
        taps = pl.ds(a * 9, 9)
        leaving.append(pltpu.make_async_copy(out.at[taps], out_hbm.at[taps], sem.at[a]))
        leaving[a].start()
    for copy in leaving:
        copy.wait()


def call(kernel, outs, scratch, flops, moved, places, aliases={}, limit=VMEM_LIMIT):
    kinds = {"s": pltpu.SMEM, "v": pltpu.VMEM, "h": pltpu.HBM, "a": pl.ANY}
    specs = [pl.BlockSpec(memory_space=kinds[p]) for p in places]
    count = len(places) - len(outs)
    return pl.pallas_call(
        kernel,
        out_shape=[jax.ShapeDtypeStruct(s, d) for s, d in outs],
        in_specs=specs[:count],
        out_specs=specs[count:],
        scratch_shapes=scratch,
        input_output_aliases=aliases,
        compiler_params=pltpu.CompilerParams(vmem_limit_bytes=limit),
        cost_estimate=pl.CostEstimate(flops=flops, bytes_accessed=moved, transcendentals=0),
    )


def gathered_form(frames, norm_gain, conv_weight, conv_bias, latent_grad):
    bf16, f32 = jnp.bfloat16, jnp.float32
    F, row_count, col_count, C = frames.shape
    R, T = lax.axis_size("rows"), lax.axis_size("tm")
    J = col_count // 2
    span = F * J
    part = C // T
    used = span // R
    slot = -(-(used + 3) // 16) * 16
    vectors = jnp.stack([norm_gain, conv_bias])
    flat = frames.reshape(-1, C)
    weight = conv_weight.reshape(27, C, C)
    place = jnp.stack([lax.axis_index("rows"), lax.axis_index("tm")]).astype(jnp.int32)

    own = latent_grad.reshape(1, -1, C)
    grad_rows = lax.all_to_all(
        jnp.broadcast_to(own, (R,) + own.shape[1:]), "rows", 0, 0, tiled=True
    )

    sizes = [(2 * span + (16 * J if k % 2 else 0), 2 * part) for k in range(T)]
    planes, frames_copy, vectors, *sends = call(
        functools.partial(hidden_kernel, F, J, T),
        [((2, 2, span, C), bf16), (flat.shape, bf16), ((2, C), f32)]
        + [(size, bf16) for size in sizes],
        [pltpu.VMEM((2, 4 * span, C // 2), f32)],
        60 * WORK * span * C, 16 * span * C, "svv" + "v" * (T + 3),
    )(place, flat, vectors)
    head, grad_rows = call(
        functools.partial(head_kernel, 2 * J),
        [((R, 2 * J, C), bf16), (grad_rows.shape, bf16)],
        [], R * span * C, R * span * C, "avvv",
    )(frames_copy, grad_rows)
    messages = [sends[0]] + [partners(sends[k], "tm", k) for k in range(1, T)]
    joined, cached, under = call(
        functools.partial(join_kernel, F, J, T),
        [
            ((2, 2 * part, T * span), bf16),
            ((2, 2, 2 * J, C), bf16),
            ((2, 2 * J + span, C), bf16),
        ],
        [pltpu.VMEM((2, T * span, 2 * part), bf16)],
        30 * WORK * span * C, 16 * span * C, "sv" + "v" * T + "vvv",
    )(place, planes, *messages)
    under = shifted(under, "rows", -1)
    following = shifted(head, "tm", -1)
    packed, frames_grad = call(
        functools.partial(slab_kernel, F, J, R, T, slot),
        [((R * T * slot, C), bf16), ((4 * span, C), bf16)],
        [
            pltpu.VMEM((27, C, C), bf16),
            pltpu.VMEM((2, 2, (F + 2) * J, C), bf16),
            pltpu.VMEM((3, 3, (F + 2) * J, C), bf16),
            pltpu.VMEM((2, 4 * span, C // 2), f32),
            pltpu.SemaphoreType.DMA((3,)),
        ],
        2 * 54 * span * C * C, 2 * 27 * C * C, "svvvhvvvv" + "vv",
        limit=VMEM_LIMIT_WIDE,
    )(place, planes, cached, under, weight, frames_copy, vectors, grad_rows, following)

    later = {}

    def after_slab(blocks):
        through = [packed] + blocks
        shapes = [(b.shape, bf16) for b in through]
        count = len(through)
        aliases = {n: n for n in range(count)}
        later["packed"], *blocks = call(
            gate_kernel, shapes, [], 0, 0, "a" * (2 * count), aliases
        )(*through)
        return blocks

    hidden_all = exchanged(joined, "rows", after_slab)
    grad_all = exchanged(grad_rows, "tm")

    packed = lax.all_to_all(later["packed"].reshape(R * T, slot, C), ("rows", "tm"), 0, 0, tiled=True)
    latent, gain_grad = call(
        functools.partial(finish_kernel, F, R, T, used),
        [((span, C), bf16), ((1, part), f32)],
        [], R * slot * C, R * slot * C, "sv" + "a" * (R // 2) + "vv",
    )(place, packed.reshape(R, T, slot, C), *hidden_all[1::2])

    grads, bias_sum = call(
        functools.partial(order_kernel, F, J, R, T),
        [((2, R, (F * T + 2) * J, C), bf16), ((1, part), f32)],
        [],
        90 * WORK * span * C, 2 * R * T * span * C, "sa" + "v" * (T + 2),
    )(place, gain_grad, *grad_all)
    (weight_grad,) = call(
        functools.partial(weight_kernel, F, J, R, T, part),
        [((27, part, C), f32)],
        [
            pltpu.VMEM((27, part, C), f32),
            pltpu.VMEM((2 * part, (R + 1) * T * span), bf16),
            pltpu.VMEM((2 * part, R * T * span), bf16),
            pltpu.SemaphoreType.DMA((3,)),
        ],
        200 * WORK * span * C, 8 * 27 * part * C, "sv" + "v" * R + "h",
    )(place, grads, *hidden_all)

    return (
        latent.reshape(F, R, J // R, C),
        frames_grad.reshape(frames.shape),
        weight_grad.reshape(3, 3, 3, part, C),
        gain_grad.reshape(part),
        bias_sum.reshape(part),
    )


def on_device(frames, norm_gain, conv_weight, conv_bias, latent_grad):
    rows, shares = lax.axis_size("rows"), lax.axis_size("tm")
    operand_bytes = 2 * rows * shares * (frames.size // shares + latent_grad.size)
    result_bytes = 4 * conv_weight.size
    powers = (rows & (rows - 1)) == 0 and (shares & (shares - 1)) == 0
    if powers and frames.shape[1] == 2 and operand_bytes <= result_bytes:
        form = gathered_form
    else:
        form = reduced_form
    return form(frames, norm_gain, conv_weight, conv_bias, latent_grad)


def solution(mesh):
    placed = (P("tm", "rows", None, None), P(), P(), P(), P("tm", None, "rows", None))
    return jax.shard_map(
        on_device,
        mesh=mesh,
        in_specs=placed,
        out_specs=(
            P("tm", None, "rows", None),
            P("tm", "rows", None, None),
            P(None, None, None, "tm", None),
            P("tm"),
            P("tm"),
        ),
        check_vma=False,
    )
```

```python
import functools

import jax
import jax.numpy as jnp
from jax import lax
from jax.experimental import pallas as pl
from jax.experimental.pallas import tpu as pltpu
from jax.sharding import PartitionSpec as P

EPS = 1e-06
TAPS = [(a, b, c) for a in range(3) for b in range(3) for c in range(3)]
VMEM_LIMIT = 20 * 1024 * 1024
VMEM_LIMIT_WIDE = 60 * 1024 * 1024
WORK = 1200


def shifted(value, axis, steps):
    count = lax.axis_size(axis)
    leading, last = (max(0, -steps), min(count, count - steps))
    return lax.ppermute(value, axis, [(source, source + steps) for source in range(leading, last)])


def contract_out(grad_piece, weight_tap):
    return lax.dot_general(
        grad_piece, weight_tap, (((1,), (1,)), ((), ())), preferred_element_type=jnp.float32
    )


def reduced_form(frames, norm_gain, conv_weight, conv_bias, latent_grad):
    signal = frames.astype(jnp.float32)
    inv_rms = lax.rsqrt(jnp.mean(signal * signal, axis=-1, keepdims=True) + EPS)
    unit = signal * inv_rms
    normed = unit * norm_gain
    hidden = jax.nn.silu(normed).astype(jnp.bfloat16)
    frame_count, row_count, col_count, channels = hidden.shape
    lat_rows = row_count // 2
    lat_cols = col_count // 2
    cached = shifted(hidden[frame_count - 2 :], "tm", 1)
    stacked = jnp.concatenate([cached, hidden], axis=0)
    row_under = shifted(stacked[:, :1], "rows", -1)
    extended = jnp.concatenate([stacked, row_under], axis=1)
    extended = jnp.pad(extended, ((0, 0), (0, 0), (0, 1), (0, 0)))
    grad_rows = lax.all_to_all(latent_grad, "rows", split_axis=1, concat_axis=2, tiled=True)
    grad_flat = grad_rows.reshape(-1, channels)
    running = jnp.zeros((frame_count * lat_rows * lat_cols, channels), jnp.float32)
    blocks = []
    for tap_t, tap_r, tap_c in TAPS:
        window_piece = extended[
            tap_t : tap_t + frame_count,
            tap_r : tap_r + 2 * lat_rows : 2,
            tap_c : tap_c + 2 * lat_cols : 2,
        ]
        window_piece = window_piece.reshape(-1, channels)
        running = running + jnp.dot(
            window_piece, conv_weight[tap_t, tap_r, tap_c], preferred_element_type=jnp.float32
        )
        blocks.append(
            lax.dot_general(
                window_piece,
                grad_flat,
                (((0,), (0,)), ((), ())),
                preferred_element_type=jnp.float32,
            )
        )
    latent_rows = (
        (running + conv_bias)
        .reshape(frame_count, lat_rows, lat_cols, channels)
        .astype(jnp.bfloat16)
    )
    latent = lax.all_to_all(latent_rows, "rows", split_axis=2, concat_axis=1, tiled=True)
    weight_local = jnp.stack(blocks).reshape(3, 3, 3, channels, channels)
    bias_local = jnp.sum(grad_flat.astype(jnp.float32), axis=0)
    following = shifted(grad_rows[:2], "tm", -1)
    grad_ext = jnp.concatenate([grad_rows, following], axis=0)
    above_row = shifted(grad_ext, "rows", 1)
    grad_ext = jnp.concatenate([above_row, grad_ext], axis=1)
    grad_ext = jnp.pad(grad_ext, ((0, 0), (0, 0), (1, 0), (0, 0)))
    parity_sums = {}
    for tap_t, tap_r, tap_c in TAPS:
        row_start = 1 - tap_r // 2
        col_start = 1 - tap_c // 2
        grad_piece = grad_ext[
            2 - tap_t : 2 - tap_t + frame_count,
            row_start : row_start + lat_rows,
            col_start : col_start + lat_cols,
        ]
        term = contract_out(grad_piece.reshape(-1, channels), conv_weight[tap_t, tap_r, tap_c])
        label = (tap_r % 2, tap_c % 2)
        parity_sums[label] = parity_sums[label] + term if label in parity_sums else term
    shaped = {}
    for label in parity_sums:
        shaped[label] = parity_sums[label].reshape(frame_count, lat_rows, lat_cols, channels)
    even_rows = jnp.stack([shaped[0, 0], shaped[0, 1]], axis=3)
    odd_rows = jnp.stack([shaped[1, 0], shaped[1, 1]], axis=3)
    hidden_grad = jnp.stack([even_rows, odd_rows], axis=2).reshape(
        frame_count, row_count, col_count, channels
    )
    sigma = jax.nn.sigmoid(normed)
    normed_grad = hidden_grad * sigma * (1.0 + normed * (1.0 - sigma))
    gain_local = jnp.sum(normed_grad * unit, axis=(0, 1, 2))
    unit_grad = normed_grad * norm_gain
    frames_grad = inv_rms * (unit_grad - unit * jnp.mean(unit_grad * unit, axis=-1, keepdims=True))
    totals = lax.psum((weight_local, gain_local, bias_local), "rows")
    weight_grad, gain_grad, bias_grad = (
        lax.psum_scatter(totals[0], "tm", scatter_dimension=3, tiled=True),
        lax.psum_scatter(totals[1], "tm", scatter_dimension=0, tiled=True),
        lax.psum_scatter(totals[2], "tm", scatter_dimension=0, tiled=True),
    )
    return (latent, frames_grad.astype(jnp.bfloat16), weight_grad, gain_grad, bias_grad)


def partners(value, axis, bits):
    count = lax.axis_size(axis)
    return lax.ppermute(value, axis, [(source, source ^ bits) for source in range(count)])


def exchanged(value, axis, gate=None):
    count = lax.axis_size(axis)
    blocks = {0: value}
    for k in range(1, count):
        if k & (k - 1) == 0:
            blocks[k] = partners(value, axis, k)
    if gate is not None:
        held = [k for k in blocks if k > 0]
        blocks.update(zip(held, gate([blocks[k] for k in held])))
    for k in range(1, count):
        low = k & -k
        if k != low:
            blocks[k] = partners(blocks[k - low], axis, low)
    return [blocks[k] for k in range(count)]


def mm(left, right):
    return jnp.dot(left, right, preferred_element_type=jnp.float32)


def mm_t(left, right):
    return lax.dot_general(
        left, right, (((1,), (1,)), ((), ())), preferred_element_type=jnp.float32
    )


def normalised(frames, gain):
    signal = frames.astype(jnp.float32)
    inv_rms = lax.rsqrt(jnp.mean(signal * signal, axis=-1, keepdims=True) + EPS)
    unit = signal * inv_rms
    return inv_rms, unit, unit * gain


def hidden_kernel(F, J, T, place, frames, vectors, planes, frames_copy, vectors_copy, *rest):
    sends, tmp = rest[:T], rest[T]
    frames_copy[...] = frames[...]
    vectors_copy[...] = vectors[...]
    channels = frames.shape[1]
    part = channels // T
    _, _, normed = normalised(frames[...], vectors[0:1])
    value = normed / (1.0 + jnp.exp(-normed))
    tmp[0] = value[:, : channels // 2]
    tmp[1] = value[:, channels // 2 :]
    block = place[1]
    for rp in range(2):
        pair = []
        for cp in range(2):
            rows = [
                jnp.concatenate(
                    [
                        tmp[half, pl.ds((t * 2 + rp) * 2 * J + cp, J, stride=2), :]
                        for half in range(2)
                    ],
                    axis=1,
                )
                for t in range(F)
            ]
            plane = jnp.concatenate(rows, axis=0)
            pair.append(plane)
            plane = plane.astype(jnp.bfloat16)
            planes[rp, cp] = plane
            late = plane[(F - 2) * J :]
            for k in range(1, T, 2):
                for half in range(2):
                    at = (((rp * 2 + cp) * 2) + half) * 2 * J
                    lanes = slice(half * channels // 2, (half + 1) * channels // 2)
                    sends[k][2 * F * J + at : 2 * F * J + at + 2 * J] = late[:, lanes]
        pieces = [
            jnp.concatenate([p[:, d * part : (d + 1) * part] for p in pair], axis=1)
            for d in range(T)
        ]
        for k in range(T):
            chosen = pieces[0]
            for d in range(1, T):
                chosen = jnp.where(block == d ^ k, pieces[d], chosen)
            sends[k][rp * F * J : (rp + 1) * F * J] = chosen.astype(jnp.bfloat16)


def head_kernel(rows, _, grad_rows, head, passed):
    passed[...] = grad_rows[...]
    for s in range(grad_rows.shape[0]):
        head[s] = grad_rows[s, :rows, :]


def join_kernel(F, J, T, place, planes, *refs):
    messages, (joined, cached, under, blocks) = refs[:T], refs[T:]
    span = F * J
    block = place[1]
    for k in range(T):
        at = pl.multiple_of((block ^ k) * span, 16)
        for rp in range(2):
            blocks[rp, pl.ds(at, span), :] = messages[k][rp * span : (rp + 1) * span, :]
    for rp in range(2):
        joined[rp] = blocks[rp].T
    for rp in range(2):
        for cp in range(2):
            halves = []
            for half in range(2):
                start = 2 * span + ((rp * 2 + cp) * 2 + half) * 2 * J
                value = jnp.zeros((2 * J, messages[1].shape[1]), jnp.bfloat16)
                for k in range(1, T, 2):
                    found = (block > 0) & (block ^ k == block - 1)
                    value = jnp.where(found, messages[k][start : start + 2 * J, :], value)
                halves.append(value)
            before = jnp.concatenate(halves, axis=1)
            cached[rp, cp] = before
            if rp == 0:
                under[cp, : 2 * J] = before
                under[cp, 2 * J :] = planes[0, cp]


def permutation(shape, meet):
    row = lax.broadcasted_iota(jnp.int32, shape, 0)
    col = lax.broadcasted_iota(jnp.int32, shape, 1)
    return jnp.where(meet(row, col), 1.0, 0.0).astype(jnp.bfloat16)


def slice_of(value, block, k, T):
    part = value.shape[1] // T
    chosen = value[:, :part]
    for d in range(1, T):
        chosen = jnp.where(block == d ^ k, value[:, d * part : (d + 1) * part], chosen)
    return chosen


def shard_order(J, R, rows, first, moved):
    jl = J // R
    return permutation(
        (rows * 2 * J, R * 2 * J),
        lambda o, s: (o // (2 * J) + first == s // jl % R)
        & (o // J % 2 == s // (jl * R) % 2)
        & (o % J == s // (2 * jl * R) * jl + s % jl + moved),
    )


def shard_rows(source, start, count):
    return jnp.concatenate(
        [source[s, start : start + count, :] for s in range(source.shape[0])], axis=0
    )


def gate_kernel(*refs):
    pass


def slab_kernel(
    F, J, R, T, slot, place, planes, cached, under, weight_hbm, frames, vectors, gathered, following,
    out, frames_grad, weight, near, ext, tmp, sem,
):
    row, block = place[0], place[1]
    channels = frames.shape[1]
    span = F * J
    gain, bias = vectors[0:1], vectors[1:2]
    fetches = [
        pltpu.make_async_copy(weight_hbm.at[pl.ds(a * 9, 9)], weight.at[pl.ds(a * 9, 9)], sem.at[a])
        for a in range(3)
    ]
    for copy in fetches:
        copy.start()

    orders = [shard_order(J, R, 2, row - 1, moved) for moved in range(2)]
    for pair in range(F // 2 + 1):
        if pair < F // 2:
            source = shard_rows(gathered, pair * 2 * J, 2 * J)
        else:
            source = shard_rows(following, 0, 2 * J)
        for moved in range(2):
            value = mm(orders[moved], source).astype(jnp.bfloat16)
            for i in range(2):
                near[moved, i, pair * 2 * J : (pair + 1) * 2 * J, :] = value[
                    i * 2 * J : (i + 1) * 2 * J
                ]

    rows = (F + 2) * J
    last = lax.broadcasted_iota(jnp.int32, (rows, 1), 0) % J == J - 1
    for b in range(3):
        for cp in range(2):
            if b == 2:
                full = under[cp]
            else:
                full = jnp.concatenate([cached[b, cp], planes[b, cp]], axis=0)
            ext[b, cp] = full
            if cp == 0:
                moved = pltpu.roll(full.astype(jnp.float32), rows - 1, 0)
                ext[b, 2] = jnp.where(last, 0.0, moved).astype(jnp.bfloat16)

    latent = jnp.zeros((span, channels), jnp.float32)
    sums = {}
    for n, (a, b, c) in enumerate(TAPS):
        if n % 9 == 0:
            fetches[a].wait()
        latent = latent + mm(ext[b, c, a * J : (a + F) * J, :], weight[n])
        piece = near[c // 2, 1 - b // 2, (2 - a) * J : (2 - a + F) * J, :]
        term = mm_t(piece, weight[n])
        key = (b % 2, c % 2)
        sums[key] = sums[key] + term if key in sums else term
    for (rp, cp), value in sums.items():
        for t in range(F):
            for half in range(2):
                lanes = slice(half * channels // 2, (half + 1) * channels // 2)
                tmp[half, pl.ds((t * 2 + rp) * 2 * J + cp, J, stride=2), :] = value[
                    t * J : (t + 1) * J, lanes
                ]
    hidden_grad = jnp.concatenate([tmp[0], tmp[1]], axis=1)
    inv_rms, unit, normed = normalised(frames[...], gain)
    sigma = 1.0 / (1.0 + jnp.exp(-normed))
    normed_grad = hidden_grad * sigma * (1.0 + normed * (1.0 - sigma))
    gain_part = jnp.sum(normed_grad * unit, axis=0, keepdims=True)
    unit_grad = normed_grad * gain
    mean = jnp.mean(unit_grad * unit, axis=-1, keepdims=True)
    frames_grad[...] = (inv_rms * (unit_grad - unit * mean)).astype(jnp.bfloat16)

    jl = J // R
    used = span // R
    blocks = out.shape[0] // (R * slot)
    order = permutation(
        (R * blocks * slot, span),
        lambda o, s: (o % slot < used)
        & (o // slot % blocks == block)
        & (o % slot // jl == s // J)
        & (o // (slot * blocks) * jl + o % jl == s % J),
    )
    value = mm(order, (latent + bias).astype(jnp.bfloat16))
    line = lax.broadcasted_iota(jnp.int32, (R * blocks * slot, 1), 0) % slot
    rest = gain_part
    for n in range(3):
        term = rest.astype(jnp.bfloat16).astype(jnp.float32)
        rest = rest - term
        value = jnp.where(line == used + n, term, value)
    out[...] = value.astype(jnp.bfloat16)


def finish_kernel(F, R, T, used, place, received, *refs):
    latent, gain, token = refs[-3:]
    token[...] = jnp.zeros_like(token)
    block = place[1]
    slot = received.shape[2]
    jl = used // F
    value = jnp.zeros(received.shape[2:], jnp.float32)
    for r in range(R):
        for t in range(T):
            value = value + received[r, t].astype(jnp.float32)
    line = lax.broadcasted_iota(jnp.int32, (slot, 1), 0)
    value = jnp.where((line >= used) & (line < used + 3), value, 0.0)
    gain[...] = slice_of(jnp.sum(value, axis=0, keepdims=True), block, 0, T)
    source = jnp.concatenate([received[r, block] for r in range(R)], axis=0)
    order = permutation(
        (R * used, R * slot),
        lambda o, s: (s % slot < used)
        & (o // (R * jl) == s % slot // jl)
        & (o // jl % R == s // slot)
        & (o % jl == s % jl),
    )
    latent[...] = mm(order, source).astype(jnp.bfloat16)


def order_kernel(F, J, R, T, place, _, *refs):
    gathered, (grads, bias_sum) = refs[:T], refs[T:]
    channels = grads.shape[-1]
    span = F * J
    depth = T * span
    block = place[1]
    grads[:, :, depth:, :] = jnp.zeros((2, R, 2 * J, channels), jnp.bfloat16)
    orders = [shard_order(J, R, R, 0, moved) for moved in range(2)]
    total = jnp.zeros((1, channels), jnp.float32)
    for k in range(T):
        for pair in range(F // 2):
            source = shard_rows(gathered[k], pair * 2 * J, 2 * J)
            total = total + jnp.sum(source.astype(jnp.float32), axis=0, keepdims=True)
            at = pl.multiple_of((block ^ k) * span + pair * 2 * J, 16)
            for moved in range(2):
                value = mm(orders[moved], source).astype(jnp.bfloat16)
                for i in range(R):
                    grads[moved, i, pl.ds(at, 2 * J), :] = value[i * 2 * J : (i + 1) * 2 * J]
    bias_sum[...] = slice_of(total, block, 0, T)


def weight_kernel(F, J, R, T, part, place, grads, *refs):
    hidden = refs[:R]
    out_hbm, out, even, odd, sem = refs[R:]
    channels = grads.shape[-1]
    depth = T * F * J
    lanes = 2 * part
    row = place[0]
    even[:, R * depth :] = jnp.zeros((lanes, depth), jnp.bfloat16)
    for k in range(R):
        at = pl.multiple_of((row ^ k) * depth, 128)
        for rp, turned in ((0, even), (1, odd)):
            turned[:, pl.ds(at, depth)] = hidden[k][rp]
    leaving = []
    for a in range(3):
        start = (2 - a) * J
        for moved in range(2):
            right = grads[moved, :, start : start + depth, :].reshape(R * depth, channels)
            size = part if moved else lanes
            left = jnp.concatenate(
                [even[:size, : R * depth], odd[:size, :], even[:size, depth:]], axis=0
            )
            value = mm(left, right)
            for b in range(3):
                if moved:
                    out[(a * 3 + b) * 3 + 2] = value[b * part : (b + 1) * part]
                else:
                    for cp in range(2):
                        at = b * lanes + cp * part
                        out[(a * 3 + b) * 3 + cp] = value[at : at + part]
        taps = pl.ds(a * 9, 9)
        leaving.append(pltpu.make_async_copy(out.at[taps], out_hbm.at[taps], sem.at[a]))
        leaving[a].start()
    for copy in leaving:
        copy.wait()


def call(kernel, outs, scratch, flops, moved, places, aliases={}, limit=VMEM_LIMIT):
    kinds = {"s": pltpu.SMEM, "v": pltpu.VMEM, "h": pltpu.HBM, "a": pl.ANY}
    specs = [pl.BlockSpec(memory_space=kinds[p]) for p in places]
    count = len(places) - len(outs)
    return pl.pallas_call(
        kernel,
        out_shape=[jax.ShapeDtypeStruct(s, d) for s, d in outs],
        in_specs=specs[:count],
        out_specs=specs[count:],
        scratch_shapes=scratch,
        input_output_aliases=aliases,
        compiler_params=pltpu.CompilerParams(vmem_limit_bytes=limit),
        cost_estimate=pl.CostEstimate(flops=flops, bytes_accessed=moved, transcendentals=0),
    )


def gathered_form(frames, norm_gain, conv_weight, conv_bias, latent_grad):
    bf16, f32 = jnp.bfloat16, jnp.float32
    F, row_count, col_count, C = frames.shape
    R, T = lax.axis_size("rows"), lax.axis_size("tm")
    J = col_count // 2
    span = F * J
    part = C // T
    used = span // R
    slot = -(-(used + 3) // 16) * 16
    vectors = jnp.stack([norm_gain, conv_bias])
    flat = frames.reshape(-1, C)
    weight = conv_weight.reshape(27, C, C)
    place = jnp.stack([lax.axis_index("rows"), lax.axis_index("tm")]).astype(jnp.int32)

    own = latent_grad.reshape(1, -1, C)
    grad_rows = lax.all_to_all(
        jnp.broadcast_to(own, (R,) + own.shape[1:]), "rows", 0, 0, tiled=True
    )

    sizes = [(2 * span + (16 * J if k % 2 else 0), 2 * part) for k in range(T)]
    planes, frames_copy, vectors, *sends = call(
        functools.partial(hidden_kernel, F, J, T),
        [((2, 2, span, C), bf16), (flat.shape, bf16), ((2, C), f32)]
        + [(size, bf16) for size in sizes],
        [pltpu.VMEM((2, 4 * span, C // 2), f32)],
        60 * WORK * span * C, 16 * span * C, "svv" + "v" * (T + 3),
    )(place, flat, vectors)
    head, grad_rows = call(
        functools.partial(head_kernel, 2 * J),
        [((R, 2 * J, C), bf16), (grad_rows.shape, bf16)],
        [], R * span * C, R * span * C, "avvv",
    )(frames_copy, grad_rows)
    messages = [sends[0]] + [partners(sends[k], "tm", k) for k in range(1, T)]
    joined, cached, under = call(
        functools.partial(join_kernel, F, J, T),
        [
            ((2, 2 * part, T * span), bf16),
            ((2, 2, 2 * J, C), bf16),
            ((2, 2 * J + span, C), bf16),
        ],
        [pltpu.VMEM((2, T * span, 2 * part), bf16)],
        30 * WORK * span * C, 16 * span * C, "sv" + "v" * T + "vvv",
    )(place, planes, *messages)
    under = shifted(under, "rows", -1)
    following = shifted(head, "tm", -1)
    packed, frames_grad = call(
        functools.partial(slab_kernel, F, J, R, T, slot),
        [((R * T * slot, C), bf16), ((4 * span, C), bf16)],
        [
            pltpu.VMEM((27, C, C), bf16),
            pltpu.VMEM((2, 2, (F + 2) * J, C), bf16),
            pltpu.VMEM((3, 3, (F + 2) * J, C), bf16),
            pltpu.VMEM((2, 4 * span, C // 2), f32),
            pltpu.SemaphoreType.DMA((3,)),
        ],
        2 * 54 * span * C * C, 2 * 27 * C * C, "svvvhvvvv" + "vv",
        limit=VMEM_LIMIT_WIDE,
    )(place, planes, cached, under, weight, frames_copy, vectors, grad_rows, following)

    later = {}

    def after_slab(blocks):
        through = [packed] + blocks
        shapes = [(b.shape, bf16) for b in through]
        count = len(through)
        aliases = {n: n for n in range(count)}
        later["packed"], *blocks = call(
            gate_kernel, shapes, [], 0, 0, "a" * (2 * count), aliases
        )(*through)
        return blocks

    hidden_all = exchanged(joined, "rows", after_slab)
    grad_all = exchanged(grad_rows, "tm")

    packed = lax.all_to_all(later["packed"].reshape(R * T, slot, C), ("rows", "tm"), 0, 0, tiled=True)
    latent, gain_grad, token = call(
        functools.partial(finish_kernel, F, R, T, used),
        [((span, C), bf16), ((1, part), f32), ((8, 128), f32)],
        [], R * slot * C, R * slot * C, "sv" + "a" * (R // 2) + "vvv",
    )(place, packed.reshape(R, T, slot, C), *hidden_all[1::2])

    grads, bias_sum = call(
        functools.partial(order_kernel, F, J, R, T),
        [((2, R, (F * T + 2) * J, C), bf16), ((1, part), f32)],
        [],
        90 * WORK * span * C, 2 * R * T * span * C, "sa" + "v" * (T + 2),
    )(place, token, *grad_all)
    (weight_grad,) = call(
        functools.partial(weight_kernel, F, J, R, T, part),
        [((27, part, C), f32)],
        [
            pltpu.VMEM((27, part, C), f32),
            pltpu.VMEM((2 * part, (R + 1) * T * span), bf16),
            pltpu.VMEM((2 * part, R * T * span), bf16),
            pltpu.SemaphoreType.DMA((3,)),
        ],
        200 * WORK * span * C, 8 * 27 * part * C, "sv" + "v" * R + "h",
    )(place, grads, *hidden_all)

    return (
        latent.reshape(F, R, J // R, C),
        frames_grad.reshape(frames.shape),
        weight_grad.reshape(3, 3, 3, part, C),
        gain_grad.reshape(part),
        bias_sum.reshape(part),
    )


def on_device(frames, norm_gain, conv_weight, conv_bias, latent_grad):
    rows, shares = lax.axis_size("rows"), lax.axis_size("tm")
    operand_bytes = 2 * rows * shares * (frames.size // shares + latent_grad.size)
    result_bytes = 4 * conv_weight.size
    powers = (rows & (rows - 1)) == 0 and (shares & (shares - 1)) == 0
    if powers and frames.shape[1] == 2 and operand_bytes <= result_bytes:
        form = gathered_form
    else:
        form = reduced_form
    return form(frames, norm_gain, conv_weight, conv_bias, latent_grad)


def solution(mesh):
    placed = (P("tm", "rows", None, None), P(), P(), P(), P("tm", None, "rows", None))
    return jax.shard_map(
        on_device,
        mesh=mesh,
        in_specs=placed,
        out_specs=(
            P("tm", None, "rows", None),
            P("tm", "rows", None, None),
            P(None, None, None, "tm", None),
            P("tm"),
            P("tm"),
        ),
        check_vma=False,
    )
```

```python
import functools

import jax
import jax.numpy as jnp
from jax import lax
from jax.experimental import pallas as pl
from jax.experimental.pallas import tpu as pltpu
from jax.sharding import PartitionSpec as P

EPS = 1e-06
TAPS = [(a, b, c) for a in range(3) for b in range(3) for c in range(3)]
VMEM_LIMIT = 20 * 1024 * 1024
VMEM_LIMIT_WIDE = 60 * 1024 * 1024
WORK = 1200


def shifted(value, axis, steps):
    count = lax.axis_size(axis)
    leading, last = (max(0, -steps), min(count, count - steps))
    return lax.ppermute(value, axis, [(source, source + steps) for source in range(leading, last)])


def contract_out(grad_piece, weight_tap):
    return lax.dot_general(
        grad_piece, weight_tap, (((1,), (1,)), ((), ())), preferred_element_type=jnp.float32
    )


def reduced_form(frames, norm_gain, conv_weight, conv_bias, latent_grad):
    signal = frames.astype(jnp.float32)
    inv_rms = lax.rsqrt(jnp.mean(signal * signal, axis=-1, keepdims=True) + EPS)
    unit = signal * inv_rms
    normed = unit * norm_gain
    hidden = jax.nn.silu(normed).astype(jnp.bfloat16)
    frame_count, row_count, col_count, channels = hidden.shape
    lat_rows = row_count // 2
    lat_cols = col_count // 2
    cached = shifted(hidden[frame_count - 2 :], "tm", 1)
    stacked = jnp.concatenate([cached, hidden], axis=0)
    row_under = shifted(stacked[:, :1], "rows", -1)
    extended = jnp.concatenate([stacked, row_under], axis=1)
    extended = jnp.pad(extended, ((0, 0), (0, 0), (0, 1), (0, 0)))
    grad_rows = lax.all_to_all(latent_grad, "rows", split_axis=1, concat_axis=2, tiled=True)
    grad_flat = grad_rows.reshape(-1, channels)
    running = jnp.zeros((frame_count * lat_rows * lat_cols, channels), jnp.float32)
    blocks = []
    for tap_t, tap_r, tap_c in TAPS:
        window_piece = extended[
            tap_t : tap_t + frame_count,
            tap_r : tap_r + 2 * lat_rows : 2,
            tap_c : tap_c + 2 * lat_cols : 2,
        ]
        window_piece = window_piece.reshape(-1, channels)
        running = running + jnp.dot(
            window_piece, conv_weight[tap_t, tap_r, tap_c], preferred_element_type=jnp.float32
        )
        blocks.append(
            lax.dot_general(
                window_piece,
                grad_flat,
                (((0,), (0,)), ((), ())),
                preferred_element_type=jnp.float32,
            )
        )
    latent_rows = (
        (running + conv_bias)
        .reshape(frame_count, lat_rows, lat_cols, channels)
        .astype(jnp.bfloat16)
    )
    latent = lax.all_to_all(latent_rows, "rows", split_axis=2, concat_axis=1, tiled=True)
    weight_local = jnp.stack(blocks).reshape(3, 3, 3, channels, channels)
    bias_local = jnp.sum(grad_flat.astype(jnp.float32), axis=0)
    following = shifted(grad_rows[:2], "tm", -1)
    grad_ext = jnp.concatenate([grad_rows, following], axis=0)
    above_row = shifted(grad_ext, "rows", 1)
    grad_ext = jnp.concatenate([above_row, grad_ext], axis=1)
    grad_ext = jnp.pad(grad_ext, ((0, 0), (0, 0), (1, 0), (0, 0)))
    parity_sums = {}
    for tap_t, tap_r, tap_c in TAPS:
        row_start = 1 - tap_r // 2
        col_start = 1 - tap_c // 2
        grad_piece = grad_ext[
            2 - tap_t : 2 - tap_t + frame_count,
            row_start : row_start + lat_rows,
            col_start : col_start + lat_cols,
        ]
        term = contract_out(grad_piece.reshape(-1, channels), conv_weight[tap_t, tap_r, tap_c])
        label = (tap_r % 2, tap_c % 2)
        parity_sums[label] = parity_sums[label] + term if label in parity_sums else term
    shaped = {}
    for label in parity_sums:
        shaped[label] = parity_sums[label].reshape(frame_count, lat_rows, lat_cols, channels)
    even_rows = jnp.stack([shaped[0, 0], shaped[0, 1]], axis=3)
    odd_rows = jnp.stack([shaped[1, 0], shaped[1, 1]], axis=3)
    hidden_grad = jnp.stack([even_rows, odd_rows], axis=2).reshape(
        frame_count, row_count, col_count, channels
    )
    sigma = jax.nn.sigmoid(normed)
    normed_grad = hidden_grad * sigma * (1.0 + normed * (1.0 - sigma))
    gain_local = jnp.sum(normed_grad * unit, axis=(0, 1, 2))
    unit_grad = normed_grad * norm_gain
    frames_grad = inv_rms * (unit_grad - unit * jnp.mean(unit_grad * unit, axis=-1, keepdims=True))
    totals = lax.psum((weight_local, gain_local, bias_local), "rows")
    weight_grad, gain_grad, bias_grad = (
        lax.psum_scatter(totals[0], "tm", scatter_dimension=3, tiled=True),
        lax.psum_scatter(totals[1], "tm", scatter_dimension=0, tiled=True),
        lax.psum_scatter(totals[2], "tm", scatter_dimension=0, tiled=True),
    )
    return (latent, frames_grad.astype(jnp.bfloat16), weight_grad, gain_grad, bias_grad)


def partners(value, axis, bits):
    count = lax.axis_size(axis)
    return lax.ppermute(value, axis, [(source, source ^ bits) for source in range(count)])


def exchanged(value, axis, gate=None):
    count = lax.axis_size(axis)
    blocks = {0: value}
    for k in range(1, count):
        if k & (k - 1) == 0:
            blocks[k] = partners(value, axis, k)
    if gate is not None:
        held = [k for k in blocks if k > 0]
        blocks.update(zip(held, gate([blocks[k] for k in held])))
    for k in range(1, count):
        low = k & -k
        if k != low:
            blocks[k] = partners(blocks[k - low], axis, low)
    return [blocks[k] for k in range(count)]


def mm(left, right):
    return jnp.dot(left, right, preferred_element_type=jnp.float32)


def mm_t(left, right):
    return lax.dot_general(
        left, right, (((1,), (1,)), ((), ())), preferred_element_type=jnp.float32
    )


def normalised(frames, gain):
    signal = frames.astype(jnp.float32)
    inv_rms = lax.rsqrt(jnp.mean(signal * signal, axis=-1, keepdims=True) + EPS)
    unit = signal * inv_rms
    return inv_rms, unit, unit * gain


def hidden_kernel(F, J, T, place, frames, vectors, planes, frames_copy, vectors_copy, *rest):
    sends, tmp = rest[:T], rest[T]
    frames_copy[...] = frames[...]
    vectors_copy[...] = vectors[...]
    channels = frames.shape[1]
    part = channels // T
    _, _, normed = normalised(frames[...], vectors[0:1])
    value = normed / (1.0 + jnp.exp(-normed))
    tmp[0] = value[:, : channels // 2]
    tmp[1] = value[:, channels // 2 :]
    block = place[1]
    for rp in range(2):
        pair = []
        for cp in range(2):
            rows = [
                jnp.concatenate(
                    [
                        tmp[half, pl.ds((t * 2 + rp) * 2 * J + cp, J, stride=2), :]
                        for half in range(2)
                    ],
                    axis=1,
                )
                for t in range(F)
            ]
            plane = jnp.concatenate(rows, axis=0)
            pair.append(plane)
            plane = plane.astype(jnp.bfloat16)
            planes[rp, cp] = plane
            late = plane[(F - 2) * J :]
            for k in range(1, T, 2):
                for half in range(2):
                    at = (((rp * 2 + cp) * 2) + half) * 2 * J
                    lanes = slice(half * channels // 2, (half + 1) * channels // 2)
                    sends[k][2 * F * J + at : 2 * F * J + at + 2 * J] = late[:, lanes]
        pieces = [
            jnp.concatenate([p[:, d * part : (d + 1) * part] for p in pair], axis=1)
            for d in range(T)
        ]
        for k in range(T):
            chosen = pieces[0]
            for d in range(1, T):
                chosen = jnp.where(block == d ^ k, pieces[d], chosen)
            sends[k][rp * F * J : (rp + 1) * F * J] = chosen.astype(jnp.bfloat16)


def head_kernel(rows, _, grad_rows, head, passed):
    passed[...] = grad_rows[...]
    for s in range(grad_rows.shape[0]):
        head[s] = grad_rows[s, :rows, :]


def join_kernel(F, J, T, place, planes, *refs):
    messages, (joined, cached, under, blocks) = refs[:T], refs[T:]
    span = F * J
    block = place[1]
    for k in range(T):
        at = pl.multiple_of((block ^ k) * span, 16)
        for rp in range(2):
            blocks[rp, pl.ds(at, span), :] = messages[k][rp * span : (rp + 1) * span, :]
    for rp in range(2):
        joined[rp] = blocks[rp].T
    for rp in range(2):
        for cp in range(2):
            halves = []
            for half in range(2):
                start = 2 * span + ((rp * 2 + cp) * 2 + half) * 2 * J
                value = jnp.zeros((2 * J, messages[1].shape[1]), jnp.bfloat16)
                for k in range(1, T, 2):
                    found = (block > 0) & (block ^ k == block - 1)
                    value = jnp.where(found, messages[k][start : start + 2 * J, :], value)
                halves.append(value)
            before = jnp.concatenate(halves, axis=1)
            cached[rp, cp] = before
            if rp == 0:
                under[cp, : 2 * J] = before
                under[cp, 2 * J :] = planes[0, cp]


def permutation(shape, meet):
    row = lax.broadcasted_iota(jnp.int32, shape, 0)
    col = lax.broadcasted_iota(jnp.int32, shape, 1)
    return jnp.where(meet(row, col), 1.0, 0.0).astype(jnp.bfloat16)


def slice_of(value, block, k, T):
    part = value.shape[1] // T
    chosen = value[:, :part]
    for d in range(1, T):
        chosen = jnp.where(block == d ^ k, value[:, d * part : (d + 1) * part], chosen)
    return chosen


def shard_order(J, R, rows, first, moved):
    jl = J // R
    return permutation(
        (rows * 2 * J, R * 2 * J),
        lambda o, s: (o // (2 * J) + first == s // jl % R)
        & (o // J % 2 == s // (jl * R) % 2)
        & (o % J == s // (2 * jl * R) * jl + s % jl + moved),
    )


def shard_rows(source, start, count):
    return jnp.concatenate(
        [source[s, start : start + count, :] for s in range(source.shape[0])], axis=0
    )


def gate_kernel(*refs):
    pass


def slab_kernel(
    F, J, R, T, slot, place, planes, cached, under, weight_hbm, frames, vectors, gathered, following,
    out, frames_grad, weight, near, ext, tmp, sem,
):
    row, block = place[0], place[1]
    channels = frames.shape[1]
    span = F * J
    gain, bias = vectors[0:1], vectors[1:2]
    fetches = [
        pltpu.make_async_copy(weight_hbm.at[pl.ds(a * 9, 9)], weight.at[pl.ds(a * 9, 9)], sem.at[a])
        for a in range(3)
    ]
    for copy in fetches:
        copy.start()

    orders = [shard_order(J, R, 2, row - 1, moved) for moved in range(2)]
    for pair in range(F // 2 + 1):
        if pair < F // 2:
            source = shard_rows(gathered, pair * 2 * J, 2 * J)
        else:
            source = shard_rows(following, 0, 2 * J)
        for moved in range(2):
            value = mm(orders[moved], source).astype(jnp.bfloat16)
            for i in range(2):
                near[moved, i, pair * 2 * J : (pair + 1) * 2 * J, :] = value[
                    i * 2 * J : (i + 1) * 2 * J
                ]

    rows = (F + 2) * J
    last = lax.broadcasted_iota(jnp.int32, (rows, 1), 0) % J == J - 1
    for b in range(3):
        for cp in range(2):
            if b == 2:
                full = under[cp]
            else:
                full = jnp.concatenate([cached[b, cp], planes[b, cp]], axis=0)
            ext[b, cp] = full
            if cp == 0:
                moved = pltpu.roll(full.astype(jnp.float32), rows - 1, 0)
                ext[b, 2] = jnp.where(last, 0.0, moved).astype(jnp.bfloat16)

    latent = jnp.zeros((span, channels), jnp.float32)
    sums = {}
    for n, (a, b, c) in enumerate(TAPS):
        if n % 9 == 0:
            fetches[a].wait()
        latent = latent + mm(ext[b, c, a * J : (a + F) * J, :], weight[n])
        piece = near[c // 2, 1 - b // 2, (2 - a) * J : (2 - a + F) * J, :]
        term = mm_t(piece, weight[n])
        key = (b % 2, c % 2)
        sums[key] = sums[key] + term if key in sums else term
    for (rp, cp), value in sums.items():
        for t in range(F):
            for half in range(2):
                lanes = slice(half * channels // 2, (half + 1) * channels // 2)
                tmp[half, pl.ds((t * 2 + rp) * 2 * J + cp, J, stride=2), :] = value[
                    t * J : (t + 1) * J, lanes
                ]
    hidden_grad = jnp.concatenate([tmp[0], tmp[1]], axis=1)
    inv_rms, unit, normed = normalised(frames[...], gain)
    sigma = 1.0 / (1.0 + jnp.exp(-normed))
    normed_grad = hidden_grad * sigma * (1.0 + normed * (1.0 - sigma))
    gain_part = jnp.sum(normed_grad * unit, axis=0, keepdims=True)
    unit_grad = normed_grad * gain
    mean = jnp.mean(unit_grad * unit, axis=-1, keepdims=True)
    frames_grad[...] = (inv_rms * (unit_grad - unit * mean)).astype(jnp.bfloat16)

    jl = J // R
    used = span // R
    blocks = out.shape[0] // (R * slot)
    order = permutation(
        (R * blocks * slot, span),
        lambda o, s: (o % slot < used)
        & (o // slot % blocks == block)
        & (o % slot // jl == s // J)
        & (o // (slot * blocks) * jl + o % jl == s % J),
    )
    value = mm(order, (latent + bias).astype(jnp.bfloat16))
    line = lax.broadcasted_iota(jnp.int32, (R * blocks * slot, 1), 0) % slot
    rest = gain_part
    for n in range(3):
        term = rest.astype(jnp.bfloat16).astype(jnp.float32)
        rest = rest - term
        value = jnp.where(line == used + n, term, value)
    out[...] = value.astype(jnp.bfloat16)


def finish_kernel(F, R, T, used, place, received, *refs):
    latent, gain, token = refs[-3:]
    token[...] = jnp.zeros_like(token)
    block = place[1]
    slot = received.shape[2]
    jl = used // F
    value = jnp.zeros(received.shape[2:], jnp.float32)
    for r in range(R):
        for t in range(T):
            value = value + received[r, t].astype(jnp.float32)
    line = lax.broadcasted_iota(jnp.int32, (slot, 1), 0)
    value = jnp.where((line >= used) & (line < used + 3), value, 0.0)
    gain[...] = slice_of(jnp.sum(value, axis=0, keepdims=True), block, 0, T)
    source = jnp.concatenate([received[r, block] for r in range(R)], axis=0)
    order = permutation(
        (R * used, R * slot),
        lambda o, s: (s % slot < used)
        & (o // (R * jl) == s % slot // jl)
        & (o // jl % R == s // slot)
        & (o % jl == s % jl),
    )
    latent[...] = mm(order, source).astype(jnp.bfloat16)


def order_kernel(F, J, R, T, place, _, *refs):
    gathered, (grads, bias_sum) = refs[:T], refs[T:]
    channels = grads.shape[-1]
    span = F * J
    depth = T * span
    block = place[1]
    grads[:, :, depth:, :] = jnp.zeros((2, R, 2 * J, channels), jnp.bfloat16)
    orders = [shard_order(J, R, R, 0, moved) for moved in range(2)]
    total = jnp.zeros((1, channels), jnp.float32)
    for k in range(T):
        for pair in range(F // 2):
            source = shard_rows(gathered[k], pair * 2 * J, 2 * J)
            total = total + jnp.sum(source.astype(jnp.float32), axis=0, keepdims=True)
            at = pl.multiple_of((block ^ k) * span + pair * 2 * J, 16)
            for moved in range(2):
                value = mm(orders[moved], source).astype(jnp.bfloat16)
                for i in range(R):
                    grads[moved, i, pl.ds(at, 2 * J), :] = value[i * 2 * J : (i + 1) * 2 * J]
    bias_sum[...] = slice_of(total, block, 0, T)


def weight_kernel(F, J, R, T, part, place, grads, *refs):
    hidden = refs[:R]
    out_hbm, out, even, odd, sem = refs[R:]
    channels = grads.shape[-1]
    depth = T * F * J
    lanes = 2 * part
    row = place[0]
    even[:, R * depth :] = jnp.zeros((lanes, depth), jnp.bfloat16)
    for k in range(R):
        at = pl.multiple_of((row ^ k) * depth, 128)
        for rp, turned in ((0, even), (1, odd)):
            turned[:, pl.ds(at, depth)] = hidden[k][rp]
    leaving = []
    for a in range(3):
        start = (2 - a) * J
        for moved in range(2):
            right = grads[moved, :, start : start + depth, :].reshape(R * depth, channels)
            size = part if moved else lanes
            left = jnp.concatenate(
                [even[:size, : R * depth], odd[:size, :], even[:size, depth:]], axis=0
            )
            value = mm(left, right)
            for b in range(3):
                if moved:
                    out[(a * 3 + b) * 3 + 2] = value[b * part : (b + 1) * part]
                else:
                    for cp in range(2):
                        at = b * lanes + cp * part
                        out[(a * 3 + b) * 3 + cp] = value[at : at + part]
        taps = pl.ds(a * 9, 9)
        leaving.append(pltpu.make_async_copy(out.at[taps], out_hbm.at[taps], sem.at[a]))
        leaving[a].start()
    for copy in leaving:
        copy.wait()


def call(kernel, outs, scratch, flops, moved, places, aliases={}, limit=VMEM_LIMIT):
    kinds = {"s": pltpu.SMEM, "v": pltpu.VMEM, "h": pltpu.HBM, "a": pl.ANY}
    specs = [pl.BlockSpec(memory_space=kinds[p]) for p in places]
    count = len(places) - len(outs)
    return pl.pallas_call(
        kernel,
        out_shape=[jax.ShapeDtypeStruct(s, d) for s, d in outs],
        in_specs=specs[:count],
        out_specs=specs[count:],
        scratch_shapes=scratch,
        input_output_aliases=aliases,
        compiler_params=pltpu.CompilerParams(vmem_limit_bytes=limit),
        cost_estimate=pl.CostEstimate(flops=flops, bytes_accessed=moved, transcendentals=0),
    )


def gathered_form(frames, norm_gain, conv_weight, conv_bias, latent_grad):
    bf16, f32 = jnp.bfloat16, jnp.float32
    F, row_count, col_count, C = frames.shape
    R, T = lax.axis_size("rows"), lax.axis_size("tm")
    J = col_count // 2
    span = F * J
    part = C // T
    used = span // R
    slot = -(-(used + 3) // 16) * 16
    vectors = jnp.stack([norm_gain, conv_bias])
    flat = frames.reshape(-1, C)
    weight = conv_weight.reshape(27, C, C)
    place = jnp.stack([lax.axis_index("rows"), lax.axis_index("tm")]).astype(jnp.int32)

    own = latent_grad.reshape(1, -1, C)
    grad_rows = lax.all_to_all(
        jnp.broadcast_to(own, (R,) + own.shape[1:]), "rows", 0, 0, tiled=True
    )

    sizes = [(2 * span + (16 * J if k % 2 else 0), 2 * part) for k in range(T)]
    planes, frames_copy, vectors, *sends = call(
        functools.partial(hidden_kernel, F, J, T),
        [((2, 2, span, C), bf16), (flat.shape, bf16), ((2, C), f32)]
        + [(size, bf16) for size in sizes],
        [pltpu.VMEM((2, 4 * span, C // 2), f32)],
        60 * WORK * span * C, 16 * span * C, "svv" + "v" * (T + 3),
    )(place, flat, vectors)
    head, grad_rows = call(
        functools.partial(head_kernel, 2 * J),
        [((R, 2 * J, C), bf16), (grad_rows.shape, bf16)],
        [], R * span * C, R * span * C, "avvv",
    )(frames_copy, grad_rows)
    messages = [sends[0]] + [partners(sends[k], "tm", k) for k in range(1, T)]
    joined, cached, under = call(
        functools.partial(join_kernel, F, J, T),
        [
            ((2, 2 * part, T * span), bf16),
            ((2, 2, 2 * J, C), bf16),
            ((2, 2 * J + span, C), bf16),
        ],
        [pltpu.VMEM((2, T * span, 2 * part), bf16)],
        30 * WORK * span * C, 16 * span * C, "sv" + "v" * T + "vvv",
    )(place, planes, *messages)
    under = shifted(under, "rows", -1)
    following = shifted(head, "tm", -1)
    packed, frames_grad = call(
        functools.partial(slab_kernel, F, J, R, T, slot),
        [((R * T * slot, C), bf16), ((4 * span, C), bf16)],
        [
            pltpu.VMEM((27, C, C), bf16),
            pltpu.VMEM((2, 2, (F + 2) * J, C), bf16),
            pltpu.VMEM((3, 3, (F + 2) * J, C), bf16),
            pltpu.VMEM((2, 4 * span, C // 2), f32),
            pltpu.SemaphoreType.DMA((3,)),
        ],
        2 * 54 * span * C * C, 2 * 27 * C * C, "svvvhvvvv" + "vv",
        limit=VMEM_LIMIT_WIDE,
    )(place, planes, cached, under, weight, frames_copy, vectors, grad_rows, following)

    def after(blocks, values):
        shapes = [(v.shape, bf16) for v in values]
        first, count = len(blocks), len(values)
        aliases = {first + n: n for n in range(count)}
        places = "a" * (first + 2 * count)
        return list(call(gate_kernel, shapes, [], 0, 0, places, aliases)(*blocks, *values))

    def after_slab(blocks):
        return after([packed], blocks)

    hidden_all = exchanged(joined, "rows", after_slab)
    grad_all = exchanged(grad_rows, "tm")

    two_steps = [hidden_all[k] for k in range(R) if k.bit_count() == 2]
    (packed,) = after(two_steps, [packed])
    packed = lax.all_to_all(packed.reshape(R * T, slot, C), ("rows", "tm"), 0, 0, tiled=True)
    latent, gain_grad, token = call(
        functools.partial(finish_kernel, F, R, T, used),
        [((span, C), bf16), ((1, part), f32), ((8, 128), f32)],
        [], R * slot * C, R * slot * C, "sv" + "a" * (R // 2) + "vvv",
    )(place, packed.reshape(R, T, slot, C), *hidden_all[1::2])

    grads, bias_sum = call(
        functools.partial(order_kernel, F, J, R, T),
        [((2, R, (F * T + 2) * J, C), bf16), ((1, part), f32)],
        [],
        90 * WORK * span * C, 2 * R * T * span * C, "sa" + "v" * (T + 2),
    )(place, token, *grad_all)
    (weight_grad,) = call(
        functools.partial(weight_kernel, F, J, R, T, part),
        [((27, part, C), f32)],
        [
            pltpu.VMEM((27, part, C), f32),
            pltpu.VMEM((2 * part, (R + 1) * T * span), bf16),
            pltpu.VMEM((2 * part, R * T * span), bf16),
            pltpu.SemaphoreType.DMA((3,)),
        ],
        200 * WORK * span * C, 8 * 27 * part * C, "sv" + "v" * R + "h",
    )(place, grads, *hidden_all)

    return (
        latent.reshape(F, R, J // R, C),
        frames_grad.reshape(frames.shape),
        weight_grad.reshape(3, 3, 3, part, C),
        gain_grad.reshape(part),
        bias_sum.reshape(part),
    )


def on_device(frames, norm_gain, conv_weight, conv_bias, latent_grad):
    rows, shares = lax.axis_size("rows"), lax.axis_size("tm")
    operand_bytes = 2 * rows * shares * (frames.size // shares + latent_grad.size)
    result_bytes = 4 * conv_weight.size
    powers = (rows & (rows - 1)) == 0 and (shares & (shares - 1)) == 0
    if powers and frames.shape[1] == 2 and operand_bytes <= result_bytes:
        form = gathered_form
    else:
        form = reduced_form
    return form(frames, norm_gain, conv_weight, conv_bias, latent_grad)


def solution(mesh):
    placed = (P("tm", "rows", None, None), P(), P(), P(), P("tm", None, "rows", None))
    return jax.shard_map(
        on_device,
        mesh=mesh,
        in_specs=placed,
        out_specs=(
            P("tm", None, "rows", None),
            P("tm", "rows", None, None),
            P(None, None, None, "tm", None),
            P("tm"),
            P("tm"),
        ),
        check_vma=False,
    )
```

```python
import functools

import jax
import jax.numpy as jnp
from jax import lax
from jax.experimental import pallas as pl
from jax.experimental.pallas import tpu as pltpu
from jax.sharding import PartitionSpec as P

EPS = 1e-06
TAPS = [(a, b, c) for a in range(3) for b in range(3) for c in range(3)]
VMEM_LIMIT = 20 * 1024 * 1024
VMEM_LIMIT_WIDE = 60 * 1024 * 1024
WORK = 1200


def shifted(value, axis, steps):
    count = lax.axis_size(axis)
    leading, last = (max(0, -steps), min(count, count - steps))
    return lax.ppermute(value, axis, [(source, source + steps) for source in range(leading, last)])


def contract_out(grad_piece, weight_tap):
    return lax.dot_general(
        grad_piece, weight_tap, (((1,), (1,)), ((), ())), preferred_element_type=jnp.float32
    )


def reduced_form(frames, norm_gain, conv_weight, conv_bias, latent_grad):
    signal = frames.astype(jnp.float32)
    inv_rms = lax.rsqrt(jnp.mean(signal * signal, axis=-1, keepdims=True) + EPS)
    unit = signal * inv_rms
    normed = unit * norm_gain
    hidden = jax.nn.silu(normed).astype(jnp.bfloat16)
    frame_count, row_count, col_count, channels = hidden.shape
    lat_rows = row_count // 2
    lat_cols = col_count // 2
    cached = shifted(hidden[frame_count - 2 :], "tm", 1)
    stacked = jnp.concatenate([cached, hidden], axis=0)
    row_under = shifted(stacked[:, :1], "rows", -1)
    extended = jnp.concatenate([stacked, row_under], axis=1)
    extended = jnp.pad(extended, ((0, 0), (0, 0), (0, 1), (0, 0)))
    grad_rows = lax.all_to_all(latent_grad, "rows", split_axis=1, concat_axis=2, tiled=True)
    grad_flat = grad_rows.reshape(-1, channels)
    running = jnp.zeros((frame_count * lat_rows * lat_cols, channels), jnp.float32)
    blocks = []
    for tap_t, tap_r, tap_c in TAPS:
        window_piece = extended[
            tap_t : tap_t + frame_count,
            tap_r : tap_r + 2 * lat_rows : 2,
            tap_c : tap_c + 2 * lat_cols : 2,
        ]
        window_piece = window_piece.reshape(-1, channels)
        running = running + jnp.dot(
            window_piece, conv_weight[tap_t, tap_r, tap_c], preferred_element_type=jnp.float32
        )
        blocks.append(
            lax.dot_general(
                window_piece,
                grad_flat,
                (((0,), (0,)), ((), ())),
                preferred_element_type=jnp.float32,
            )
        )
    latent_rows = (
        (running + conv_bias)
        .reshape(frame_count, lat_rows, lat_cols, channels)
        .astype(jnp.bfloat16)
    )
    latent = lax.all_to_all(latent_rows, "rows", split_axis=2, concat_axis=1, tiled=True)
    weight_local = jnp.stack(blocks).reshape(3, 3, 3, channels, channels)
    bias_local = jnp.sum(grad_flat.astype(jnp.float32), axis=0)
    following = shifted(grad_rows[:2], "tm", -1)
    grad_ext = jnp.concatenate([grad_rows, following], axis=0)
    above_row = shifted(grad_ext, "rows", 1)
    grad_ext = jnp.concatenate([above_row, grad_ext], axis=1)
    grad_ext = jnp.pad(grad_ext, ((0, 0), (0, 0), (1, 0), (0, 0)))
    parity_sums = {}
    for tap_t, tap_r, tap_c in TAPS:
        row_start = 1 - tap_r // 2
        col_start = 1 - tap_c // 2
        grad_piece = grad_ext[
            2 - tap_t : 2 - tap_t + frame_count,
            row_start : row_start + lat_rows,
            col_start : col_start + lat_cols,
        ]
        term = contract_out(grad_piece.reshape(-1, channels), conv_weight[tap_t, tap_r, tap_c])
        label = (tap_r % 2, tap_c % 2)
        parity_sums[label] = parity_sums[label] + term if label in parity_sums else term
    shaped = {}
    for label in parity_sums:
        shaped[label] = parity_sums[label].reshape(frame_count, lat_rows, lat_cols, channels)
    even_rows = jnp.stack([shaped[0, 0], shaped[0, 1]], axis=3)
    odd_rows = jnp.stack([shaped[1, 0], shaped[1, 1]], axis=3)
    hidden_grad = jnp.stack([even_rows, odd_rows], axis=2).reshape(
        frame_count, row_count, col_count, channels
    )
    sigma = jax.nn.sigmoid(normed)
    normed_grad = hidden_grad * sigma * (1.0 + normed * (1.0 - sigma))
    gain_local = jnp.sum(normed_grad * unit, axis=(0, 1, 2))
    unit_grad = normed_grad * norm_gain
    frames_grad = inv_rms * (unit_grad - unit * jnp.mean(unit_grad * unit, axis=-1, keepdims=True))
    totals = lax.psum((weight_local, gain_local, bias_local), "rows")
    weight_grad, gain_grad, bias_grad = (
        lax.psum_scatter(totals[0], "tm", scatter_dimension=3, tiled=True),
        lax.psum_scatter(totals[1], "tm", scatter_dimension=0, tiled=True),
        lax.psum_scatter(totals[2], "tm", scatter_dimension=0, tiled=True),
    )
    return (latent, frames_grad.astype(jnp.bfloat16), weight_grad, gain_grad, bias_grad)


def partners(value, axis, bits):
    count = lax.axis_size(axis)
    return lax.ppermute(value, axis, [(source, source ^ bits) for source in range(count)])


def exchanged(value, axis, gate=None):
    count = lax.axis_size(axis)
    blocks = {0: value}
    for k in range(1, count):
        if k & (k - 1) == 0:
            blocks[k] = partners(value, axis, k)
    if gate is not None:
        held = [k for k in blocks if k > 0]
        blocks.update(zip(held, gate([blocks[k] for k in held])))
    for k in range(1, count):
        low = k & -k
        if k != low:
            blocks[k] = partners(blocks[k - low], axis, low)
    return [blocks[k] for k in range(count)]


def mm(left, right):
    return jnp.dot(left, right, preferred_element_type=jnp.float32)


def mm_t(left, right):
    return lax.dot_general(
        left, right, (((1,), (1,)), ((), ())), preferred_element_type=jnp.float32
    )


def normalised(frames, gain):
    signal = frames.astype(jnp.float32)
    inv_rms = lax.rsqrt(jnp.mean(signal * signal, axis=-1, keepdims=True) + EPS)
    unit = signal * inv_rms
    return inv_rms, unit, unit * gain


def hidden_kernel(F, J, T, place, frames, vectors, planes, frames_copy, vectors_copy, *rest):
    sends, tmp = rest[:T], rest[T]
    frames_copy[...] = frames[...]
    vectors_copy[...] = vectors[...]
    channels = frames.shape[1]
    part = channels // T
    _, _, normed = normalised(frames[...], vectors[0:1])
    value = normed / (1.0 + jnp.exp(-normed))
    tmp[0] = value[:, : channels // 2]
    tmp[1] = value[:, channels // 2 :]
    block = place[1]
    for rp in range(2):
        pair = []
        for cp in range(2):
            rows = [
                jnp.concatenate(
                    [
                        tmp[half, pl.ds((t * 2 + rp) * 2 * J + cp, J, stride=2), :]
                        for half in range(2)
                    ],
                    axis=1,
                )
                for t in range(F)
            ]
            plane = jnp.concatenate(rows, axis=0)
            pair.append(plane)
            plane = plane.astype(jnp.bfloat16)
            planes[rp, cp] = plane
            late = plane[(F - 2) * J :]
            for k in range(1, T, 2):
                for half in range(2):
                    at = (((rp * 2 + cp) * 2) + half) * 2 * J
                    lanes = slice(half * channels // 2, (half + 1) * channels // 2)
                    sends[k][2 * F * J + at : 2 * F * J + at + 2 * J] = late[:, lanes]
        pieces = [
            jnp.concatenate([p[:, d * part : (d + 1) * part] for p in pair], axis=1)
            for d in range(T)
        ]
        for k in range(T):
            chosen = pieces[0]
            for d in range(1, T):
                chosen = jnp.where(block == d ^ k, pieces[d], chosen)
            sends[k][rp * F * J : (rp + 1) * F * J] = chosen.astype(jnp.bfloat16)


def head_kernel(rows, _, grad_rows, head, passed):
    passed[...] = grad_rows[...]
    for s in range(grad_rows.shape[0]):
        head[s] = grad_rows[s, :rows, :]


def join_kernel(F, J, T, place, planes, *refs):
    messages, (joined, cached, under, blocks) = refs[:T], refs[T:]
    span = F * J
    block = place[1]
    for k in range(T):
        at = pl.multiple_of((block ^ k) * span, 16)
        for rp in range(2):
            blocks[rp, pl.ds(at, span), :] = messages[k][rp * span : (rp + 1) * span, :]
    for rp in range(2):
        joined[rp] = blocks[rp].T
    for rp in range(2):
        for cp in range(2):
            halves = []
            for half in range(2):
                start = 2 * span + ((rp * 2 + cp) * 2 + half) * 2 * J
                value = jnp.zeros((2 * J, messages[1].shape[1]), jnp.bfloat16)
                for k in range(1, T, 2):
                    found = (block > 0) & (block ^ k == block - 1)
                    value = jnp.where(found, messages[k][start : start + 2 * J, :], value)
                halves.append(value)
            before = jnp.concatenate(halves, axis=1)
            cached[rp, cp] = before
            if rp == 0:
                under[cp, : 2 * J] = before
                under[cp, 2 * J :] = planes[0, cp]


def permutation(shape, meet):
    row = lax.broadcasted_iota(jnp.int32, shape, 0)
    col = lax.broadcasted_iota(jnp.int32, shape, 1)
    return jnp.where(meet(row, col), 1.0, 0.0).astype(jnp.bfloat16)


def slice_of(value, block, k, T):
    part = value.shape[1] // T
    chosen = value[:, :part]
    for d in range(1, T):
        chosen = jnp.where(block == d ^ k, value[:, d * part : (d + 1) * part], chosen)
    return chosen


def shard_order(J, R, rows, first, moved):
    jl = J // R
    return permutation(
        (rows * 2 * J, R * 2 * J),
        lambda o, s: (o // (2 * J) + first == s // jl % R)
        & (o // J % 2 == s // (jl * R) % 2)
        & (o % J == s // (2 * jl * R) * jl + s % jl + moved),
    )


def shard_rows(source, start, count):
    return jnp.concatenate(
        [source[s, start : start + count, :] for s in range(source.shape[0])], axis=0
    )


def gate_kernel(*refs):
    pass


def slab_kernel(
    F, J, R, T, slot, place, planes, cached, under, weight_hbm, frames, vectors, gathered, following,
    out, frames_grad, weight, near, ext, tmp, sem,
):
    row, block = place[0], place[1]
    channels = frames.shape[1]
    span = F * J
    gain, bias = vectors[0:1], vectors[1:2]
    fetches = [
        pltpu.make_async_copy(weight_hbm.at[pl.ds(a * 9, 9)], weight.at[pl.ds(a * 9, 9)], sem.at[a])
        for a in range(3)
    ]
    for copy in fetches:
        copy.start()

    orders = [shard_order(J, R, 2, row - 1, moved) for moved in range(2)]
    for pair in range(F // 2 + 1):
        if pair < F // 2:
            source = shard_rows(gathered, pair * 2 * J, 2 * J)
        else:
            source = shard_rows(following, 0, 2 * J)
        for moved in range(2):
            value = mm(orders[moved], source).astype(jnp.bfloat16)
            for i in range(2):
                near[moved, i, pair * 2 * J : (pair + 1) * 2 * J, :] = value[
                    i * 2 * J : (i + 1) * 2 * J
                ]

    rows = (F + 2) * J
    last = lax.broadcasted_iota(jnp.int32, (rows, 1), 0) % J == J - 1
    for b in range(3):
        for cp in range(2):
            if b == 2:
                full = under[cp]
            else:
                full = jnp.concatenate([cached[b, cp], planes[b, cp]], axis=0)
            ext[b, cp] = full
            if cp == 0:
                moved = pltpu.roll(full.astype(jnp.float32), rows - 1, 0)
                ext[b, 2] = jnp.where(last, 0.0, moved).astype(jnp.bfloat16)

    latent = jnp.zeros((span, channels), jnp.float32)
    sums = {}
    for n, (a, b, c) in enumerate(TAPS):
        if n % 9 == 0:
            fetches[a].wait()
        latent = latent + mm(ext[b, c, a * J : (a + F) * J, :], weight[n])
        piece = near[c // 2, 1 - b // 2, (2 - a) * J : (2 - a + F) * J, :]
        term = mm_t(piece, weight[n])
        key = (b % 2, c % 2)
        sums[key] = sums[key] + term if key in sums else term
    for (rp, cp), value in sums.items():
        for t in range(F):
            for half in range(2):
                lanes = slice(half * channels // 2, (half + 1) * channels // 2)
                tmp[half, pl.ds((t * 2 + rp) * 2 * J + cp, J, stride=2), :] = value[
                    t * J : (t + 1) * J, lanes
                ]
    hidden_grad = jnp.concatenate([tmp[0], tmp[1]], axis=1)
    inv_rms, unit, normed = normalised(frames[...], gain)
    sigma = 1.0 / (1.0 + jnp.exp(-normed))
    normed_grad = hidden_grad * sigma * (1.0 + normed * (1.0 - sigma))
    gain_part = jnp.sum(normed_grad * unit, axis=0, keepdims=True)
    unit_grad = normed_grad * gain
    mean = jnp.mean(unit_grad * unit, axis=-1, keepdims=True)
    frames_grad[...] = (inv_rms * (unit_grad - unit * mean)).astype(jnp.bfloat16)

    jl = J // R
    used = span // R
    order = permutation(
        (R * slot, span),
        lambda o, s: (o % slot < used)
        & (o % slot // jl == s // J)
        & (o // slot * jl + o % jl == s % J),
    )
    value = mm(order, (latent + bias).astype(jnp.bfloat16))
    line = lax.broadcasted_iota(jnp.int32, (R * slot, 1), 0) % slot
    rest = jnp.concatenate([slice_of(gain_part, block, k, T) for k in range(T)], axis=1)
    for n in range(3):
        term = rest.astype(jnp.bfloat16).astype(jnp.float32)
        rest = rest - term
        value = jnp.where(line == used + n, term, value)
    out[...] = value.astype(jnp.bfloat16)


def gain_kernel(T, used, received, *refs):
    parts = refs[-T:]
    value = jnp.zeros(received.shape[1:], jnp.float32)
    for s in range(received.shape[0]):
        value = value + received[s].astype(jnp.float32)
    line = lax.broadcasted_iota(jnp.int32, (received.shape[1], 1), 0)
    value = jnp.where((line >= used) & (line < used + 3), value, 0.0)
    value = jnp.sum(value, axis=0, keepdims=True)
    part = received.shape[2] // T
    for k in range(T):
        parts[k][...] = value[:, k * part : (k + 1) * part]


def order_kernel(F, J, R, T, place, *refs):
    gathered, (grads, bias_sum) = refs[:T], refs[T:]
    channels = grads.shape[-1]
    span = F * J
    depth = T * span
    block = place[1]
    grads[:, :, depth:, :] = jnp.zeros((2, R, 2 * J, channels), jnp.bfloat16)
    orders = [shard_order(J, R, R, 0, moved) for moved in range(2)]
    total = jnp.zeros((1, channels), jnp.float32)
    for k in range(T):
        for pair in range(F // 2):
            source = shard_rows(gathered[k], pair * 2 * J, 2 * J)
            total = total + jnp.sum(source.astype(jnp.float32), axis=0, keepdims=True)
            at = pl.multiple_of((block ^ k) * span + pair * 2 * J, 16)
            for moved in range(2):
                value = mm(orders[moved], source).astype(jnp.bfloat16)
                for i in range(R):
                    grads[moved, i, pl.ds(at, 2 * J), :] = value[i * 2 * J : (i + 1) * 2 * J]
    bias_sum[...] = slice_of(total, block, 0, T)


def weight_kernel(F, J, R, T, part, place, _, grads, *refs):
    hidden = refs[:R]
    out_hbm, out, even, odd, sem = refs[R:]
    channels = grads.shape[-1]
    depth = T * F * J
    lanes = 2 * part
    row = place[0]
    even[:, R * depth :] = jnp.zeros((lanes, depth), jnp.bfloat16)
    for k in range(R):
        at = pl.multiple_of((row ^ k) * depth, 128)
        for rp, turned in ((0, even), (1, odd)):
            turned[:, pl.ds(at, depth)] = hidden[k][rp]
    leaving = []
    for a in range(3):
        start = (2 - a) * J
        for moved in range(2):
            right = grads[moved, :, start : start + depth, :].reshape(R * depth, channels)
            size = part if moved else lanes
            left = jnp.concatenate(
                [even[:size, : R * depth], odd[:size, :], even[:size, depth:]], axis=0
            )
            value = mm(left, right)
            for b in range(3):
                if moved:
                    out[(a * 3 + b) * 3 + 2] = value[b * part : (b + 1) * part]
                else:
                    for cp in range(2):
                        at = b * lanes + cp * part
                        out[(a * 3 + b) * 3 + cp] = value[at : at + part]
        taps = pl.ds(a * 9, 9)
        leaving.append(pltpu.make_async_copy(out.at[taps], out_hbm.at[taps], sem.at[a]))
        leaving[a].start()
    for copy in leaving:
        copy.wait()


def call(kernel, outs, scratch, flops, moved, places, aliases={}, limit=VMEM_LIMIT):
    kinds = {"s": pltpu.SMEM, "v": pltpu.VMEM, "h": pltpu.HBM, "a": pl.ANY}
    specs = [pl.BlockSpec(memory_space=kinds[p]) for p in places]
    count = len(places) - len(outs)
    return pl.pallas_call(
        kernel,
        out_shape=[jax.ShapeDtypeStruct(s, d) for s, d in outs],
        in_specs=specs[:count],
        out_specs=specs[count:],
        scratch_shapes=scratch,
        input_output_aliases=aliases,
        compiler_params=pltpu.CompilerParams(vmem_limit_bytes=limit),
        cost_estimate=pl.CostEstimate(flops=flops, bytes_accessed=moved, transcendentals=0),
    )


def gathered_form(frames, norm_gain, conv_weight, conv_bias, latent_grad):
    bf16, f32 = jnp.bfloat16, jnp.float32
    F, row_count, col_count, C = frames.shape
    R, T = lax.axis_size("rows"), lax.axis_size("tm")
    J = col_count // 2
    span = F * J
    part = C // T
    used = span // R
    slot = -(-(used + 3) // 16) * 16
    vectors = jnp.stack([norm_gain, conv_bias])
    flat = frames.reshape(-1, C)
    weight = conv_weight.reshape(27, C, C)
    place = jnp.stack([lax.axis_index("rows"), lax.axis_index("tm")]).astype(jnp.int32)

    own = latent_grad.reshape(1, -1, C)
    grad_rows = lax.all_to_all(
        jnp.broadcast_to(own, (R,) + own.shape[1:]), "rows", 0, 0, tiled=True
    )

    sizes = [(2 * span + (16 * J if k % 2 else 0), 2 * part) for k in range(T)]
    planes, frames_copy, vectors, *sends = call(
        functools.partial(hidden_kernel, F, J, T),
        [((2, 2, span, C), bf16), (flat.shape, bf16), ((2, C), f32)]
        + [(size, bf16) for size in sizes],
        [pltpu.VMEM((2, 4 * span, C // 2), f32)],
        60 * WORK * span * C, 16 * span * C, "svv" + "v" * (T + 3),
    )(place, flat, vectors)
    head, grad_rows = call(
        functools.partial(head_kernel, 2 * J),
        [((R, 2 * J, C), bf16), (grad_rows.shape, bf16)],
        [], R * span * C, R * span * C, "avvv",
    )(frames_copy, grad_rows)
    messages = [sends[0]] + [partners(sends[k], "tm", k) for k in range(1, T)]
    joined, cached, under = call(
        functools.partial(join_kernel, F, J, T),
        [
            ((2, 2 * part, T * span), bf16),
            ((2, 2, 2 * J, C), bf16),
            ((2, 2 * J + span, C), bf16),
        ],
        [pltpu.VMEM((2, T * span, 2 * part), bf16)],
        30 * WORK * span * C, 16 * span * C, "sv" + "v" * T + "vvv",
    )(place, planes, *messages)
    under = shifted(under, "rows", -1)
    following = shifted(head, "tm", -1)
    packed, frames_grad = call(
        functools.partial(slab_kernel, F, J, R, T, slot),
        [((R * slot, C), bf16), ((4 * span, C), bf16)],
        [
            pltpu.VMEM((27, C, C), bf16),
            pltpu.VMEM((2, 2, (F + 2) * J, C), bf16),
            pltpu.VMEM((3, 3, (F + 2) * J, C), bf16),
            pltpu.VMEM((2, 4 * span, C // 2), f32),
            pltpu.SemaphoreType.DMA((3,)),
        ],
        2 * 54 * span * C * C, 2 * 27 * C * C, "svvvhvvvv" + "vv",
        limit=VMEM_LIMIT_WIDE,
    )(place, planes, cached, under, weight, frames_copy, vectors, grad_rows, following)

    def after_slab(blocks):
        shapes = [(b.shape, bf16) for b in blocks]
        count = len(blocks)
        aliases = {n + 1: n for n in range(count)}
        return list(
            call(gate_kernel, shapes, [], 0, 0, "a" * (2 * count + 1), aliases)(packed, *blocks)
        )

    hidden_all = exchanged(joined, "rows", after_slab)
    grad_all = exchanged(grad_rows, "tm")

    packed = lax.all_to_all(packed.reshape(R, slot, C), "rows", 0, 0, tiled=True)
    latent = packed[:, :used].reshape(R, F, J // R, C).transpose(1, 0, 2, 3)
    gains = call(
        functools.partial(gain_kernel, T, used),
        [((1, part), f32)] * T,
        [], R * slot * C, R * slot * C, "v" + "a" * (R // 2) + "v" * T,
    )(packed, *hidden_all[1::2])
    gain_grad = gains[0]
    for k in range(1, T):
        gain_grad = gain_grad + partners(gains[k], "tm", k)

    grads, bias_sum = call(
        functools.partial(order_kernel, F, J, R, T),
        [((2, R, (F * T + 2) * J, C), bf16), ((1, part), f32)],
        [],
        90 * WORK * span * C, 2 * R * T * span * C, "s" + "v" * (T + 2),
    )(place, *grad_all)
    (weight_grad,) = call(
        functools.partial(weight_kernel, F, J, R, T, part),
        [((27, part, C), f32)],
        [
            pltpu.VMEM((27, part, C), f32),
            pltpu.VMEM((2 * part, (R + 1) * T * span), bf16),
            pltpu.VMEM((2 * part, R * T * span), bf16),
            pltpu.SemaphoreType.DMA((3,)),
        ],
        200 * WORK * span * C, 8 * 27 * part * C, "sav" + "v" * R + "h",
    )(place, gains[0], grads, *hidden_all)

    return (
        latent,
        frames_grad.reshape(frames.shape),
        weight_grad.reshape(3, 3, 3, part, C),
        gain_grad.reshape(part),
        bias_sum.reshape(part),
    )


def on_device(frames, norm_gain, conv_weight, conv_bias, latent_grad):
    rows, shares = lax.axis_size("rows"), lax.axis_size("tm")
    operand_bytes = 2 * rows * shares * (frames.size // shares + latent_grad.size)
    result_bytes = 4 * conv_weight.size
    powers = (rows & (rows - 1)) == 0 and (shares & (shares - 1)) == 0
    if powers and frames.shape[1] == 2 and operand_bytes <= result_bytes:
        form = gathered_form
    else:
        form = reduced_form
    return form(frames, norm_gain, conv_weight, conv_bias, latent_grad)


def solution(mesh):
    placed = (P("tm", "rows", None, None), P(), P(), P(), P("tm", None, "rows", None))
    return jax.shard_map(
        on_device,
        mesh=mesh,
        in_specs=placed,
        out_specs=(
            P("tm", None, "rows", None),
            P("tm", "rows", None, None),
            P(None, None, None, "tm", None),
            P("tm"),
            P("tm"),
        ),
        check_vma=False,
    )
```

```python
import functools

import jax
import jax.numpy as jnp
from jax import lax
from jax.experimental import pallas as pl
from jax.experimental.pallas import tpu as pltpu
from jax.sharding import PartitionSpec as P

EPS = 1e-06
TAPS = [(a, b, c) for a in range(3) for b in range(3) for c in range(3)]
VMEM_LIMIT = 20 * 1024 * 1024
VMEM_LIMIT_WIDE = 60 * 1024 * 1024
WORK = 1200


def shifted(value, axis, steps):
    count = lax.axis_size(axis)
    leading, last = (max(0, -steps), min(count, count - steps))
    return lax.ppermute(value, axis, [(source, source + steps) for source in range(leading, last)])


def contract_out(grad_piece, weight_tap):
    return lax.dot_general(
        grad_piece, weight_tap, (((1,), (1,)), ((), ())), preferred_element_type=jnp.float32
    )


def reduced_form(frames, norm_gain, conv_weight, conv_bias, latent_grad):
    signal = frames.astype(jnp.float32)
    inv_rms = lax.rsqrt(jnp.mean(signal * signal, axis=-1, keepdims=True) + EPS)
    unit = signal * inv_rms
    normed = unit * norm_gain
    hidden = jax.nn.silu(normed).astype(jnp.bfloat16)
    frame_count, row_count, col_count, channels = hidden.shape
    lat_rows = row_count // 2
    lat_cols = col_count // 2
    cached = shifted(hidden[frame_count - 2 :], "tm", 1)
    stacked = jnp.concatenate([cached, hidden], axis=0)
    row_under = shifted(stacked[:, :1], "rows", -1)
    extended = jnp.concatenate([stacked, row_under], axis=1)
    extended = jnp.pad(extended, ((0, 0), (0, 0), (0, 1), (0, 0)))
    grad_rows = lax.all_to_all(latent_grad, "rows", split_axis=1, concat_axis=2, tiled=True)
    grad_flat = grad_rows.reshape(-1, channels)
    running = jnp.zeros((frame_count * lat_rows * lat_cols, channels), jnp.float32)
    blocks = []
    for tap_t, tap_r, tap_c in TAPS:
        window_piece = extended[
            tap_t : tap_t + frame_count,
            tap_r : tap_r + 2 * lat_rows : 2,
            tap_c : tap_c + 2 * lat_cols : 2,
        ]
        window_piece = window_piece.reshape(-1, channels)
        running = running + jnp.dot(
            window_piece, conv_weight[tap_t, tap_r, tap_c], preferred_element_type=jnp.float32
        )
        blocks.append(
            lax.dot_general(
                window_piece,
                grad_flat,
                (((0,), (0,)), ((), ())),
                preferred_element_type=jnp.float32,
            )
        )
    latent_rows = (
        (running + conv_bias)
        .reshape(frame_count, lat_rows, lat_cols, channels)
        .astype(jnp.bfloat16)
    )
    latent = lax.all_to_all(latent_rows, "rows", split_axis=2, concat_axis=1, tiled=True)
    weight_local = jnp.stack(blocks).reshape(3, 3, 3, channels, channels)
    bias_local = jnp.sum(grad_flat.astype(jnp.float32), axis=0)
    following = shifted(grad_rows[:2], "tm", -1)
    grad_ext = jnp.concatenate([grad_rows, following], axis=0)
    above_row = shifted(grad_ext, "rows", 1)
    grad_ext = jnp.concatenate([above_row, grad_ext], axis=1)
    grad_ext = jnp.pad(grad_ext, ((0, 0), (0, 0), (1, 0), (0, 0)))
    parity_sums = {}
    for tap_t, tap_r, tap_c in TAPS:
        row_start = 1 - tap_r // 2
        col_start = 1 - tap_c // 2
        grad_piece = grad_ext[
            2 - tap_t : 2 - tap_t + frame_count,
            row_start : row_start + lat_rows,
            col_start : col_start + lat_cols,
        ]
        term = contract_out(grad_piece.reshape(-1, channels), conv_weight[tap_t, tap_r, tap_c])
        label = (tap_r % 2, tap_c % 2)
        parity_sums[label] = parity_sums[label] + term if label in parity_sums else term
    shaped = {}
    for label in parity_sums:
        shaped[label] = parity_sums[label].reshape(frame_count, lat_rows, lat_cols, channels)
    even_rows = jnp.stack([shaped[0, 0], shaped[0, 1]], axis=3)
    odd_rows = jnp.stack([shaped[1, 0], shaped[1, 1]], axis=3)
    hidden_grad = jnp.stack([even_rows, odd_rows], axis=2).reshape(
        frame_count, row_count, col_count, channels
    )
    sigma = jax.nn.sigmoid(normed)
    normed_grad = hidden_grad * sigma * (1.0 + normed * (1.0 - sigma))
    gain_local = jnp.sum(normed_grad * unit, axis=(0, 1, 2))
    unit_grad = normed_grad * norm_gain
    frames_grad = inv_rms * (unit_grad - unit * jnp.mean(unit_grad * unit, axis=-1, keepdims=True))
    totals = lax.psum((weight_local, gain_local, bias_local), "rows")
    weight_grad, gain_grad, bias_grad = (
        lax.psum_scatter(totals[0], "tm", scatter_dimension=3, tiled=True),
        lax.psum_scatter(totals[1], "tm", scatter_dimension=0, tiled=True),
        lax.psum_scatter(totals[2], "tm", scatter_dimension=0, tiled=True),
    )
    return (latent, frames_grad.astype(jnp.bfloat16), weight_grad, gain_grad, bias_grad)


def partners(value, axis, bits):
    count = lax.axis_size(axis)
    return lax.ppermute(value, axis, [(source, source ^ bits) for source in range(count)])


def exchanged(value, axis, gate=None):
    count = lax.axis_size(axis)
    blocks = {0: value}
    for k in range(1, count):
        if k & (k - 1) == 0:
            blocks[k] = partners(value, axis, k)
    if gate is not None:
        held = [k for k in blocks if k > 0]
        blocks.update(zip(held, gate([blocks[k] for k in held])))
    for k in range(1, count):
        low = k & -k
        if k != low:
            blocks[k] = partners(blocks[k - low], axis, low)
    return [blocks[k] for k in range(count)]


def mm(left, right):
    return jnp.dot(left, right, preferred_element_type=jnp.float32)


def mm_t(left, right):
    return lax.dot_general(
        left, right, (((1,), (1,)), ((), ())), preferred_element_type=jnp.float32
    )


def normalised(frames, gain):
    signal = frames.astype(jnp.float32)
    inv_rms = lax.rsqrt(jnp.mean(signal * signal, axis=-1, keepdims=True) + EPS)
    unit = signal * inv_rms
    return inv_rms, unit, unit * gain


def hidden_kernel(F, J, T, place, frames, vectors, planes, frames_copy, vectors_copy, *rest):
    sends, tmp = rest[:T], rest[T]
    frames_copy[...] = frames[...]
    vectors_copy[...] = vectors[...]
    channels = frames.shape[1]
    part = channels // T
    _, _, normed = normalised(frames[...], vectors[0:1])
    value = normed / (1.0 + jnp.exp(-normed))
    tmp[0] = value[:, : channels // 2]
    tmp[1] = value[:, channels // 2 :]
    block = place[1]
    for rp in range(2):
        pair = []
        for cp in range(2):
            rows = [
                jnp.concatenate(
                    [
                        tmp[half, pl.ds((t * 2 + rp) * 2 * J + cp, J, stride=2), :]
                        for half in range(2)
                    ],
                    axis=1,
                )
                for t in range(F)
            ]
            plane = jnp.concatenate(rows, axis=0)
            pair.append(plane)
            plane = plane.astype(jnp.bfloat16)
            planes[rp, cp] = plane
            late = plane[(F - 2) * J :]
            for k in range(1, T, 2):
                for half in range(2):
                    at = (((rp * 2 + cp) * 2) + half) * 2 * J
                    lanes = slice(half * channels // 2, (half + 1) * channels // 2)
                    sends[k][2 * F * J + at : 2 * F * J + at + 2 * J] = late[:, lanes]
        pieces = [
            jnp.concatenate([p[:, d * part : (d + 1) * part] for p in pair], axis=1)
            for d in range(T)
        ]
        for k in range(T):
            chosen = pieces[0]
            for d in range(1, T):
                chosen = jnp.where(block == d ^ k, pieces[d], chosen)
            sends[k][rp * F * J : (rp + 1) * F * J] = chosen.astype(jnp.bfloat16)


def head_kernel(rows, _, grad_rows, head, passed):
    passed[...] = grad_rows[...]
    for s in range(grad_rows.shape[0]):
        head[s] = grad_rows[s, :rows, :]


def total_kernel(*refs):
    total = refs[0][...]
    for ref in refs[1:-1]:
        total = total + ref[...]
    refs[-1][...] = total


def join_kernel(F, J, T, place, planes, *refs):
    messages, (joined, cached, under, blocks) = refs[:T], refs[T:]
    span = F * J
    block = place[1]
    for k in range(T):
        at = pl.multiple_of((block ^ k) * span, 16)
        for rp in range(2):
            blocks[rp, pl.ds(at, span), :] = messages[k][rp * span : (rp + 1) * span, :]
    for rp in range(2):
        joined[rp] = blocks[rp].T
    for rp in range(2):
        for cp in range(2):
            halves = []
            for half in range(2):
                start = 2 * span + ((rp * 2 + cp) * 2 + half) * 2 * J
                value = jnp.zeros((2 * J, messages[1].shape[1]), jnp.bfloat16)
                for k in range(1, T, 2):
                    found = (block > 0) & (block ^ k == block - 1)
                    value = jnp.where(found, messages[k][start : start + 2 * J, :], value)
                halves.append(value)
            before = jnp.concatenate(halves, axis=1)
            cached[rp, cp] = before
            if rp == 0:
                under[cp, : 2 * J] = before
                under[cp, 2 * J :] = planes[0, cp]


def permutation(shape, meet):
    row = lax.broadcasted_iota(jnp.int32, shape, 0)
    col = lax.broadcasted_iota(jnp.int32, shape, 1)
    return jnp.where(meet(row, col), 1.0, 0.0).astype(jnp.bfloat16)


def slice_of(value, block, k, T):
    part = value.shape[1] // T
    chosen = value[:, :part]
    for d in range(1, T):
        chosen = jnp.where(block == d ^ k, value[:, d * part : (d + 1) * part], chosen)
    return chosen


def shard_order(J, R, rows, first, moved):
    jl = J // R
    return permutation(
        (rows * 2 * J, R * 2 * J),
        lambda o, s: (o // (2 * J) + first == s // jl % R)
        & (o // J % 2 == s // (jl * R) % 2)
        & (o % J == s // (2 * jl * R) * jl + s % jl + moved),
    )


def shard_rows(source, start, count):
    return jnp.concatenate(
        [source[s, start : start + count, :] for s in range(source.shape[0])], axis=0
    )


def gate_kernel(*refs):
    pass


def slab_kernel(
    F, J, R, T, slot, place, planes, cached, under, weight_hbm, frames, vectors, gathered, following,
    out, frames_grad, weight, near, ext, tmp, sem,
):
    row, block = place[0], place[1]
    channels = frames.shape[1]
    span = F * J
    gain, bias = vectors[0:1], vectors[1:2]
    fetches = [
        pltpu.make_async_copy(weight_hbm.at[pl.ds(a * 9, 9)], weight.at[pl.ds(a * 9, 9)], sem.at[a])
        for a in range(3)
    ]
    for copy in fetches:
        copy.start()

    orders = [shard_order(J, R, 2, row - 1, moved) for moved in range(2)]
    for pair in range(F // 2 + 1):
        if pair < F // 2:
            source = shard_rows(gathered, pair * 2 * J, 2 * J)
        else:
            source = shard_rows(following, 0, 2 * J)
        for moved in range(2):
            value = mm(orders[moved], source).astype(jnp.bfloat16)
            for i in range(2):
                near[moved, i, pair * 2 * J : (pair + 1) * 2 * J, :] = value[
                    i * 2 * J : (i + 1) * 2 * J
                ]

    rows = (F + 2) * J
    last = lax.broadcasted_iota(jnp.int32, (rows, 1), 0) % J == J - 1
    for b in range(3):
        for cp in range(2):
            if b == 2:
                full = under[cp]
            else:
                full = jnp.concatenate([cached[b, cp], planes[b, cp]], axis=0)
            ext[b, cp] = full
            if cp == 0:
                moved = pltpu.roll(full.astype(jnp.float32), rows - 1, 0)
                ext[b, 2] = jnp.where(last, 0.0, moved).astype(jnp.bfloat16)

    latent = jnp.zeros((span, channels), jnp.float32)
    sums = {}
    for n, (a, b, c) in enumerate(TAPS):
        if n % 9 == 0:
            fetches[a].wait()
        latent = latent + mm(ext[b, c, a * J : (a + F) * J, :], weight[n])
        piece = near[c // 2, 1 - b // 2, (2 - a) * J : (2 - a + F) * J, :]
        term = mm_t(piece, weight[n])
        key = (b % 2, c % 2)
        sums[key] = sums[key] + term if key in sums else term
    for (rp, cp), value in sums.items():
        for t in range(F):
            for half in range(2):
                lanes = slice(half * channels // 2, (half + 1) * channels // 2)
                tmp[half, pl.ds((t * 2 + rp) * 2 * J + cp, J, stride=2), :] = value[
                    t * J : (t + 1) * J, lanes
                ]
    hidden_grad = jnp.concatenate([tmp[0], tmp[1]], axis=1)
    inv_rms, unit, normed = normalised(frames[...], gain)
    sigma = 1.0 / (1.0 + jnp.exp(-normed))
    normed_grad = hidden_grad * sigma * (1.0 + normed * (1.0 - sigma))
    gain_part = jnp.sum(normed_grad * unit, axis=0, keepdims=True)
    unit_grad = normed_grad * gain
    mean = jnp.mean(unit_grad * unit, axis=-1, keepdims=True)
    frames_grad[...] = (inv_rms * (unit_grad - unit * mean)).astype(jnp.bfloat16)

    jl = J // R
    used = span // R
    order = permutation(
        (R * slot, span),
        lambda o, s: (o % slot < used)
        & (o % slot // jl == s // J)
        & (o // slot * jl + o % jl == s % J),
    )
    value = mm(order, (latent + bias).astype(jnp.bfloat16))
    line = lax.broadcasted_iota(jnp.int32, (R * slot, 1), 0) % slot
    rest = jnp.concatenate([slice_of(gain_part, block, k, T) for k in range(T)], axis=1)
    for n in range(3):
        term = rest.astype(jnp.bfloat16).astype(jnp.float32)
        rest = rest - term
        value = jnp.where(line == used + n, term, value)
    out[...] = value.astype(jnp.bfloat16)


def gain_kernel(T, used, received, *refs):
    parts = refs[-T:]
    value = jnp.zeros(received.shape[1:], jnp.float32)
    for s in range(received.shape[0]):
        value = value + received[s].astype(jnp.float32)
    line = lax.broadcasted_iota(jnp.int32, (received.shape[1], 1), 0)
    value = jnp.where((line >= used) & (line < used + 3), value, 0.0)
    value = jnp.sum(value, axis=0, keepdims=True)
    part = received.shape[2] // T
    for k in range(T):
        parts[k][...] = value[:, k * part : (k + 1) * part]


def order_kernel(F, J, R, T, place, *refs):
    gathered, (grads, bias_sum) = refs[:T], refs[T:]
    channels = grads.shape[-1]
    span = F * J
    depth = T * span
    block = place[1]
    grads[:, :, depth:, :] = jnp.zeros((2, R, 2 * J, channels), jnp.bfloat16)
    orders = [shard_order(J, R, R, 0, moved) for moved in range(2)]
    total = jnp.zeros((1, channels), jnp.float32)
    for k in range(T):
        for pair in range(F // 2):
            source = shard_rows(gathered[k], pair * 2 * J, 2 * J)
            total = total + jnp.sum(source.astype(jnp.float32), axis=0, keepdims=True)
            at = pl.multiple_of((block ^ k) * span + pair * 2 * J, 16)
            for moved in range(2):
                value = mm(orders[moved], source).astype(jnp.bfloat16)
                for i in range(R):
                    grads[moved, i, pl.ds(at, 2 * J), :] = value[i * 2 * J : (i + 1) * 2 * J]
    bias_sum[...] = slice_of(total, block, 0, T)


def weight_kernel(F, J, R, T, part, place, gain, grads, *refs):
    hidden = refs[:R]
    out_hbm, gain_out, out, even, odd, sem = refs[R:]
    gain_out[...] = gain[...]
    channels = grads.shape[-1]
    depth = T * F * J
    lanes = 2 * part
    row = place[0]
    even[:, R * depth :] = jnp.zeros((lanes, depth), jnp.bfloat16)
    for k in range(R):
        at = pl.multiple_of((row ^ k) * depth, 128)
        for rp, turned in ((0, even), (1, odd)):
            turned[:, pl.ds(at, depth)] = hidden[k][rp]
    leaving = []
    for a in range(3):
        start = (2 - a) * J
        for moved in range(2):
            right = grads[moved, :, start : start + depth, :].reshape(R * depth, channels)
            size = part if moved else lanes
            left = jnp.concatenate(
                [even[:size, : R * depth], odd[:size, :], even[:size, depth:]], axis=0
            )
            value = mm(left, right)
            for b in range(3):
                if moved:
                    out[(a * 3 + b) * 3 + 2] = value[b * part : (b + 1) * part]
                else:
                    for cp in range(2):
                        at = b * lanes + cp * part
                        out[(a * 3 + b) * 3 + cp] = value[at : at + part]
        taps = pl.ds(a * 9, 9)
        leaving.append(pltpu.make_async_copy(out.at[taps], out_hbm.at[taps], sem.at[a]))
        leaving[a].start()
    for copy in leaving:
        copy.wait()


def call(kernel, outs, scratch, flops, moved, places, aliases={}, limit=VMEM_LIMIT):
    kinds = {"s": pltpu.SMEM, "v": pltpu.VMEM, "h": pltpu.HBM, "a": pl.ANY}
    specs = [pl.BlockSpec(memory_space=kinds[p]) for p in places]
    count = len(places) - len(outs)
    return pl.pallas_call(
        kernel,
        out_shape=[jax.ShapeDtypeStruct(s, d) for s, d in outs],
        in_specs=specs[:count],
        out_specs=specs[count:],
        scratch_shapes=scratch,
        input_output_aliases=aliases,
        compiler_params=pltpu.CompilerParams(vmem_limit_bytes=limit),
        cost_estimate=pl.CostEstimate(flops=flops, bytes_accessed=moved, transcendentals=0),
    )


def gathered_form(frames, norm_gain, conv_weight, conv_bias, latent_grad):
    bf16, f32 = jnp.bfloat16, jnp.float32
    F, row_count, col_count, C = frames.shape
    R, T = lax.axis_size("rows"), lax.axis_size("tm")
    J = col_count // 2
    span = F * J
    part = C // T
    used = span // R
    slot = -(-(used + 3) // 16) * 16
    vectors = jnp.stack([norm_gain, conv_bias])
    flat = frames.reshape(-1, C)
    weight = conv_weight.reshape(27, C, C)
    place = jnp.stack([lax.axis_index("rows"), lax.axis_index("tm")]).astype(jnp.int32)

    own = latent_grad.reshape(1, -1, C)
    grad_rows = lax.all_to_all(
        jnp.broadcast_to(own, (R,) + own.shape[1:]), "rows", 0, 0, tiled=True
    )

    sizes = [(2 * span + (16 * J if k % 2 else 0), 2 * part) for k in range(T)]
    planes, frames_copy, vectors, *sends = call(
        functools.partial(hidden_kernel, F, J, T),
        [((2, 2, span, C), bf16), (flat.shape, bf16), ((2, C), f32)]
        + [(size, bf16) for size in sizes],
        [pltpu.VMEM((2, 4 * span, C // 2), f32)],
        60 * WORK * span * C, 16 * span * C, "svv" + "v" * (T + 3),
    )(place, flat, vectors)
    messages = [sends[0]] + [partners(sends[k], "tm", k) for k in range(1, T)]
    head, grad_rows = call(
        functools.partial(head_kernel, 2 * J),
        [((R, 2 * J, C), bf16), (grad_rows.shape, bf16)],
        [], R * span * C, R * span * C, "avvv",
    )(messages[1], grad_rows)
    joined, cached, under = call(
        functools.partial(join_kernel, F, J, T),
        [
            ((2, 2 * part, T * span), bf16),
            ((2, 2, 2 * J, C), bf16),
            ((2, 2 * J + span, C), bf16),
        ],
        [pltpu.VMEM((2, T * span, 2 * part), bf16)],
        30 * WORK * span * C, 16 * span * C, "sv" + "v" * T + "vvv",
    )(place, planes, *messages)
    under = shifted(under, "rows", -1)
    following = shifted(head, "tm", -1)
    packed, frames_grad = call(
        functools.partial(slab_kernel, F, J, R, T, slot),
        [((R * slot, C), bf16), ((4 * span, C), bf16)],
        [
            pltpu.VMEM((27, C, C), bf16),
            pltpu.VMEM((2, 2, (F + 2) * J, C), bf16),
            pltpu.VMEM((3, 3, (F + 2) * J, C), bf16),
            pltpu.VMEM((2, 4 * span, C // 2), f32),
            pltpu.SemaphoreType.DMA((3,)),
        ],
        2 * 54 * span * C * C, 2 * 27 * C * C, "svvvhvvvv" + "vv",
        limit=VMEM_LIMIT_WIDE,
    )(place, planes, cached, under, weight, frames_copy, vectors, grad_rows, following)

    def after_slab(blocks):
        shapes = [(b.shape, bf16) for b in blocks]
        count = len(blocks)
        aliases = {n + 1: n for n in range(count)}
        return list(
            call(gate_kernel, shapes, [], 0, 0, "a" * (2 * count + 1), aliases)(packed, *blocks)
        )

    hidden_all = exchanged(joined, "rows", after_slab)
    grad_all = exchanged(grad_rows, "tm")

    packed = lax.all_to_all(packed.reshape(R, slot, C), "rows", 0, 0, tiled=True)
    latent = packed[:, :used].reshape(R, F, J // R, C).transpose(1, 0, 2, 3)
    gains = call(
        functools.partial(gain_kernel, T, used),
        [((1, part), f32)] * T,
        [], R * slot * C, R * slot * C, "v" + "a" * (R // 2) + "v" * T,
    )(packed, *hidden_all[1::2])
    grads, bias_sum = call(
        functools.partial(order_kernel, F, J, R, T),
        [((2, R, (F * T + 2) * J, C), bf16), ((1, part), f32)],
        [],
        90 * WORK * span * C, 2 * R * T * span * C, "s" + "v" * (T + 2),
    )(place, *grad_all)
    weight_grad, own_gain = call(
        functools.partial(weight_kernel, F, J, R, T, part),
        [((27, part, C), f32), ((1, part), f32)],
        [
            pltpu.VMEM((27, part, C), f32),
            pltpu.VMEM((2 * part, (R + 1) * T * span), bf16),
            pltpu.VMEM((2 * part, R * T * span), bf16),
            pltpu.SemaphoreType.DMA((3,)),
        ],
        200 * WORK * span * C, 8 * 27 * part * C, "svv" + "v" * R + "hv",
    )(place, gains[0], grads, *hidden_all)

    terms = [own_gain] + [partners(gains[k], "tm", k) for k in range(1, T)]
    (gain_grad,) = call(
        total_kernel, [((1, part), f32)], [], T * part, 4 * T * part, "v" * (T + 1)
    )(*terms)
    return (
        latent,
        frames_grad.reshape(frames.shape),
        weight_grad.reshape(3, 3, 3, part, C),
        gain_grad.reshape(part),
        bias_sum.reshape(part),
    )


def on_device(frames, norm_gain, conv_weight, conv_bias, latent_grad):
    rows, shares = lax.axis_size("rows"), lax.axis_size("tm")
    operand_bytes = 2 * rows * shares * (frames.size // shares + latent_grad.size)
    result_bytes = 4 * conv_weight.size
    powers = (rows & (rows - 1)) == 0 and (shares & (shares - 1)) == 0
    if powers and frames.shape[1] == 2 and operand_bytes <= result_bytes:
        form = gathered_form
    else:
        form = reduced_form
    return form(frames, norm_gain, conv_weight, conv_bias, latent_grad)


def solution(mesh):
    placed = (P("tm", "rows", None, None), P(), P(), P(), P("tm", None, "rows", None))
    return jax.shard_map(
        on_device,
        mesh=mesh,
        in_specs=placed,
        out_specs=(
            P("tm", None, "rows", None),
            P("tm", "rows", None, None),
            P(None, None, None, "tm", None),
            P("tm"),
            P("tm"),
        ),
        check_vma=False,
    )
```

```python
import functools

import jax
import jax.numpy as jnp
from jax import lax
from jax.experimental import pallas as pl
from jax.experimental.pallas import tpu as pltpu
from jax.sharding import PartitionSpec as P

EPS = 1e-06
TAPS = [(a, b, c) for a in range(3) for b in range(3) for c in range(3)]
VMEM_LIMIT = 20 * 1024 * 1024
VMEM_LIMIT_WIDE = 60 * 1024 * 1024
WORK = 1200


def shifted(value, axis, steps):
    count = lax.axis_size(axis)
    leading, last = (max(0, -steps), min(count, count - steps))
    return lax.ppermute(value, axis, [(source, source + steps) for source in range(leading, last)])


def contract_out(grad_piece, weight_tap):
    return lax.dot_general(
        grad_piece, weight_tap, (((1,), (1,)), ((), ())), preferred_element_type=jnp.float32
    )


def reduced_form(frames, norm_gain, conv_weight, conv_bias, latent_grad):
    signal = frames.astype(jnp.float32)
    inv_rms = lax.rsqrt(jnp.mean(signal * signal, axis=-1, keepdims=True) + EPS)
    unit = signal * inv_rms
    normed = unit * norm_gain
    hidden = jax.nn.silu(normed).astype(jnp.bfloat16)
    frame_count, row_count, col_count, channels = hidden.shape
    lat_rows = row_count // 2
    lat_cols = col_count // 2
    cached = shifted(hidden[frame_count - 2 :], "tm", 1)
    stacked = jnp.concatenate([cached, hidden], axis=0)
    row_under = shifted(stacked[:, :1], "rows", -1)
    extended = jnp.concatenate([stacked, row_under], axis=1)
    extended = jnp.pad(extended, ((0, 0), (0, 0), (0, 1), (0, 0)))
    grad_rows = lax.all_to_all(latent_grad, "rows", split_axis=1, concat_axis=2, tiled=True)
    grad_flat = grad_rows.reshape(-1, channels)
    running = jnp.zeros((frame_count * lat_rows * lat_cols, channels), jnp.float32)
    blocks = []
    for tap_t, tap_r, tap_c in TAPS:
        window_piece = extended[
            tap_t : tap_t + frame_count,
            tap_r : tap_r + 2 * lat_rows : 2,
            tap_c : tap_c + 2 * lat_cols : 2,
        ]
        window_piece = window_piece.reshape(-1, channels)
        running = running + jnp.dot(
            window_piece, conv_weight[tap_t, tap_r, tap_c], preferred_element_type=jnp.float32
        )
        blocks.append(
            lax.dot_general(
                window_piece,
                grad_flat,
                (((0,), (0,)), ((), ())),
                preferred_element_type=jnp.float32,
            )
        )
    latent_rows = (
        (running + conv_bias)
        .reshape(frame_count, lat_rows, lat_cols, channels)
        .astype(jnp.bfloat16)
    )
    latent = lax.all_to_all(latent_rows, "rows", split_axis=2, concat_axis=1, tiled=True)
    weight_local = jnp.stack(blocks).reshape(3, 3, 3, channels, channels)
    bias_local = jnp.sum(grad_flat.astype(jnp.float32), axis=0)
    following = shifted(grad_rows[:2], "tm", -1)
    grad_ext = jnp.concatenate([grad_rows, following], axis=0)
    above_row = shifted(grad_ext, "rows", 1)
    grad_ext = jnp.concatenate([above_row, grad_ext], axis=1)
    grad_ext = jnp.pad(grad_ext, ((0, 0), (0, 0), (1, 0), (0, 0)))
    parity_sums = {}
    for tap_t, tap_r, tap_c in TAPS:
        row_start = 1 - tap_r // 2
        col_start = 1 - tap_c // 2
        grad_piece = grad_ext[
            2 - tap_t : 2 - tap_t + frame_count,
            row_start : row_start + lat_rows,
            col_start : col_start + lat_cols,
        ]
        term = contract_out(grad_piece.reshape(-1, channels), conv_weight[tap_t, tap_r, tap_c])
        label = (tap_r % 2, tap_c % 2)
        parity_sums[label] = parity_sums[label] + term if label in parity_sums else term
    shaped = {}
    for label in parity_sums:
        shaped[label] = parity_sums[label].reshape(frame_count, lat_rows, lat_cols, channels)
    even_rows = jnp.stack([shaped[0, 0], shaped[0, 1]], axis=3)
    odd_rows = jnp.stack([shaped[1, 0], shaped[1, 1]], axis=3)
    hidden_grad = jnp.stack([even_rows, odd_rows], axis=2).reshape(
        frame_count, row_count, col_count, channels
    )
    sigma = jax.nn.sigmoid(normed)
    normed_grad = hidden_grad * sigma * (1.0 + normed * (1.0 - sigma))
    gain_local = jnp.sum(normed_grad * unit, axis=(0, 1, 2))
    unit_grad = normed_grad * norm_gain
    frames_grad = inv_rms * (unit_grad - unit * jnp.mean(unit_grad * unit, axis=-1, keepdims=True))
    totals = lax.psum((weight_local, gain_local, bias_local), "rows")
    weight_grad, gain_grad, bias_grad = (
        lax.psum_scatter(totals[0], "tm", scatter_dimension=3, tiled=True),
        lax.psum_scatter(totals[1], "tm", scatter_dimension=0, tiled=True),
        lax.psum_scatter(totals[2], "tm", scatter_dimension=0, tiled=True),
    )
    return (latent, frames_grad.astype(jnp.bfloat16), weight_grad, gain_grad, bias_grad)


def partners(value, axis, bits):
    count = lax.axis_size(axis)
    return lax.ppermute(value, axis, [(source, source ^ bits) for source in range(count)])


def exchanged(value, axis, gate=None):
    count = lax.axis_size(axis)
    blocks = {0: value}
    for k in range(1, count):
        if k & (k - 1) == 0:
            blocks[k] = partners(value, axis, k)
    if gate is not None:
        held = [k for k in blocks if k > 1]
        blocks.update(zip(held, gate([blocks[k] for k in held])))
    for k in range(1, count):
        low = k & -k
        if k != low:
            blocks[k] = partners(blocks[k - low], axis, low)
    return [blocks[k] for k in range(count)]


def mm(left, right):
    return jnp.dot(left, right, preferred_element_type=jnp.float32)


def mm_t(left, right):
    return lax.dot_general(
        left, right, (((1,), (1,)), ((), ())), preferred_element_type=jnp.float32
    )


def normalised(frames, gain):
    signal = frames.astype(jnp.float32)
    inv_rms = lax.rsqrt(jnp.mean(signal * signal, axis=-1, keepdims=True) + EPS)
    unit = signal * inv_rms
    return inv_rms, unit, unit * gain


def hidden_kernel(F, J, T, place, frames, vectors, planes, kept, *rest):
    sends, tmp = rest[:T], rest[T]
    count = frames.shape[0]
    kept[:count] = frames[...].astype(jnp.float32)
    kept[count:] = jnp.zeros((kept.shape[0] - count, kept.shape[1]), jnp.float32)
    kept[count : count + 2] = vectors[...]
    channels = frames.shape[1]
    part = channels // T
    _, _, normed = normalised(frames[...], vectors[0:1])
    value = normed / (1.0 + jnp.exp(-normed))
    tmp[0] = value[:, : channels // 2]
    tmp[1] = value[:, channels // 2 :]
    block = place[1]
    for rp in range(2):
        pair = []
        for cp in range(2):
            rows = [
                jnp.concatenate(
                    [
                        tmp[half, pl.ds((t * 2 + rp) * 2 * J + cp, J, stride=2), :]
                        for half in range(2)
                    ],
                    axis=1,
                )
                for t in range(F)
            ]
            plane = jnp.concatenate(rows, axis=0)
            pair.append(plane)
            plane = plane.astype(jnp.bfloat16)
            planes[rp, cp] = plane
            late = plane[(F - 2) * J :]
            for k in range(1, T, 2):
                for half in range(2):
                    at = (((rp * 2 + cp) * 2) + half) * 2 * J
                    lanes = slice(half * channels // 2, (half + 1) * channels // 2)
                    sends[k][2 * F * J + at : 2 * F * J + at + 2 * J] = late[:, lanes]
        pieces = [
            jnp.concatenate([p[:, d * part : (d + 1) * part] for p in pair], axis=1)
            for d in range(T)
        ]
        for k in range(T):
            chosen = pieces[0]
            for d in range(1, T):
                chosen = jnp.where(block == d ^ k, pieces[d], chosen)
            sends[k][rp * F * J : (rp + 1) * F * J] = chosen.astype(jnp.bfloat16)


def head_kernel(rows, _, grad_rows, head, passed):
    passed[...] = grad_rows[...]
    for s in range(grad_rows.shape[0]):
        head[s] = grad_rows[s, :rows, :]


def join_kernel(F, J, T, place, planes, *refs):
    messages, (joined, cached, under, blocks) = refs[:T], refs[T:]
    span = F * J
    block = place[1]
    for k in range(T):
        at = pl.multiple_of((block ^ k) * span, 16)
        for rp in range(2):
            blocks[rp, pl.ds(at, span), :] = messages[k][rp * span : (rp + 1) * span, :]
    for rp in range(2):
        joined[rp] = blocks[rp].T
    for rp in range(2):
        for cp in range(2):
            halves = []
            for half in range(2):
                start = 2 * span + ((rp * 2 + cp) * 2 + half) * 2 * J
                value = jnp.zeros((2 * J, messages[1].shape[1]), jnp.bfloat16)
                for k in range(1, T, 2):
                    found = (block > 0) & (block ^ k == block - 1)
                    value = jnp.where(found, messages[k][start : start + 2 * J, :], value)
                halves.append(value)
            before = jnp.concatenate(halves, axis=1)
            cached[rp, cp] = before
            if rp == 0:
                under[cp, : 2 * J] = before
                under[cp, 2 * J :] = planes[0, cp]


def permutation(shape, meet):
    row = lax.broadcasted_iota(jnp.int32, shape, 0)
    col = lax.broadcasted_iota(jnp.int32, shape, 1)
    return jnp.where(meet(row, col), 1.0, 0.0).astype(jnp.bfloat16)


def slice_of(value, block, k, T):
    part = value.shape[1] // T
    chosen = value[:, :part]
    for d in range(1, T):
        chosen = jnp.where(block == d ^ k, value[:, d * part : (d + 1) * part], chosen)
    return chosen


def shard_order(J, R, rows, first, moved):
    jl = J // R
    return permutation(
        (rows * 2 * J, R * 2 * J),
        lambda o, s: (o // (2 * J) + first == s // jl % R)
        & (o // J % 2 == s // (jl * R) % 2)
        & (o % J == s // (2 * jl * R) * jl + s % jl + moved),
    )


def shard_rows(source, start, count):
    return jnp.concatenate(
        [source[s, start : start + count, :] for s in range(source.shape[0])], axis=0
    )


def gate_kernel(*refs):
    pass


def slab_kernel(
    F, J, R, T, slot, place, planes, cached, under, weight_hbm, kept, gathered, following,
    out, frames_grad, weight, near, ext, tmp, sem,
):
    row, block = place[0], place[1]
    channels = kept.shape[1]
    span = F * J
    gain, bias = kept[4 * span : 4 * span + 1], kept[4 * span + 1 : 4 * span + 2]
    fetches = [
        pltpu.make_async_copy(weight_hbm.at[pl.ds(a * 9, 9)], weight.at[pl.ds(a * 9, 9)], sem.at[a])
        for a in range(3)
    ]
    for copy in fetches:
        copy.start()

    orders = [shard_order(J, R, 2, row - 1, moved) for moved in range(2)]
    for pair in range(F // 2 + 1):
        if pair < F // 2:
            source = shard_rows(gathered, pair * 2 * J, 2 * J)
        else:
            source = shard_rows(following, 0, 2 * J)
        for moved in range(2):
            value = mm(orders[moved], source).astype(jnp.bfloat16)
            for i in range(2):
                near[moved, i, pair * 2 * J : (pair + 1) * 2 * J, :] = value[
                    i * 2 * J : (i + 1) * 2 * J
                ]

    rows = (F + 2) * J
    last = lax.broadcasted_iota(jnp.int32, (rows, 1), 0) % J == J - 1
    for b in range(3):
        for cp in range(2):
            if b == 2:
                full = under[cp]
            else:
                full = jnp.concatenate([cached[b, cp], planes[b, cp]], axis=0)
            ext[b, cp] = full
            if cp == 0:
                moved = pltpu.roll(full.astype(jnp.float32), rows - 1, 0)
                ext[b, 2] = jnp.where(last, 0.0, moved).astype(jnp.bfloat16)

    latent = jnp.zeros((span, channels), jnp.float32)
    sums = {}
    for n, (a, b, c) in enumerate(TAPS):
        if n % 9 == 0:
            fetches[a].wait()
        latent = latent + mm(ext[b, c, a * J : (a + F) * J, :], weight[n])
        piece = near[c // 2, 1 - b // 2, (2 - a) * J : (2 - a + F) * J, :]
        term = mm_t(piece, weight[n])
        key = (b % 2, c % 2)
        sums[key] = sums[key] + term if key in sums else term
    for (rp, cp), value in sums.items():
        for t in range(F):
            for half in range(2):
                lanes = slice(half * channels // 2, (half + 1) * channels // 2)
                tmp[half, pl.ds((t * 2 + rp) * 2 * J + cp, J, stride=2), :] = value[
                    t * J : (t + 1) * J, lanes
                ]
    hidden_grad = jnp.concatenate([tmp[0], tmp[1]], axis=1)
    inv_rms, unit, normed = normalised(kept[: 4 * span], gain)
    sigma = 1.0 / (1.0 + jnp.exp(-normed))
    normed_grad = hidden_grad * sigma * (1.0 + normed * (1.0 - sigma))
    gain_part = jnp.sum(normed_grad * unit, axis=0, keepdims=True)
    unit_grad = normed_grad * gain
    mean = jnp.mean(unit_grad * unit, axis=-1, keepdims=True)
    frames_grad[...] = (inv_rms * (unit_grad - unit * mean)).astype(jnp.bfloat16)

    jl = J // R
    used = span // R
    order = permutation(
        (R * slot, span),
        lambda o, s: (o % slot < used)
        & (o % slot // jl == s // J)
        & (o // slot * jl + o % jl == s % J),
    )
    value = mm(order, (latent + bias).astype(jnp.bfloat16))
    line = lax.broadcasted_iota(jnp.int32, (R * slot, 1), 0) % slot
    rest = jnp.concatenate([slice_of(gain_part, block, k, T) for k in range(T)], axis=1)
    for n in range(3):
        term = rest.astype(jnp.bfloat16).astype(jnp.float32)
        rest = rest - term
        value = jnp.where(line == used + n, term, value)
    out[...] = value.astype(jnp.bfloat16)


def gain_kernel(T, used, received, *refs):
    parts = refs[-T:]
    value = jnp.zeros(received.shape[1:], jnp.float32)
    for s in range(received.shape[0]):
        value = value + received[s].astype(jnp.float32)
    line = lax.broadcasted_iota(jnp.int32, (received.shape[1], 1), 0)
    value = jnp.where((line >= used) & (line < used + 3), value, 0.0)
    value = jnp.sum(value, axis=0, keepdims=True)
    part = received.shape[2] // T
    for k in range(T):
        parts[k][...] = value[:, k * part : (k + 1) * part]


def order_kernel(F, J, R, T, place, *refs):
    gathered, (grads, bias_sum) = refs[:T], refs[T:]
    channels = grads.shape[-1]
    span = F * J
    depth = T * span
    block = place[1]
    grads[:, :, depth:, :] = jnp.zeros((2, R, 2 * J, channels), jnp.bfloat16)
    orders = [shard_order(J, R, R, 0, moved) for moved in range(2)]
    total = jnp.zeros((1, channels), jnp.float32)
    for k in range(T):
        for pair in range(F // 2):
            source = shard_rows(gathered[k], pair * 2 * J, 2 * J)
            total = total + jnp.sum(source.astype(jnp.float32), axis=0, keepdims=True)
            at = pl.multiple_of((block ^ k) * span + pair * 2 * J, 16)
            for moved in range(2):
                value = mm(orders[moved], source).astype(jnp.bfloat16)
                for i in range(R):
                    grads[moved, i, pl.ds(at, 2 * J), :] = value[i * 2 * J : (i + 1) * 2 * J]
    bias_sum[...] = slice_of(total, block, 0, T)


def weight_kernel(F, J, R, T, part, place, _, grads, *refs):
    hidden = refs[:R]
    out_hbm, out, even, odd, sem = refs[R:]
    channels = grads.shape[-1]
    depth = T * F * J
    lanes = 2 * part
    row = place[0]
    even[:, R * depth :] = jnp.zeros((lanes, depth), jnp.bfloat16)
    for k in range(R):
        at = pl.multiple_of((row ^ k) * depth, 128)
        for rp, turned in ((0, even), (1, odd)):
            turned[:, pl.ds(at, depth)] = hidden[k][rp]
    leaving = []
    for a in range(3):
        start = (2 - a) * J
        for moved in range(2):
            right = grads[moved, :, start : start + depth, :].reshape(R * depth, channels)
            size = part if moved else lanes
            left = jnp.concatenate(
                [even[:size, : R * depth], odd[:size, :], even[:size, depth:]], axis=0
            )
            value = mm(left, right)
            for b in range(3):
                if moved:
                    out[(a * 3 + b) * 3 + 2] = value[b * part : (b + 1) * part]
                else:
                    for cp in range(2):
                        at = b * lanes + cp * part
                        out[(a * 3 + b) * 3 + cp] = value[at : at + part]
        taps = pl.ds(a * 9, 9)
        leaving.append(pltpu.make_async_copy(out.at[taps], out_hbm.at[taps], sem.at[a]))
        leaving[a].start()
    for copy in leaving:
        copy.wait()


def call(kernel, outs, scratch, flops, moved, places, aliases={}, limit=VMEM_LIMIT):
    kinds = {"s": pltpu.SMEM, "v": pltpu.VMEM, "h": pltpu.HBM, "a": pl.ANY}
    specs = [pl.BlockSpec(memory_space=kinds[p]) for p in places]
    count = len(places) - len(outs)
    return pl.pallas_call(
        kernel,
        out_shape=[jax.ShapeDtypeStruct(s, d) for s, d in outs],
        in_specs=specs[:count],
        out_specs=specs[count:],
        scratch_shapes=scratch,
        input_output_aliases=aliases,
        compiler_params=pltpu.CompilerParams(vmem_limit_bytes=limit),
        cost_estimate=pl.CostEstimate(flops=flops, bytes_accessed=moved, transcendentals=0),
    )


def gathered_form(frames, norm_gain, conv_weight, conv_bias, latent_grad):
    bf16, f32 = jnp.bfloat16, jnp.float32
    F, row_count, col_count, C = frames.shape
    R, T = lax.axis_size("rows"), lax.axis_size("tm")
    J = col_count // 2
    span = F * J
    part = C // T
    used = span // R
    slot = -(-(used + 3) // 16) * 16
    vectors = jnp.stack([norm_gain, conv_bias])
    flat = frames.reshape(-1, C)
    weight = conv_weight.reshape(27, C, C)
    place = jnp.stack([lax.axis_index("rows"), lax.axis_index("tm")]).astype(jnp.int32)

    own = latent_grad.reshape(1, -1, C)
    grad_rows = lax.all_to_all(
        jnp.broadcast_to(own, (R,) + own.shape[1:]), "rows", 0, 0, tiled=True
    )

    sizes = [(2 * span + (16 * J if k % 2 else 0), 2 * part) for k in range(T)]
    planes, kept, *sends = call(
        functools.partial(hidden_kernel, F, J, T),
        [((2, 2, span, C), bf16), ((4 * span + 8, C), f32)]
        + [(size, bf16) for size in sizes],
        [pltpu.VMEM((2, 4 * span, C // 2), f32)],
        60 * WORK * span * C, 16 * span * C, "svv" + "v" * (T + 2),
    )(place, flat, vectors)
    head, grad_rows = call(
        functools.partial(head_kernel, 2 * J),
        [((R, 2 * J, C), bf16), (grad_rows.shape, bf16)],
        [], R * span * C, R * span * C, "avvv",
    )(kept, grad_rows)
    messages = [sends[0]] + [partners(sends[k], "tm", k) for k in range(1, T)]
    joined, cached, under = call(
        functools.partial(join_kernel, F, J, T),
        [
            ((2, 2 * part, T * span), bf16),
            ((2, 2, 2 * J, C), bf16),
            ((2, 2 * J + span, C), bf16),
        ],
        [pltpu.VMEM((2, T * span, 2 * part), bf16)],
        30 * WORK * span * C, 16 * span * C, "sv" + "v" * T + "vvv",
    )(place, planes, *messages)
    under = shifted(under, "rows", -1)
    following = shifted(head, "tm", -1)
    packed, frames_grad = call(
        functools.partial(slab_kernel, F, J, R, T, slot),
        [((R * slot, C), bf16), ((4 * span, C), bf16)],
        [
            pltpu.VMEM((27, C, C), bf16),
            pltpu.VMEM((2, 2, (F + 2) * J, C), bf16),
            pltpu.VMEM((3, 3, (F + 2) * J, C), bf16),
            pltpu.VMEM((2, 4 * span, C // 2), f32),
            pltpu.SemaphoreType.DMA((3,)),
        ],
        2 * 54 * span * C * C, 2 * 27 * C * C, "svvvhvvv" + "vv",
        limit=VMEM_LIMIT_WIDE,
    )(place, planes, cached, under, weight, kept, grad_rows, following)

    def after_slab(blocks):
        shapes = [(b.shape, bf16) for b in blocks]
        count = len(blocks)
        aliases = {n + 1: n for n in range(count)}
        return list(
            call(gate_kernel, shapes, [], 0, 0, "a" * (2 * count + 1), aliases)(packed, *blocks)
        )

    hidden_all = exchanged(joined, "rows", after_slab)
    grad_all = exchanged(grad_rows, "tm")

    packed = lax.all_to_all(packed.reshape(R, slot, C), "rows", 0, 0, tiled=True)
    latent = packed[:, :used].reshape(R, F, J // R, C).transpose(1, 0, 2, 3)
    gains = call(
        functools.partial(gain_kernel, T, used),
        [((1, part), f32)] * T,
        [], R * slot * C, R * slot * C, "v" + "a" * (R // 2) + "v" * T,
    )(packed, *hidden_all[1::2])
    gain_grad = gains[0]
    for k in range(1, T):
        gain_grad = gain_grad + partners(gains[k], "tm", k)

    grads, bias_sum = call(
        functools.partial(order_kernel, F, J, R, T),
        [((2, R, (F * T + 2) * J, C), bf16), ((1, part), f32)],
        [],
        90 * WORK * span * C, 2 * R * T * span * C, "s" + "v" * (T + 2),
    )(place, *grad_all)
    (weight_grad,) = call(
        functools.partial(weight_kernel, F, J, R, T, part),
        [((27, part, C), f32)],
        [
            pltpu.VMEM((27, part, C), f32),
            pltpu.VMEM((2 * part, (R + 1) * T * span), bf16),
            pltpu.VMEM((2 * part, R * T * span), bf16),
            pltpu.SemaphoreType.DMA((3,)),
        ],
        200 * WORK * span * C, 8 * 27 * part * C, "sav" + "v" * R + "h",
    )(place, gains[0], grads, *hidden_all)

    return (
        latent,
        frames_grad.reshape(frames.shape),
        weight_grad.reshape(3, 3, 3, part, C),
        gain_grad.reshape(part),
        bias_sum.reshape(part),
    )


def on_device(frames, norm_gain, conv_weight, conv_bias, latent_grad):
    rows, shares = lax.axis_size("rows"), lax.axis_size("tm")
    operand_bytes = 2 * rows * shares * (frames.size // shares + latent_grad.size)
    result_bytes = 4 * conv_weight.size
    powers = (rows & (rows - 1)) == 0 and (shares & (shares - 1)) == 0
    if powers and frames.shape[1] == 2 and operand_bytes <= result_bytes:
        form = gathered_form
    else:
        form = reduced_form
    return form(frames, norm_gain, conv_weight, conv_bias, latent_grad)


def solution(mesh):
    placed = (P("tm", "rows", None, None), P(), P(), P(), P("tm", None, "rows", None))
    return jax.shard_map(
        on_device,
        mesh=mesh,
        in_specs=placed,
        out_specs=(
            P("tm", None, "rows", None),
            P("tm", "rows", None, None),
            P(None, None, None, "tm", None),
            P("tm"),
            P("tm"),
        ),
        check_vma=False,
    )
```

```python
import functools

import jax
import jax.numpy as jnp
from jax import lax
from jax.experimental import pallas as pl
from jax.experimental.pallas import tpu as pltpu
from jax.sharding import PartitionSpec as P

EPS = 1e-06
TAPS = [(a, b, c) for a in range(3) for b in range(3) for c in range(3)]
VMEM_LIMIT = 20 * 1024 * 1024
VMEM_LIMIT_WIDE = 60 * 1024 * 1024
WORK = 1200


def shifted(value, axis, steps):
    count = lax.axis_size(axis)
    leading, last = (max(0, -steps), min(count, count - steps))
    return lax.ppermute(value, axis, [(source, source + steps) for source in range(leading, last)])


def contract_out(grad_piece, weight_tap):
    return lax.dot_general(
        grad_piece, weight_tap, (((1,), (1,)), ((), ())), preferred_element_type=jnp.float32
    )


def reduced_form(frames, norm_gain, conv_weight, conv_bias, latent_grad):
    signal = frames.astype(jnp.float32)
    inv_rms = lax.rsqrt(jnp.mean(signal * signal, axis=-1, keepdims=True) + EPS)
    unit = signal * inv_rms
    normed = unit * norm_gain
    hidden = jax.nn.silu(normed).astype(jnp.bfloat16)
    frame_count, row_count, col_count, channels = hidden.shape
    lat_rows = row_count // 2
    lat_cols = col_count // 2
    cached = shifted(hidden[frame_count - 2 :], "tm", 1)
    stacked = jnp.concatenate([cached, hidden], axis=0)
    row_under = shifted(stacked[:, :1], "rows", -1)
    extended = jnp.concatenate([stacked, row_under], axis=1)
    extended = jnp.pad(extended, ((0, 0), (0, 0), (0, 1), (0, 0)))
    grad_rows = lax.all_to_all(latent_grad, "rows", split_axis=1, concat_axis=2, tiled=True)
    grad_flat = grad_rows.reshape(-1, channels)
    running = jnp.zeros((frame_count * lat_rows * lat_cols, channels), jnp.float32)
    blocks = []
    for tap_t, tap_r, tap_c in TAPS:
        window_piece = extended[
            tap_t : tap_t + frame_count,
            tap_r : tap_r + 2 * lat_rows : 2,
            tap_c : tap_c + 2 * lat_cols : 2,
        ]
        window_piece = window_piece.reshape(-1, channels)
        running = running + jnp.dot(
            window_piece, conv_weight[tap_t, tap_r, tap_c], preferred_element_type=jnp.float32
        )
        blocks.append(
            lax.dot_general(
                window_piece,
                grad_flat,
                (((0,), (0,)), ((), ())),
                preferred_element_type=jnp.float32,
            )
        )
    latent_rows = (
        (running + conv_bias)
        .reshape(frame_count, lat_rows, lat_cols, channels)
        .astype(jnp.bfloat16)
    )
    latent = lax.all_to_all(latent_rows, "rows", split_axis=2, concat_axis=1, tiled=True)
    weight_local = jnp.stack(blocks).reshape(3, 3, 3, channels, channels)
    bias_local = jnp.sum(grad_flat.astype(jnp.float32), axis=0)
    following = shifted(grad_rows[:2], "tm", -1)
    grad_ext = jnp.concatenate([grad_rows, following], axis=0)
    above_row = shifted(grad_ext, "rows", 1)
    grad_ext = jnp.concatenate([above_row, grad_ext], axis=1)
    grad_ext = jnp.pad(grad_ext, ((0, 0), (0, 0), (1, 0), (0, 0)))
    parity_sums = {}
    for tap_t, tap_r, tap_c in TAPS:
        row_start = 1 - tap_r // 2
        col_start = 1 - tap_c // 2
        grad_piece = grad_ext[
            2 - tap_t : 2 - tap_t + frame_count,
            row_start : row_start + lat_rows,
            col_start : col_start + lat_cols,
        ]
        term = contract_out(grad_piece.reshape(-1, channels), conv_weight[tap_t, tap_r, tap_c])
        label = (tap_r % 2, tap_c % 2)
        parity_sums[label] = parity_sums[label] + term if label in parity_sums else term
    shaped = {}
    for label in parity_sums:
        shaped[label] = parity_sums[label].reshape(frame_count, lat_rows, lat_cols, channels)
    even_rows = jnp.stack([shaped[0, 0], shaped[0, 1]], axis=3)
    odd_rows = jnp.stack([shaped[1, 0], shaped[1, 1]], axis=3)
    hidden_grad = jnp.stack([even_rows, odd_rows], axis=2).reshape(
        frame_count, row_count, col_count, channels
    )
    sigma = jax.nn.sigmoid(normed)
    normed_grad = hidden_grad * sigma * (1.0 + normed * (1.0 - sigma))
    gain_local = jnp.sum(normed_grad * unit, axis=(0, 1, 2))
    unit_grad = normed_grad * norm_gain
    frames_grad = inv_rms * (unit_grad - unit * jnp.mean(unit_grad * unit, axis=-1, keepdims=True))
    totals = lax.psum((weight_local, gain_local, bias_local), "rows")
    weight_grad, gain_grad, bias_grad = (
        lax.psum_scatter(totals[0], "tm", scatter_dimension=3, tiled=True),
        lax.psum_scatter(totals[1], "tm", scatter_dimension=0, tiled=True),
        lax.psum_scatter(totals[2], "tm", scatter_dimension=0, tiled=True),
    )
    return (latent, frames_grad.astype(jnp.bfloat16), weight_grad, gain_grad, bias_grad)


def partners(value, axis, bits):
    count = lax.axis_size(axis)
    return lax.ppermute(value, axis, [(source, source ^ bits) for source in range(count)])


def exchanged(value, axis, gate=None):
    count = lax.axis_size(axis)
    blocks = {0: value}
    for k in range(1, count):
        if k & (k - 1) == 0:
            blocks[k] = partners(value, axis, k)
    if gate is not None:
        held = [k for k in blocks if k > 1]
        blocks.update(zip(held, gate([blocks[k] for k in held])))
    for k in range(1, count):
        low = k & -k
        if k != low:
            blocks[k] = partners(blocks[k - low], axis, low)
    return [blocks[k] for k in range(count)]


def mm(left, right):
    return jnp.dot(left, right, preferred_element_type=jnp.float32)


def mm_t(left, right):
    return lax.dot_general(
        left, right, (((1,), (1,)), ((), ())), preferred_element_type=jnp.float32
    )


def normalised(frames, gain):
    signal = frames.astype(jnp.float32)
    inv_rms = lax.rsqrt(jnp.mean(signal * signal, axis=-1, keepdims=True) + EPS)
    unit = signal * inv_rms
    return inv_rms, unit, unit * gain


def hidden_kernel(F, J, T, place, frames, vectors, planes, kept, *rest):
    sends, tmp = rest[:T], rest[T]
    count = frames.shape[0]
    kept[:count] = frames[...]
    line = lax.broadcasted_iota(jnp.int32, (16, 1), 0)
    rest, tail = vectors[...], jnp.zeros((16, kept.shape[1]), jnp.float32)
    for n in range(3):
        term = rest.astype(jnp.bfloat16).astype(jnp.float32)
        rest = rest - term
        tail = jnp.where(line == n, term[0:1], jnp.where(line == 3 + n, term[1:2], tail))
    kept[count:] = tail.astype(jnp.bfloat16)
    channels = frames.shape[1]
    part = channels // T
    _, _, normed = normalised(frames[...], vectors[0:1])
    value = normed / (1.0 + jnp.exp(-normed))
    tmp[0] = value[:, : channels // 2]
    tmp[1] = value[:, channels // 2 :]
    block = place[1]
    for rp in range(2):
        pair = []
        for cp in range(2):
            rows = [
                jnp.concatenate(
                    [
                        tmp[half, pl.ds((t * 2 + rp) * 2 * J + cp, J, stride=2), :]
                        for half in range(2)
                    ],
                    axis=1,
                )
                for t in range(F)
            ]
            plane = jnp.concatenate(rows, axis=0)
            pair.append(plane)
            plane = plane.astype(jnp.bfloat16)
            planes[rp, cp] = plane
            late = plane[(F - 2) * J :]
            for k in range(1, T, 2):
                for half in range(2):
                    at = (((rp * 2 + cp) * 2) + half) * 2 * J
                    lanes = slice(half * channels // 2, (half + 1) * channels // 2)
                    sends[k][2 * F * J + at : 2 * F * J + at + 2 * J] = late[:, lanes]
        pieces = [
            jnp.concatenate([p[:, d * part : (d + 1) * part] for p in pair], axis=1)
            for d in range(T)
        ]
        for k in range(T):
            chosen = pieces[0]
            for d in range(1, T):
                chosen = jnp.where(block == d ^ k, pieces[d], chosen)
            sends[k][rp * F * J : (rp + 1) * F * J] = chosen.astype(jnp.bfloat16)


def head_kernel(rows, _, grad_rows, head, passed):
    passed[...] = grad_rows[...]
    for s in range(grad_rows.shape[0]):
        head[s] = grad_rows[s, :rows, :]


def join_kernel(F, J, T, place, planes, *refs):
    messages, (joined, cached, under, blocks) = refs[:T], refs[T:]
    span = F * J
    block = place[1]
    for k in range(T):
        at = pl.multiple_of((block ^ k) * span, 16)
        for rp in range(2):
            blocks[rp, pl.ds(at, span), :] = messages[k][rp * span : (rp + 1) * span, :]
    for rp in range(2):
        joined[rp] = blocks[rp].T
    for rp in range(2):
        for cp in range(2):
            halves = []
            for half in range(2):
                start = 2 * span + ((rp * 2 + cp) * 2 + half) * 2 * J
                value = jnp.zeros((2 * J, messages[1].shape[1]), jnp.bfloat16)
                for k in range(1, T, 2):
                    found = (block > 0) & (block ^ k == block - 1)
                    value = jnp.where(found, messages[k][start : start + 2 * J, :], value)
                halves.append(value)
            before = jnp.concatenate(halves, axis=1)
            cached[rp, cp] = before
            if rp == 0:
                under[cp, : 2 * J] = before
                under[cp, 2 * J :] = planes[0, cp]


def permutation(shape, meet):
    row = lax.broadcasted_iota(jnp.int32, shape, 0)
    col = lax.broadcasted_iota(jnp.int32, shape, 1)
    return jnp.where(meet(row, col), 1.0, 0.0).astype(jnp.bfloat16)


def slice_of(value, block, k, T):
    part = value.shape[1] // T
    chosen = value[:, :part]
    for d in range(1, T):
        chosen = jnp.where(block == d ^ k, value[:, d * part : (d + 1) * part], chosen)
    return chosen


def shard_order(J, R, rows, first, moved):
    jl = J // R
    return permutation(
        (rows * 2 * J, R * 2 * J),
        lambda o, s: (o // (2 * J) + first == s // jl % R)
        & (o // J % 2 == s // (jl * R) % 2)
        & (o % J == s // (2 * jl * R) * jl + s % jl + moved),
    )


def shard_rows(source, start, count):
    return jnp.concatenate(
        [source[s, start : start + count, :] for s in range(source.shape[0])], axis=0
    )


def gate_kernel(*refs):
    pass


def slab_kernel(
    F, J, R, T, slot, place, planes, cached, under, weight_hbm, kept, gathered, following,
    out, frames_grad, weight, near, ext, tmp, sem,
):
    row, block = place[0], place[1]
    channels = kept.shape[1]
    span = F * J
    tail = kept[4 * span :].astype(jnp.float32)
    gain = tail[0:1] + tail[1:2] + tail[2:3]
    bias = tail[3:4] + tail[4:5] + tail[5:6]
    fetches = [
        pltpu.make_async_copy(weight_hbm.at[pl.ds(a * 9, 9)], weight.at[pl.ds(a * 9, 9)], sem.at[a])
        for a in range(3)
    ]
    for copy in fetches:
        copy.start()

    orders = [shard_order(J, R, 2, row - 1, moved) for moved in range(2)]
    for pair in range(F // 2 + 1):
        if pair < F // 2:
            source = shard_rows(gathered, pair * 2 * J, 2 * J)
        else:
            source = shard_rows(following, 0, 2 * J)
        for moved in range(2):
            value = mm(orders[moved], source).astype(jnp.bfloat16)
            for i in range(2):
                near[moved, i, pair * 2 * J : (pair + 1) * 2 * J, :] = value[
                    i * 2 * J : (i + 1) * 2 * J
                ]

    rows = (F + 2) * J
    last = lax.broadcasted_iota(jnp.int32, (rows, 1), 0) % J == J - 1
    for b in range(3):
        for cp in range(2):
            if b == 2:
                full = under[cp]
            else:
                full = jnp.concatenate([cached[b, cp], planes[b, cp]], axis=0)
            ext[b, cp] = full
            if cp == 0:
                moved = pltpu.roll(full.astype(jnp.float32), rows - 1, 0)
                ext[b, 2] = jnp.where(last, 0.0, moved).astype(jnp.bfloat16)

    latent = jnp.zeros((span, channels), jnp.float32)
    sums = {}
    for n, (a, b, c) in enumerate(TAPS):
        if n % 9 == 0:
            fetches[a].wait()
        latent = latent + mm(ext[b, c, a * J : (a + F) * J, :], weight[n])
        piece = near[c // 2, 1 - b // 2, (2 - a) * J : (2 - a + F) * J, :]
        term = mm_t(piece, weight[n])
        key = (b % 2, c % 2)
        sums[key] = sums[key] + term if key in sums else term
    for (rp, cp), value in sums.items():
        for t in range(F):
            for half in range(2):
                lanes = slice(half * channels // 2, (half + 1) * channels // 2)
                tmp[half, pl.ds((t * 2 + rp) * 2 * J + cp, J, stride=2), :] = value[
                    t * J : (t + 1) * J, lanes
                ]
    hidden_grad = jnp.concatenate([tmp[0], tmp[1]], axis=1)
    inv_rms, unit, normed = normalised(kept[: 4 * span], gain)
    sigma = 1.0 / (1.0 + jnp.exp(-normed))
    normed_grad = hidden_grad * sigma * (1.0 + normed * (1.0 - sigma))
    gain_part = jnp.sum(normed_grad * unit, axis=0, keepdims=True)
    unit_grad = normed_grad * gain
    mean = jnp.mean(unit_grad * unit, axis=-1, keepdims=True)
    frames_grad[...] = (inv_rms * (unit_grad - unit * mean)).astype(jnp.bfloat16)

    jl = J // R
    used = span // R
    order = permutation(
        (R * slot, span),
        lambda o, s: (o % slot < used)
        & (o % slot // jl == s // J)
        & (o // slot * jl + o % jl == s % J),
    )
    value = mm(order, (latent + bias).astype(jnp.bfloat16))
    line = lax.broadcasted_iota(jnp.int32, (R * slot, 1), 0) % slot
    rest = jnp.concatenate([slice_of(gain_part, block, k, T) for k in range(T)], axis=1)
    for n in range(3):
        term = rest.astype(jnp.bfloat16).astype(jnp.float32)
        rest = rest - term
        value = jnp.where(line == used + n, term, value)
    out[...] = value.astype(jnp.bfloat16)


def gain_kernel(T, used, received, *refs):
    parts = refs[-T:]
    value = jnp.zeros(received.shape[1:], jnp.float32)
    for s in range(received.shape[0]):
        value = value + received[s].astype(jnp.float32)
    line = lax.broadcasted_iota(jnp.int32, (received.shape[1], 1), 0)
    value = jnp.where((line >= used) & (line < used + 3), value, 0.0)
    value = jnp.sum(value, axis=0, keepdims=True)
    part = received.shape[2] // T
    for k in range(T):
        parts[k][...] = value[:, k * part : (k + 1) * part]


def order_kernel(F, J, R, T, place, *refs):
    gathered, (grads, bias_sum) = refs[:T], refs[T:]
    channels = grads.shape[-1]
    span = F * J
    depth = T * span
    block = place[1]
    grads[:, :, depth:, :] = jnp.zeros((2, R, 2 * J, channels), jnp.bfloat16)
    orders = [shard_order(J, R, R, 0, moved) for moved in range(2)]
    total = jnp.zeros((1, channels), jnp.float32)
    for k in range(T):
        for pair in range(F // 2):
            source = shard_rows(gathered[k], pair * 2 * J, 2 * J)
            total = total + jnp.sum(source.astype(jnp.float32), axis=0, keepdims=True)
            at = pl.multiple_of((block ^ k) * span + pair * 2 * J, 16)
            for moved in range(2):
                value = mm(orders[moved], source).astype(jnp.bfloat16)
                for i in range(R):
                    grads[moved, i, pl.ds(at, 2 * J), :] = value[i * 2 * J : (i + 1) * 2 * J]
    bias_sum[...] = slice_of(total, block, 0, T)


def weight_kernel(F, J, R, T, part, place, _, grads, *refs):
    hidden = refs[:R]
    out_hbm, out, even, odd, sem = refs[R:]
    channels = grads.shape[-1]
    depth = T * F * J
    lanes = 2 * part
    row = place[0]
    even[:, R * depth :] = jnp.zeros((lanes, depth), jnp.bfloat16)
    for k in range(R):
        at = pl.multiple_of((row ^ k) * depth, 128)
        for rp, turned in ((0, even), (1, odd)):
            turned[:, pl.ds(at, depth)] = hidden[k][rp]
    leaving = []
    for a in range(3):
        start = (2 - a) * J
        for moved in range(2):
            right = grads[moved, :, start : start + depth, :].reshape(R * depth, channels)
            size = part if moved else lanes
            left = jnp.concatenate(
                [even[:size, : R * depth], odd[:size, :], even[:size, depth:]], axis=0
            )
            value = mm(left, right)
            for b in range(3):
                if moved:
                    out[(a * 3 + b) * 3 + 2] = value[b * part : (b + 1) * part]
                else:
                    for cp in range(2):
                        at = b * lanes + cp * part
                        out[(a * 3 + b) * 3 + cp] = value[at : at + part]
        taps = pl.ds(a * 9, 9)
        leaving.append(pltpu.make_async_copy(out.at[taps], out_hbm.at[taps], sem.at[a]))
        leaving[a].start()
    for copy in leaving:
        copy.wait()


def call(kernel, outs, scratch, flops, moved, places, aliases={}, limit=VMEM_LIMIT):
    kinds = {"s": pltpu.SMEM, "v": pltpu.VMEM, "h": pltpu.HBM, "a": pl.ANY}
    specs = [pl.BlockSpec(memory_space=kinds[p]) for p in places]
    count = len(places) - len(outs)
    return pl.pallas_call(
        kernel,
        out_shape=[jax.ShapeDtypeStruct(s, d) for s, d in outs],
        in_specs=specs[:count],
        out_specs=specs[count:],
        scratch_shapes=scratch,
        input_output_aliases=aliases,
        compiler_params=pltpu.CompilerParams(vmem_limit_bytes=limit),
        cost_estimate=pl.CostEstimate(flops=flops, bytes_accessed=moved, transcendentals=0),
    )


def gathered_form(frames, norm_gain, conv_weight, conv_bias, latent_grad):
    bf16, f32 = jnp.bfloat16, jnp.float32
    F, row_count, col_count, C = frames.shape
    R, T = lax.axis_size("rows"), lax.axis_size("tm")
    J = col_count // 2
    span = F * J
    part = C // T
    used = span // R
    slot = -(-(used + 3) // 16) * 16
    vectors = jnp.stack([norm_gain, conv_bias])
    flat = frames.reshape(-1, C)
    weight = conv_weight.reshape(27, C, C)
    place = jnp.stack([lax.axis_index("rows"), lax.axis_index("tm")]).astype(jnp.int32)

    own = latent_grad.reshape(1, -1, C)
    grad_rows = lax.all_to_all(
        jnp.broadcast_to(own, (R,) + own.shape[1:]), "rows", 0, 0, tiled=True
    )

    sizes = [(2 * span + (16 * J if k % 2 else 0), 2 * part) for k in range(T)]
    planes, kept, *sends = call(
        functools.partial(hidden_kernel, F, J, T),
        [((2, 2, span, C), bf16), ((4 * span + 16, C), bf16)]
        + [(size, bf16) for size in sizes],
        [pltpu.VMEM((2, 4 * span, C // 2), f32)],
        60 * WORK * span * C, 16 * span * C, "svv" + "v" * (T + 2),
    )(place, flat, vectors)
    head, grad_rows = call(
        functools.partial(head_kernel, 2 * J),
        [((R, 2 * J, C), bf16), (grad_rows.shape, bf16)],
        [], R * span * C, R * span * C, "avvv",
    )(kept, grad_rows)
    messages = [sends[0]] + [partners(sends[k], "tm", k) for k in range(1, T)]
    joined, cached, under = call(
        functools.partial(join_kernel, F, J, T),
        [
            ((2, 2 * part, T * span), bf16),
            ((2, 2, 2 * J, C), bf16),
            ((2, 2 * J + span, C), bf16),
        ],
        [pltpu.VMEM((2, T * span, 2 * part), bf16)],
        30 * WORK * span * C, 16 * span * C, "sv" + "v" * T + "vvv",
    )(place, planes, *messages)
    under = shifted(under, "rows", -1)
    following = shifted(head, "tm", -1)
    packed, frames_grad = call(
        functools.partial(slab_kernel, F, J, R, T, slot),
        [((R * slot, C), bf16), ((4 * span, C), bf16)],
        [
            pltpu.VMEM((27, C, C), bf16),
            pltpu.VMEM((2, 2, (F + 2) * J, C), bf16),
            pltpu.VMEM((3, 3, (F + 2) * J, C), bf16),
            pltpu.VMEM((2, 4 * span, C // 2), f32),
            pltpu.SemaphoreType.DMA((3,)),
        ],
        2 * 54 * span * C * C, 2 * 27 * C * C, "svvvhvvv" + "vv",
        limit=VMEM_LIMIT_WIDE,
    )(place, planes, cached, under, weight, kept, grad_rows, following)

    def after_slab(blocks):
        shapes = [(b.shape, bf16) for b in blocks]
        count = len(blocks)
        aliases = {n + 1: n for n in range(count)}
        return list(
            call(gate_kernel, shapes, [], 0, 0, "a" * (2 * count + 1), aliases)(packed, *blocks)
        )

    hidden_all = exchanged(joined, "rows", after_slab)
    grad_all = exchanged(grad_rows, "tm")

    packed = lax.all_to_all(packed.reshape(R, slot, C), "rows", 0, 0, tiled=True)
    latent = packed[:, :used].reshape(R, F, J // R, C).transpose(1, 0, 2, 3)
    gains = call(
        functools.partial(gain_kernel, T, used),
        [((1, part), f32)] * T,
        [], R * slot * C, R * slot * C, "v" + "a" * (R // 2) + "v" * T,
    )(packed, *hidden_all[1::2])
    gain_grad = gains[0]
    for k in range(1, T):
        gain_grad = gain_grad + partners(gains[k], "tm", k)

    grads, bias_sum = call(
        functools.partial(order_kernel, F, J, R, T),
        [((2, R, (F * T + 2) * J, C), bf16), ((1, part), f32)],
        [],
        90 * WORK * span * C, 2 * R * T * span * C, "s" + "v" * (T + 2),
    )(place, *grad_all)
    (weight_grad,) = call(
        functools.partial(weight_kernel, F, J, R, T, part),
        [((27, part, C), f32)],
        [
            pltpu.VMEM((27, part, C), f32),
            pltpu.VMEM((2 * part, (R + 1) * T * span), bf16),
            pltpu.VMEM((2 * part, R * T * span), bf16),
            pltpu.SemaphoreType.DMA((3,)),
        ],
        200 * WORK * span * C, 8 * 27 * part * C, "sav" + "v" * R + "h",
    )(place, gains[0], grads, *hidden_all)

    return (
        latent,
        frames_grad.reshape(frames.shape),
        weight_grad.reshape(3, 3, 3, part, C),
        gain_grad.reshape(part),
        bias_sum.reshape(part),
    )


def on_device(frames, norm_gain, conv_weight, conv_bias, latent_grad):
    rows, shares = lax.axis_size("rows"), lax.axis_size("tm")
    operand_bytes = 2 * rows * shares * (frames.size // shares + latent_grad.size)
    result_bytes = 4 * conv_weight.size
    powers = (rows & (rows - 1)) == 0 and (shares & (shares - 1)) == 0
    if powers and frames.shape[1] == 2 and operand_bytes <= result_bytes:
        form = gathered_form
    else:
        form = reduced_form
    return form(frames, norm_gain, conv_weight, conv_bias, latent_grad)


def solution(mesh):
    placed = (P("tm", "rows", None, None), P(), P(), P(), P("tm", None, "rows", None))
    return jax.shard_map(
        on_device,
        mesh=mesh,
        in_specs=placed,
        out_specs=(
            P("tm", None, "rows", None),
            P("tm", "rows", None, None),
            P(None, None, None, "tm", None),
            P("tm"),
            P("tm"),
        ),
        check_vma=False,
    )
```
